32 devices in a mesh: seq: 8 (over y, x, core), exp: 4 (over z).
Axes of the slice: x: 2, y: 2, z: 4, core: 2. Of those that a mesh axis runs over, the one named last changes fastest.
Arguments:
- inputs: bfloat16 [4, 1024, 768], P('exp', 'seq'), may hold values from -6 to 6
- encoder: bfloat16 [512, 768], replicated, may hold values from -6 to 6
- lengths: int32 [4, 8], P('exp'), may hold values from 1 to 960, as said below
- buckets: int32 [128], replicated, may hold values from 0 to 31, as said below
- routes: int32 [4, 1024, 1], P('exp', 'seq'), may hold values from 0 to 3
- norm_gains: float32 [3, 768], replicated, may hold values from 0.25 to 1.75
- self_qkv: bfloat16 [768, 2304], replicated, may hold values from -0.21875 to 0.21875
- self_out: bfloat16 [768, 768], replicated, may hold values from -1.75 to 1.75
- cross_q: bfloat16 [768, 768], replicated, may hold values from -0.21875 to 0.21875
- cross_kv: bfloat16 [768, 1536], replicated, may hold values from -0.21875 to 0.21875
- cross_out: bfloat16 [768, 768], replicated, may hold values from -1.75 to 1.75
- rel_bias: float32 [32, 12], replicated, may hold values from -4 to 4
- router: bfloat16 [768, 4], replicated, may hold values from -0.21875 to 0.21875
- expert_in: bfloat16 [4, 768, 3072], P('exp'), may hold values from -0.21875 to 0.21875
- expert_out: bfloat16 [4, 3072, 768], P('exp'), may hold values from -0.4375 to 0.4375
- cotangent: bfloat16 [4, 1024, 768], P('exp', 'seq'), may hold values from -6 to 6
Outputs:
- layer_out: bfloat16 [4, 1024, 768], P('exp', 'seq')
- grad_input: float32 [4, 1024, 768], P('exp', 'seq')
- grad_encoder: float32 [512, 768], P(('seq', 'exp'))
- grad_gains: float32 [3, 768], replicated
- grad_self_qkv: float32 [768, 2304], replicated
- grad_self_out: float32 [768, 768], replicated
- grad_cross_q: float32 [768, 768], replicated
- grad_cross_kv: float32 [768, 1536], replicated
- grad_cross_out: float32 [768, 768], replicated
- grad_rel_bias: float32 [32, 12], replicated
- grad_router: float32 [768, 4], replicated
- grad_expert_in: float32 [4, 768, 3072], P('exp', 'seq')
- grad_expert_out: float32 [4, 3072, 768], P('exp', 'seq')
The draws below stay inside these ranges and needn't reach their ends.
Inputs may be any that keep to these rules, and one draw needn't show every extreme that they name: In each group the 8 lengths sum to 1024; one of them, at a place drawn from the seed, is 960, and the others sum to 64. buckets[d] = d for d < 16; never falling in d; 31 at d = 127.
All inputs are finite; a program needn't handle non-finite values.
Results may differ from the reference program's by a relative error of at most 0.03.
Values may be sent and summed in bfloat16 or wider, within the bound.
A program may use at most 256 MiB of HBM per device.

```python
import math
import jax
import jax.numpy as jnp
from jax import lax

D = 768
H = 12
HD = 64
FF = 3072
NB = 32
DIST = 128
TOK_DEV = 128
DOCS = 8
ENC = 512
GROUPS = 4
STREAM = 1024
EXPERTS = 4
CAP = 40
N_SEQ = 8


def draw_lengths(key, part):
    key = jax.random.fold_in(key, 11)
    half_dev = TOK_DEV // 2

    def one_group(group_key):
        key_cut, key_mix, key_place = jax.random.split(group_key, 3)
        cut_points = jnp.sort(jax.random.permutation(key_cut, half_dev - 2)[:DOCS - 3] + 1).astype(jnp.int32)
        bounds = jnp.concatenate([jnp.zeros((1,), jnp.int32), cut_points, jnp.full((1,), half_dev - 1, jnp.int32)])
        shorts = jnp.concatenate([bounds[1:] - bounds[:-1], jnp.ones((1,), jnp.int32)])
        shorts = jax.random.permutation(key_mix, shorts)
        long_slot = jax.random.randint(key_place, (), 0, DOCS)
        positions = jnp.arange(DOCS)
        source = jnp.clip(jnp.where(positions > long_slot, positions - 1, positions), 0, DOCS - 2)
        return jnp.where(positions == long_slot, STREAM - half_dev, shorts[source]).astype(jnp.int32)
    return jax.vmap(one_group)(jax.random.split(key, GROUPS))


def draw_buckets(key, part):
    key = jax.random.fold_in(key, 23)
    steps_up = jax.random.randint(key, (DIST,), 0, 2)
    distance = jnp.arange(DIST)
    grown = NB // 2 - 1 + jnp.cumsum(jnp.where(distance >= NB // 2, steps_up, 0))
    stepped = jnp.where(distance < NB // 2, distance, jnp.minimum(grown, NB - 1))
    return jnp.where(distance == DIST - 1, NB - 1, stepped).astype(jnp.int32)


def steps_of(own_key, extent, shards, low, largest):
    def one(axis_at, shards_of):
        draws = jax.random.uniform(jax.random.fold_in(jax.random.fold_in(own_key, 6), axis_at), (shards_of,), jnp.float32, low / len(shards), largest / len(shards))
        return jnp.repeat(jnp.exp(draws), extent[axis_at] // shards_of).reshape((-1,) + (1,) * (len(extent) - axis_at - 1))

    level = one(*shards[0])
    for cut in shards[1:]:
        level = level * one(*cut)
    return level


def distinct(stream_key, rows, amount, top, lift):
    order = jax.random.permutation(jax.random.fold_in(stream_key, 1), amount)
    pull = order
    for power in range(3):
        pull = pull * pull // amount
    pull = pull * lift // amount
    lots = jax.random.randint(jax.random.fold_in(stream_key, 2), (rows, amount), 0, 4096) + pull
    fixed_rows = jax.random.permutation(jax.random.fold_in(stream_key, 3), rows)[jnp.arange(amount) % rows]
    lots = jnp.where(jnp.arange(rows)[:, None] == fixed_rows[None, :], 1 << 14, lots)
    score = lots * amount + jnp.arange(amount)
    return lax.top_k(score.astype(jnp.int32), top)[1].astype(jnp.int32)


def noise(rng, shape, width, limit, pieces=(), held_as=jnp.bfloat16):
    factor_of = steps_of(rng, shape, pieces, -0.22, 0.18) if pieces else 1.0
    array = jax.random.normal(rng, shape, jnp.float32) * width * factor_of
    return jnp.minimum(jnp.maximum(array, -limit), limit).astype(held_as)


def setup_inputs(seed: int = 0) -> dict:
    key_list = jax.random.split(jax.random.key(seed), 17)
    inputs = noise(key_list[0], (GROUPS, STREAM, D), 1.0, 6.0, ((0, 4), (1, 8)))
    encoder = noise(key_list[1], (ENC, D), 1.0, 6.0)
    lengths = draw_lengths(jax.random.fold_in(key_list[16], 71), 0)
    buckets = draw_buckets(jax.random.fold_in(key_list[16], 71), 0)
    routes = distinct(key_list[4], GROUPS * STREAM, EXPERTS, 1, 4096).reshape((GROUPS, STREAM, 1))
    norm_gains = jnp.clip(1.0 + 0.15 * jax.random.normal(key_list[5], (3, D), jnp.float32), 0.25, 1.75)
    self_qkv = noise(key_list[6], (D, 3 * D), D ** -0.5, 0.21875)
    self_out = noise(key_list[7], (D, D), (D // 64) ** -0.5, 1.75)
    cross_q = noise(key_list[8], (D, D), D ** -0.5, 0.21875)
    cross_kv = noise(key_list[9], (D, 2 * D), D ** -0.5, 0.21875)
    cross_out = noise(key_list[10], (D, D), (D // 64) ** -0.5, 1.75)
    rel_bias = noise(key_list[11], (NB, H), 1.0, 4.0, (), jnp.float32)
    router = noise(key_list[12], (D, EXPERTS), D ** -0.5, 0.21875)
    expert_in = noise(key_list[13], (EXPERTS, D, FF), D ** -0.5, 0.21875, ((0, 4),))
    expert_out = noise(key_list[14], (EXPERTS, FF, D), (FF // 16) ** -0.5, 0.4375, ((0, 4),))
    cotangent = noise(key_list[15], (GROUPS, STREAM, D), 1.0, 6.0, ((0, 4), (1, 8)))
    return {"inputs": inputs, "encoder": encoder, "lengths": lengths, "buckets": buckets, "routes": routes, "norm_gains": norm_gains, "self_qkv": self_qkv, "self_out": self_out, "cross_q": cross_q, "cross_kv": cross_kv, "cross_out": cross_out, "rel_bias": rel_bias, "router": router, "expert_in": expert_in, "expert_out": expert_out, "cotangent": cotangent}


@jax.custom_vjp
def low(v):
    return lax.optimization_barrier(v.astype(jnp.bfloat16)).astype(jnp.float32)

@jax.custom_vjp
def low_back(v):
    return v

def low_keep(v):
    return (low(v), None)

def low_pass(kept, grad):
    return (grad,)

def back_keep(v):
    return (v, None)

def back_low(kept, grad):
    return (low(grad),)
low.defvjp(low_keep, low_pass)
low_back.defvjp(back_keep, back_low)
epsilon = 1e-06
masked_out = -1e+30
highest = lax.Precision.HIGHEST

def rounded_both(value):
    return low(low_back(value))

def matmul(left, right):
    return jnp.dot(left, right, precision=highest)

def rms_norm(value, gain):
    return value * lax.rsqrt(lax.optimization_barrier(jnp.mean(value * value, axis=-1, keepdims=True)) + epsilon) * gain

def doc_index(positions, doc_ends):
    return lax.optimization_barrier(jnp.sum((positions[:, None] >= doc_ends[None, :]).astype(jnp.int32), axis=1))

def attend(queries, keys_all, values_all, adjust, block_rows):

    def one_block(block_id):
        offset = (block_id * block_rows).astype(jnp.int32)
        query_block = lax.dynamic_slice_in_dim(queries, offset, block_rows, 0)
        scores = jnp.einsum('qhd,khd->hqk', query_block, keys_all, precision=highest) * 0.125
        scores, allowed = adjust(scores, offset)
        scores = jnp.where(allowed, low_back(scores), masked_out)
        top_score = lax.optimization_barrier(jnp.max(scores, axis=-1, keepdims=True))
        weights_raw = jnp.where(allowed, jnp.exp(scores - top_score), 0.0)
        probability = weights_raw / lax.optimization_barrier(jnp.sum(weights_raw, axis=-1, keepdims=True))
        return jnp.einsum('hqk,khd->qhd', low(probability), values_all, precision=highest)
    blocks = lax.map(jax.checkpoint(one_block), jnp.arange(queries.shape[0] // block_rows).astype(jnp.int32))
    return blocks.reshape(queries.shape[0], -1)

def reference(inputs, encoder, lengths, buckets, routes, norm_gains, self_qkv, self_out, cross_q, cross_kv, cross_out, rel_bias, router, expert_in, expert_out, cotangent):
    block_rows = math.gcd(STREAM, 512)
    stream_pos = jnp.arange(STREAM).astype(jnp.int32)
    bucket_pick = (buckets[:, None] == jnp.arange(NB).astype(jnp.int32)[None, :]).astype(jnp.float32)
    expert_ids = jnp.arange(EXPERTS).astype(jnp.int32)

    def cross_adjust(scores, offset):
        return (scores, jnp.ones((1, 1, 1), dtype=bool))

    def forward(hidden, enc_rows, gains, w_qkv, w_self, w_query, w_pair, w_cross, rel_table, w_router, w_in, w_out):
        table = matmul(bucket_pick, rel_table).T
        enc_kv = rounded_both(matmul(enc_rows, w_pair))
        cross_keys = enc_kv[:, :D].reshape(ENC, H, HD)
        cross_values = enc_kv[:, D:].reshape(ENC, H, HD)
        results = []
        for group_id in range(GROUPS):
            doc_ids = doc_index(stream_pos, jnp.cumsum(lengths[group_id]).astype(jnp.int32))
            normed = low(rms_norm(hidden[group_id], gains[0]))
            qkv_all = rounded_both(matmul(normed, w_qkv))
            queries = qkv_all[:, :D].reshape(STREAM, H, HD)
            keys_all = qkv_all[:, D:2 * D].reshape(STREAM, H, HD)
            values_all = qkv_all[:, 2 * D:].reshape(STREAM, H, HD)

            def self_adjust(scores, offset, doc_ids=doc_ids, table=table):
                query_pos = offset + jnp.arange(block_rows).astype(jnp.int32)
                distance = jnp.clip(query_pos[:, None] - stream_pos[None, :], 0, DIST - 1)
                query_doc = lax.dynamic_slice_in_dim(doc_ids, offset, block_rows, 0)
                allowed = (stream_pos[None, :] <= query_pos[:, None]) & (doc_ids[None, :] == query_doc[:, None])
                return (scores + jnp.take(table, distance, axis=1), allowed[None])
            attended = rounded_both(attend(queries, keys_all, values_all, self_adjust, block_rows))
            after_self = hidden[group_id] + low_back(matmul(attended, w_self))
            normed_two = low(rms_norm(after_self, gains[1]))
            cross_queries = rounded_both(matmul(normed_two, w_query)).reshape(STREAM, H, HD)
            cross_att = rounded_both(attend(cross_queries, cross_keys, cross_values, cross_adjust, block_rows))
            after_cross = after_self + low_back(matmul(cross_att, w_cross))
            routed_in = low(rms_norm(after_cross, gains[2]))
            gates = jax.nn.softmax(matmul(routed_in, w_router), axis=-1)
            chosen = routes[group_id, :, 0][:, None] == expert_ids[None, :]
            running = jnp.cumsum(chosen.reshape(N_SEQ, TOK_DEV, EXPERTS).astype(jnp.int32), axis=1).reshape(STREAM, EXPERTS)
            slots = lax.optimization_barrier(jnp.sum(jnp.where(chosen, running, 0), axis=1)) - 1
            weight = lax.optimization_barrier(jnp.sum(jnp.where(chosen, gates, 0.0), axis=1)) * (slots < CAP).astype(jnp.float32)
            expert_x = low_back(routed_in)
            merged = jnp.zeros((STREAM, D), jnp.float32)
            for expert_id in range(EXPERTS):
                inner_pre = low_back(matmul(expert_x, w_in[expert_id]))
                active = low(jax.nn.gelu(inner_pre, approximate=True))
                merged = merged + jnp.where(chosen[:, expert_id:expert_id + 1], rounded_both(matmul(active, w_out[expert_id])), 0.0)
            results.append(after_cross + weight[:, None] * merged)
        return jnp.stack(results)
    floats = [argument.astype(jnp.float32) for argument in (inputs, encoder, norm_gains, self_qkv, self_out, cross_q, cross_kv, cross_out, rel_bias, router, expert_in, expert_out)]
    layer_out, pull_back = jax.vjp(forward, *floats)
    gradients = pull_back(cotangent.astype(jnp.float32))
    return (layer_out.astype(jnp.bfloat16), gradients[0], gradients[1], gradients[2], gradients[3], gradients[4], gradients[5], gradients[6], gradients[7], gradients[8], gradients[9], gradients[10], gradients[11])
```

```python
import functools
import math

import jax
import jax.numpy as jnp
from jax import lax
from jax.experimental import pallas as pl
from jax.experimental.pallas import tpu as pltpu
from jax.sharding import PartitionSpec as P

H = 12
HD = 64


epsilon = 1e-06
masked_out = -1e30
highest = lax.Precision.HIGHEST


def rms_norm(value, gain):
    return value * lax.rsqrt(jnp.mean(value * value, axis=-1, keepdims=True) + epsilon) * gain


def split_heads(value):
    return value.reshape(value.shape[0], H, HD)


def doc_index(positions, doc_ends):
    return jnp.sum((positions[:, None] >= doc_ends[None, :]).astype(jnp.int32), axis=1)


def band_pick(offset_gap, query_rows, key_rows, table_span):
    band_len = query_rows + key_rows + 1
    column = jnp.arange(band_len, dtype=jnp.int32)
    distance = jnp.clip(offset_gap + query_rows - column, 0, table_span - 1)
    return (distance[:, None] == jnp.arange(table_span, dtype=jnp.int32)[None, :]).astype(
        jnp.float32
    )


def relative_bias(table, offset_gap, query_rows, key_rows):
    head_count = table.shape[0]
    band_len = query_rows + key_rows + 1
    band = jnp.dot(
        table, band_pick(offset_gap, query_rows, key_rows, table.shape[1]).T, precision=highest
    )
    tiled = jnp.broadcast_to(band[:, None, :], (head_count, query_rows, band_len)).reshape(
        head_count, query_rows * band_len
    )
    skewed = tiled[:, : query_rows * (band_len - 1)].reshape(head_count, query_rows, band_len - 1)
    return skewed[:, :, query_rows : query_rows + key_rows]


def table_terms(score_grads, offset_gap, table_span):
    head_count, query_rows, key_rows = score_grads.shape
    band_len = query_rows + key_rows + 1
    placed = jnp.pad(score_grads.astype(jnp.float32), ((0, 0), (0, 0), (query_rows, 0)))
    flat = jnp.pad(
        placed.reshape(head_count, query_rows * (band_len - 1)), ((0, 0), (0, query_rows))
    )
    diagonal_sums = jnp.sum(flat.reshape(head_count, query_rows, band_len), axis=1)
    return jnp.dot(
        diagonal_sums, band_pick(offset_gap, query_rows, key_rows, table_span), precision=highest
    )


def self_scores(queries, query_start, keys_part, key_start, doc_ends, table):
    query_rows = queries.shape[0]
    key_rows = keys_part.shape[0]
    query_pos = query_start + jnp.arange(query_rows, dtype=jnp.int32)
    key_pos = key_start + jnp.arange(key_rows, dtype=jnp.int32)
    offset_gap = query_start - key_start
    raw_scores = (
        jnp.einsum(
            "qhd,khd->hqk",
            split_heads(queries),
            split_heads(keys_part),
            preferred_element_type=jnp.float32,
        )
        * 0.125
    )
    allowed = (key_pos[None, :] <= query_pos[:, None]) & (
        doc_index(key_pos, doc_ends)[None, :] == doc_index(query_pos, doc_ends)[:, None]
    )
    scores = jnp.where(
        allowed[None],
        raw_scores + relative_bias(table, offset_gap, query_rows, key_rows),
        masked_out,
    )
    return (scores, allowed[None], offset_gap)


def over_blocks(step, running, pieces):
    rows_total = pieces[0].shape[0]
    block_rows = math.gcd(rows_total, 512)
    block_count = rows_total // block_rows
    stacked = tuple(
        (member.reshape(block_count, block_rows, *member.shape[1:]) for member in pieces)
    )

    def scan_step(inner_running, block_input):
        block_id, members = block_input
        return (step(inner_running, members, block_id * block_rows), None)

    result, ignored = lax.scan(
        scan_step, running, (jnp.arange(block_count, dtype=jnp.int32), stacked)
    )
    return result


def streamed(
    inputs,
    encoder,
    lengths,
    buckets,
    routes,
    norm_gains,
    self_qkv,
    self_out,
    cross_q,
    cross_kv,
    cross_out,
    rel_bias,
    router,
    expert_in,
    expert_out,
    cotangent,
):
    hidden = inputs[0].astype(jnp.float32)
    rows_dev = hidden.shape[0]
    model_width = hidden.shape[1]
    seq_count = lax.axis_size("seq")
    seq_index = lax.axis_index("seq")
    own_start = seq_index * rows_dev
    doc_ends = jnp.cumsum(lengths[0])
    bucket_pick = (
        buckets[:, None] == jnp.arange(rel_bias.shape[0], dtype=jnp.int32)[None, :]
    ).astype(jnp.float32)
    table = jnp.dot(bucket_pick, rel_bias, precision=highest).T
    normed_one, norm_one_back = jax.vjp(rms_norm, hidden, norm_gains[0])
    normed_one = normed_one.astype(jnp.bfloat16)
    qkv_all = jnp.dot(normed_one, self_qkv, preferred_element_type=jnp.float32).astype(jnp.bfloat16)
    queries = qkv_all[:, :model_width]
    keys_own = qkv_all[:, model_width : 2 * model_width]
    values_own = qkv_all[:, 2 * model_width :]

    def forward_step(running, pieces, key_start):
        top_old, denominator, summed = running
        keys_part, values_part = pieces
        scores, allowed, offset_gap = self_scores(
            queries, own_start, keys_part, key_start, doc_ends, table
        )
        top_new = jnp.maximum(top_old, jnp.max(scores, axis=-1))
        weights_raw = jnp.where(allowed, jnp.exp(scores - top_new[..., None]), 0.0)
        rescale = jnp.exp(top_old - top_new)
        denominator = denominator * rescale + jnp.sum(weights_raw, axis=-1)
        summed = summed * rescale[..., None] + jnp.einsum(
            "hqk,khd->hqd",
            weights_raw.astype(jnp.bfloat16),
            split_heads(values_part),
            preferred_element_type=jnp.float32,
        )
        return (top_new, denominator, summed)

    start_state = (
        jnp.full((H, rows_dev), masked_out, jnp.float32),
        jnp.zeros((H, rows_dev), jnp.float32),
        jnp.zeros((H, rows_dev, HD), jnp.float32),
    )
    top_score, denominator, summed = over_blocks(
        forward_step,
        start_state,
        (
            lax.all_gather(keys_own, "seq", axis=0, tiled=True),
            lax.all_gather(values_own, "seq", axis=0, tiled=True),
        ),
    )
    log_total = top_score + jnp.log(denominator)
    attended_full = (
        (summed / denominator[..., None]).transpose(1, 0, 2).reshape(rows_dev, model_width)
    )
    attended = attended_full.astype(jnp.bfloat16)
    after_self = hidden + jnp.dot(attended, self_out, preferred_element_type=jnp.float32)
    enc_kv = jnp.dot(encoder, cross_kv, preferred_element_type=jnp.float32).astype(jnp.bfloat16)
    cross_keys = split_heads(enc_kv[:, :model_width])
    cross_values = split_heads(enc_kv[:, model_width:])
    normed_two, norm_two_back = jax.vjp(rms_norm, after_self, norm_gains[1])
    normed_two = normed_two.astype(jnp.bfloat16)
    cross_queries = jnp.dot(normed_two, cross_q, preferred_element_type=jnp.float32).astype(
        jnp.bfloat16
    )
    cross_scores = (
        jnp.einsum(
            "qhd,khd->hqk",
            split_heads(cross_queries),
            cross_keys,
            preferred_element_type=jnp.float32,
        )
        * 0.125
    )
    cross_raw = jnp.exp(cross_scores - jnp.max(cross_scores, axis=-1, keepdims=True))
    cross_prob = cross_raw / jnp.sum(cross_raw, axis=-1, keepdims=True)
    cross_prob_low = cross_prob.astype(jnp.bfloat16)
    cross_att = (
        jnp.einsum("hqk,khd->qhd", cross_prob_low, cross_values, preferred_element_type=jnp.float32)
        .reshape(rows_dev, model_width)
        .astype(jnp.bfloat16)
    )
    after_cross = after_self + jnp.dot(cross_att, cross_out, preferred_element_type=jnp.float32)
    normed_three, norm_three_back = jax.vjp(rms_norm, after_cross, norm_gains[2])
    routed_in = normed_three.astype(jnp.bfloat16)
    gates = jax.nn.softmax(jnp.dot(routed_in, router, preferred_element_type=jnp.float32), axis=-1)
    expert_total = router.shape[1]
    local_experts = expert_in.shape[0]
    capacity = 5 * rows_dev // (4 * expert_total)
    route_ids = routes[0, :, 0]
    chosen = route_ids[:, None] == jnp.arange(expert_total, dtype=jnp.int32)[None, :]
    slots = jnp.sum(jnp.where(chosen, jnp.cumsum(chosen.astype(jnp.int32), axis=0), 0), axis=1) - 1
    kept = slots < capacity
    picked_gate = jnp.sum(jnp.where(chosen, gates, 0.0), axis=1)
    gate_used = picked_gate * kept.astype(jnp.float32)
    target = jnp.where(kept, route_ids * capacity + slots, -1)
    dispatch = (
        jnp.arange(expert_total * capacity, dtype=jnp.int32)[:, None] == target[None, :]
    ).astype(jnp.bfloat16)
    outgoing = (
        jnp.dot(dispatch, routed_in, preferred_element_type=jnp.float32)
        .astype(jnp.bfloat16)
        .reshape(expert_total, capacity, model_width)
    )
    arrived = lax.all_to_all(outgoing, "exp", split_axis=0, concat_axis=0, tiled=True).reshape(
        -1, local_experts, capacity, model_width
    )
    inner_pre = jnp.einsum("secd,edf->secf", arrived, expert_in, preferred_element_type=jnp.float32)
    active = jax.nn.gelu(inner_pre, approximate=True).astype(jnp.bfloat16)
    produced = jnp.einsum(
        "secf,efd->secd", active, expert_out, preferred_element_type=jnp.float32
    ).astype(jnp.bfloat16)
    returned = lax.all_to_all(
        produced.reshape(-1, capacity, model_width), "exp", split_axis=0, concat_axis=0, tiled=True
    )
    expert_rows = jnp.dot(
        dispatch.T, returned.reshape(-1, model_width), preferred_element_type=jnp.float32
    )
    layer_out = after_cross + gate_used[:, None] * expert_rows
    upstream = cotangent[0].astype(jnp.float32)
    made_grad = (upstream * gate_used[:, None]).astype(jnp.bfloat16)
    sent_grad = (
        jnp.dot(dispatch, made_grad, preferred_element_type=jnp.float32)
        .astype(jnp.bfloat16)
        .reshape(expert_total, capacity, model_width)
    )
    grad_arrived = lax.all_to_all(
        sent_grad, "exp", split_axis=0, concat_axis=0, tiled=True
    ).reshape(-1, local_experts, capacity, model_width)
    inner_again = jnp.einsum(
        "secd,edf->secf", arrived, expert_in, preferred_element_type=jnp.float32
    )
    active_again, gelu_back = jax.vjp(
        lambda value: jax.nn.gelu(value, approximate=True), inner_again
    )
    grad_out_w = jnp.einsum(
        "secf,secd->efd",
        active_again.astype(jnp.bfloat16),
        grad_arrived,
        preferred_element_type=jnp.float32,
    )
    grad_active = jnp.einsum(
        "secd,efd->secf", grad_arrived, expert_out, preferred_element_type=jnp.float32
    )
    grad_inner = gelu_back(grad_active)[0].astype(jnp.bfloat16)
    grad_in_w = jnp.einsum(
        "secd,secf->edf", arrived, grad_inner, preferred_element_type=jnp.float32
    )
    grad_sent_x = jnp.einsum(
        "secf,edf->secd", grad_inner, expert_in, preferred_element_type=jnp.float32
    ).astype(jnp.bfloat16)
    grad_back = lax.all_to_all(
        grad_sent_x.reshape(-1, capacity, model_width),
        "exp",
        split_axis=0,
        concat_axis=0,
        tiled=True,
    )
    grad_routed = jnp.dot(
        dispatch.T, grad_back.reshape(-1, model_width), preferred_element_type=jnp.float32
    )
    expert_sums = (
        lax.psum_scatter(grad_in_w, "seq", scatter_dimension=1, tiled=True),
        lax.psum_scatter(grad_out_w, "seq", scatter_dimension=1, tiled=True),
    )
    gate_grad = jnp.sum(upstream * expert_rows, axis=1) * kept.astype(jnp.float32)
    logit_grad = gates * (
        jnp.where(chosen, gate_grad[:, None], 0.0) - (picked_gate * gate_grad)[:, None]
    )
    router_grad = jnp.dot(routed_in.astype(jnp.float32).T, logit_grad, precision=highest)
    grad_normed_three = (
        jnp.dot(logit_grad, router.astype(jnp.float32).T, precision=highest) + grad_routed
    )
    grad_after_cross, gain_three = norm_three_back(grad_normed_three)
    grad_after_cross = grad_after_cross + upstream
    cross_branch = grad_after_cross.astype(jnp.bfloat16)
    cross_out_grad = jnp.dot(cross_att.T, cross_branch, preferred_element_type=jnp.float32)
    grad_cross_att = split_heads(
        jnp.dot(cross_branch, cross_out.T, preferred_element_type=jnp.float32).astype(jnp.bfloat16)
    )
    cross_prob_grad = jnp.einsum(
        "qhd,khd->hqk", grad_cross_att, cross_values, preferred_element_type=jnp.float32
    )
    cross_delta = jnp.sum(cross_prob * cross_prob_grad, axis=-1, keepdims=True)
    cross_score_grad = (cross_prob * (cross_prob_grad - cross_delta)).astype(jnp.bfloat16)
    grad_cross_queries = (
        (
            jnp.einsum(
                "hqk,khd->qhd", cross_score_grad, cross_keys, preferred_element_type=jnp.float32
            )
            * 0.125
        )
        .reshape(rows_dev, model_width)
        .astype(jnp.bfloat16)
    )
    grad_enc_keys = (
        jnp.einsum(
            "hqk,qhd->khd",
            cross_score_grad,
            split_heads(cross_queries),
            preferred_element_type=jnp.float32,
        )
        * 0.125
    )
    grad_enc_values = jnp.einsum(
        "hqk,qhd->khd", cross_prob_low, grad_cross_att, preferred_element_type=jnp.float32
    )
    enc_terms = jnp.concatenate(
        [grad_enc_keys.reshape(-1, model_width), grad_enc_values.reshape(-1, model_width)], axis=1
    )
    enc_grad_rows = lax.psum_scatter(
        enc_terms, ("seq", "exp"), scatter_dimension=0, tiled=True
    ).astype(jnp.bfloat16)
    enc_count = enc_grad_rows.shape[0]
    flat_index = seq_index * lax.axis_size("exp") + lax.axis_index("exp")
    own_enc = lax.dynamic_slice_in_dim(encoder, flat_index * enc_count, enc_count, 0)
    grad_encoder = jnp.dot(enc_grad_rows, cross_kv.T, preferred_element_type=jnp.float32)
    pair_grad = jnp.dot(own_enc.T, enc_grad_rows, preferred_element_type=jnp.float32)
    query_w_grad = jnp.dot(normed_two.T, grad_cross_queries, preferred_element_type=jnp.float32)
    grad_normed_two = jnp.dot(grad_cross_queries, cross_q.T, preferred_element_type=jnp.float32)
    grad_after_self, gain_two = norm_two_back(grad_normed_two)
    grad_after_self = grad_after_self + grad_after_cross
    self_branch = grad_after_self.astype(jnp.bfloat16)
    self_out_grad = jnp.dot(attended.T, self_branch, preferred_element_type=jnp.float32)
    grad_attended = jnp.dot(self_branch, self_out.T, preferred_element_type=jnp.float32).astype(
        jnp.bfloat16
    )
    row_delta = jnp.sum(
        split_heads(grad_attended).astype(jnp.float32) * split_heads(attended_full), axis=-1
    ).T
    stats_all = (
        lax.all_gather(log_total.T, "seq", axis=0, tiled=True),
        lax.all_gather(row_delta.T, "seq", axis=0, tiled=True),
    )

    def query_step(running, pieces, query_start):
        kv_grad, query_grads, table_grad = running
        queries_part, grads_part = pieces
        piece_rows = queries_part.shape[0]
        lse_part = lax.dynamic_slice_in_dim(stats_all[0], query_start, piece_rows, 0).T
        delta_part = lax.dynamic_slice_in_dim(stats_all[1], query_start, piece_rows, 0).T
        scores, allowed, offset_gap = self_scores(
            queries_part, query_start, keys_own, own_start, doc_ends, table
        )
        probability = jnp.where(allowed, jnp.exp(scores - lse_part[..., None]), 0.0)
        prob_grad = jnp.einsum(
            "qhd,khd->hqk",
            split_heads(grads_part),
            split_heads(values_own),
            preferred_element_type=jnp.float32,
        )
        score_grad = (probability * (prob_grad - delta_part[..., None])).astype(jnp.bfloat16)
        key_grad = (
            jnp.einsum(
                "hqk,qhd->khd",
                score_grad,
                split_heads(queries_part),
                preferred_element_type=jnp.float32,
            )
            * 0.125
        )
        value_grad = jnp.einsum(
            "hqk,qhd->khd",
            probability.astype(jnp.bfloat16),
            split_heads(grads_part),
            preferred_element_type=jnp.float32,
        )
        kv_grad = kv_grad + jnp.concatenate(
            [key_grad.reshape(-1, model_width), value_grad.reshape(-1, model_width)], axis=1
        )
        table_grad = table_grad + table_terms(score_grad, offset_gap, table.shape[1])
        query_part_grad = jnp.einsum(
            "hqk,khd->qhd", score_grad, split_heads(keys_own), preferred_element_type=jnp.float32
        ).reshape(piece_rows, model_width)
        current = lax.dynamic_slice_in_dim(query_grads, query_start, piece_rows, 0)
        query_grads = lax.dynamic_update_slice_in_dim(
            query_grads, current + query_part_grad, query_start, 0
        )
        return (kv_grad, query_grads, table_grad)

    back_start = (
        jnp.zeros((rows_dev, 2 * model_width), jnp.float32),
        jnp.zeros((seq_count * rows_dev, model_width), jnp.float32),
        jnp.zeros(table.shape, jnp.float32),
    )
    kv_grad, query_buffer, table_grad = over_blocks(
        query_step,
        back_start,
        (
            lax.all_gather(queries, "seq", axis=0, tiled=True),
            lax.all_gather(grad_attended, "seq", axis=0, tiled=True),
        ),
    )
    query_grad = lax.psum_scatter(query_buffer, "seq", scatter_dimension=0, tiled=True)
    qkv_grad = jnp.concatenate(
        [(query_grad * 0.125).astype(jnp.bfloat16), kv_grad.astype(jnp.bfloat16)], axis=1
    )
    qkv_w_grad = jnp.dot(normed_one.T, qkv_grad, preferred_element_type=jnp.float32)
    grad_normed_one = jnp.dot(qkv_grad, self_qkv.T, preferred_element_type=jnp.float32)
    grad_hidden, gain_one = norm_one_back(grad_normed_one)
    grad_input = grad_hidden + grad_after_self
    rel_grad = jnp.dot(bucket_pick.T, table_grad.T, precision=highest)
    summed_grads = lax.psum(
        (
            jnp.stack([gain_one, gain_two, gain_three]),
            qkv_w_grad,
            self_out_grad,
            query_w_grad,
            pair_grad,
            cross_out_grad,
            rel_grad,
            router_grad,
        ),
        ("seq", "exp"),
    )
    return (
        layer_out.astype(jnp.bfloat16)[None],
        grad_input[None],
        grad_encoder,
        summed_grads[0],
        summed_grads[1],
        summed_grads[2],
        summed_grads[3],
        summed_grads[4],
        summed_grads[5],
        summed_grads[6],
        summed_grads[7],
        expert_sums[0],
        expert_sums[1],
    )


F32 = jnp.float32
BF16 = jnp.bfloat16
MESH = pl.DeviceIdType.MESH
ANY = pl.BlockSpec(memory_space=pl.ANY)
VMEM = pl.BlockSpec(memory_space=pltpu.VMEM)
SMEM = pl.BlockSpec(memory_space=pltpu.SMEM)
LANES = 128


def nn(a, b):
    return lax.dot_general(a, b, (((1,), (0,)), ((), ())), preferred_element_type=F32)


def nt(a, b):
    return lax.dot_general(a, b, (((1,), (1,)), ((), ())), preferred_element_type=F32)


def tn(a, b):
    return lax.dot_general(a, b, (((0,), (0,)), ((), ())), preferred_element_type=F32)


def rms_scale(a):
    return lax.rsqrt(jnp.mean(a * a, axis=-1, keepdims=True) + epsilon)


def pair_lanes(p):
    return pl.ds(pl.multiple_of(p * LANES, LANES), LANES)


def head_stack(pair):
    lane = lax.broadcasted_iota(jnp.int32, pair.shape, 1)
    zero = jnp.zeros_like(pair)
    return jnp.concatenate([jnp.where(lane < HD, pair, zero), jnp.where(lane < HD, zero, pair)], axis=0)


def head_unstack(both, rows):
    feature = lax.broadcasted_iota(jnp.int32, (both.shape[0], rows), 0)
    return jnp.where(feature < HD, both[:, :rows], both[:, rows:]).T


def seq_peers(seq_index, chips):
    core = lax.rem(seq_index, 2)
    chip = lax.div(seq_index, 2)
    partner = seq_index + 1 - 2 * core
    others = [lax.rem(chip + d, chips) * 2 + core for d in range(1, chips)]
    sources = [lax.rem(chip - d + chips, chips) * 2 + core for d in range(1, chips)]
    return core, chip, partner, others, sources


def enter(devices):
    barrier = pltpu.get_barrier_semaphore()
    for device in devices:
        pl.semaphore_signal(barrier, inc=1, device_id=device, device_id_type=MESH)
    pl.semaphore_wait(barrier, len(devices))


def remote(src, dst, send_sem, recv_sem, device):
    return pltpu.make_async_remote_copy(
        src_ref=src, dst_ref=dst, send_sem=send_sem, recv_sem=recv_sem, device_id=device, device_id_type=MESH
    )


def forward_kernel(
    seq_count, capacity, stride,
    x_ref, encoder_hbm, lengths_ref, buckets_ref, routes_ref, gains_ref, qkv_hbm, self_out_hbm, cross_q_hbm,
    cross_kv_hbm, cross_out_hbm, rel_ref, router_ref, g_ref,
    n1_hbm, kv_hbm, p_hbm, pc_hbm, ekv_hbm, q_ref, o_ref, n2_ref, qc_ref, oc_ref, x3_ref, r1_ref, r2_ref, gates_ref,
    place_ref, xs_ref, dms_ref,
    n1_all, kv_all, prob, cross_prob, ekv, scores, mask, w_qkv, w_self, w_cq, w_ckv, w_co, enc, table_ref,
    load_sem, store_sem, send_sem, recv_sem,
):
    chips = seq_count // 2
    rows, width = x_ref.shape
    span = seq_count * rows
    pairs = width // LANES
    me = lax.axis_index("seq")
    core, chip, partner, others, sources = seq_peers(me, chips)

    loads = [
        pltpu.make_async_copy(src, dst, load_sem.at[i])
        for i, (src, dst) in enumerate(
            [(qkv_hbm, w_qkv), (cross_kv_hbm, w_ckv), (encoder_hbm, enc), (self_out_hbm, w_self), (cross_q_hbm, w_cq),
             (cross_out_hbm, w_co)]
        )
    ]
    for load in loads:
        load.start()
    x = x_ref[...].astype(F32)
    n1_all[me] = (x * rms_scale(x) * gains_ref[0:1, :]).astype(BF16)
    enter([{"seq": partner}] + [{"seq": other} for other in others])
    own = remote(n1_all.at[me], n1_all.at[me], send_sem.at[0], recv_sem.at[0], {"seq": partner})
    direct = [
        remote(n1_all.at[me], n1_all.at[me], send_sem.at[d], recv_sem.at[d], {"seq": others[d - 1]})
        for d in range(1, chips)
    ]
    own.start()
    for copy in direct:
        copy.start()

    loads[0].wait()
    q = nn(n1_all[me], w_qkv[:, :width]).astype(BF16)
    q_ref[...] = q * jnp.asarray(0.125, BF16)
    loads[1].wait()
    loads[2].wait()
    ekv[...] = nn(enc[...], w_ckv[...]).astype(BF16)
    store_ekv = pltpu.make_async_copy(ekv, ekv_hbm, store_sem.at[0])
    store_ekv.start()
    pick = (buckets_ref[...] == lax.broadcasted_iota(jnp.int32, (rel_ref.shape[0], LANES), 0)).astype(F32)
    table = lax.dot_general(
        rel_ref[...], pick, (((0,), (0,)), ((), ())), precision=highest, preferred_element_type=F32
    )
    table = table - table[:, LANES - 1 :]
    table_ref[...] = jnp.concatenate([jnp.zeros_like(table), table], axis=1)
    query_pos = me * rows + lax.broadcasted_iota(jnp.int32, (1, rows), 1)
    start = jnp.zeros((1, rows), jnp.int32)
    end = jnp.int32(0)
    for i in range(lengths_ref.shape[1]):
        end = end + lengths_ref[0, i]
        start = jnp.where(end <= query_pos, end, start)
    key_pos = lax.broadcasted_iota(jnp.int32, (span, rows), 0)
    seen = jnp.where((key_pos >= start) & (key_pos <= query_pos), 0.0, masked_out)
    mask[...] = jnp.concatenate([seen, seen], axis=1)

    forwards = []
    for d in range(1, chips):
        direct[d - 1].wait_recv()
        block = n1_all.at[sources[d - 1]]
        forward = remote(
            block, block, send_sem.at[chips - 1 + d], recv_sem.at[chips - 1 + d], {"seq": partner}
        )
        forward.start()
        forwards.append(forward)
    own.wait_recv()
    for forward in forwards:
        forward.wait_recv()
    store_n1 = pltpu.make_async_copy(n1_all, n1_hbm, store_sem.at[1])
    store_n1.start()

    @pl.loop(0, chips)
    def _(c):
        part = n1_all[pl.ds(c * 2, 2)].reshape(2 * rows, width)
        at = pl.ds(pl.multiple_of(c * 2 * rows, 2 * rows), 2 * rows)
        kv_all[at, :] = nn(part, w_qkv[:, width:]).astype(BF16)

    store_kv = pltpu.make_async_copy(kv_all, kv_hbm, store_sem.at[2])
    store_kv.start()

    near = pl.ds(pl.multiple_of(me * rows, rows), 2 * rows)

    @pl.loop(0, pairs)
    def _(p):
        lanes = pair_lanes(p)
        q_both = head_stack(q_ref[:, lanes])
        scores[pl.ds(rows, span), :] = nt(kv_all[:, lanes], q_both) + mask[...]
        biases = []
        for h in range(2):
            band = jnp.broadcast_to(table_ref[pl.ds(2 * p + h, 1), :], (2 * rows, 2 * LANES))
            biases.append(pltpu.roll(band, 0, 1, stride=1, stride_axis=0)[:, :rows])
        scores[near, :] = scores[near, :] + jnp.concatenate(biases, axis=1)
        s = scores[pl.ds(rows, span), :]
        weights = jnp.exp(s - jnp.max(s, axis=0, keepdims=True))
        weights = (weights * (1.0 / jnp.sum(weights, axis=0, keepdims=True))).astype(BF16)
        prob[p] = weights
        both = tn(kv_all[:, pair_lanes(pairs + p)], weights)
        o_ref[:, lanes] = head_unstack(both, rows).astype(BF16)

    store_p = pltpu.make_async_copy(prob, p_hbm, store_sem.at[3])
    store_p.start()
    loads[3].wait()
    loads[4].wait()
    loads[5].wait()
    r1 = x_ref[...].astype(F32) + nn(o_ref[...], w_self[...])
    r1_ref[...] = r1
    n2 = (r1 * rms_scale(r1) * gains_ref[1:2, :]).astype(BF16)
    n2_ref[...] = n2
    qc_ref[...] = nn(n2, w_cq[...]).astype(BF16) * jnp.asarray(0.125, BF16)

    @pl.loop(0, pairs)
    def _(p):
        lanes = pair_lanes(p)
        s = nt(ekv[:, lanes], head_stack(qc_ref[:, lanes]))
        weights = jnp.exp(s - jnp.max(s, axis=0, keepdims=True))
        weights = (weights * (1.0 / jnp.sum(weights, axis=0, keepdims=True))).astype(BF16)
        cross_prob[p] = weights
        both = tn(ekv[:, pair_lanes(pairs + p)], weights)
        oc_ref[:, lanes] = head_unstack(both, rows).astype(BF16)

    store_pc = pltpu.make_async_copy(cross_prob, pc_hbm, store_sem.at[4])
    store_pc.start()
    r2 = r1_ref[...] + nn(oc_ref[...], w_co[...])
    r2_ref[...] = r2
    x3 = (r2 * rms_scale(r2) * gains_ref[2:3, :]).astype(BF16)
    x3_ref[...] = x3
    experts = router_ref.shape[1]
    logits = nn(x3, router_ref[...])
    top = jnp.exp(logits - jnp.max(logits, axis=-1, keepdims=True))
    gates = top / jnp.sum(top, axis=-1, keepdims=True)
    gates_ref[...] = gates
    route = routes_ref[...]
    chosen = (route == lax.broadcasted_iota(jnp.int32, (rows, experts), 1)).astype(F32)
    earlier = (
        lax.broadcasted_iota(jnp.int32, (rows, rows), 1) < lax.broadcasted_iota(jnp.int32, (rows, rows), 0)
    ).astype(BF16)
    slot = jnp.sum(nn(earlier, chosen.astype(BF16)) * chosen, axis=1, keepdims=True).astype(jnp.int32)
    kept = slot < capacity
    gate_used = jnp.sum(gates * chosen, axis=1, keepdims=True) * kept.astype(F32)
    target = jnp.where(kept, route * stride + slot, -1)
    place = (
        lax.broadcasted_iota(jnp.int32, (rows, experts * stride), 1) == target
    ).astype(BF16)
    place_ref[...] = place
    xs_ref[...] = tn(place, x3).astype(BF16)
    made_grad = (g_ref[...].astype(F32) * gate_used).astype(BF16)
    dms_ref[...] = tn(place, made_grad).astype(BF16)

    own.wait_send()
    for copy in direct + forwards:
        copy.wait_send()
    for store in (store_ekv, store_n1, store_kv, store_p, store_pc):
        store.wait()


def forward_call(seq_count, capacity, stride, x, encoder, lengths, buckets, routes, gains, w_qkv, w_self, w_cq, w_ckv,
                 w_co, rel, router, g):
    rows, width = x.shape
    span = seq_count * rows
    pairs = width // LANES
    enc_rows = encoder.shape[0]
    experts = router.shape[1]
    chips = seq_count // 2
    shape = jax.ShapeDtypeStruct
    wide = shape((rows, width), BF16)
    outs = (
        shape((seq_count, rows, width), BF16), shape((span, 2 * width), BF16), shape((pairs, span, 2 * rows), BF16),
        shape((pairs, enc_rows, 2 * rows), BF16), shape((enc_rows, 2 * width), BF16), wide, wide, wide, wide, wide, wide,
        shape((rows, width), F32), shape((rows, width), F32), shape((rows, experts), F32),
        shape((rows, experts * stride), BF16), shape((experts * stride, width), BF16), shape((experts * stride, width), BF16),
    )
    return pl.pallas_call(
        functools.partial(forward_kernel, seq_count, capacity, stride),
        out_shape=outs,
        in_specs=[VMEM, ANY, SMEM, VMEM, VMEM, VMEM, ANY, ANY, ANY, ANY, ANY, VMEM, VMEM, VMEM],
        out_specs=tuple([ANY] * 5 + [VMEM] * 12),
        scratch_shapes=[
            pltpu.VMEM((seq_count, rows, width), BF16), pltpu.VMEM((span, 2 * width), BF16),
            pltpu.VMEM((pairs, span, 2 * rows), BF16), pltpu.VMEM((pairs, enc_rows, 2 * rows), BF16),
            pltpu.VMEM((enc_rows, 2 * width), BF16), pltpu.VMEM((span + rows, 2 * rows), F32),
            pltpu.VMEM((span, 2 * rows), F32), pltpu.VMEM(w_qkv.shape, BF16), pltpu.VMEM(w_self.shape, BF16),
            pltpu.VMEM(w_cq.shape, BF16), pltpu.VMEM(w_ckv.shape, BF16), pltpu.VMEM(w_co.shape, BF16),
            pltpu.VMEM(encoder.shape, BF16), pltpu.VMEM((rel.shape[1], 2 * LANES), F32),
            pltpu.SemaphoreType.DMA((6,)), pltpu.SemaphoreType.DMA((5,)),
            pltpu.SemaphoreType.DMA((2 * chips - 1,)), pltpu.SemaphoreType.DMA((2 * chips - 1,)),
        ],
        compiler_params=pltpu.CompilerParams(collective_id=0, has_side_effects=True, vmem_limit_bytes=56 << 20),
        name="forward",
    )(x, encoder, lengths, buckets, routes, gains, w_qkv, w_self, w_cq, w_ckv, w_co, rel, router, g)


def fused(inputs, encoder, lengths, buckets, routes, norm_gains, self_qkv, self_out, cross_q, cross_kv, cross_out,
          rel_bias, router, expert_in, expert_out, cotangent):
    seq_count = lax.axis_size("seq")
    seq_index = lax.axis_index("seq")
    rows, width = inputs.shape[1:]
    experts = router.shape[1]
    capacity = 5 * rows // (4 * experts)
    stride = -(-capacity // 16) * 16
    (n1_all, kv_all, prob, cross_prob, ekv, q, o, n2, qc, oc, x3, r1, r2, gates, place, xs, dms) = forward_call(
        seq_count, capacity, stride, inputs[0], encoder, lengths, buckets[None, :], routes[0], norm_gains, self_qkv,
        self_out, cross_q, cross_kv, cross_out, rel_bias, router, cotangent[0])
    pairs = width // LANES
    hidden = inputs[0].astype(F32)
    upstream = cotangent[0].astype(F32)
    a2a = lambda v: lax.all_to_all(v.reshape(experts, stride, width), "exp", split_axis=0, concat_axis=0, tiled=True)
    arrived = a2a(xs).reshape(-1, width)
    grad_arrived = a2a(dms).reshape(-1, width)
    hid, gelu_back = jax.vjp(lambda v: jax.nn.gelu(v, approximate=True), nn(arrived, expert_in[0]))
    act = hid.astype(BF16)
    made = nn(act, expert_out[0]).astype(BF16)
    expert_rows = nn(place, a2a(made).reshape(-1, width))
    chosen = (routes[0] == jnp.arange(experts)[None, :])
    picked = jnp.sum(jnp.where(chosen, gates, 0.0), axis=1, keepdims=True)
    kept = jnp.sum(place.astype(F32), axis=1, keepdims=True)
    layer_out = r2 + picked * kept * expert_rows
    dh = gelu_back(nt(grad_arrived, expert_out[0]))[0].astype(BF16)
    gout = tn(act, grad_arrived)
    gin = tn(arrived, dh)
    dx3 = nn(place, a2a(nt(dh, expert_in[0]).astype(BF16)).reshape(-1, width))
    expert_sums = (
        lax.psum_scatter(gin[None], "seq", scatter_dimension=1, tiled=True),
        lax.psum_scatter(gout[None], "seq", scatter_dimension=1, tiled=True),
    )
    gate_grad = jnp.sum(upstream * expert_rows, axis=1, keepdims=True) * kept
    dl = gates * (jnp.where(chosen, gate_grad, 0.0) - picked * gate_grad)
    router_grad = jnp.dot(x3.astype(F32).T, dl, precision=highest)
    dx3 = dx3 + jnp.dot(dl, router.astype(F32).T, precision=highest)
    _, back3 = jax.vjp(rms_norm, r2, norm_gains[2])
    dr2, gain3 = back3(dx3)
    dr2 = dr2 + upstream
    do2 = dr2.astype(BF16)
    cross_out_grad = tn(oc, do2)
    doc2 = nt(do2, cross_out).astype(BF16)
    heads = lambda v: v.reshape(v.shape[0], H, HD)
    unstack = lambda v: v.reshape(pairs, -1, 2, rows).transpose(0, 2, 1, 3).reshape(H, -1, rows)
    pc = unstack(cross_prob).astype(F32)
    kc, vc = heads(ekv[:, :width]), heads(ekv[:, width:])
    dp = jnp.einsum("qhd,khd->hkq", heads(doc2), vc, preferred_element_type=F32)
    dc = (pc * (dp - jnp.sum(pc * dp, axis=1, keepdims=True))).astype(BF16)
    dqc = (jnp.einsum("hkq,khd->qhd", dc, kc, preferred_element_type=F32) * 0.125).reshape(rows, width).astype(BF16)
    dkc = jnp.einsum("hkq,qhd->khd", dc, heads(qc), preferred_element_type=F32).reshape(-1, width)
    dvc = jnp.einsum("hkq,qhd->khd", pc.astype(BF16), heads(doc2), preferred_element_type=F32).reshape(-1, width)
    dekv = lax.psum_scatter(jnp.concatenate([dkc, dvc], axis=1), ("seq", "exp"), scatter_dimension=0, tiled=True).astype(BF16)
    enc_count = dekv.shape[0]
    flat_index = seq_index * lax.axis_size("exp") + lax.axis_index("exp")
    own_enc = lax.dynamic_slice_in_dim(encoder, flat_index * enc_count, enc_count, 0)
    grad_encoder = nt(dekv, cross_kv)
    pair_grad = tn(own_enc, dekv)
    cq_grad = tn(n2, dqc)
    _, back2 = jax.vjp(rms_norm, r1, norm_gains[1])
    dr1, gain2 = back2(nt(dqc, cross_q))
    dr1 = dr1 + dr2
    do1 = dr1.astype(BF16)
    self_out_grad = tn(o, do1)
    dob = nt(do1, self_out).astype(BF16)
    pr = unstack(prob).astype(F32)
    k, v = heads(kv_all[:, :width]), heads(kv_all[:, width:])
    dp = jnp.einsum("qhd,khd->hkq", heads(dob), v, preferred_element_type=F32)
    ds = (pr * (dp - jnp.sum(pr * dp, axis=1, keepdims=True))).astype(BF16)
    dq = (jnp.einsum("hkq,khd->qhd", ds, k, preferred_element_type=F32) * 0.125).reshape(rows, width).astype(BF16)
    dk = jnp.einsum("hkq,qhd->khd", ds, heads(q), preferred_element_type=F32).reshape(-1, width)
    dv = jnp.einsum("hkq,qhd->khd", pr.astype(BF16), heads(dob), preferred_element_type=F32).reshape(-1, width)
    dkv = lax.psum_scatter(jnp.concatenate([dk, dv], axis=1), "seq", scatter_dimension=0, tiled=True).astype(BF16)
    distance = jnp.clip(seq_index * rows + jnp.arange(rows)[None, :] - jnp.arange(seq_count * rows)[:, None], 0, 127)
    table_grad = jax.vmap(lambda d: jnp.zeros((128,), F32).at[distance.reshape(-1)].add(d.reshape(-1).astype(F32)))(ds)
    bucket_pick = (buckets[:, None] == jnp.arange(rel_bias.shape[0])[None, :]).astype(F32)
    rel_grad = jnp.dot(bucket_pick.T, table_grad.T, precision=highest)
    dqkv = jnp.concatenate([dq, dkv], axis=1)
    qkv_grad = tn(n1_all[seq_index], dqkv)
    _, back1 = jax.vjp(rms_norm, hidden, norm_gains[0])
    dx, gain1 = back1(nt(dqkv, self_qkv))
    grad_input = dx + dr1
    summed = lax.psum((jnp.stack([gain1, gain2, gain3]), qkv_grad, self_out_grad, cq_grad, pair_grad, cross_out_grad,
                       rel_grad, router_grad), ("seq", "exp"))
    return (layer_out.astype(BF16)[None], grad_input[None], grad_encoder, *summed, *expert_sums)


def on_device(*operands):
    if lax.axis_size("seq") * operands[0].shape[1] <= 1024 and lax.axis_size("seq") % 2 == 0:
        return fused(*operands)
    return streamed(*operands)


def solution(mesh):
    in_specs = (
        P("exp", "seq", None),
        P(),
        P("exp", None),
        P(),
        P("exp", "seq", None),
        P(),
        P(),
        P(),
        P(),
        P(),
        P(),
        P(),
        P(),
        P("exp", None, None),
        P("exp", None, None),
        P("exp", "seq", None),
    )
    out_specs = (
        P("exp", "seq", None),
        P("exp", "seq", None),
        P(("seq", "exp"), None),
        P(),
        P(),
        P(),
        P(),
        P(),
        P(),
        P(),
        P(),
        P("exp", "seq", None),
        P("exp", "seq", None),
    )
    return jax.shard_map(
        on_device, mesh=mesh, in_specs=in_specs, out_specs=out_specs, check_vma=False
    )
```

```python
import functools
import math

import jax
import jax.numpy as jnp
from jax import lax
from jax.experimental import pallas as pl
from jax.experimental.pallas import tpu as pltpu
from jax.sharding import PartitionSpec as P

H = 12
HD = 64


epsilon = 1e-06
masked_out = -1e30
highest = lax.Precision.HIGHEST


def rms_norm(value, gain):
    return value * lax.rsqrt(jnp.mean(value * value, axis=-1, keepdims=True) + epsilon) * gain


def split_heads(value):
    return value.reshape(value.shape[0], H, HD)


def doc_index(positions, doc_ends):
    return jnp.sum((positions[:, None] >= doc_ends[None, :]).astype(jnp.int32), axis=1)


def band_pick(offset_gap, query_rows, key_rows, table_span):
    band_len = query_rows + key_rows + 1
    column = jnp.arange(band_len, dtype=jnp.int32)
    distance = jnp.clip(offset_gap + query_rows - column, 0, table_span - 1)
    return (distance[:, None] == jnp.arange(table_span, dtype=jnp.int32)[None, :]).astype(
        jnp.float32
    )


def relative_bias(table, offset_gap, query_rows, key_rows):
    head_count = table.shape[0]
    band_len = query_rows + key_rows + 1
    band = jnp.dot(
        table, band_pick(offset_gap, query_rows, key_rows, table.shape[1]).T, precision=highest
    )
    tiled = jnp.broadcast_to(band[:, None, :], (head_count, query_rows, band_len)).reshape(
        head_count, query_rows * band_len
    )
    skewed = tiled[:, : query_rows * (band_len - 1)].reshape(head_count, query_rows, band_len - 1)
    return skewed[:, :, query_rows : query_rows + key_rows]


def table_terms(score_grads, offset_gap, table_span):
    head_count, query_rows, key_rows = score_grads.shape
    band_len = query_rows + key_rows + 1
    placed = jnp.pad(score_grads.astype(jnp.float32), ((0, 0), (0, 0), (query_rows, 0)))
    flat = jnp.pad(
        placed.reshape(head_count, query_rows * (band_len - 1)), ((0, 0), (0, query_rows))
    )
    diagonal_sums = jnp.sum(flat.reshape(head_count, query_rows, band_len), axis=1)
    return jnp.dot(
        diagonal_sums, band_pick(offset_gap, query_rows, key_rows, table_span), precision=highest
    )


def self_scores(queries, query_start, keys_part, key_start, doc_ends, table):
    query_rows = queries.shape[0]
    key_rows = keys_part.shape[0]
    query_pos = query_start + jnp.arange(query_rows, dtype=jnp.int32)
    key_pos = key_start + jnp.arange(key_rows, dtype=jnp.int32)
    offset_gap = query_start - key_start
    raw_scores = (
        jnp.einsum(
            "qhd,khd->hqk",
            split_heads(queries),
            split_heads(keys_part),
            preferred_element_type=jnp.float32,
        )
        * 0.125
    )
    allowed = (key_pos[None, :] <= query_pos[:, None]) & (
        doc_index(key_pos, doc_ends)[None, :] == doc_index(query_pos, doc_ends)[:, None]
    )
    scores = jnp.where(
        allowed[None],
        raw_scores + relative_bias(table, offset_gap, query_rows, key_rows),
        masked_out,
    )
    return (scores, allowed[None], offset_gap)


def over_blocks(step, running, pieces):
    rows_total = pieces[0].shape[0]
    block_rows = math.gcd(rows_total, 512)
    block_count = rows_total // block_rows
    stacked = tuple(
        (member.reshape(block_count, block_rows, *member.shape[1:]) for member in pieces)
    )

    def scan_step(inner_running, block_input):
        block_id, members = block_input
        return (step(inner_running, members, block_id * block_rows), None)

    result, ignored = lax.scan(
        scan_step, running, (jnp.arange(block_count, dtype=jnp.int32), stacked)
    )
    return result


def streamed(
    inputs,
    encoder,
    lengths,
    buckets,
    routes,
    norm_gains,
    self_qkv,
    self_out,
    cross_q,
    cross_kv,
    cross_out,
    rel_bias,
    router,
    expert_in,
    expert_out,
    cotangent,
):
    hidden = inputs[0].astype(jnp.float32)
    rows_dev = hidden.shape[0]
    model_width = hidden.shape[1]
    seq_count = lax.axis_size("seq")
    seq_index = lax.axis_index("seq")
    own_start = seq_index * rows_dev
    doc_ends = jnp.cumsum(lengths[0])
    bucket_pick = (
        buckets[:, None] == jnp.arange(rel_bias.shape[0], dtype=jnp.int32)[None, :]
    ).astype(jnp.float32)
    table = jnp.dot(bucket_pick, rel_bias, precision=highest).T
    normed_one, norm_one_back = jax.vjp(rms_norm, hidden, norm_gains[0])
    normed_one = normed_one.astype(jnp.bfloat16)
    qkv_all = jnp.dot(normed_one, self_qkv, preferred_element_type=jnp.float32).astype(jnp.bfloat16)
    queries = qkv_all[:, :model_width]
    keys_own = qkv_all[:, model_width : 2 * model_width]
    values_own = qkv_all[:, 2 * model_width :]

    def forward_step(running, pieces, key_start):
        top_old, denominator, summed = running
        keys_part, values_part = pieces
        scores, allowed, offset_gap = self_scores(
            queries, own_start, keys_part, key_start, doc_ends, table
        )
        top_new = jnp.maximum(top_old, jnp.max(scores, axis=-1))
        weights_raw = jnp.where(allowed, jnp.exp(scores - top_new[..., None]), 0.0)
        rescale = jnp.exp(top_old - top_new)
        denominator = denominator * rescale + jnp.sum(weights_raw, axis=-1)
        summed = summed * rescale[..., None] + jnp.einsum(
            "hqk,khd->hqd",
            weights_raw.astype(jnp.bfloat16),
            split_heads(values_part),
            preferred_element_type=jnp.float32,
        )
        return (top_new, denominator, summed)

    start_state = (
        jnp.full((H, rows_dev), masked_out, jnp.float32),
        jnp.zeros((H, rows_dev), jnp.float32),
        jnp.zeros((H, rows_dev, HD), jnp.float32),
    )
    top_score, denominator, summed = over_blocks(
        forward_step,
        start_state,
        (
            lax.all_gather(keys_own, "seq", axis=0, tiled=True),
            lax.all_gather(values_own, "seq", axis=0, tiled=True),
        ),
    )
    log_total = top_score + jnp.log(denominator)
    attended_full = (
        (summed / denominator[..., None]).transpose(1, 0, 2).reshape(rows_dev, model_width)
    )
    attended = attended_full.astype(jnp.bfloat16)
    after_self = hidden + jnp.dot(attended, self_out, preferred_element_type=jnp.float32)
    enc_kv = jnp.dot(encoder, cross_kv, preferred_element_type=jnp.float32).astype(jnp.bfloat16)
    cross_keys = split_heads(enc_kv[:, :model_width])
    cross_values = split_heads(enc_kv[:, model_width:])
    normed_two, norm_two_back = jax.vjp(rms_norm, after_self, norm_gains[1])
    normed_two = normed_two.astype(jnp.bfloat16)
    cross_queries = jnp.dot(normed_two, cross_q, preferred_element_type=jnp.float32).astype(
        jnp.bfloat16
    )
    cross_scores = (
        jnp.einsum(
            "qhd,khd->hqk",
            split_heads(cross_queries),
            cross_keys,
            preferred_element_type=jnp.float32,
        )
        * 0.125
    )
    cross_raw = jnp.exp(cross_scores - jnp.max(cross_scores, axis=-1, keepdims=True))
    cross_prob = cross_raw / jnp.sum(cross_raw, axis=-1, keepdims=True)
    cross_prob_low = cross_prob.astype(jnp.bfloat16)
    cross_att = (
        jnp.einsum("hqk,khd->qhd", cross_prob_low, cross_values, preferred_element_type=jnp.float32)
        .reshape(rows_dev, model_width)
        .astype(jnp.bfloat16)
    )
    after_cross = after_self + jnp.dot(cross_att, cross_out, preferred_element_type=jnp.float32)
    normed_three, norm_three_back = jax.vjp(rms_norm, after_cross, norm_gains[2])
    routed_in = normed_three.astype(jnp.bfloat16)
    gates = jax.nn.softmax(jnp.dot(routed_in, router, preferred_element_type=jnp.float32), axis=-1)
    expert_total = router.shape[1]
    local_experts = expert_in.shape[0]
    capacity = 5 * rows_dev // (4 * expert_total)
    route_ids = routes[0, :, 0]
    chosen = route_ids[:, None] == jnp.arange(expert_total, dtype=jnp.int32)[None, :]
    slots = jnp.sum(jnp.where(chosen, jnp.cumsum(chosen.astype(jnp.int32), axis=0), 0), axis=1) - 1
    kept = slots < capacity
    picked_gate = jnp.sum(jnp.where(chosen, gates, 0.0), axis=1)
    gate_used = picked_gate * kept.astype(jnp.float32)
    target = jnp.where(kept, route_ids * capacity + slots, -1)
    dispatch = (
        jnp.arange(expert_total * capacity, dtype=jnp.int32)[:, None] == target[None, :]
    ).astype(jnp.bfloat16)
    outgoing = (
        jnp.dot(dispatch, routed_in, preferred_element_type=jnp.float32)
        .astype(jnp.bfloat16)
        .reshape(expert_total, capacity, model_width)
    )
    arrived = lax.all_to_all(outgoing, "exp", split_axis=0, concat_axis=0, tiled=True).reshape(
        -1, local_experts, capacity, model_width
    )
    inner_pre = jnp.einsum("secd,edf->secf", arrived, expert_in, preferred_element_type=jnp.float32)
    active = jax.nn.gelu(inner_pre, approximate=True).astype(jnp.bfloat16)
    produced = jnp.einsum(
        "secf,efd->secd", active, expert_out, preferred_element_type=jnp.float32
    ).astype(jnp.bfloat16)
    returned = lax.all_to_all(
        produced.reshape(-1, capacity, model_width), "exp", split_axis=0, concat_axis=0, tiled=True
    )
    expert_rows = jnp.dot(
        dispatch.T, returned.reshape(-1, model_width), preferred_element_type=jnp.float32
    )
    layer_out = after_cross + gate_used[:, None] * expert_rows
    upstream = cotangent[0].astype(jnp.float32)
    made_grad = (upstream * gate_used[:, None]).astype(jnp.bfloat16)
    sent_grad = (
        jnp.dot(dispatch, made_grad, preferred_element_type=jnp.float32)
        .astype(jnp.bfloat16)
        .reshape(expert_total, capacity, model_width)
    )
    grad_arrived = lax.all_to_all(
        sent_grad, "exp", split_axis=0, concat_axis=0, tiled=True
    ).reshape(-1, local_experts, capacity, model_width)
    inner_again = jnp.einsum(
        "secd,edf->secf", arrived, expert_in, preferred_element_type=jnp.float32
    )
    active_again, gelu_back = jax.vjp(
        lambda value: jax.nn.gelu(value, approximate=True), inner_again
    )
    grad_out_w = jnp.einsum(
        "secf,secd->efd",
        active_again.astype(jnp.bfloat16),
        grad_arrived,
        preferred_element_type=jnp.float32,
    )
    grad_active = jnp.einsum(
        "secd,efd->secf", grad_arrived, expert_out, preferred_element_type=jnp.float32
    )
    grad_inner = gelu_back(grad_active)[0].astype(jnp.bfloat16)
    grad_in_w = jnp.einsum(
        "secd,secf->edf", arrived, grad_inner, preferred_element_type=jnp.float32
    )
    grad_sent_x = jnp.einsum(
        "secf,edf->secd", grad_inner, expert_in, preferred_element_type=jnp.float32
    ).astype(jnp.bfloat16)
    grad_back = lax.all_to_all(
        grad_sent_x.reshape(-1, capacity, model_width),
        "exp",
        split_axis=0,
        concat_axis=0,
        tiled=True,
    )
    grad_routed = jnp.dot(
        dispatch.T, grad_back.reshape(-1, model_width), preferred_element_type=jnp.float32
    )
    expert_sums = (
        lax.psum_scatter(grad_in_w, "seq", scatter_dimension=1, tiled=True),
        lax.psum_scatter(grad_out_w, "seq", scatter_dimension=1, tiled=True),
    )
    gate_grad = jnp.sum(upstream * expert_rows, axis=1) * kept.astype(jnp.float32)
    logit_grad = gates * (
        jnp.where(chosen, gate_grad[:, None], 0.0) - (picked_gate * gate_grad)[:, None]
    )
    router_grad = jnp.dot(routed_in.astype(jnp.float32).T, logit_grad, precision=highest)
    grad_normed_three = (
        jnp.dot(logit_grad, router.astype(jnp.float32).T, precision=highest) + grad_routed
    )
    grad_after_cross, gain_three = norm_three_back(grad_normed_three)
    grad_after_cross = grad_after_cross + upstream
    cross_branch = grad_after_cross.astype(jnp.bfloat16)
    cross_out_grad = jnp.dot(cross_att.T, cross_branch, preferred_element_type=jnp.float32)
    grad_cross_att = split_heads(
        jnp.dot(cross_branch, cross_out.T, preferred_element_type=jnp.float32).astype(jnp.bfloat16)
    )
    cross_prob_grad = jnp.einsum(
        "qhd,khd->hqk", grad_cross_att, cross_values, preferred_element_type=jnp.float32
    )
    cross_delta = jnp.sum(cross_prob * cross_prob_grad, axis=-1, keepdims=True)
    cross_score_grad = (cross_prob * (cross_prob_grad - cross_delta)).astype(jnp.bfloat16)
    grad_cross_queries = (
        (
            jnp.einsum(
                "hqk,khd->qhd", cross_score_grad, cross_keys, preferred_element_type=jnp.float32
            )
            * 0.125
        )
        .reshape(rows_dev, model_width)
        .astype(jnp.bfloat16)
    )
    grad_enc_keys = (
        jnp.einsum(
            "hqk,qhd->khd",
            cross_score_grad,
            split_heads(cross_queries),
            preferred_element_type=jnp.float32,
        )
        * 0.125
    )
    grad_enc_values = jnp.einsum(
        "hqk,qhd->khd", cross_prob_low, grad_cross_att, preferred_element_type=jnp.float32
    )
    enc_terms = jnp.concatenate(
        [grad_enc_keys.reshape(-1, model_width), grad_enc_values.reshape(-1, model_width)], axis=1
    )
    enc_grad_rows = lax.psum_scatter(
        enc_terms, ("seq", "exp"), scatter_dimension=0, tiled=True
    ).astype(jnp.bfloat16)
    enc_count = enc_grad_rows.shape[0]
    flat_index = seq_index * lax.axis_size("exp") + lax.axis_index("exp")
    own_enc = lax.dynamic_slice_in_dim(encoder, flat_index * enc_count, enc_count, 0)
    grad_encoder = jnp.dot(enc_grad_rows, cross_kv.T, preferred_element_type=jnp.float32)
    pair_grad = jnp.dot(own_enc.T, enc_grad_rows, preferred_element_type=jnp.float32)
    query_w_grad = jnp.dot(normed_two.T, grad_cross_queries, preferred_element_type=jnp.float32)
    grad_normed_two = jnp.dot(grad_cross_queries, cross_q.T, preferred_element_type=jnp.float32)
    grad_after_self, gain_two = norm_two_back(grad_normed_two)
    grad_after_self = grad_after_self + grad_after_cross
    self_branch = grad_after_self.astype(jnp.bfloat16)
    self_out_grad = jnp.dot(attended.T, self_branch, preferred_element_type=jnp.float32)
    grad_attended = jnp.dot(self_branch, self_out.T, preferred_element_type=jnp.float32).astype(
        jnp.bfloat16
    )
    row_delta = jnp.sum(
        split_heads(grad_attended).astype(jnp.float32) * split_heads(attended_full), axis=-1
    ).T
    stats_all = (
        lax.all_gather(log_total.T, "seq", axis=0, tiled=True),
        lax.all_gather(row_delta.T, "seq", axis=0, tiled=True),
    )

    def query_step(running, pieces, query_start):
        kv_grad, query_grads, table_grad = running
        queries_part, grads_part = pieces
        piece_rows = queries_part.shape[0]
        lse_part = lax.dynamic_slice_in_dim(stats_all[0], query_start, piece_rows, 0).T
        delta_part = lax.dynamic_slice_in_dim(stats_all[1], query_start, piece_rows, 0).T
        scores, allowed, offset_gap = self_scores(
            queries_part, query_start, keys_own, own_start, doc_ends, table
        )
        probability = jnp.where(allowed, jnp.exp(scores - lse_part[..., None]), 0.0)
        prob_grad = jnp.einsum(
            "qhd,khd->hqk",
            split_heads(grads_part),
            split_heads(values_own),
            preferred_element_type=jnp.float32,
        )
        score_grad = (probability * (prob_grad - delta_part[..., None])).astype(jnp.bfloat16)
        key_grad = (
            jnp.einsum(
                "hqk,qhd->khd",
                score_grad,
                split_heads(queries_part),
                preferred_element_type=jnp.float32,
            )
            * 0.125
        )
        value_grad = jnp.einsum(
            "hqk,qhd->khd",
            probability.astype(jnp.bfloat16),
            split_heads(grads_part),
            preferred_element_type=jnp.float32,
        )
        kv_grad = kv_grad + jnp.concatenate(
            [key_grad.reshape(-1, model_width), value_grad.reshape(-1, model_width)], axis=1
        )
        table_grad = table_grad + table_terms(score_grad, offset_gap, table.shape[1])
        query_part_grad = jnp.einsum(
            "hqk,khd->qhd", score_grad, split_heads(keys_own), preferred_element_type=jnp.float32
        ).reshape(piece_rows, model_width)
        current = lax.dynamic_slice_in_dim(query_grads, query_start, piece_rows, 0)
        query_grads = lax.dynamic_update_slice_in_dim(
            query_grads, current + query_part_grad, query_start, 0
        )
        return (kv_grad, query_grads, table_grad)

    back_start = (
        jnp.zeros((rows_dev, 2 * model_width), jnp.float32),
        jnp.zeros((seq_count * rows_dev, model_width), jnp.float32),
        jnp.zeros(table.shape, jnp.float32),
    )
    kv_grad, query_buffer, table_grad = over_blocks(
        query_step,
        back_start,
        (
            lax.all_gather(queries, "seq", axis=0, tiled=True),
            lax.all_gather(grad_attended, "seq", axis=0, tiled=True),
        ),
    )
    query_grad = lax.psum_scatter(query_buffer, "seq", scatter_dimension=0, tiled=True)
    qkv_grad = jnp.concatenate(
        [(query_grad * 0.125).astype(jnp.bfloat16), kv_grad.astype(jnp.bfloat16)], axis=1
    )
    qkv_w_grad = jnp.dot(normed_one.T, qkv_grad, preferred_element_type=jnp.float32)
    grad_normed_one = jnp.dot(qkv_grad, self_qkv.T, preferred_element_type=jnp.float32)
    grad_hidden, gain_one = norm_one_back(grad_normed_one)
    grad_input = grad_hidden + grad_after_self
    rel_grad = jnp.dot(bucket_pick.T, table_grad.T, precision=highest)
    summed_grads = lax.psum(
        (
            jnp.stack([gain_one, gain_two, gain_three]),
            qkv_w_grad,
            self_out_grad,
            query_w_grad,
            pair_grad,
            cross_out_grad,
            rel_grad,
            router_grad,
        ),
        ("seq", "exp"),
    )
    return (
        layer_out.astype(jnp.bfloat16)[None],
        grad_input[None],
        grad_encoder,
        summed_grads[0],
        summed_grads[1],
        summed_grads[2],
        summed_grads[3],
        summed_grads[4],
        summed_grads[5],
        summed_grads[6],
        summed_grads[7],
        expert_sums[0],
        expert_sums[1],
    )


F32 = jnp.float32
BF16 = jnp.bfloat16
MESH = pl.DeviceIdType.MESH
ANY = pl.BlockSpec(memory_space=pl.ANY)
VMEM = pl.BlockSpec(memory_space=pltpu.VMEM)
SMEM = pl.BlockSpec(memory_space=pltpu.SMEM)
LANES = 128


def nn(a, b):
    return lax.dot_general(a, b, (((1,), (0,)), ((), ())), preferred_element_type=F32)


def nt(a, b):
    return lax.dot_general(a, b, (((1,), (1,)), ((), ())), preferred_element_type=F32)


def tn(a, b):
    return lax.dot_general(a, b, (((0,), (0,)), ((), ())), preferred_element_type=F32)


def rms_scale(a):
    return lax.rsqrt(jnp.mean(a * a, axis=-1, keepdims=True) + epsilon)


def pair_lanes(p):
    return pl.ds(pl.multiple_of(p * LANES, LANES), LANES)


def head_stack(pair):
    lane = lax.broadcasted_iota(jnp.int32, pair.shape, 1)
    zero = jnp.zeros_like(pair)
    return jnp.concatenate([jnp.where(lane < HD, pair, zero), jnp.where(lane < HD, zero, pair)], axis=0)


def head_unstack(both, rows):
    feature = lax.broadcasted_iota(jnp.int32, (both.shape[0], rows), 0)
    return jnp.where(feature < HD, both[:, :rows], both[:, rows:]).T


def seq_peers(seq_index, chips):
    core = lax.rem(seq_index, 2)
    chip = lax.div(seq_index, 2)
    partner = seq_index + 1 - 2 * core
    others = [lax.rem(chip + d, chips) * 2 + core for d in range(1, chips)]
    sources = [lax.rem(chip - d + chips, chips) * 2 + core for d in range(1, chips)]
    return core, chip, partner, others, sources


def enter(devices):
    barrier = pltpu.get_barrier_semaphore()
    for device in devices:
        pl.semaphore_signal(barrier, inc=1, device_id=device, device_id_type=MESH)
    pl.semaphore_wait(barrier, len(devices))


def remote(src, dst, send_sem, recv_sem, device):
    return pltpu.make_async_remote_copy(
        src_ref=src, dst_ref=dst, send_sem=send_sem, recv_sem=recv_sem, device_id=device, device_id_type=MESH
    )


def forward_kernel(
    seq_count, capacity, stride,
    x_ref, encoder_hbm, lengths_ref, buckets_ref, routes_ref, gains_ref, qkv_hbm, self_out_hbm, cross_q_hbm,
    cross_kv_hbm, cross_out_hbm, rel_ref, router_ref, g_ref,
    n1_hbm, kv_hbm, p_hbm, pc_hbm, ekv_hbm, q_ref, o_ref, n2_ref, qc_ref, oc_ref, x3_ref, r1_ref, r2_ref, gates_ref,
    place_ref, xs_ref, dms_ref,
    n1_all, kv_all, prob, cross_prob, ekv, scores, mask, w_qkv, w_self, w_cq, w_ckv, w_co, enc, table_ref,
    load_sem, store_sem, send_sem, recv_sem,
):
    chips = seq_count // 2
    rows, width = x_ref.shape
    span = seq_count * rows
    pairs = width // LANES
    me = lax.axis_index("seq")
    core, chip, partner, others, sources = seq_peers(me, chips)

    loads = [
        pltpu.make_async_copy(src, dst, load_sem.at[i])
        for i, (src, dst) in enumerate(
            [(qkv_hbm, w_qkv), (cross_kv_hbm, w_ckv), (encoder_hbm, enc), (self_out_hbm, w_self), (cross_q_hbm, w_cq),
             (cross_out_hbm, w_co)]
        )
    ]
    for load in loads:
        load.start()
    x = x_ref[...].astype(F32)
    n1_all[me] = (x * rms_scale(x) * gains_ref[0:1, :]).astype(BF16)
    enter([{"seq": partner}] + [{"seq": other} for other in others])
    own = remote(n1_all.at[me], n1_all.at[me], send_sem.at[0], recv_sem.at[0], {"seq": partner})
    direct = [
        remote(n1_all.at[me], n1_all.at[me], send_sem.at[d], recv_sem.at[d], {"seq": others[d - 1]})
        for d in range(1, chips)
    ]
    own.start()
    for copy in direct:
        copy.start()

    loads[0].wait()
    q = nn(n1_all[me], w_qkv[:, :width]).astype(BF16)
    q_ref[...] = q * jnp.asarray(0.125, BF16)
    loads[1].wait()
    loads[2].wait()
    ekv[...] = nn(enc[...], w_ckv[...]).astype(BF16)
    store_ekv = pltpu.make_async_copy(ekv, ekv_hbm, store_sem.at[0])
    store_ekv.start()
    pick = (buckets_ref[...] == lax.broadcasted_iota(jnp.int32, (rel_ref.shape[0], LANES), 0)).astype(F32)
    table = lax.dot_general(
        rel_ref[...], pick, (((0,), (0,)), ((), ())), precision=highest, preferred_element_type=F32
    )
    table = table - table[:, LANES - 1 :]
    table_ref[...] = jnp.concatenate([jnp.zeros_like(table), table], axis=1)
    query_pos = me * rows + lax.broadcasted_iota(jnp.int32, (1, rows), 1)
    start = jnp.zeros((1, rows), jnp.int32)
    end = jnp.int32(0)
    for i in range(lengths_ref.shape[1]):
        end = end + lengths_ref[0, i]
        start = jnp.where(end <= query_pos, end, start)
    key_pos = lax.broadcasted_iota(jnp.int32, (span, rows), 0)
    seen = jnp.where((key_pos >= start) & (key_pos <= query_pos), 0.0, masked_out)
    mask[...] = jnp.concatenate([seen, seen], axis=1)

    forwards = []
    for d in range(1, chips):
        direct[d - 1].wait_recv()
        block = n1_all.at[sources[d - 1]]
        forward = remote(
            block, block, send_sem.at[chips - 1 + d], recv_sem.at[chips - 1 + d], {"seq": partner}
        )
        forward.start()
        forwards.append(forward)
    own.wait_recv()
    for forward in forwards:
        forward.wait_recv()
    store_n1 = pltpu.make_async_copy(n1_all, n1_hbm, store_sem.at[1])
    store_n1.start()

    @pl.loop(0, chips)
    def _(c):
        part = n1_all[pl.ds(c * 2, 2)].reshape(2 * rows, width)
        at = pl.ds(pl.multiple_of(c * 2 * rows, 2 * rows), 2 * rows)
        kv_all[at, :] = nn(part, w_qkv[:, width:]).astype(BF16)

    store_kv = pltpu.make_async_copy(kv_all, kv_hbm, store_sem.at[2])
    store_kv.start()

    near = pl.ds(pl.multiple_of(me * rows, rows), 2 * rows)

    @pl.loop(0, pairs)
    def _(p):
        lanes = pair_lanes(p)
        q_both = head_stack(q_ref[:, lanes])
        scores[pl.ds(rows, span), :] = nt(kv_all[:, lanes], q_both) + mask[...]
        biases = []
        for h in range(2):
            band = jnp.broadcast_to(table_ref[pl.ds(2 * p + h, 1), :], (2 * rows, 2 * LANES))
            biases.append(pltpu.roll(band, 0, 1, stride=1, stride_axis=0)[:, :rows])
        scores[near, :] = scores[near, :] + jnp.concatenate(biases, axis=1)
        s = scores[pl.ds(rows, span), :]
        weights = jnp.exp(s - jnp.max(s, axis=0, keepdims=True))
        weights = (weights * (1.0 / jnp.sum(weights, axis=0, keepdims=True))).astype(BF16)
        prob[p] = weights
        both = tn(kv_all[:, pair_lanes(pairs + p)], weights)
        o_ref[:, lanes] = head_unstack(both, rows).astype(BF16)

    store_p = pltpu.make_async_copy(prob, p_hbm, store_sem.at[3])
    store_p.start()
    loads[3].wait()
    loads[4].wait()
    loads[5].wait()
    r1 = x_ref[...].astype(F32) + nn(o_ref[...], w_self[...])
    r1_ref[...] = r1
    n2 = (r1 * rms_scale(r1) * gains_ref[1:2, :]).astype(BF16)
    n2_ref[...] = n2
    qc_ref[...] = nn(n2, w_cq[...]).astype(BF16) * jnp.asarray(0.125, BF16)

    @pl.loop(0, pairs)
    def _(p):
        lanes = pair_lanes(p)
        s = nt(ekv[:, lanes], head_stack(qc_ref[:, lanes]))
        weights = jnp.exp(s - jnp.max(s, axis=0, keepdims=True))
        weights = (weights * (1.0 / jnp.sum(weights, axis=0, keepdims=True))).astype(BF16)
        cross_prob[p] = weights
        both = tn(ekv[:, pair_lanes(pairs + p)], weights)
        oc_ref[:, lanes] = head_unstack(both, rows).astype(BF16)

    store_pc = pltpu.make_async_copy(cross_prob, pc_hbm, store_sem.at[4])
    store_pc.start()
    r2 = r1_ref[...] + nn(oc_ref[...], w_co[...])
    r2_ref[...] = r2
    x3 = (r2 * rms_scale(r2) * gains_ref[2:3, :]).astype(BF16)
    x3_ref[...] = x3
    experts = router_ref.shape[1]
    logits = nn(x3, router_ref[...])
    top = jnp.exp(logits - jnp.max(logits, axis=-1, keepdims=True))
    gates = top / jnp.sum(top, axis=-1, keepdims=True)
    gates_ref[...] = gates
    route = routes_ref[...]
    chosen = (route == lax.broadcasted_iota(jnp.int32, (rows, experts), 1)).astype(F32)
    earlier = (
        lax.broadcasted_iota(jnp.int32, (rows, rows), 1) < lax.broadcasted_iota(jnp.int32, (rows, rows), 0)
    ).astype(BF16)
    slot = jnp.sum(nn(earlier, chosen.astype(BF16)) * chosen, axis=1, keepdims=True).astype(jnp.int32)
    kept = slot < capacity
    gate_used = jnp.sum(gates * chosen, axis=1, keepdims=True) * kept.astype(F32)
    target = jnp.where(kept, route * stride + slot, -1)
    place = (
        lax.broadcasted_iota(jnp.int32, (rows, experts * stride), 1) == target
    ).astype(BF16)
    place_ref[...] = place
    xs_ref[...] = tn(place, x3).astype(BF16)
    made_grad = (g_ref[...].astype(F32) * gate_used).astype(BF16)
    dms_ref[...] = tn(place, made_grad).astype(BF16)

    own.wait_send()
    for copy in direct + forwards:
        copy.wait_send()
    for store in (store_ekv, store_n1, store_kv, store_p, store_pc):
        store.wait()


def forward_call(seq_count, capacity, stride, x, encoder, lengths, buckets, routes, gains, w_qkv, w_self, w_cq, w_ckv,
                 w_co, rel, router, g):
    rows, width = x.shape
    span = seq_count * rows
    pairs = width // LANES
    enc_rows = encoder.shape[0]
    experts = router.shape[1]
    chips = seq_count // 2
    shape = jax.ShapeDtypeStruct
    wide = shape((rows, width), BF16)
    outs = (
        shape((seq_count, rows, width), BF16), shape((span, 2 * width), BF16), shape((pairs, span, 2 * rows), BF16),
        shape((pairs, enc_rows, 2 * rows), BF16), shape((enc_rows, 2 * width), BF16), wide, wide, wide, wide, wide, wide,
        shape((rows, width), F32), shape((rows, width), F32), shape((rows, experts), F32),
        shape((rows, experts * stride), BF16), shape((experts * stride, width), BF16), shape((experts * stride, width), BF16),
    )
    return pl.pallas_call(
        functools.partial(forward_kernel, seq_count, capacity, stride),
        out_shape=outs,
        in_specs=[VMEM, ANY, SMEM, VMEM, VMEM, VMEM, ANY, ANY, ANY, ANY, ANY, VMEM, VMEM, VMEM],
        out_specs=tuple([ANY] * 5 + [VMEM] * 12),
        scratch_shapes=[
            pltpu.VMEM((seq_count, rows, width), BF16), pltpu.VMEM((span, 2 * width), BF16),
            pltpu.VMEM((pairs, span, 2 * rows), BF16), pltpu.VMEM((pairs, enc_rows, 2 * rows), BF16),
            pltpu.VMEM((enc_rows, 2 * width), BF16), pltpu.VMEM((span + rows, 2 * rows), F32),
            pltpu.VMEM((span, 2 * rows), F32), pltpu.VMEM(w_qkv.shape, BF16), pltpu.VMEM(w_self.shape, BF16),
            pltpu.VMEM(w_cq.shape, BF16), pltpu.VMEM(w_ckv.shape, BF16), pltpu.VMEM(w_co.shape, BF16),
            pltpu.VMEM(encoder.shape, BF16), pltpu.VMEM((rel.shape[1], 2 * LANES), F32),
            pltpu.SemaphoreType.DMA((6,)), pltpu.SemaphoreType.DMA((5,)),
            pltpu.SemaphoreType.DMA((2 * chips - 1,)), pltpu.SemaphoreType.DMA((2 * chips - 1,)),
        ],
        compiler_params=pltpu.CompilerParams(collective_id=0, has_side_effects=True, vmem_limit_bytes=56 << 20),
        name="forward",
    )(x, encoder, lengths, buckets, routes, gains, w_qkv, w_self, w_cq, w_ckv, w_co, rel, router, g)


def expert_peers(exp_index, experts):
    return [lax.rem(exp_index + d, experts) for d in range(1, experts)]


def gelu_parts(hid):
    root, cubic = 0.7978845608028654, 0.044715
    square = hid * hid
    bent = jnp.tanh(root * hid * (1.0 + cubic * square))
    half = 0.5 * (1.0 + bent)
    return hid * half, half + 0.5 * hid * (1.0 - bent * bent) * (root + 3.0 * root * cubic * square)


def experts_kernel(
    seq_count, experts, stride,
    xs_ref, dms_ref, w_in_hbm, w_out_hbm,
    made_ref, dx_ref, x_hbm, dm_hbm,
    x_all, dm_all, made_out, made_back, dx_out, dx_back, act, slope, w_in, w_out,
    load_sem, own_sem, store_sem, zx_send, zx_recv, zd_send, zd_recv, zm_send, zm_recv, zg_send, zg_recv,
    x_send, x_recv, d_send, d_recv,
):
    chips = seq_count // 2
    width = xs_ref.shape[-1]
    rows = experts * stride
    hidden = w_in.shape[1]
    chunk = width
    me = lax.axis_index("seq")
    mine = lax.axis_index("exp")
    core, chip, partner, others, sources = seq_peers(me, chips)
    peers = expert_peers(mine, experts)
    loads = [
        pltpu.make_async_copy(w_in_hbm, w_in, load_sem.at[0]),
        pltpu.make_async_copy(w_out_hbm, w_out, load_sem.at[1]),
    ]
    for load in loads:
        load.start()
    own_copies = [
        pltpu.make_async_copy(xs_ref.at[mine], x_all.at[me, mine], own_sem.at[0]),
        pltpu.make_async_copy(dms_ref.at[mine], dm_all.at[me, mine], own_sem.at[1]),
    ]
    for copy in own_copies:
        copy.start()
    enter([{"seq": partner}] + [{"seq": other} for other in others] + [{"exp": peer} for peer in peers])

    def over_exp(src, dst, send, recv):
        copies = [
            remote(src.at[peer], dst.at[mine], send.at[d], recv.at[d], {"exp": peer}) for d, peer in enumerate(peers)
        ]
        for copy in copies:
            copy.start()
        return copies

    def over_seq(buffer, send, recv):
        copies = [remote(buffer.at[me], buffer.at[me], send.at[0], recv.at[0], {"seq": partner})] + [
            remote(buffer.at[me], buffer.at[me], send.at[d], recv.at[d], {"seq": others[d - 1]}) for d in range(1, chips)
        ]
        for copy in copies:
            copy.start()
        return copies

    def pass_on(copies, buffer, send, recv):
        forwards = []
        for d in range(1, chips):
            copies[d].wait_recv()
            block = buffer.at[sources[d - 1]]
            forward = remote(block, block, send.at[chips - 1 + d], recv.at[chips - 1 + d], {"seq": partner})
            forward.start()
            forwards.append(forward)
        return forwards

    x_moves = over_exp(xs_ref, x_all.at[me], zx_send, zx_recv)
    dm_moves = over_exp(dms_ref, dm_all.at[me], zd_send, zd_recv)
    own_copies[0].wait()
    for move in x_moves:
        move.wait_recv()
    x_copies = over_seq(x_all, x_send, x_recv)
    x = x_all[me].reshape(rows, width)
    loads[0].wait()
    loads[1].wait()
    made = jnp.zeros((rows, width), F32)
    for n in range(hidden // chunk):
        at = slice(n * chunk, (n + 1) * chunk)
        value, derivative = gelu_parts(nn(x, w_in[:, at]))
        slope[:, at] = derivative
        value = value.astype(BF16)
        made = made + nn(value, w_out[at, :])
    made_out[...] = made.astype(BF16).reshape(experts, stride, width)
    made_moves = over_exp(made_out, made_back, zm_send, zm_recv)
    made_back[mine] = made_out[mine]

    own_copies[1].wait()
    for move in dm_moves:
        move.wait_recv()
    dm_copies = over_seq(dm_all, d_send, d_recv)
    dm = dm_all[me].reshape(rows, width)
    dx = jnp.zeros((rows, width), F32)
    for n in range(hidden // chunk):
        at = slice(n * chunk, (n + 1) * chunk)
        dh = (nt(dm, w_out[at, :]) * slope[:, at]).astype(BF16)
        dx = dx + nt(dh, w_in[:, at])
    dx_out[...] = dx.astype(BF16).reshape(experts, stride, width)
    dx_moves = over_exp(dx_out, dx_back, zg_send, zg_recv)
    dx_back[mine] = dx_out[mine]

    x_forwards = pass_on(x_copies, x_all, x_send, x_recv)
    for move in made_moves:
        move.wait_recv()
    made_ref[...] = made_back[...]
    dm_forwards = pass_on(dm_copies, dm_all, d_send, d_recv)
    for move in dx_moves:
        move.wait_recv()
    dx_ref[...] = dx_back[...]
    x_copies[0].wait_recv()
    for forward in x_forwards:
        forward.wait_recv()
    store_x = pltpu.make_async_copy(x_all, x_hbm, store_sem.at[0])
    store_x.start()
    dm_copies[0].wait_recv()
    for forward in dm_forwards:
        forward.wait_recv()
    store_dm = pltpu.make_async_copy(dm_all, dm_hbm, store_sem.at[1])
    store_dm.start()
    for copy in x_moves + dm_moves + made_moves + dx_moves + x_copies + dm_copies + x_forwards + dm_forwards:
        copy.wait_send()
    store_x.wait()
    store_dm.wait()


def experts_call(seq_count, experts, stride, xs, dms, w_in, w_out):
    width = xs.shape[-1]
    chips = seq_count // 2
    shape = jax.ShapeDtypeStruct
    block = (experts, stride, width)
    every = (seq_count,) + block
    dma = lambda n: pltpu.SemaphoreType.DMA((n,))
    z = experts - 1
    return pl.pallas_call(
        functools.partial(experts_kernel, seq_count, experts, stride),
        out_shape=(shape(block, BF16), shape(block, BF16), shape(every, BF16), shape(every, BF16)),
        in_specs=[VMEM, VMEM, ANY, ANY],
        out_specs=(VMEM, VMEM, ANY, ANY),
        scratch_shapes=[
            pltpu.VMEM(every, BF16), pltpu.VMEM(every, BF16), pltpu.VMEM(block, BF16), pltpu.VMEM(block, BF16),
            pltpu.VMEM(block, BF16), pltpu.VMEM(block, BF16), pltpu.VMEM((8, 128), BF16),
            pltpu.VMEM((experts * stride, w_in.shape[1]), F32), pltpu.VMEM(w_in.shape, BF16), pltpu.VMEM(w_out.shape, BF16),
            dma(2), dma(2), dma(2), dma(z), dma(z), dma(z), dma(z), dma(z), dma(z), dma(z), dma(z),
            dma(2 * chips - 1), dma(2 * chips - 1), dma(2 * chips - 1), dma(2 * chips - 1),
        ],
        compiler_params=pltpu.CompilerParams(collective_id=1, has_side_effects=True, vmem_limit_bytes=56 << 20),
        name="experts",
    )(xs.reshape(block), dms.reshape(block), w_in, w_out)


def rms_back(a, gain, grad):
    scale = rms_scale(a)
    weighted = grad * gain
    da = scale * weighted - a * (scale * scale * scale * jnp.mean(a * weighted, axis=-1, keepdims=True))
    return da, jnp.sum(grad * (a * scale), axis=0, keepdims=True)


def in_two(value):
    high = value.astype(BF16)
    return high, (value - high.astype(F32)).astype(BF16)


def backward_kernel(
    seq_count, experts,
    made_ref, dxb_ref, g_ref, x_ref, r1_ref, r2_ref, gates_ref, place_ref, routes_ref, x3_ref, n2_ref, o_ref, oc_ref,
    q_ref, qc_ref, gains_ref, router_ref, buckets_ref, kv_hbm, p_hbm, pc_hbm, ekv_hbm, co_hbm, cq_hbm, so_hbm, qkv_hbm,
    out_ref, dx_ref, dqkv_t_ref, squares_ref, dekv_ref, small_ref,
    kv_all, prob, cross_prob, ekv, w_co, w_cq, w_so, w_qkv, dr_ref, doc_ref, dqc_ref, dqkv_ref, ds_ref, diag_ref, total_ref,
    e_out, e_pair, e_chip, e_mine, e_exp, t_out, t_pair, t_chip, w_out, w_pair, w_chip,
    load_sem, ep_send, ep_recv, ec_send, ec_recv, ee_send, ee_recv, tp_send, tp_recv, tc_send, tc_recv,
    wp_send, wp_recv, wc_send, wc_recv,
):
    chips = seq_count // 2
    rows, width = x_ref.shape
    span = seq_count * rows
    pairs = width // LANES
    me = lax.axis_index("seq")
    mine = lax.axis_index("exp")
    core, chip, partner, others, sources = seq_peers(me, chips)
    other_core = 1 - core
    other_chips = [lax.rem(chip + d, chips) for d in range(1, chips)]
    peers = expert_peers(mine, experts)
    loads = [
        pltpu.make_async_copy(src, dst, load_sem.at[i])
        for i, (src, dst) in enumerate(
            [(co_hbm, w_co), (ekv_hbm, ekv), (pc_hbm, cross_prob), (cq_hbm, w_cq), (so_hbm, w_so), (kv_hbm, kv_all),
             (p_hbm, prob), (qkv_hbm, w_qkv)]
        )
    ]
    for load in loads:
        load.start()
    enter([{"seq": partner}] + [{"seq": other} for other in others] + [{"exp": peer} for peer in peers])

    made = nn(place_ref[...], made_ref[...])
    kept = jnp.sum(place_ref[...].astype(F32), axis=1, keepdims=True)
    gates = gates_ref[...]
    chosen = (routes_ref[...] == lax.broadcasted_iota(jnp.int32, gates.shape, 1)).astype(F32)
    picked = jnp.sum(gates * chosen, axis=1, keepdims=True)
    g = g_ref[...].astype(F32)
    out_ref[...] = (r2_ref[...] + (picked * kept) * made).astype(BF16)
    gate_grad = jnp.sum(g * made, axis=1, keepdims=True) * kept
    dl = gates * (chosen * gate_grad - picked * gate_grad)
    dl_high, dl_low = in_two(dl)
    x3 = x3_ref[...]
    small_ref[...] = jnp.zeros_like(small_ref)
    small_ref[4 : 4 + experts, :] = tn(dl_high, x3) + tn(dl_low, x3)
    dx3 = nn(place_ref[...], dxb_ref[...]) + nt(dl_high, router_ref[...]) + nt(dl_low, router_ref[...])
    da, dw = rms_back(r2_ref[...], gains_ref[2:3, :], dx3)
    small_ref[2:3, :] = dw
    dr_ref[...] = g + da
    do2 = dr_ref[...].astype(BF16)
    loads[0].wait()
    doc_ref[...] = nt(do2, w_co[...]).astype(BF16)

    part = width // seq_count

    def square_start(i, left, right):
        grad = tn(left, right).astype(BF16).reshape(chips, 2, part, width)
        at = pl.ds(i * part, part)
        for k in range(2):
            w_out[k, :, at, :] = grad[:, k]
        copy = remote(w_out.at[other_core, :, at, :], w_pair.at[:, at, :], wp_send.at[i], wp_recv.at[i], {"seq": partner})
        copy.start()
        return copy

    def square_chips(i, pair_copy):
        at = pl.ds(i * part, part)
        pair_copy.wait_recv()
        w_out[core, :, at, :] = (w_out[core, :, at, :].astype(F32) + w_pair[:, at, :].astype(F32)).astype(BF16)
        copies = [
            remote(w_out.at[core, other_chips[d], at, :], w_chip.at[d, at, :], wc_send.at[i, d], wc_recv.at[i, d],
                   {"seq": others[d]})
            for d in range(chips - 1)
        ]
        for copy in copies:
            copy.start()
        return copies

    def square_sum(i, copies):
        at = pl.ds(i * part, part)
        total = w_out[core, chip, at, :].astype(F32)
        for d, copy in enumerate(copies):
            copy.wait_recv()
            total = total + w_chip[d, at, :].astype(F32)
        squares_ref[at, :] = total.astype(BF16)

    co_pair = square_start(2, oc_ref[...], do2)

    loads[1].wait()
    loads[2].wait()
    enc_rows = ekv.shape[0]
    enc_part = enc_rows // seq_count

    @pl.loop(0, pairs)
    def _(p):
        lanes, value_lanes = pair_lanes(p), pair_lanes(pairs + p)
        doc_both = head_stack(doc_ref[:, lanes])
        weights = cross_prob[p]
        wide = weights.astype(F32)
        dp = nt(ekv[:, value_lanes], doc_both)
        dc = (wide * (dp - jnp.sum(wide * dp, axis=0, keepdims=True))).astype(BF16)
        dk = nn(dc, head_stack(qc_ref[:, lanes])).astype(BF16).reshape(chips, 2, enc_part, LANES)
        dv = nn(weights, doc_both).astype(BF16).reshape(chips, 2, enc_part, LANES)
        for k in range(2):
            e_out[k, :, :, lanes] = dk[:, k]
            e_out[k, :, :, value_lanes] = dv[:, k]
        dqc_ref[:, lanes] = (head_unstack(tn(ekv[:, lanes], dc), rows) * 0.125).astype(BF16)

    e_pair_copy = remote(e_out.at[other_core], e_pair, ep_send.at[0], ep_recv.at[0], {"seq": partner})
    e_pair_copy.start()
    co_chips = square_chips(2, co_pair)
    dqc = dqc_ref[...]
    loads[3].wait()
    loads[4].wait()
    da, dw = rms_back(r1_ref[...], gains_ref[1:2, :], nt(dqc, w_cq[...]))
    small_ref[1:2, :] = dw
    dr_ref[...] = dr_ref[...] + da
    do1 = dr_ref[...].astype(BF16)
    doc_ref[...] = nt(do1, w_so[...]).astype(BF16)
    e_pair_copy.wait_recv()
    e_out[core] = (e_out[core].astype(F32) + e_pair[...].astype(F32)).astype(BF16)
    e_chip_copies = [
        remote(e_out.at[core, other_chips[d]], e_chip.at[d], ec_send.at[d], ec_recv.at[d], {"seq": others[d]})
        for d in range(chips - 1)
    ]
    for copy in e_chip_copies:
        copy.start()
    cq_pair = square_start(1, n2_ref[...], dqc)
    so_pair = square_start(0, o_ref[...], do1)
    cq_chips = square_chips(1, cq_pair)
    so_chips = square_chips(0, so_pair)

    loads[5].wait()
    loads[6].wait()
    ds_ref[pl.ds(0, rows), :] = jnp.zeros((rows, 2 * rows), BF16)
    near = pl.ds(pl.multiple_of(me * rows, rows), 2 * rows)
    flip = (
        lax.broadcasted_iota(jnp.int32, (2 * rows, 2 * rows), 0) + lax.broadcasted_iota(jnp.int32, (2 * rows, 2 * rows), 1)
        == 2 * rows - 1
    ).astype(BF16)

    def pair_copy(p):
        return remote(t_out.at[p, other_core], t_pair.at[p], tp_send.at[p], tp_recv.at[p], {"seq": partner})

    def chip_copies(p):
        return [
            remote(t_out.at[p, core, other_chips[d]], t_chip.at[p, d], tc_send.at[p, d], tc_recv.at[p, d], {"seq": others[d]})
            for d in range(chips - 1)
        ]

    @pl.loop(0, pairs + 2)
    def _(t):
        @pl.when(t < pairs)
        def _():
            p = jnp.minimum(t, pairs - 1)
            lanes, value_lanes = pair_lanes(p), pair_lanes(pairs + p)
            do_both = head_stack(doc_ref[:, lanes])
            weights = prob[p]
            wide = weights.astype(F32)
            dp = nt(kv_all[:, value_lanes], do_both)
            ds_wide = wide * (dp - jnp.sum(wide * dp, axis=0, keepdims=True))
            ds = ds_wide.astype(BF16)
            ds_ref[pl.ds(rows, span), :] = ds
            total_ref[pl.ds(p, 1), :] = jnp.sum(ds.astype(F32), axis=0, keepdims=True)
            dk = nn(ds, head_stack(q_ref[:, lanes])).astype(BF16).reshape(chips, 2, rows, LANES)
            dv = nn(weights, do_both).astype(BF16).reshape(chips, 2, rows, LANES)
            for k in range(2):
                t_out[p, k, :, :, :LANES] = dk[:, k]
                t_out[p, k, :, :, LANES:] = dv[:, k]
            pair_copy(p).start()
            dqkv_ref[:, lanes] = (head_unstack(tn(kv_all[:, lanes], ds), rows) * 0.125).astype(BF16)
            turned = nn(flip, ds_ref[near, :])
            for h in range(2):
                one = turned[:, h * rows : (h + 1) * rows]
                one = jnp.concatenate([one, jnp.zeros_like(one)], axis=1)
                one = pltpu.roll(one, 1, 1, stride=1, stride_axis=0)
                diag_ref[pl.ds(2 * p + h, 1), :] = jnp.sum(one, axis=0, keepdims=True)

        @pl.when((t >= 1) & (t <= pairs))
        def _():
            p = jnp.clip(t - 1, 0, pairs - 1)
            pair_copy(p).wait_recv()
            t_out[p, core] = (t_out[p, core].astype(F32) + t_pair[p].astype(F32)).astype(BF16)
            for copy in chip_copies(p):
                copy.start()

        @pl.when(t >= 2)
        def _():
            p = jnp.clip(t - 2, 0, pairs - 1)
            total = t_out[p, core, chip].astype(F32)
            for d, copy in enumerate(chip_copies(p)):
                copy.wait_recv()
                total = total + t_chip[p, d].astype(F32)
            dqkv_ref[:, pair_lanes(pairs + p)] = total[:, :LANES].astype(BF16)
            dqkv_ref[:, pair_lanes(2 * pairs + p)] = total[:, LANES:].astype(BF16)

    dqkv = dqkv_ref[...]
    loads[7].wait()
    x = x_ref[...].astype(F32)
    da, dw = rms_back(x, gains_ref[0:1, :], nt(dqkv, w_qkv[...]))
    small_ref[0:1, :] = dw
    dx_ref[...] = dr_ref[...] + da
    dqkv_t_ref[...] = dqkv.T

    heads = 2 * pairs
    table = diag_ref[:, 2 * rows - LANES :]
    totals = total_ref[...]
    first = jnp.sum(totals[:, :rows], axis=1, keepdims=True)
    second = jnp.sum(totals[:, rows:], axis=1, keepdims=True)
    head = lax.broadcasted_iota(jnp.int32, (heads, pairs), 0)
    pair = lax.broadcasted_iota(jnp.int32, (heads, pairs), 1)
    spread = lambda odd, v: jnp.dot((head == 2 * pair + odd).astype(F32), v, precision=highest, preferred_element_type=F32)
    whole = spread(0, jnp.broadcast_to(first, (pairs, LANES))) + spread(1, jnp.broadcast_to(second, (pairs, LANES)))
    rest = whole - jnp.sum(table, axis=1, keepdims=True)
    lane = lax.broadcasted_iota(jnp.int32, table.shape, 1)
    table = table + jnp.where(lane == LANES - 1, rest, 0.0)
    bucket = lax.broadcasted_iota(jnp.int32, (LANES, LANES), 0)
    pick = (buckets_ref[...] == bucket).astype(F32)
    small_ref[8 : 8 + heads, :LANES] = lax.dot_general(
        table, pick, (((1,), (1,)), ((), ())), precision=highest, preferred_element_type=F32
    )

    total = e_out[core, chip].astype(F32)
    for d, copy in enumerate(e_chip_copies):
        copy.wait_recv()
        total = total + e_chip[d].astype(F32)
    e_mine[...] = total.astype(BF16).reshape(e_mine.shape)
    e_exp_copies = [
        remote(e_mine.at[peer], e_exp.at[d], ee_send.at[d], ee_recv.at[d], {"exp": peer}) for d, peer in enumerate(peers)
    ]
    for copy in e_exp_copies:
        copy.start()
    square_sum(2, co_chips)
    square_sum(1, cq_chips)
    square_sum(0, so_chips)
    total = e_mine[mine].astype(F32)
    for d, copy in enumerate(e_exp_copies):
        copy.wait_recv()
        total = total + e_exp[d].astype(F32)
    dekv_ref[...] = total.astype(BF16)

    for copy in [co_pair, cq_pair, so_pair, e_pair_copy] + co_chips + cq_chips + so_chips + e_chip_copies + e_exp_copies:
        copy.wait_send()

    @pl.loop(0, pairs)
    def _(p):
        pair_copy(p).wait_send()
        for copy in chip_copies(p):
            copy.wait_send()


def backward_call(seq_count, experts, made, dxb, g, x, r1, r2, gates, place, routes, x3, n2, o, oc, q, qc, gains, router,
                  buckets, kv, p, pc, ekv, co, cq, so, qkv):
    rows, width = x.shape
    span = seq_count * rows
    pairs = width // LANES
    chips = seq_count // 2
    enc_rows = ekv.shape[0]
    part = 3 * width // seq_count
    enc_part = enc_rows // seq_count
    shape = jax.ShapeDtypeStruct
    dma = lambda *n: pltpu.SemaphoreType.DMA(n)
    vmem = pltpu.VMEM
    return pl.pallas_call(
        functools.partial(backward_kernel, seq_count, experts),
        out_shape=(
            shape((rows, width), BF16), shape((rows, width), F32), shape((3 * width, rows), BF16), shape((part, width), BF16),
            shape((enc_part // experts, 2 * width), BF16), shape((24, width), F32),
        ),
        in_specs=[VMEM] * 18 + [ANY] * 8,
        out_specs=(VMEM,) * 6,
        scratch_shapes=[
            vmem((span, 2 * width), BF16), vmem((pairs, span, 2 * rows), BF16), vmem((pairs, enc_rows, 2 * rows), BF16),
            vmem((enc_rows, 2 * width), BF16), vmem(co.shape, BF16), vmem(cq.shape, BF16), vmem(so.shape, BF16),
            vmem(qkv.shape, BF16), vmem((rows, width), F32), vmem((rows, width), BF16), vmem((rows, width), BF16),
            vmem((rows, 3 * width), BF16), vmem((span + rows, 2 * rows), BF16), vmem((2 * pairs, 2 * rows), F32),
            vmem((pairs, 2 * rows), F32),
            vmem((2, chips, enc_part, 2 * width), BF16), vmem((chips, enc_part, 2 * width), BF16),
            vmem((chips - 1, enc_part, 2 * width), BF16), vmem((experts, enc_part // experts, 2 * width), BF16),
            vmem((experts - 1, enc_part // experts, 2 * width), BF16),
            vmem((pairs, 2, chips, rows, 2 * LANES), BF16), vmem((pairs, chips, rows, 2 * LANES), BF16),
            vmem((pairs, chips - 1, rows, 2 * LANES), BF16),
            vmem((2, chips, part, width), BF16), vmem((chips, part, width), BF16), vmem((chips - 1, part, width), BF16),
            dma(8), dma(1), dma(1), dma(chips - 1), dma(chips - 1), dma(experts - 1), dma(experts - 1), dma(pairs), dma(pairs),
            dma(pairs, chips - 1), dma(pairs, chips - 1), dma(3), dma(3), dma(3, chips - 1), dma(3, chips - 1),
        ],
        compiler_params=pltpu.CompilerParams(collective_id=2, has_side_effects=True, vmem_limit_bytes=60 << 20),
        name="backward",
    )(made, dxb, g, x, r1, r2, gates, place, routes, x3, n2, o, oc, q, qc, gains, router, buckets, kv, p, pc, ekv, co, cq, so, qkv)


def weights_kernel(
    seq_count, experts,
    dqkv_t_ref, squares_ref, dekv_ref, small_ref, n1_hbm, x_hbm, dm_hbm, w_in_hbm, w_out_hbm, ckv_hbm,
    square_out_ref, qkv_out_ref, dekv_out_ref, small_out_ref, gin_ref, gout_ref, genc_ref,
    n1_all, x_all, dm_all, w_in, w_out, w_ckv, right, turned, mine_q, sq_slots, q_slots, sq_all, q_all, dekv_all, gin_out, gin_in,
    small_a, small_b, small_c, small_pair, small_chip, small_exp,
    load_sem, r_send, r_recv, sz_send, sz_recv, sg_send, sg_recv, sa_send, sa_recv, qz_send, qz_recv, qg_send, qg_recv,
    qa_send, qa_recv, ez_send, ez_recv, ea_send, ea_recv, g_send, g_recv, s1_send, s1_recv, s2_send, s2_recv, s3_send, s3_recv,
):
    chips = seq_count // 2
    part, width = squares_ref.shape
    rows = dqkv_t_ref.shape[1]
    me = lax.axis_index("seq")
    mine = lax.axis_index("exp")
    core, chip, partner, others, sources = seq_peers(me, chips)
    peers = expert_peers(mine, experts)
    everyone = [lax.rem(me + d, seq_count) for d in range(1, seq_count)]
    hidden = w_in.shape[1]
    at_hidden = pl.ds(pl.multiple_of(me * hidden, hidden), hidden)
    loads = [
        pltpu.make_async_copy(src, dst, load_sem.at[i])
        for i, (src, dst) in enumerate(
            [(n1_hbm, n1_all), (x_hbm, x_all), (w_in_hbm.at[:, at_hidden], w_in), (dm_hbm, dm_all),
             (w_out_hbm.at[at_hidden, :], w_out), (ckv_hbm, w_ckv)]
        )
    ]
    for load in loads:
        load.start()
    enter([{"seq": device} for device in everyone] + [{"exp": peer} for peer in peers])
    started = []

    def send(src, dst, send_sem, recv_sem, device):
        copy = remote(src, dst, send_sem, recv_sem, device)
        copy.start()
        started.append(copy)
        return copy

    own_lanes = pl.ds(pl.multiple_of(me * rows, rows), rows)
    own_rows = pl.ds(pl.multiple_of(me * part, part), part)
    rights = [
        send(dqkv_t_ref.at[pl.ds(pl.multiple_of(peer * part, part), part), :], right.at[:, own_lanes], r_send.at[d], r_recv.at[d],
             {"seq": peer})
        for d, peer in enumerate(everyone)
    ]
    right[:, own_lanes] = dqkv_t_ref[own_rows, :]

    half_rows, half_lanes = part // 2, width // (experts // 2)

    def quarter(e):
        return (
            pl.ds(pl.multiple_of(lax.div(e, experts // 2) * half_rows, half_rows), half_rows),
            pl.ds(pl.multiple_of(lax.rem(e, experts // 2) * half_lanes, half_lanes), half_lanes),
        )

    def scatter_exp(src, slots, sends, recvs):
        return [
            send(src.at[quarter(peer)], slots.at[d], sends.at[d], recvs.at[d], {"exp": peer}) for d, peer in enumerate(peers)
        ]

    def gather_exp(src, slots, copies, every, sends, recvs):
        total = src[quarter(mine)].astype(F32)
        for d, copy in enumerate(copies):
            copy.wait_recv()
            total = total + slots[d].astype(F32)
        block = (me,) + quarter(mine)
        every[block] = total.astype(BF16)
        return [
            send(every.at[block], every.at[block], sends.at[d], recvs.at[d], {"exp": peer}) for d, peer in enumerate(peers)
        ]

    def gather_seq(every, block, copies, sends, recvs):
        for copy in copies:
            copy.wait_recv()
        return [send(every.at[block], every.at[block], sends.at[d], recvs.at[d], {"seq": others[d - 1]}) for d in range(1, chips)] + [
            send(every.at[block], every.at[block], sends.at[0], recvs.at[0], {"seq": partner})
        ]

    def pass_on(every, copies, sends, recvs):
        forwards = []
        for d in range(1, chips):
            copies[d - 1].wait_recv()
            block = every.at[sources[d - 1]]
            forwards.append(send(block, block, sends.at[chips - 1 + d], recvs.at[chips - 1 + d], {"seq": partner}))
        return forwards

    sq_scatter = scatter_exp(squares_ref, sq_slots, sz_send, sz_recv)
    dekv_all[me, mine] = dekv_ref[...]
    e_exp = [
        send(dekv_all.at[me, mine], dekv_all.at[me, mine], ez_send.at[d], ez_recv.at[d], {"exp": peer})
        for d, peer in enumerate(peers)
    ]
    small_a[...] = small_ref[...]
    s_pair = send(small_a, small_pair, s1_send.at[0], s1_recv.at[0], {"seq": partner})

    for load in loads[:1]:
        load.wait()
    for copy in rights:
        copy.wait_recv()
    turned[...] = nn(right[...], n1_all[...].reshape(seq_count * rows, width)).astype(BF16)
    q_scatter = scatter_exp(turned, q_slots, qz_send, qz_recv)
    sq_gather = gather_exp(squares_ref, sq_slots, sq_scatter, sq_all, sg_send, sg_recv)
    e_seq = gather_seq(dekv_all, me, e_exp, ea_send, ea_recv)
    s_pair.wait_recv()
    small_b[...] = small_a[...] + small_pair[...]
    s_chip = [
        send(small_b, small_chip.at[d], s2_send.at[d], s2_recv.at[d], {"seq": others[d]}) for d in range(chips - 1)
    ]

    for load in loads[1:5]:
        load.wait()
    x = x_all[...].reshape(-1, width)
    value, slope = gelu_parts(nn(x, w_in[...]))
    dm = dm_all[...].reshape(-1, width)
    gout_ref[...] = tn(value.astype(BF16), dm)
    sq_seq = gather_seq(sq_all, me, sq_gather, sa_send, sa_recv)
    dh = (nt(dm, w_out[...]) * slope).astype(BF16)
    gin_out[...] = tn(x, dh).astype(BF16).reshape(gin_out.shape)
    gins = [
        send(gin_out.at[peer], gin_in.at[:, at_hidden], g_send.at[d], g_recv.at[d], {"seq": peer})
        for d, peer in enumerate(everyone)
    ]
    gin_in[:, at_hidden] = gin_out[me]
    q_gather = gather_exp(turned, q_slots, q_scatter, q_all, qg_send, qg_recv)
    e_forwards = pass_on(dekv_all, e_seq, ea_send, ea_recv)
    loads[5].wait()
    genc_ref[...] = nt(dekv_ref[...], w_ckv[...])
    total = small_b[...]
    for d, copy in enumerate(s_chip):
        copy.wait_recv()
        total = total + small_chip[d]
    small_c[...] = total
    s_exp = [send(small_c, small_exp.at[d], s3_send.at[d], s3_recv.at[d], {"exp": peer}) for d, peer in enumerate(peers)]
    q_seq = gather_seq(q_all, me, q_gather, qa_send, qa_recv)
    sq_forwards = pass_on(sq_all, sq_seq, sa_send, sa_recv)
    total = small_c[...]
    for d, copy in enumerate(s_exp):
        copy.wait_recv()
        total = total + small_exp[d]
    small_out_ref[...] = total
    for copy in gins:
        copy.wait_recv()
    gin_ref[...] = gin_in[...]
    e_seq[-1].wait_recv()
    for copy in e_forwards:
        copy.wait_recv()
    dekv_out_ref[...] = dekv_all[...]
    sq_seq[-1].wait_recv()
    for copy in sq_forwards:
        copy.wait_recv()
    square_out_ref[...] = sq_all[...]
    q_forwards = pass_on(q_all, q_seq, qa_send, qa_recv)
    q_seq[-1].wait_recv()
    for copy in q_forwards:
        copy.wait_recv()
    qkv_out_ref[...] = q_all[...]
    for copy in started:
        copy.wait_send()


def weights_call(seq_count, experts, dqkv_t, squares, dekv, small, n1_all, x_all, dm_all, w_in, w_out, ckv):
    part, width = squares.shape
    chips = seq_count // 2
    hidden = w_in.shape[1] // seq_count
    shape = jax.ShapeDtypeStruct
    vmem = pltpu.VMEM
    dma = lambda n: pltpu.SemaphoreType.DMA((n,))
    every = (seq_count, part, width)
    every_e = (seq_count, experts) + dekv.shape
    d_part = width // seq_count
    z, c, a = experts - 1, chips - 1, 2 * chips - 1
    return pl.pallas_call(
        functools.partial(weights_kernel, seq_count, experts),
        out_shape=(
            shape(every, BF16), shape(every, BF16), shape(every_e, BF16), shape(small.shape, F32),
            shape((d_part, w_in.shape[1]), BF16), shape((hidden, width), F32), shape((dekv.shape[0], width), F32),
        ),
        in_specs=[VMEM] * 4 + [ANY] * 6,
        out_specs=(VMEM,) * 7,
        scratch_shapes=[
            vmem(n1_all.shape, BF16), vmem(x_all.shape, BF16), vmem(dm_all.shape, BF16), vmem((width, hidden), BF16),
            vmem((hidden, width), BF16), vmem(ckv.shape, BF16), vmem((part, seq_count * dqkv_t.shape[1]), BF16),
            vmem((part, width), BF16), vmem((8, 128), BF16), vmem((z, part // 2, width // (experts // 2)), BF16),
            vmem((z, part // 2, width // (experts // 2)), BF16), vmem(every, BF16), vmem(every, BF16), vmem(every_e, BF16),
            vmem((seq_count, d_part, hidden), BF16), vmem((d_part, w_in.shape[1]), BF16),
            vmem(small.shape, F32), vmem(small.shape, F32), vmem(small.shape, F32), vmem(small.shape, F32),
            vmem((c,) + small.shape, F32), vmem((z,) + small.shape, F32),
            dma(6), dma(seq_count - 1), dma(seq_count - 1), dma(z), dma(z), dma(z), dma(z), dma(a), dma(a),
            dma(z), dma(z), dma(z), dma(z), dma(a), dma(a), dma(z), dma(z), dma(a), dma(a),
            dma(seq_count - 1), dma(seq_count - 1), dma(1), dma(1), dma(c), dma(c), dma(z), dma(z),
        ],
        compiler_params=pltpu.CompilerParams(collective_id=3, has_side_effects=True, vmem_limit_bytes=60 << 20),
        name="weights",
    )(dqkv_t, squares, dekv, small, n1_all, x_all, dm_all, w_in, w_out, ckv)


def finish_kernel(
    experts, square_ref, qkv_ref, dekv_ref, small_ref, gin_ref, gout_ref, genc_ref, layer_ref, dx_ref, enc_ref,
    layer_out, dx_out, genc_out, gains_out, qkv_hbm, so_hbm, cq_hbm, ckv_hbm, co_hbm, rel_out, router_out, gin_out, gout_out,
    squares, qkv, ckv, sem,
):
    seq_count, part, width = square_ref.shape
    each = part // 3
    copies = []

    def store(src, dst):
        copy = pltpu.make_async_copy(src, dst, sem.at[len(copies)])
        copy.start()
        copies.append(copy)

    for i, out in enumerate((so_hbm, cq_hbm, co_hbm)):
        for s in range(seq_count):
            squares[i, s * each : (s + 1) * each, :] = square_ref[s, i * each : (i + 1) * each, :].astype(F32)
        store(squares.at[i], out)
    flat = qkv_ref[...].reshape(seq_count * part, width)
    for n in range(3):
        for block in range(width // LANES):
            at = slice(n * width + block * LANES, n * width + (block + 1) * LANES)
            qkv[:, at] = flat[at, :].astype(F32).T
        at = slice(n * width, (n + 1) * width)
        store(qkv.at[:, at], qkv_hbm.at[:, at])
    dekv = dekv_ref[...].reshape(-1, 2 * width)
    for n in range(2):
        at = slice(n * width, (n + 1) * width)
        ckv[:, at] = tn(enc_ref[...], dekv[:, at])
        store(ckv.at[:, at], ckv_hbm.at[:, at])
    layer_out[...] = layer_ref[...]
    dx_out[...] = dx_ref[...]
    genc_out[...] = genc_ref[...]
    gains_out[...] = small_ref[0:3, :]
    router_out[...] = small_ref[4 : 4 + experts, :].T
    heads, buckets = rel_out.shape[1], rel_out.shape[0]
    rel_out[...] = small_ref[8 : 8 + heads, :buckets].T
    gin_out[...] = gin_ref[...].astype(F32)
    gout_out[...] = gout_ref[...]
    for copy in copies:
        copy.wait()


def finish_call(experts, buckets, square, qkv, dekv, small, gin, gout, genc, layer, dx, enc):
    seq_count, part, width = square.shape
    shape = jax.ShapeDtypeStruct
    return pl.pallas_call(
        functools.partial(finish_kernel, experts),
        out_shape=(
            shape(layer.shape, BF16), shape(dx.shape, F32), shape(genc.shape, F32), shape((3, width), F32),
            shape((width, 3 * width), F32), shape((width, width), F32), shape((width, width), F32), shape((width, 2 * width), F32),
            shape((width, width), F32), shape((buckets, width // HD), F32), shape((width, experts), F32), shape(gin.shape, F32),
            shape(gout.shape, F32),
        ),
        in_specs=[VMEM] * 10,
        out_specs=(VMEM,) * 4 + (ANY,) * 5 + (VMEM,) * 4,
        scratch_shapes=[
            pltpu.VMEM((3, width, width), F32), pltpu.VMEM((width, 3 * width), F32), pltpu.VMEM((width, 2 * width), F32),
            pltpu.SemaphoreType.DMA((8,)),
        ],
        compiler_params=pltpu.CompilerParams(vmem_limit_bytes=60 << 20),
        name="finish",
    )(square, qkv, dekv, small, gin, gout, genc, layer, dx, enc)


def fused(inputs, encoder, lengths, buckets, routes, norm_gains, self_qkv, self_out, cross_q, cross_kv, cross_out,
          rel_bias, router, expert_in, expert_out, cotangent):
    seq_count = lax.axis_size("seq")
    rows, width = inputs.shape[1:]
    experts = router.shape[1]
    capacity = 5 * rows // (4 * experts)
    stride = -(-capacity // 16) * 16
    (n1_all, kv_all, prob, cross_prob, ekv, q, o, n2, qc, oc, x3, r1, r2, gates, place, xs, dms) = forward_call(
        seq_count, capacity, stride, inputs[0], encoder, lengths, buckets[None, :], routes[0], norm_gains, self_qkv,
        self_out, cross_q, cross_kv, cross_out, rel_bias, router, cotangent[0])
    made, dxb, x_all, dm_all = experts_call(seq_count, experts, stride, xs, dms, expert_in[0], expert_out[0])
    (layer_out, grad_input, dqkv_t, squares, dekv, small) = backward_call(
        seq_count, experts, made.reshape(-1, width), dxb.reshape(-1, width), cotangent[0], inputs[0], r1, r2, gates, place,
        routes[0], x3, n2, o, oc, q, qc, norm_gains, router, buckets[None, :], kv_all, prob, cross_prob, ekv, cross_out,
        cross_q, self_out, self_qkv)
    square_all, qkv_all, dekv_all, small, gin, gout, grad_encoder = weights_call(
        seq_count, experts, dqkv_t, squares, dekv, small, n1_all, x_all, dm_all, expert_in[0], expert_out[0], cross_kv)
    (layer_out, grad_input, grad_encoder, gains, g_qkv, g_so, g_cq, g_ckv, g_co, g_rel, g_router, gin, gout) = finish_call(
        experts, rel_bias.shape[0], square_all, qkv_all, dekv_all, small, gin, gout, grad_encoder, layer_out, grad_input, encoder)
    return (layer_out[None], grad_input[None], grad_encoder, gains, g_qkv, g_so, g_cq, g_ckv, g_co, g_rel, g_router,
            gin[None], gout[None])


def on_device(*operands):
    if lax.axis_size("seq") * operands[0].shape[1] <= 1024 and lax.axis_size("seq") % 2 == 0:
        return fused(*operands)
    return streamed(*operands)


def solution(mesh):
    in_specs = (
        P("exp", "seq", None),
        P(),
        P("exp", None),
        P(),
        P("exp", "seq", None),
        P(),
        P(),
        P(),
        P(),
        P(),
        P(),
        P(),
        P(),
        P("exp", None, None),
        P("exp", None, None),
        P("exp", "seq", None),
    )
    out_specs = (
        P("exp", "seq", None),
        P("exp", "seq", None),
        P(("seq", "exp"), None),
        P(),
        P(),
        P(),
        P(),
        P(),
        P(),
        P(),
        P(),
        P("exp", "seq", None),
        P("exp", "seq", None),
    )
    return jax.shard_map(
        on_device, mesh=mesh, in_specs=in_specs, out_specs=out_specs, check_vma=False
    )
```

```python
import functools
import math

import jax
import jax.numpy as jnp
from jax import lax
from jax.experimental import pallas as pl
from jax.experimental.pallas import tpu as pltpu
from jax.sharding import PartitionSpec as P

H = 12
HD = 64


epsilon = 1e-06
masked_out = -1e30
highest = lax.Precision.HIGHEST


def rms_norm(value, gain):
    return value * lax.rsqrt(jnp.mean(value * value, axis=-1, keepdims=True) + epsilon) * gain


def split_heads(value):
    return value.reshape(value.shape[0], H, HD)


def doc_index(positions, doc_ends):
    return jnp.sum((positions[:, None] >= doc_ends[None, :]).astype(jnp.int32), axis=1)


def band_pick(offset_gap, query_rows, key_rows, table_span):
    band_len = query_rows + key_rows + 1
    column = jnp.arange(band_len, dtype=jnp.int32)
    distance = jnp.clip(offset_gap + query_rows - column, 0, table_span - 1)
    return (distance[:, None] == jnp.arange(table_span, dtype=jnp.int32)[None, :]).astype(
        jnp.float32
    )


def relative_bias(table, offset_gap, query_rows, key_rows):
    head_count = table.shape[0]
    band_len = query_rows + key_rows + 1
    band = jnp.dot(
        table, band_pick(offset_gap, query_rows, key_rows, table.shape[1]).T, precision=highest
    )
    tiled = jnp.broadcast_to(band[:, None, :], (head_count, query_rows, band_len)).reshape(
        head_count, query_rows * band_len
    )
    skewed = tiled[:, : query_rows * (band_len - 1)].reshape(head_count, query_rows, band_len - 1)
    return skewed[:, :, query_rows : query_rows + key_rows]


def table_terms(score_grads, offset_gap, table_span):
    head_count, query_rows, key_rows = score_grads.shape
    band_len = query_rows + key_rows + 1
    placed = jnp.pad(score_grads.astype(jnp.float32), ((0, 0), (0, 0), (query_rows, 0)))
    flat = jnp.pad(
        placed.reshape(head_count, query_rows * (band_len - 1)), ((0, 0), (0, query_rows))
    )
    diagonal_sums = jnp.sum(flat.reshape(head_count, query_rows, band_len), axis=1)
    return jnp.dot(
        diagonal_sums, band_pick(offset_gap, query_rows, key_rows, table_span), precision=highest
    )


def self_scores(queries, query_start, keys_part, key_start, doc_ends, table):
    query_rows = queries.shape[0]
    key_rows = keys_part.shape[0]
    query_pos = query_start + jnp.arange(query_rows, dtype=jnp.int32)
    key_pos = key_start + jnp.arange(key_rows, dtype=jnp.int32)
    offset_gap = query_start - key_start
    raw_scores = (
        jnp.einsum(
            "qhd,khd->hqk",
            split_heads(queries),
            split_heads(keys_part),
            preferred_element_type=jnp.float32,
        )
        * 0.125
    )
    allowed = (key_pos[None, :] <= query_pos[:, None]) & (
        doc_index(key_pos, doc_ends)[None, :] == doc_index(query_pos, doc_ends)[:, None]
    )
    scores = jnp.where(
        allowed[None],
        raw_scores + relative_bias(table, offset_gap, query_rows, key_rows),
        masked_out,
    )
    return (scores, allowed[None], offset_gap)


def over_blocks(step, running, pieces):
    rows_total = pieces[0].shape[0]
    block_rows = math.gcd(rows_total, 512)
    block_count = rows_total // block_rows
    stacked = tuple(
        (member.reshape(block_count, block_rows, *member.shape[1:]) for member in pieces)
    )

    def scan_step(inner_running, block_input):
        block_id, members = block_input
        return (step(inner_running, members, block_id * block_rows), None)

    result, ignored = lax.scan(
        scan_step, running, (jnp.arange(block_count, dtype=jnp.int32), stacked)
    )
    return result


def streamed(
    inputs,
    encoder,
    lengths,
    buckets,
    routes,
    norm_gains,
    self_qkv,
    self_out,
    cross_q,
    cross_kv,
    cross_out,
    rel_bias,
    router,
    expert_in,
    expert_out,
    cotangent,
):
    hidden = inputs[0].astype(jnp.float32)
    rows_dev = hidden.shape[0]
    model_width = hidden.shape[1]
    seq_count = lax.axis_size("seq")
    seq_index = lax.axis_index("seq")
    own_start = seq_index * rows_dev
    doc_ends = jnp.cumsum(lengths[0])
    bucket_pick = (
        buckets[:, None] == jnp.arange(rel_bias.shape[0], dtype=jnp.int32)[None, :]
    ).astype(jnp.float32)
    table = jnp.dot(bucket_pick, rel_bias, precision=highest).T
    normed_one, norm_one_back = jax.vjp(rms_norm, hidden, norm_gains[0])
    normed_one = normed_one.astype(jnp.bfloat16)
    qkv_all = jnp.dot(normed_one, self_qkv, preferred_element_type=jnp.float32).astype(jnp.bfloat16)
    queries = qkv_all[:, :model_width]
    keys_own = qkv_all[:, model_width : 2 * model_width]
    values_own = qkv_all[:, 2 * model_width :]

    def forward_step(running, pieces, key_start):
        top_old, denominator, summed = running
        keys_part, values_part = pieces
        scores, allowed, offset_gap = self_scores(
            queries, own_start, keys_part, key_start, doc_ends, table
        )
        top_new = jnp.maximum(top_old, jnp.max(scores, axis=-1))
        weights_raw = jnp.where(allowed, jnp.exp(scores - top_new[..., None]), 0.0)
        rescale = jnp.exp(top_old - top_new)
        denominator = denominator * rescale + jnp.sum(weights_raw, axis=-1)
        summed = summed * rescale[..., None] + jnp.einsum(
            "hqk,khd->hqd",
            weights_raw.astype(jnp.bfloat16),
            split_heads(values_part),
            preferred_element_type=jnp.float32,
        )
        return (top_new, denominator, summed)

    start_state = (
        jnp.full((H, rows_dev), masked_out, jnp.float32),
        jnp.zeros((H, rows_dev), jnp.float32),
        jnp.zeros((H, rows_dev, HD), jnp.float32),
    )
    top_score, denominator, summed = over_blocks(
        forward_step,
        start_state,
        (
            lax.all_gather(keys_own, "seq", axis=0, tiled=True),
            lax.all_gather(values_own, "seq", axis=0, tiled=True),
        ),
    )
    log_total = top_score + jnp.log(denominator)
    attended_full = (
        (summed / denominator[..., None]).transpose(1, 0, 2).reshape(rows_dev, model_width)
    )
    attended = attended_full.astype(jnp.bfloat16)
    after_self = hidden + jnp.dot(attended, self_out, preferred_element_type=jnp.float32)
    enc_kv = jnp.dot(encoder, cross_kv, preferred_element_type=jnp.float32).astype(jnp.bfloat16)
    cross_keys = split_heads(enc_kv[:, :model_width])
    cross_values = split_heads(enc_kv[:, model_width:])
    normed_two, norm_two_back = jax.vjp(rms_norm, after_self, norm_gains[1])
    normed_two = normed_two.astype(jnp.bfloat16)
    cross_queries = jnp.dot(normed_two, cross_q, preferred_element_type=jnp.float32).astype(
        jnp.bfloat16
    )
    cross_scores = (
        jnp.einsum(
            "qhd,khd->hqk",
            split_heads(cross_queries),
            cross_keys,
            preferred_element_type=jnp.float32,
        )
        * 0.125
    )
    cross_raw = jnp.exp(cross_scores - jnp.max(cross_scores, axis=-1, keepdims=True))
    cross_prob = cross_raw / jnp.sum(cross_raw, axis=-1, keepdims=True)
    cross_prob_low = cross_prob.astype(jnp.bfloat16)
    cross_att = (
        jnp.einsum("hqk,khd->qhd", cross_prob_low, cross_values, preferred_element_type=jnp.float32)
        .reshape(rows_dev, model_width)
        .astype(jnp.bfloat16)
    )
    after_cross = after_self + jnp.dot(cross_att, cross_out, preferred_element_type=jnp.float32)
    normed_three, norm_three_back = jax.vjp(rms_norm, after_cross, norm_gains[2])
    routed_in = normed_three.astype(jnp.bfloat16)
    gates = jax.nn.softmax(jnp.dot(routed_in, router, preferred_element_type=jnp.float32), axis=-1)
    expert_total = router.shape[1]
    local_experts = expert_in.shape[0]
    capacity = 5 * rows_dev // (4 * expert_total)
    route_ids = routes[0, :, 0]
    chosen = route_ids[:, None] == jnp.arange(expert_total, dtype=jnp.int32)[None, :]
    slots = jnp.sum(jnp.where(chosen, jnp.cumsum(chosen.astype(jnp.int32), axis=0), 0), axis=1) - 1
    kept = slots < capacity
    picked_gate = jnp.sum(jnp.where(chosen, gates, 0.0), axis=1)
    gate_used = picked_gate * kept.astype(jnp.float32)
    target = jnp.where(kept, route_ids * capacity + slots, -1)
    dispatch = (
        jnp.arange(expert_total * capacity, dtype=jnp.int32)[:, None] == target[None, :]
    ).astype(jnp.bfloat16)
    outgoing = (
        jnp.dot(dispatch, routed_in, preferred_element_type=jnp.float32)
        .astype(jnp.bfloat16)
        .reshape(expert_total, capacity, model_width)
    )
    arrived = lax.all_to_all(outgoing, "exp", split_axis=0, concat_axis=0, tiled=True).reshape(
        -1, local_experts, capacity, model_width
    )
    inner_pre = jnp.einsum("secd,edf->secf", arrived, expert_in, preferred_element_type=jnp.float32)
    active = jax.nn.gelu(inner_pre, approximate=True).astype(jnp.bfloat16)
    produced = jnp.einsum(
        "secf,efd->secd", active, expert_out, preferred_element_type=jnp.float32
    ).astype(jnp.bfloat16)
    returned = lax.all_to_all(
        produced.reshape(-1, capacity, model_width), "exp", split_axis=0, concat_axis=0, tiled=True
    )
    expert_rows = jnp.dot(
        dispatch.T, returned.reshape(-1, model_width), preferred_element_type=jnp.float32
    )
    layer_out = after_cross + gate_used[:, None] * expert_rows
    upstream = cotangent[0].astype(jnp.float32)
    made_grad = (upstream * gate_used[:, None]).astype(jnp.bfloat16)
    sent_grad = (
        jnp.dot(dispatch, made_grad, preferred_element_type=jnp.float32)
        .astype(jnp.bfloat16)
        .reshape(expert_total, capacity, model_width)
    )
    grad_arrived = lax.all_to_all(
        sent_grad, "exp", split_axis=0, concat_axis=0, tiled=True
    ).reshape(-1, local_experts, capacity, model_width)
    inner_again = jnp.einsum(
        "secd,edf->secf", arrived, expert_in, preferred_element_type=jnp.float32
    )
    active_again, gelu_back = jax.vjp(
        lambda value: jax.nn.gelu(value, approximate=True), inner_again
    )
    grad_out_w = jnp.einsum(
        "secf,secd->efd",
        active_again.astype(jnp.bfloat16),
        grad_arrived,
        preferred_element_type=jnp.float32,
    )
    grad_active = jnp.einsum(
        "secd,efd->secf", grad_arrived, expert_out, preferred_element_type=jnp.float32
    )
    grad_inner = gelu_back(grad_active)[0].astype(jnp.bfloat16)
    grad_in_w = jnp.einsum(
        "secd,secf->edf", arrived, grad_inner, preferred_element_type=jnp.float32
    )
    grad_sent_x = jnp.einsum(
        "secf,edf->secd", grad_inner, expert_in, preferred_element_type=jnp.float32
    ).astype(jnp.bfloat16)
    grad_back = lax.all_to_all(
        grad_sent_x.reshape(-1, capacity, model_width),
        "exp",
        split_axis=0,
        concat_axis=0,
        tiled=True,
    )
    grad_routed = jnp.dot(
        dispatch.T, grad_back.reshape(-1, model_width), preferred_element_type=jnp.float32
    )
    expert_sums = (
        lax.psum_scatter(grad_in_w, "seq", scatter_dimension=1, tiled=True),
        lax.psum_scatter(grad_out_w, "seq", scatter_dimension=1, tiled=True),
    )
    gate_grad = jnp.sum(upstream * expert_rows, axis=1) * kept.astype(jnp.float32)
    logit_grad = gates * (
        jnp.where(chosen, gate_grad[:, None], 0.0) - (picked_gate * gate_grad)[:, None]
    )
    router_grad = jnp.dot(routed_in.astype(jnp.float32).T, logit_grad, precision=highest)
    grad_normed_three = (
        jnp.dot(logit_grad, router.astype(jnp.float32).T, precision=highest) + grad_routed
    )
    grad_after_cross, gain_three = norm_three_back(grad_normed_three)
    grad_after_cross = grad_after_cross + upstream
    cross_branch = grad_after_cross.astype(jnp.bfloat16)
    cross_out_grad = jnp.dot(cross_att.T, cross_branch, preferred_element_type=jnp.float32)
    grad_cross_att = split_heads(
        jnp.dot(cross_branch, cross_out.T, preferred_element_type=jnp.float32).astype(jnp.bfloat16)
    )
    cross_prob_grad = jnp.einsum(
        "qhd,khd->hqk", grad_cross_att, cross_values, preferred_element_type=jnp.float32
    )
    cross_delta = jnp.sum(cross_prob * cross_prob_grad, axis=-1, keepdims=True)
    cross_score_grad = (cross_prob * (cross_prob_grad - cross_delta)).astype(jnp.bfloat16)
    grad_cross_queries = (
        (
            jnp.einsum(
                "hqk,khd->qhd", cross_score_grad, cross_keys, preferred_element_type=jnp.float32
            )
            * 0.125
        )
        .reshape(rows_dev, model_width)
        .astype(jnp.bfloat16)
    )
    grad_enc_keys = (
        jnp.einsum(
            "hqk,qhd->khd",
            cross_score_grad,
            split_heads(cross_queries),
            preferred_element_type=jnp.float32,
        )
        * 0.125
    )
    grad_enc_values = jnp.einsum(
        "hqk,qhd->khd", cross_prob_low, grad_cross_att, preferred_element_type=jnp.float32
    )
    enc_terms = jnp.concatenate(
        [grad_enc_keys.reshape(-1, model_width), grad_enc_values.reshape(-1, model_width)], axis=1
    )
    enc_grad_rows = lax.psum_scatter(
        enc_terms, ("seq", "exp"), scatter_dimension=0, tiled=True
    ).astype(jnp.bfloat16)
    enc_count = enc_grad_rows.shape[0]
    flat_index = seq_index * lax.axis_size("exp") + lax.axis_index("exp")
    own_enc = lax.dynamic_slice_in_dim(encoder, flat_index * enc_count, enc_count, 0)
    grad_encoder = jnp.dot(enc_grad_rows, cross_kv.T, preferred_element_type=jnp.float32)
    pair_grad = jnp.dot(own_enc.T, enc_grad_rows, preferred_element_type=jnp.float32)
    query_w_grad = jnp.dot(normed_two.T, grad_cross_queries, preferred_element_type=jnp.float32)
    grad_normed_two = jnp.dot(grad_cross_queries, cross_q.T, preferred_element_type=jnp.float32)
    grad_after_self, gain_two = norm_two_back(grad_normed_two)
    grad_after_self = grad_after_self + grad_after_cross
    self_branch = grad_after_self.astype(jnp.bfloat16)
    self_out_grad = jnp.dot(attended.T, self_branch, preferred_element_type=jnp.float32)
    grad_attended = jnp.dot(self_branch, self_out.T, preferred_element_type=jnp.float32).astype(
        jnp.bfloat16
    )
    row_delta = jnp.sum(
        split_heads(grad_attended).astype(jnp.float32) * split_heads(attended_full), axis=-1
    ).T
    stats_all = (
        lax.all_gather(log_total.T, "seq", axis=0, tiled=True),
        lax.all_gather(row_delta.T, "seq", axis=0, tiled=True),
    )

    def query_step(running, pieces, query_start):
        kv_grad, query_grads, table_grad = running
        queries_part, grads_part = pieces
        piece_rows = queries_part.shape[0]
        lse_part = lax.dynamic_slice_in_dim(stats_all[0], query_start, piece_rows, 0).T
        delta_part = lax.dynamic_slice_in_dim(stats_all[1], query_start, piece_rows, 0).T
        scores, allowed, offset_gap = self_scores(
            queries_part, query_start, keys_own, own_start, doc_ends, table
        )
        probability = jnp.where(allowed, jnp.exp(scores - lse_part[..., None]), 0.0)
        prob_grad = jnp.einsum(
            "qhd,khd->hqk",
            split_heads(grads_part),
            split_heads(values_own),
            preferred_element_type=jnp.float32,
        )
        score_grad = (probability * (prob_grad - delta_part[..., None])).astype(jnp.bfloat16)
        key_grad = (
            jnp.einsum(
                "hqk,qhd->khd",
                score_grad,
                split_heads(queries_part),
                preferred_element_type=jnp.float32,
            )
            * 0.125
        )
        value_grad = jnp.einsum(
            "hqk,qhd->khd",
            probability.astype(jnp.bfloat16),
            split_heads(grads_part),
            preferred_element_type=jnp.float32,
        )
        kv_grad = kv_grad + jnp.concatenate(
            [key_grad.reshape(-1, model_width), value_grad.reshape(-1, model_width)], axis=1
        )
        table_grad = table_grad + table_terms(score_grad, offset_gap, table.shape[1])
        query_part_grad = jnp.einsum(
            "hqk,khd->qhd", score_grad, split_heads(keys_own), preferred_element_type=jnp.float32
        ).reshape(piece_rows, model_width)
        current = lax.dynamic_slice_in_dim(query_grads, query_start, piece_rows, 0)
        query_grads = lax.dynamic_update_slice_in_dim(
            query_grads, current + query_part_grad, query_start, 0
        )
        return (kv_grad, query_grads, table_grad)

    back_start = (
        jnp.zeros((rows_dev, 2 * model_width), jnp.float32),
        jnp.zeros((seq_count * rows_dev, model_width), jnp.float32),
        jnp.zeros(table.shape, jnp.float32),
    )
    kv_grad, query_buffer, table_grad = over_blocks(
        query_step,
        back_start,
        (
            lax.all_gather(queries, "seq", axis=0, tiled=True),
            lax.all_gather(grad_attended, "seq", axis=0, tiled=True),
        ),
    )
    query_grad = lax.psum_scatter(query_buffer, "seq", scatter_dimension=0, tiled=True)
    qkv_grad = jnp.concatenate(
        [(query_grad * 0.125).astype(jnp.bfloat16), kv_grad.astype(jnp.bfloat16)], axis=1
    )
    qkv_w_grad = jnp.dot(normed_one.T, qkv_grad, preferred_element_type=jnp.float32)
    grad_normed_one = jnp.dot(qkv_grad, self_qkv.T, preferred_element_type=jnp.float32)
    grad_hidden, gain_one = norm_one_back(grad_normed_one)
    grad_input = grad_hidden + grad_after_self
    rel_grad = jnp.dot(bucket_pick.T, table_grad.T, precision=highest)
    summed_grads = lax.psum(
        (
            jnp.stack([gain_one, gain_two, gain_three]),
            qkv_w_grad,
            self_out_grad,
            query_w_grad,
            pair_grad,
            cross_out_grad,
            rel_grad,
            router_grad,
        ),
        ("seq", "exp"),
    )
    return (
        layer_out.astype(jnp.bfloat16)[None],
        grad_input[None],
        grad_encoder,
        summed_grads[0],
        summed_grads[1],
        summed_grads[2],
        summed_grads[3],
        summed_grads[4],
        summed_grads[5],
        summed_grads[6],
        summed_grads[7],
        expert_sums[0],
        expert_sums[1],
    )


F32 = jnp.float32
BF16 = jnp.bfloat16
MESH = pl.DeviceIdType.MESH
ANY = pl.BlockSpec(memory_space=pl.ANY)
VMEM = pl.BlockSpec(memory_space=pltpu.VMEM)
SMEM = pl.BlockSpec(memory_space=pltpu.SMEM)
LANES = 128


def nn(a, b):
    return lax.dot_general(a, b, (((1,), (0,)), ((), ())), preferred_element_type=F32)


def nt(a, b):
    return lax.dot_general(a, b, (((1,), (1,)), ((), ())), preferred_element_type=F32)


def tn(a, b):
    return lax.dot_general(a, b, (((0,), (0,)), ((), ())), preferred_element_type=F32)


def rms_scale(a):
    return lax.rsqrt(jnp.mean(a * a, axis=-1, keepdims=True) + epsilon)


def pair_lanes(p):
    return pl.ds(pl.multiple_of(p * LANES, LANES), LANES)


def block_of(index, size):
    return pl.ds(pl.multiple_of(index * size, size), size)


def head_stack(pair):
    lane = lax.broadcasted_iota(jnp.int32, pair.shape, 1)
    zero = jnp.zeros_like(pair)
    return jnp.concatenate([jnp.where(lane < HD, pair, zero), jnp.where(lane < HD, zero, pair)], axis=0)


def head_unstack(both, rows):
    feature = lax.broadcasted_iota(jnp.int32, (both.shape[0], rows), 0)
    return jnp.where(feature < HD, both[:, :rows], both[:, rows:]).T


def pack_slots(value, experts):
    slots = value.shape[0] // experts
    blocks = value.shape[1] // LANES
    return jnp.stack([
        jnp.concatenate(
            [value[e * slots : (e + 1) * slots, b * LANES : (b + 1) * LANES] for b in range(blocks)], axis=0
        )
        for e in range(experts)
    ])


def unpack_slots(packed, slots):
    experts, blocks = packed.shape[0], packed.shape[1] // slots
    wide = packed.astype(F32)
    return jnp.concatenate(
        [
            jnp.concatenate([wide[e, b * slots : (b + 1) * slots] for e in range(experts)], axis=0)
            for b in range(blocks)
        ],
        axis=1,
    )


class Place:
    def __init__(self):
        self.me = lax.axis_index("seq")
        self.core = lax.rem(self.me, 2)
        self.chip = lax.div(self.me, 2)
        self.partner = self.me + 1 - 2 * self.core
        self.x_chip = self.chip + 1 - 2 * lax.rem(self.chip, 2)
        self.y_chip = lax.rem(self.chip + 2, 4)
        self.far_chip = 3 - self.chip
        self.x, self.y, self.far = (c * 2 + self.core for c in (self.x_chip, self.y_chip, self.far_chip))


def enter(devices):
    barrier = pltpu.get_barrier_semaphore()
    for device in devices:
        pl.semaphore_signal(barrier, inc=1, device_id=device, device_id_type=MESH)
    pl.semaphore_wait(barrier, len(devices))


def remote(src, dst, send_sem, recv_sem, device):
    return pltpu.make_async_remote_copy(
        src_ref=src, dst_ref=dst, send_sem=send_sem, recv_sem=recv_sem, device_id=device, device_id_type=MESH
    )


class Gather:
    def __init__(self, place, every, half, sends, recvs):
        self.place, self.every, self.half, self.sends, self.recvs = place, every, half, sends, recvs

    def copy(self, slot):
        place, every = self.place, self.every
        block, device = (
            lambda: (every.at[place.me], place.partner),
            lambda: (every.at[place.me], place.x),
            lambda: (every.at[place.me], place.y),
            lambda: (every.at[place.x, pl.ds(0, self.half)], place.y),
            lambda: (every.at[place.y, pl.ds(self.half, self.half)], place.x),
            lambda: (every.at[place.x], place.partner),
            lambda: (every.at[place.y], place.partner),
            lambda: (every.at[place.far], place.partner),
        )[slot]()
        return remote(block, block, self.sends.at[slot], self.recvs.at[slot], {"seq": device})

    def send(self, *slots):
        for slot in slots:
            self.copy(slot).start()

    def wait(self, *slots):
        for slot in slots:
            self.copy(slot).wait_recv()

    def start(self):
        self.send(1, 2, 0)

    def relay(self):
        self.wait(1)
        self.send(3)
        self.wait(2)
        self.send(4, 5, 6)

    def relay_far(self):
        self.wait(3, 4)
        self.send(7)

    def finish(self):
        self.wait(0, 5, 6, 7)

    def drain(self):
        for slot in range(8):
            self.copy(slot).wait_send()


class Scatter:
    def __init__(self, place, out, pair, turn, side, half, sems):
        self.place, self.out, self.pair, self.turn, self.side, self.half = place, out, pair, turn, side, half
        self.pair_sems, self.turn_sems, self.side_sems = sems

    def pair_copy(self):
        send, recv = self.pair_sems
        return remote(self.out.at[1 - self.place.core], self.pair, send, recv, {"seq": self.place.partner})

    def turn_copies(self):
        place = self.place
        send, recv = self.turn_sems
        far = self.out.at[place.core, place.far_chip]
        return (
            remote(far.at[pl.ds(0, self.half)], self.turn.at[0], send.at[0], recv.at[0], {"seq": place.x}),
            remote(far.at[pl.ds(self.half, self.half)], self.turn.at[1], send.at[1], recv.at[1], {"seq": place.y}),
        )

    def side_copies(self):
        place = self.place
        send, recv = self.side_sems
        return (
            remote(self.out.at[place.core, place.x_chip], self.side.at[0], send.at[0], recv.at[0], {"seq": place.x}),
            remote(self.out.at[place.core, place.y_chip], self.side.at[1], send.at[1], recv.at[1], {"seq": place.y}),
        )

    def start(self):
        self.pair_copy().start()

    def turn_on(self):
        core = self.place.core
        self.pair_copy().wait_recv()
        self.out[core] = (self.out[core].astype(F32) + self.pair[...].astype(F32)).astype(BF16)
        for copy in self.turn_copies():
            copy.start()

    def side_on(self):
        place = self.place
        first, second = pl.ds(0, self.half), pl.ds(self.half, self.half)
        from_x, from_y = self.turn_copies()
        from_x.wait_recv()
        at = (place.core, place.y_chip, first)
        self.out[at] = (self.out[at].astype(F32) + self.turn[0].astype(F32)).astype(BF16)
        from_y.wait_recv()
        at = (place.core, place.x_chip, second)
        self.out[at] = (self.out[at].astype(F32) + self.turn[1].astype(F32)).astype(BF16)
        for copy in self.side_copies():
            copy.start()

    def total(self):
        for copy in self.side_copies():
            copy.wait_recv()
        own = self.out[self.place.core, self.place.chip].astype(F32)
        return own + self.side[0].astype(F32) + self.side[1].astype(F32)

    def drain(self):
        self.pair_copy().wait_send()
        for copy in self.turn_copies() + self.side_copies():
            copy.wait_send()


def forward_kernel(
    seq_count, capacity,
    x_ref, encoder_hbm, lengths_ref, buckets_ref, routes_ref, gains_ref, qkv_hbm, self_out_hbm, cross_q_hbm,
    cross_kv_hbm, cross_out_hbm, rel_ref, router_ref, g_ref,
    n1_hbm, kv_hbm, p_hbm, pc_hbm, ekv_hbm, q_ref, o_ref, n2_ref, qc_ref, oc_ref, x3_ref, r1_ref, r2_ref, gates_ref,
    chosen_ref, place_ref, xs_ref, dms_ref,
    n1_all, kv_all, prob, cross_prob, ekv, scores, mask, w_qkv, w_self, w_cq, w_ckv, w_co, enc, table_ref,
    load_sem, store_sem, send_sem, recv_sem,
):
    rows, width = x_ref.shape
    span = seq_count * rows
    pairs = width // LANES
    place = Place()
    me = place.me

    loads = [
        pltpu.make_async_copy(src, dst, load_sem.at[i])
        for i, (src, dst) in enumerate(
            [(qkv_hbm, w_qkv), (cross_kv_hbm, w_ckv), (encoder_hbm, enc), (self_out_hbm, w_self), (cross_q_hbm, w_cq),
             (cross_out_hbm, w_co)]
        )
    ]
    for load in loads:
        load.start()
    x = x_ref[...].astype(F32)
    n1_all[me] = (x * rms_scale(x) * gains_ref[0:1, :]).astype(BF16)
    enter([{"seq": device} for device in (place.partner, place.x, place.y)])
    gather = Gather(place, n1_all, rows // 2, send_sem, recv_sem)
    gather.start()

    def project(chip):
        part = n1_all[pl.ds(chip * 2, 2)].reshape(2 * rows, width)
        kv_all[block_of(chip, 2 * rows), :] = nn(part, w_qkv[:, width:]).astype(BF16)

    loads[0].wait()
    q = nn(n1_all[me], w_qkv[:, :width]).astype(BF16)
    q_ref[...] = q * jnp.asarray(0.125, BF16)
    gather.wait(0)
    project(place.chip)
    loads[1].wait()
    loads[2].wait()
    ekv[...] = nn(enc[...], w_ckv[...]).astype(BF16)
    store_ekv = pltpu.make_async_copy(ekv, ekv_hbm, store_sem.at[0])
    store_ekv.start()
    gather.relay()
    pick = (buckets_ref[...] == lax.broadcasted_iota(jnp.int32, (rel_ref.shape[1], LANES), 0)).astype(F32)
    table = jnp.dot(rel_ref[...], pick, precision=highest, preferred_element_type=F32)
    table = table - table[:, LANES - 1 :]
    table_ref[...] = jnp.concatenate([jnp.zeros_like(table), table], axis=1)
    query_pos = me * rows + lax.broadcasted_iota(jnp.int32, (1, rows), 1)
    start = jnp.zeros((1, rows), jnp.int32)
    end = jnp.int32(0)
    for i in range(lengths_ref.shape[1]):
        end = end + lengths_ref[0, i]
        start = jnp.where(end <= query_pos, end, start)
    key_pos = lax.broadcasted_iota(jnp.int32, (span, rows), 0)
    seen = jnp.where((key_pos >= start) & (key_pos <= query_pos), 0.0, masked_out)
    mask[...] = jnp.concatenate([seen, seen], axis=1)

    gather.wait(5, 6)
    project(place.x_chip)
    project(place.y_chip)
    gather.relay_far()
    gather.wait(7)
    project(place.far_chip)
    store_n1 = pltpu.make_async_copy(n1_all, n1_hbm, store_sem.at[1])
    store_n1.start()
    store_kv = pltpu.make_async_copy(kv_all, kv_hbm, store_sem.at[2])
    store_kv.start()

    near = pl.ds(pl.multiple_of(me * rows, rows), 2 * rows)

    @pl.loop(0, pairs)
    def _(p):
        lanes = pair_lanes(p)
        q_both = head_stack(q_ref[:, lanes])
        scores[pl.ds(rows, span), :] = nt(kv_all[:, lanes], q_both) + mask[...]
        biases = []
        for h in range(2):
            band = jnp.broadcast_to(table_ref[pl.ds(2 * p + h, 1), :], (2 * rows, 2 * LANES))
            biases.append(pltpu.roll(band, 0, 1, stride=1, stride_axis=0)[:, :rows])
        scores[near, :] = scores[near, :] + jnp.concatenate(biases, axis=1)
        s = scores[pl.ds(rows, span), :]
        weights = jnp.exp(s - jnp.max(s, axis=0, keepdims=True))
        weights = (weights * (1.0 / jnp.sum(weights, axis=0, keepdims=True))).astype(BF16)
        prob[p] = weights
        both = tn(kv_all[:, pair_lanes(pairs + p)], weights)
        o_ref[:, lanes] = head_unstack(both, rows).astype(BF16)

    store_p = pltpu.make_async_copy(prob, p_hbm, store_sem.at[3])
    store_p.start()
    loads[3].wait()
    loads[4].wait()
    loads[5].wait()
    r1 = x_ref[...].astype(F32) + nn(o_ref[...], w_self[...])
    r1_ref[...] = r1
    n2 = (r1 * rms_scale(r1) * gains_ref[1:2, :]).astype(BF16)
    n2_ref[...] = n2
    qc_ref[...] = nn(n2, w_cq[...]).astype(BF16) * jnp.asarray(0.125, BF16)

    @pl.loop(0, pairs)
    def _(p):
        lanes = pair_lanes(p)
        s = nt(ekv[:, lanes], head_stack(qc_ref[:, lanes]))
        weights = jnp.exp(s - jnp.max(s, axis=0, keepdims=True))
        weights = (weights * (1.0 / jnp.sum(weights, axis=0, keepdims=True))).astype(BF16)
        cross_prob[p] = weights
        both = tn(ekv[:, pair_lanes(pairs + p)], weights)
        oc_ref[:, lanes] = head_unstack(both, rows).astype(BF16)

    store_pc = pltpu.make_async_copy(cross_prob, pc_hbm, store_sem.at[4])
    store_pc.start()
    r2 = r1_ref[...] + nn(oc_ref[...], w_co[...])
    r2_ref[...] = r2
    x3 = (r2 * rms_scale(r2) * gains_ref[2:3, :]).astype(BF16)
    x3_ref[...] = x3
    experts = router_ref.shape[0]
    logits = nt(x3, router_ref[...])
    top = jnp.exp(logits - jnp.max(logits, axis=-1, keepdims=True))
    gates = top / jnp.sum(top, axis=-1, keepdims=True)
    gates_ref[...] = gates
    chosen = (routes_ref[...] == lax.broadcasted_iota(jnp.int32, (LANES, rows), 0)).astype(F32).T[:, :experts]
    chosen_ref[...] = chosen
    earlier = (
        lax.broadcasted_iota(jnp.int32, (rows, rows), 1) < lax.broadcasted_iota(jnp.int32, (rows, rows), 0)
    ).astype(BF16)
    slot = jnp.sum(nn(earlier, chosen.astype(BF16)) * chosen, axis=1, keepdims=True).astype(jnp.int32)
    kept = slot < capacity
    gate_used = jnp.sum(gates * chosen, axis=1, keepdims=True) * kept.astype(F32)
    expert = lax.broadcasted_iota(jnp.int32, (rows, experts), 1).astype(F32)
    route = jnp.sum(chosen * expert, axis=1, keepdims=True).astype(jnp.int32)
    target = jnp.where(kept, route * capacity + slot, -1)
    slots = (lax.broadcasted_iota(jnp.int32, (rows, experts * capacity), 1) == target).astype(BF16)
    place_ref[...] = slots
    xs_ref[...] = pack_slots(tn(slots, x3), experts).astype(BF16)
    made_grad = (g_ref[...].astype(F32) * gate_used).astype(BF16)
    dms_ref[...] = pack_slots(tn(slots, made_grad), experts).astype(BF16)

    gather.drain()
    for store in (store_ekv, store_n1, store_kv, store_p, store_pc):
        store.wait()


def forward_call(seq_count, capacity, x, encoder, lengths, buckets, routes, gains, w_qkv, w_self, w_cq, w_ckv, w_co, rel,
                 router, g):
    rows, width = x.shape
    span = seq_count * rows
    pairs = width // LANES
    enc_rows = encoder.shape[0]
    experts = router.shape[0]
    shape = jax.ShapeDtypeStruct
    wide = shape((rows, width), BF16)
    packed = shape((experts, capacity * pairs, LANES), BF16)
    narrow = shape((rows, experts), F32)
    outs = (
        shape((seq_count, rows, width), BF16), shape((span, 2 * width), BF16), shape((pairs, span, 2 * rows), BF16),
        shape((pairs, enc_rows, 2 * rows), BF16), shape((enc_rows, 2 * width), BF16), wide, wide, wide, wide, wide, wide,
        shape((rows, width), F32), shape((rows, width), F32), narrow, narrow,
        shape((rows, experts * capacity), BF16), packed, packed,
    )
    return pl.pallas_call(
        functools.partial(forward_kernel, seq_count, capacity),
        out_shape=outs,
        in_specs=[VMEM, ANY, SMEM, VMEM, VMEM, VMEM, ANY, ANY, ANY, ANY, ANY, VMEM, VMEM, VMEM],
        out_specs=tuple([ANY] * 5 + [VMEM] * 13),
        scratch_shapes=[
            pltpu.VMEM((seq_count, rows, width), BF16), pltpu.VMEM((span, 2 * width), BF16),
            pltpu.VMEM((pairs, span, 2 * rows), BF16), pltpu.VMEM((pairs, enc_rows, 2 * rows), BF16),
            pltpu.VMEM((enc_rows, 2 * width), BF16), pltpu.VMEM((span + rows, 2 * rows), F32),
            pltpu.VMEM((span, 2 * rows), F32), pltpu.VMEM(w_qkv.shape, BF16), pltpu.VMEM(w_self.shape, BF16),
            pltpu.VMEM(w_cq.shape, BF16), pltpu.VMEM(w_ckv.shape, BF16), pltpu.VMEM(w_co.shape, BF16),
            pltpu.VMEM(encoder.shape, BF16), pltpu.VMEM((rel.shape[0], 2 * LANES), F32),
            pltpu.SemaphoreType.DMA((6,)), pltpu.SemaphoreType.DMA((5,)),
            pltpu.SemaphoreType.DMA((8,)), pltpu.SemaphoreType.DMA((8,)),
        ],
        compiler_params=pltpu.CompilerParams(collective_id=0, has_side_effects=True, vmem_limit_bytes=56 << 20),
        name="forward",
    )(x, encoder, lengths, buckets, routes, gains, w_qkv, w_self, w_cq, w_ckv, w_co, rel, router, g)


def expert_peers(exp_index, experts):
    return [lax.rem(exp_index + d, experts) for d in range(1, experts)]


def gelu_parts(hid):
    root, cubic = 0.7978845608028654, 0.044715
    square = hid * hid
    bent = jnp.tanh(root * hid * (1.0 + cubic * square))
    half = 0.5 * (1.0 + bent)
    return hid * half, half + 0.5 * hid * (1.0 - bent * bent) * (root + 3.0 * root * cubic * square)


def experts_kernel(
    seq_count, experts, slots,
    xs_ref, dms_ref, w_in_hbm, w_out_hbm,
    made_ref, dx_ref, x_hbm, dm_hbm,
    x_all, dm_all, x_in, dm_in, made_out, made_back, dx_out, dx_back, slope, w_in, w_out,
    load_sem, store_sem, zx_send, zx_recv, zd_send, zd_recv, zm_send, zm_recv, zg_send, zg_recv,
    x_send, x_recv, d_send, d_recv,
):
    width = x_all.shape[-1]
    rows = experts * slots
    hidden = w_in.shape[1]
    place = Place()
    mine = lax.axis_index("exp")
    peers = expert_peers(mine, experts)
    loads = [
        pltpu.make_async_copy(w_in_hbm, w_in, load_sem.at[0]),
        pltpu.make_async_copy(w_out_hbm, w_out, load_sem.at[1]),
    ]
    for load in loads:
        load.start()
    enter([{"seq": device} for device in (place.partner, place.x, place.y)] + [{"exp": peer} for peer in peers])

    def over_exp(src, dst, send, recv):
        copies = [
            remote(src.at[peer], dst.at[mine], send.at[d], recv.at[d], {"exp": peer}) for d, peer in enumerate(peers)
        ]
        for copy in copies:
            copy.start()
        dst[mine] = src[mine]
        return copies

    x_moves = over_exp(xs_ref, x_in, zx_send, zx_recv)
    dm_moves = over_exp(dms_ref, dm_in, zd_send, zd_recv)
    for move in x_moves:
        move.wait_recv()
    x_all[place.me] = unpack_slots(x_in[...], slots).astype(BF16)
    x_gather = Gather(place, x_all, rows // 2, x_send, x_recv)
    x_gather.start()
    x = x_all[place.me]
    loads[0].wait()
    loads[1].wait()
    made = jnp.zeros((rows, width), F32)
    for n in range(hidden // width):
        at = slice(n * width, (n + 1) * width)
        value, derivative = gelu_parts(nn(x, w_in[:, at]))
        slope[:, at] = derivative
        made = made + nn(value.astype(BF16), w_out[at, :])
    made_out[...] = pack_slots(made, experts).astype(BF16)
    made_moves = over_exp(made_out, made_back, zm_send, zm_recv)

    for move in dm_moves:
        move.wait_recv()
    dm_all[place.me] = unpack_slots(dm_in[...], slots).astype(BF16)
    dm_gather = Gather(place, dm_all, rows // 2, d_send, d_recv)
    dm_gather.start()
    dm = dm_all[place.me]
    dx = jnp.zeros((rows, width), F32)
    for n in range(hidden // width):
        at = slice(n * width, (n + 1) * width)
        dh = (nt(dm, w_out[at, :]) * slope[:, at]).astype(BF16)
        dx = dx + nt(dh, w_in[:, at])
    dx_out[...] = pack_slots(dx, experts).astype(BF16)
    dx_moves = over_exp(dx_out, dx_back, zg_send, zg_recv)

    x_gather.relay()
    for move in made_moves:
        move.wait_recv()
    made_ref[...] = unpack_slots(made_back[...], slots).astype(BF16)
    x_gather.relay_far()
    dm_gather.relay()
    for move in dx_moves:
        move.wait_recv()
    dx_ref[...] = unpack_slots(dx_back[...], slots).astype(BF16)
    x_gather.finish()
    store_x = pltpu.make_async_copy(x_all, x_hbm, store_sem.at[0])
    store_x.start()
    dm_gather.relay_far()
    dm_gather.finish()
    store_dm = pltpu.make_async_copy(dm_all, dm_hbm, store_sem.at[1])
    store_dm.start()
    for copy in x_moves + dm_moves + made_moves + dx_moves:
        copy.wait_send()
    x_gather.drain()
    dm_gather.drain()
    store_x.wait()
    store_dm.wait()


def experts_call(seq_count, slots, width, xs, dms, w_in, w_out):
    experts = xs.shape[0]
    rows = experts * slots
    shape = jax.ShapeDtypeStruct
    every = (seq_count, rows, width)
    dma = lambda n: pltpu.SemaphoreType.DMA((n,))
    z = experts - 1
    return pl.pallas_call(
        functools.partial(experts_kernel, seq_count, experts, slots),
        out_shape=(shape((rows, width), BF16), shape((rows, width), BF16), shape(every, BF16), shape(every, BF16)),
        in_specs=[VMEM, VMEM, ANY, ANY],
        out_specs=(VMEM, VMEM, ANY, ANY),
        scratch_shapes=[pltpu.VMEM(every, BF16)] * 2 + [pltpu.VMEM(xs.shape, BF16)] * 6 + [
            pltpu.VMEM((rows, w_in.shape[1]), F32), pltpu.VMEM(w_in.shape, BF16), pltpu.VMEM(w_out.shape, BF16),
            dma(2), dma(2)] + [dma(z)] * 8 + [dma(8)] * 4,
        compiler_params=pltpu.CompilerParams(collective_id=1, has_side_effects=True, vmem_limit_bytes=56 << 20),
        name="experts",
    )(xs, dms, w_in, w_out)


def rms_back(a, gain, grad):
    scale = rms_scale(a)
    weighted = grad * gain
    da = scale * weighted - a * (scale * scale * scale * jnp.mean(a * weighted, axis=-1, keepdims=True))
    return da, jnp.sum(grad * (a * scale), axis=0, keepdims=True)


def in_two(value):
    high = value.astype(BF16)
    return high, (value - high.astype(F32)).astype(BF16)


class Chunk:
    def __init__(self, place, quarters, mine, peers, src, slots, own, every, sems, gather_sems, local_sem):
        self.place, self.quarters, self.mine, self.peers = place, quarters, mine, peers
        self.src, self.slots, self.own, self.every = src, slots, own, every
        self.scatter_sems, self.gather_sems, self.local_sem = sems[:2], sems[2:], local_sem
        self.over_seq = Gather(place, every, src.shape[0] // 2, *gather_sems)

    def scatter_copies(self):
        send, recv = self.scatter_sems
        return [
            remote(self.src.at[self.quarters[1 + d]], self.slots.at[d], send.at[d], recv.at[d], {"exp": peer})
            for d, peer in enumerate(self.peers)
        ]

    def gather_copies(self):
        send, recv = self.gather_sems
        target = self.every.at[(self.place.me,) + self.quarters[0]]
        return [remote(self.own, target, send.at[d], recv.at[d], {"exp": peer}) for d, peer in enumerate(self.peers)]

    def local_copy(self):
        return pltpu.make_async_copy(self.own, self.every.at[(self.place.me,) + self.quarters[0]], self.local_sem)

    def over_exp(self, value):
        self.src[...] = value.astype(BF16)
        for copy in self.scatter_copies():
            copy.start()

    def back_over_exp(self):
        total = self.src[self.quarters[0]].astype(F32)
        for d, copy in enumerate(self.scatter_copies()):
            copy.wait_recv()
            total = total + self.slots[d].astype(F32)
        self.own[...] = total.astype(BF16)
        self.local_copy().start()
        for copy in self.gather_copies():
            copy.start()

    def spread(self):
        self.local_copy().wait()
        for copy in self.gather_copies():
            copy.wait_recv()
        self.over_seq.start()

    def drain(self):
        for copy in self.scatter_copies() + self.gather_copies():
            copy.wait_send()
        self.over_seq.drain()


def backward_kernel(
    seq_count, experts,
    made_ref, dxb_ref, g_ref, x_ref, r1_ref, r2_ref, gates_ref, chosen_ref, slots_ref, x3_ref, n2_ref, o_ref, oc_ref,
    q_ref, qc_ref, gains_ref, router_ref, buckets_ref, kv_hbm, p_hbm, pc_hbm, ekv_hbm, co_hbm, cq_hbm, so_hbm, qkv_hbm,
    n1_hbm, x_hbm, dm_hbm, in_hbm, out_hbm, ckv_hbm,
    out_ref, dx_ref, weights_hbm, dekv_hbm, small_out_ref, gin_ref, gout_ref, genc_ref,
    kv_all, prob, cross_prob, ekv, w_co, w_cq, w_so, w_qkv, dr_ref, doc_ref, dqc_ref, dqkv_ref, ds_ref, diag_ref, total_ref,
    e_out, e_pair, e_turn, e_side, e_mine, e_exp, dekv, t_out, t_pair, t_turn, t_side, w_out, w_pair, w_turn, w_side,
    c_src, c_slots, c_own, dqkv_t, right, n1_all, x_all, dm_all, w_ein, w_eout, w_ckv, gin_out, gin_in,
    small_a, small_b, small_c, small_pair, small_chip, small_exp,
    load_sem, local_sem, ep_send, ep_recv, et_send, et_recv, es_send, es_recv, ez_send, ez_recv, eg_send, eg_recv, ea_send, ea_recv,
    tp_send, tp_recv, tt_send, tt_recv, ts_send, ts_recv, wp_send, wp_recv, wt_send, wt_recv, ws_send, ws_recv,
    cs_send, cs_recv, cg_send, cg_recv, ca_send, ca_recv, r_send, r_recv, g_send, g_recv,
    s1_send, s1_recv, s2_send, s2_recv, s3_send, s3_recv,
):
    rows, width = x_ref.shape
    span = seq_count * rows
    pairs = width // LANES
    place = Place()
    me = place.me
    mine = lax.axis_index("exp")
    peers = expert_peers(mine, experts)
    everyone = [lax.rem(me + d, seq_count) for d in range(1, seq_count)]
    part = width // seq_count
    half_rows, half_lanes = part // 2, width // (experts // 2)
    quarters = [
        (block_of(lax.div(e, experts // 2), half_rows), block_of(lax.rem(e, experts // 2), half_lanes)) for e in [mine] + peers
    ]
    at_hidden = block_of(me, w_ein.shape[1])
    loads = [
        pltpu.make_async_copy(src, dst, load_sem.at[i])
        for i, (src, dst) in enumerate(
            [(co_hbm, w_co), (ekv_hbm, ekv), (pc_hbm, cross_prob), (cq_hbm, w_cq), (so_hbm, w_so), (kv_hbm, kv_all),
             (p_hbm, prob), (qkv_hbm, w_qkv), (n1_hbm, n1_all), (x_hbm, x_all), (in_hbm.at[:, at_hidden], w_ein),
             (dm_hbm, dm_all), (out_hbm.at[at_hidden, :], w_eout), (ckv_hbm, w_ckv)]
        )
    ]
    for load in loads:
        load.start()
    enter([{"seq": device} for device in everyone] + [{"exp": peer} for peer in peers])
    started = []

    def send(src, dst, send_sem, recv_sem, device):
        copy = remote(src, dst, send_sem, recv_sem, device)
        copy.start()
        started.append(copy)
        return copy

    enc_scatter = Scatter(
        place, e_out, e_pair, e_turn, e_side, e_turn.shape[1],
        ((ep_send.at[0], ep_recv.at[0]), (et_send, et_recv), (es_send, es_recv)),
    )
    squares = [
        Scatter(
            place, w_out.at[i], w_pair.at[i], w_turn.at[i], w_side.at[i], half_rows,
            ((wp_send.at[i], wp_recv.at[i]), (wt_send.at[i], wt_recv.at[i]), (ws_send.at[i], ws_recv.at[i])),
        )
        for i in range(3)
    ]
    chunks = [
        Chunk(
            place, quarters, mine, peers, c_src.at[i], c_slots.at[i], c_own.at[i], weights_hbm.at[i],
            (cs_send.at[i], cs_recv.at[i], cg_send.at[i], cg_recv.at[i]), (ca_send.at[i], ca_recv.at[i]), local_sem.at[i],
        )
        for i in range(6)
    ]
    dekv_gather = Gather(place, dekv_hbm, experts // 2, ea_send, ea_recv)

    def enc_over_exp():
        return [
            remote(e_mine.at[peer], e_exp.at[d], ez_send.at[d], ez_recv.at[d], {"exp": peer}) for d, peer in enumerate(peers)
        ]

    def dekv_over_exp():
        return [
            remote(dekv, dekv_hbm.at[me, mine], eg_send.at[d], eg_recv.at[d], {"exp": peer}) for d, peer in enumerate(peers)
        ]

    def dekv_local():
        return pltpu.make_async_copy(dekv, dekv_hbm.at[me, mine], local_sem.at[6])

    def square_start(i, left, right_factor):
        grad = tn(left, right_factor).astype(BF16).reshape(4, 2, part, width)
        for k in range(2):
            w_out[i, k] = grad[:, k]
        squares[i].start()

    made = nn(slots_ref[...], made_ref[...])
    kept = jnp.sum(slots_ref[...].astype(F32), axis=1, keepdims=True)
    gates = gates_ref[...]
    chosen = chosen_ref[...]
    picked = jnp.sum(gates * chosen, axis=1, keepdims=True)
    g = g_ref[...].astype(F32)
    out_ref[...] = (r2_ref[...] + (picked * kept) * made).astype(BF16)
    gate_grad = jnp.sum(g * made, axis=1, keepdims=True) * kept
    dl = gates * (chosen * gate_grad - picked * gate_grad)
    dl_high, dl_low = in_two(dl)
    x3 = x3_ref[...]
    small_a[...] = jnp.zeros_like(small_a)
    small_a[4 : 4 + experts, :width] = tn(dl_high, x3) + tn(dl_low, x3)
    dx3 = nn(slots_ref[...], dxb_ref[...]) + nn(dl_high, router_ref[...]) + nn(dl_low, router_ref[...])
    da, dw = rms_back(r2_ref[...], gains_ref[2:3, :], dx3)
    small_a[2:3, :width] = dw
    dr_ref[...] = g + da
    do2 = dr_ref[...].astype(BF16)
    loads[0].wait()
    doc_ref[...] = nt(do2, w_co[...]).astype(BF16)
    square_start(2, oc_ref[...], do2)

    loads[1].wait()
    loads[2].wait()
    enc_rows = ekv.shape[0]
    enc_part = enc_rows // seq_count

    @pl.loop(0, pairs)
    def _(p):
        lanes, value_lanes = pair_lanes(p), pair_lanes(pairs + p)
        doc_both = head_stack(doc_ref[:, lanes])
        weights = cross_prob[p]
        wide = weights.astype(F32)
        dp = nt(ekv[:, value_lanes], doc_both)
        dc = (wide * (dp - jnp.sum(wide * dp, axis=0, keepdims=True))).astype(BF16)
        dk = nn(dc, head_stack(qc_ref[:, lanes])).astype(BF16).reshape(4, 2, enc_part, LANES)
        dv = nn(weights, doc_both).astype(BF16).reshape(4, 2, enc_part, LANES)
        for k in range(2):
            e_out[k, :, :, lanes] = dk[:, k]
            e_out[k, :, :, value_lanes] = dv[:, k]
        dqc_ref[:, lanes] = (head_unstack(tn(ekv[:, lanes], dc), rows) * 0.125).astype(BF16)

    enc_scatter.start()
    squares[2].turn_on()
    dqc = dqc_ref[...]
    loads[3].wait()
    loads[4].wait()
    da, dw = rms_back(r1_ref[...], gains_ref[1:2, :], nt(dqc, w_cq[...]))
    small_a[1:2, :width] = dw
    dr_ref[...] = dr_ref[...] + da
    do1 = dr_ref[...].astype(BF16)
    doc_ref[...] = nt(do1, w_so[...]).astype(BF16)
    enc_scatter.turn_on()
    square_start(1, n2_ref[...], dqc)
    square_start(0, o_ref[...], do1)
    squares[2].side_on()
    squares[1].turn_on()
    squares[0].turn_on()

    loads[5].wait()
    loads[6].wait()
    ds_ref[pl.ds(0, rows), :] = jnp.zeros((rows, 2 * rows), BF16)
    near = pl.ds(pl.multiple_of(me * rows, rows), 2 * rows)
    flip = (
        lax.broadcasted_iota(jnp.int32, (2 * rows, 2 * rows), 0) + lax.broadcasted_iota(jnp.int32, (2 * rows, 2 * rows), 1)
        == 2 * rows - 1
    ).astype(BF16)

    def terms(p):
        return Scatter(
            place, t_out.at[p], t_pair.at[p], t_turn.at[p], t_side.at[p], rows // 2,
            ((tp_send.at[p], tp_recv.at[p]), (tt_send.at[p], tt_recv.at[p]), (ts_send.at[p], ts_recv.at[p])),
        )

    @pl.loop(0, pairs + 3)
    def _(t):
        @pl.when(t < pairs)
        def _():
            p = jnp.minimum(t, pairs - 1)
            lanes, value_lanes = pair_lanes(p), pair_lanes(pairs + p)
            do_both = head_stack(doc_ref[:, lanes])
            weights = prob[p]
            wide = weights.astype(F32)
            dp = nt(kv_all[:, value_lanes], do_both)
            ds_wide = wide * (dp - jnp.sum(wide * dp, axis=0, keepdims=True))
            ds = ds_wide.astype(BF16)
            ds_ref[pl.ds(rows, span), :] = ds
            total_ref[pl.ds(p, 1), :] = jnp.sum(ds.astype(F32), axis=0, keepdims=True)
            dk = nn(ds, head_stack(q_ref[:, lanes])).astype(BF16).reshape(4, 2, rows, LANES)
            dv = nn(weights, do_both).astype(BF16).reshape(4, 2, rows, LANES)
            for k in range(2):
                t_out[p, k, :, :, :LANES] = dk[:, k]
                t_out[p, k, :, :, LANES:] = dv[:, k]
            terms(p).start()
            dqkv_ref[:, lanes] = (head_unstack(tn(kv_all[:, lanes], ds), rows) * 0.125).astype(BF16)
            turned = nn(flip, ds_ref[near, :])
            for h in range(2):
                one = turned[:, h * rows : (h + 1) * rows]
                one = jnp.concatenate([one, jnp.zeros_like(one)], axis=1)
                one = pltpu.roll(one, 1, 1, stride=1, stride_axis=0)
                diag_ref[pl.ds(2 * p + h, 1), :] = jnp.sum(one, axis=0, keepdims=True)

        @pl.when((t >= 1) & (t <= pairs))
        def _():
            terms(jnp.clip(t - 1, 0, pairs - 1)).turn_on()

        @pl.when((t >= 2) & (t <= pairs + 1))
        def _():
            terms(jnp.clip(t - 2, 0, pairs - 1)).side_on()

        @pl.when(t >= 3)
        def _():
            p = jnp.clip(t - 3, 0, pairs - 1)
            total = terms(p).total()
            dqkv_ref[:, pair_lanes(pairs + p)] = total[:, :LANES].astype(BF16)
            dqkv_ref[:, pair_lanes(2 * pairs + p)] = total[:, LANES:].astype(BF16)

        @pl.when(t == 0)
        def _():
            enc_scatter.side_on()

        @pl.when(t == 1)
        def _():
            squares[1].side_on()
            chunks[2].over_exp(squares[2].total())

        @pl.when(t == 2)
        def _():
            squares[0].side_on()
            e_mine[...] = enc_scatter.total().astype(BF16).reshape(e_mine.shape)
            for copy in enc_over_exp():
                copy.start()

        @pl.when(t == 3)
        def _():
            chunks[1].over_exp(squares[1].total())
            chunks[2].back_over_exp()

        @pl.when(t == 4)
        def _():
            chunks[0].over_exp(squares[0].total())
            total = e_mine[mine].astype(F32)
            for d, copy in enumerate(enc_over_exp()):
                copy.wait_recv()
                total = total + e_exp[d].astype(F32)
            dekv[...] = total.astype(BF16)
            dekv_local().start()
            for copy in dekv_over_exp():
                copy.start()

        @pl.when(t == 5)
        def _():
            chunks[1].back_over_exp()

        @pl.when(t == 6)
        def _():
            chunks[0].back_over_exp()

    dqkv = dqkv_ref[...]
    dqkv_t[...] = dqkv.T
    own_lanes = block_of(me, rows)
    rights = []
    for i in range(3):
        rights.append([
            send(dqkv_t.at[pl.ds(pl.multiple_of(i * width + peer * part, part), part), :], right.at[i, :, own_lanes],
                 r_send.at[i, d], r_recv.at[i, d], {"seq": peer})
            for d, peer in enumerate(everyone)
        ])
        right[i, :, own_lanes] = dqkv_t[pl.ds(pl.multiple_of(i * width + me * part, part), part), :]
    for i in (2, 1, 0):
        chunks[i].spread()
    dekv_local().wait()
    for copy in dekv_over_exp():
        copy.wait_recv()
    dekv_gather.start()

    loads[7].wait()
    x = x_ref[...].astype(F32)
    da, dw = rms_back(x, gains_ref[0:1, :], nt(dqkv, w_qkv[...]))
    small_a[0:1, :width] = dw
    dx_ref[...] = dr_ref[...] + da
    heads = 2 * pairs
    table = diag_ref[:, 2 * rows - LANES :]
    totals = total_ref[...]
    first = jnp.sum(totals[:, :rows], axis=1, keepdims=True)
    second = jnp.sum(totals[:, rows:], axis=1, keepdims=True)
    head = lax.broadcasted_iota(jnp.int32, (heads, pairs), 0)
    pair = lax.broadcasted_iota(jnp.int32, (heads, pairs), 1)
    spread = lambda odd, v: jnp.dot((head == 2 * pair + odd).astype(F32), v, precision=highest, preferred_element_type=F32)
    whole = spread(0, jnp.broadcast_to(first, (pairs, LANES))) + spread(1, jnp.broadcast_to(second, (pairs, LANES)))
    rest = whole - jnp.sum(table, axis=1, keepdims=True)
    lane = lax.broadcasted_iota(jnp.int32, table.shape, 1)
    table = table + jnp.where(lane == LANES - 1, rest, 0.0)
    bucket = lax.broadcasted_iota(jnp.int32, (LANES, LANES), 0)
    pick = (buckets_ref[...] == bucket).astype(F32)
    by_bucket = lax.dot_general(table, pick, (((1,), (1,)), ((), ())), precision=highest, preferred_element_type=F32)
    small_a[0:8, width : width + LANES] = by_bucket[0:8]
    small_a[0 : heads - 8, width + LANES :] = by_bucket[8:heads]
    s_pair = send(small_a, small_pair, s1_send.at[0], s1_recv.at[0], {"seq": place.partner})

    loads[8].wait()
    n1 = n1_all[...].reshape(span, width)
    for i in range(3):
        for copy in rights[i]:
            copy.wait_recv()
        chunks[3 + i].over_exp(nn(right[i], n1))
    s_pair.wait_recv()
    small_b[...] = small_a[...] + small_pair[...]
    s_chip = [
        send(small_b, small_chip.at[d], s2_send.at[d], s2_recv.at[d], {"seq": device})
        for d, device in enumerate((place.x, place.y, place.far))
    ]
    for load in loads[9:13]:
        load.wait()
    xs = x_all[...].reshape(-1, width)
    value, slope = gelu_parts(nn(xs, w_ein[...]))
    dm = dm_all[...].reshape(-1, width)
    gout_ref[...] = tn(value.astype(BF16), dm)
    chunks[2].over_seq.relay()
    chunks[3].back_over_exp()
    chunks[1].over_seq.relay()
    dh = (nt(dm, w_eout[...]) * slope).astype(BF16)
    gin_out[...] = tn(xs, dh).astype(BF16).reshape(gin_out.shape)
    gins = [
        send(gin_out.at[peer], gin_in.at[:, at_hidden], g_send.at[d], g_recv.at[d], {"seq": peer})
        for d, peer in enumerate(everyone)
    ]
    gin_in[:, at_hidden] = gin_out[me]
    chunks[4].back_over_exp()
    chunks[3].spread()
    chunks[5].back_over_exp()
    chunks[0].over_seq.relay()
    dekv_gather.relay()
    chunks[4].spread()
    loads[13].wait()
    genc_ref[...] = nt(dekv[...], w_ckv[...])
    total = small_b[...]
    for d, copy in enumerate(s_chip):
        copy.wait_recv()
        total = total + small_chip[d]
    small_c[...] = total
    s_exp = [
        send(small_c, small_exp.at[d], s3_send.at[d], s3_recv.at[d], {"exp": peer}) for d, peer in enumerate(peers)
    ]
    chunks[5].spread()
    for i in (2, 1, 0):
        chunks[i].over_seq.relay_far()
    dekv_gather.relay_far()
    total = small_c[...]
    for d, copy in enumerate(s_exp):
        copy.wait_recv()
        total = total + small_exp[d]
    small_out_ref[...] = total
    for copy in gins:
        copy.wait_recv()
    gin_ref[...] = gin_in[...].astype(F32)
    for i in (3, 4, 5):
        chunks[i].over_seq.relay()
    for i in (3, 4, 5):
        chunks[i].over_seq.relay_far()
    for chunk in chunks:
        chunk.over_seq.finish()
    dekv_gather.finish()

    for copy in started + enc_over_exp() + dekv_over_exp():
        copy.wait_send()
    for scatter in squares + [enc_scatter]:
        scatter.drain()
    for chunk in chunks:
        chunk.drain()
    dekv_gather.drain()

    @pl.loop(0, pairs)
    def _(p):
        terms(p).drain()


def backward_call(seq_count, experts, made, dxb, g, x, r1, r2, gates, chosen, slots, x3, n2, o, oc, q, qc, gains, router,
                  buckets, kv, p, pc, ekv, co, cq, so, qkv, n1, x_all, dm_all, w_in, w_out, ckv):
    rows, width = x.shape
    span = seq_count * rows
    pairs = width // LANES
    enc_rows = ekv.shape[0]
    part = width // seq_count
    enc_part = enc_rows // seq_count
    own_enc = enc_part // experts
    hidden = w_in.shape[1] // seq_count
    z = experts - 1
    quarter = (part // 2, width // (experts // 2))
    small = (8, width + 2 * LANES)
    shape = jax.ShapeDtypeStruct
    dma = lambda *n: pltpu.SemaphoreType.DMA(n)
    bf = lambda *n: pltpu.VMEM(n, BF16)
    f32 = lambda *n: pltpu.VMEM(n, F32)
    return pl.pallas_call(
        functools.partial(backward_kernel, seq_count, experts),
        out_shape=(
            shape((rows, width), BF16), shape((rows, width), F32), shape((6, seq_count, part, width), BF16),
            shape((seq_count, experts, own_enc, 2 * width), BF16), shape(small, F32), shape((part, w_in.shape[1]), F32),
            shape((hidden, width), F32), shape((own_enc, width), F32),
        ),
        in_specs=[VMEM] * 18 + [ANY] * 14,
        out_specs=(VMEM, VMEM, ANY, ANY, VMEM, VMEM, VMEM, VMEM),
        scratch_shapes=[
            bf(span, 2 * width), bf(pairs, span, 2 * rows), bf(pairs, enc_rows, 2 * rows), bf(enc_rows, 2 * width),
            bf(*co.shape), bf(*cq.shape), bf(*so.shape), bf(*qkv.shape), f32(rows, width), bf(rows, width), bf(rows, width),
            bf(rows, 3 * width), bf(span + rows, 2 * rows), f32(2 * pairs, 2 * rows), f32(pairs, 2 * rows),
            bf(2, 4, enc_part, 2 * width), bf(4, enc_part, 2 * width), bf(2, enc_part // 2, 2 * width),
            bf(2, enc_part, 2 * width), bf(experts, own_enc, 2 * width), bf(z, own_enc, 2 * width), bf(own_enc, 2 * width),
            bf(pairs, 2, 4, rows, 2 * LANES), bf(pairs, 4, rows, 2 * LANES), bf(pairs, 2, rows // 2, 2 * LANES),
            bf(pairs, 2, rows, 2 * LANES),
            bf(3, 2, 4, part, width), bf(3, 4, part, width), bf(3, 2, part // 2, width), bf(3, 2, part, width),
            bf(6, part, width), bf(6, z, *quarter), bf(6, *quarter), bf(3 * width, rows), bf(3, part, span),
            bf(*n1.shape), bf(*x_all.shape), bf(*dm_all.shape), bf(width, hidden), bf(hidden, width), bf(*ckv.shape),
            bf(seq_count, part, hidden), bf(part, w_in.shape[1]),
            f32(*small), f32(*small), f32(*small), f32(*small), f32(3, *small), f32(z, *small),
            dma(14), dma(7), dma(1), dma(1), dma(2), dma(2), dma(2), dma(2), dma(z), dma(z), dma(z), dma(z), dma(8), dma(8),
            dma(pairs), dma(pairs), dma(pairs, 2), dma(pairs, 2), dma(pairs, 2), dma(pairs, 2),
            dma(3), dma(3), dma(3, 2), dma(3, 2), dma(3, 2), dma(3, 2),
            dma(6, z), dma(6, z), dma(6, z), dma(6, z), dma(6, 8), dma(6, 8),
            dma(3, seq_count - 1), dma(3, seq_count - 1), dma(seq_count - 1), dma(seq_count - 1),
            dma(1), dma(1), dma(3), dma(3), dma(z), dma(z),
        ],
        compiler_params=pltpu.CompilerParams(collective_id=2, has_side_effects=True, vmem_limit_bytes=63 << 20),
        name="backward",
    )(made, dxb, g, x, r1, r2, gates, chosen, slots, x3, n2, o, oc, q, qc, gains, router, buckets, kv, p, pc, ekv, co, cq, so,
      qkv, n1, x_all, dm_all, w_in, w_out, ckv)


def finish_kernel(
    experts, weights_hbm, dekv_hbm, enc_hbm, small_ref, layer_hbm, dx_hbm, genc_hbm, gin_hbm, gout_hbm,
    layer_out, dx_out, genc_out, gains_out, qkv_hbm, so_hbm, cq_hbm, ckv_hbm, co_hbm, rel_out, router_out, gin_out, gout_out,
    weights, dekv, enc, squares, qkv, ckv, layer, dx, genc, gin, gout, load_sem, sem,
):
    seq_count, part, width = weights.shape[1:]
    loads = [pltpu.make_async_copy(weights_hbm.at[i], weights.at[i], load_sem.at[i]) for i in range(6)] + [
        pltpu.make_async_copy(dekv_hbm, dekv, load_sem.at[6]), pltpu.make_async_copy(enc_hbm, enc, load_sem.at[7])
    ]
    through = ((gout_hbm, gout, gout_out), (gin_hbm, gin, gin_out), (dx_hbm, dx, dx_out), (layer_hbm, layer, layer_out),
               (genc_hbm, genc, genc_out))
    loads += [pltpu.make_async_copy(src, held, load_sem.at[8 + i]) for i, (src, held, _) in enumerate(through)]
    for load in loads:
        load.start()
    copies = []

    def store(src, dst):
        copy = pltpu.make_async_copy(src, dst, sem.at[len(copies)])
        copy.start()
        copies.append(copy)

    gains_out[...] = small_ref[0:3, :width]
    router_out[...] = small_ref[4 : 4 + experts, :width]
    heads, buckets = rel_out.shape
    rel_out[0:8, :] = small_ref[0:8, width : width + buckets]
    rel_out[8:heads, :] = small_ref[0 : heads - 8, width + LANES : width + LANES + buckets]
    for i, out in enumerate((so_hbm, cq_hbm, co_hbm)):
        loads[i].wait()
        squares[i] = weights[i].reshape(seq_count * part, width).astype(F32)
        store(squares.at[i], out)
    for i, (_, held, out) in enumerate(through):
        loads[8 + i].wait()
        store(held, out)
    for i in range(3):
        loads[3 + i].wait()
        at = slice(i * width, (i + 1) * width)
        for block in range(width // LANES):
            rows = slice(block * LANES, (block + 1) * LANES)
            qkv[:, i * width + block * LANES : i * width + (block + 1) * LANES] = (
                weights[3 + i].reshape(seq_count * part, width)[rows, :].astype(F32).T
            )
        store(qkv.at[:, at], qkv_hbm.at[:, at])
    loads[6].wait()
    loads[7].wait()
    for n in range(2):
        at = slice(n * width, (n + 1) * width)
        ckv[:, at] = tn(enc[...], dekv[...].reshape(enc.shape[0], 2 * width)[:, at])
        store(ckv.at[:, at], ckv_hbm.at[:, at])
    for copy in copies:
        copy.wait()


def finish_call(heads, buckets, experts, weights, dekv, enc, small, layer, dx, genc, gin, gout):
    seq_count, part, width = weights.shape[1:]
    shape = jax.ShapeDtypeStruct
    f32 = lambda *n: shape(n, F32)
    return pl.pallas_call(
        functools.partial(finish_kernel, experts),
        out_shape=(
            shape(layer.shape, BF16), f32(*dx.shape), f32(*genc.shape), f32(3, width), f32(width, 3 * width), f32(width, width),
            f32(width, width), f32(width, 2 * width), f32(width, width), f32(heads, buckets), f32(experts, width),
            f32(*gin.shape), f32(*gout.shape),
        ),
        in_specs=[ANY, ANY, ANY, VMEM, ANY, ANY, ANY, ANY, ANY],
        out_specs=(ANY, ANY, ANY, VMEM, ANY, ANY, ANY, ANY, ANY, VMEM, VMEM, ANY, ANY),
        scratch_shapes=[
            pltpu.VMEM(weights.shape, BF16), pltpu.VMEM(dekv.shape, BF16), pltpu.VMEM(enc.shape, BF16),
            pltpu.VMEM((3, width, width), F32), pltpu.VMEM((width, 3 * width), F32), pltpu.VMEM((width, 2 * width), F32),
            pltpu.VMEM(layer.shape, BF16), pltpu.VMEM(dx.shape, F32), pltpu.VMEM(genc.shape, F32), pltpu.VMEM(gin.shape, F32),
            pltpu.VMEM(gout.shape, F32), pltpu.SemaphoreType.DMA((13,)), pltpu.SemaphoreType.DMA((13,)),
        ],
        compiler_params=pltpu.CompilerParams(vmem_limit_bytes=60 << 20),
        name="finish",
    )(weights, dekv, enc, small, layer, dx, genc, gin, gout)


def fused(inputs, encoder, lengths, buckets, routes, norm_gains, self_qkv, self_out, cross_q, cross_kv, cross_out,
          rel_bias, router, expert_in, expert_out, cotangent):
    seq_count = lax.axis_size("seq")
    rows, width = inputs.shape[1:]
    experts = router.shape[1]
    capacity = 5 * rows // (4 * experts)
    buckets = buckets[None, :]
    router = router.T
    (n1_all, kv_all, prob, cross_prob, ekv, q, o, n2, qc, oc, x3, r1, r2, gates, chosen, slots, xs, dms) = forward_call(
        seq_count, capacity, inputs[0], encoder, lengths, buckets, routes.reshape(1, rows), norm_gains, self_qkv,
        self_out, cross_q, cross_kv, cross_out, rel_bias.T, router, cotangent[0])
    made, dxb, x_all, dm_all = experts_call(seq_count, capacity, width, xs, dms, expert_in[0], expert_out[0])
    (layer_out, grad_input, weights, dekv, small, gin, gout, grad_encoder) = backward_call(
        seq_count, experts, made, dxb, cotangent[0], inputs[0], r1, r2, gates, chosen, slots, x3, n2, o, oc, q, qc, norm_gains,
        router, buckets, kv_all, prob, cross_prob, ekv, cross_out, cross_q, self_out, self_qkv, n1_all, x_all, dm_all,
        expert_in[0], expert_out[0], cross_kv)
    (layer_out, grad_input, grad_encoder, gains, g_qkv, g_so, g_cq, g_ckv, g_co, g_rel, g_router, gin, gout) = finish_call(
        rel_bias.shape[1], rel_bias.shape[0], experts, weights, dekv, encoder, small, layer_out, grad_input, grad_encoder, gin,
        gout)
    return (layer_out[None], grad_input[None], grad_encoder, gains, g_qkv, g_so, g_cq, g_ckv, g_co, g_rel.T, g_router.T,
            gin[None], gout[None])


def on_device(*operands):
    if lax.axis_size("seq") == 8 and lax.axis_size("exp") == 4 and operands[0].shape[1] == 128:
        return fused(*operands)
    return streamed(*operands)


def solution(mesh):
    in_specs = (
        P("exp", "seq", None),
        P(),
        P("exp", None),
        P(),
        P("exp", "seq", None),
        P(),
        P(),
        P(),
        P(),
        P(),
        P(),
        P(),
        P(),
        P("exp", None, None),
        P("exp", None, None),
        P("exp", "seq", None),
    )
    out_specs = (
        P("exp", "seq", None),
        P("exp", "seq", None),
        P(("seq", "exp"), None),
        P(),
        P(),
        P(),
        P(),
        P(),
        P(),
        P(),
        P(),
        P("exp", "seq", None),
        P("exp", "seq", None),
    )
    return jax.shard_map(
        on_device, mesh=mesh, in_specs=in_specs, out_specs=out_specs, check_vma=False
    )
```

```python
import functools
import math

import jax
import jax.numpy as jnp
from jax import lax
from jax.experimental import pallas as pl
from jax.experimental.pallas import tpu as pltpu
from jax.sharding import PartitionSpec as P

H = 12
HD = 64


epsilon = 1e-06
masked_out = -1e30
highest = lax.Precision.HIGHEST


def rms_norm(value, gain):
    return value * lax.rsqrt(jnp.mean(value * value, axis=-1, keepdims=True) + epsilon) * gain


def split_heads(value):
    return value.reshape(value.shape[0], H, HD)


def doc_index(positions, doc_ends):
    return jnp.sum((positions[:, None] >= doc_ends[None, :]).astype(jnp.int32), axis=1)


def band_pick(offset_gap, query_rows, key_rows, table_span):
    band_len = query_rows + key_rows + 1
    column = jnp.arange(band_len, dtype=jnp.int32)
    distance = jnp.clip(offset_gap + query_rows - column, 0, table_span - 1)
    return (distance[:, None] == jnp.arange(table_span, dtype=jnp.int32)[None, :]).astype(
        jnp.float32
    )


def relative_bias(table, offset_gap, query_rows, key_rows):
    head_count = table.shape[0]
    band_len = query_rows + key_rows + 1
    band = jnp.dot(
        table, band_pick(offset_gap, query_rows, key_rows, table.shape[1]).T, precision=highest
    )
    tiled = jnp.broadcast_to(band[:, None, :], (head_count, query_rows, band_len)).reshape(
        head_count, query_rows * band_len
    )
    skewed = tiled[:, : query_rows * (band_len - 1)].reshape(head_count, query_rows, band_len - 1)
    return skewed[:, :, query_rows : query_rows + key_rows]


def table_terms(score_grads, offset_gap, table_span):
    head_count, query_rows, key_rows = score_grads.shape
    band_len = query_rows + key_rows + 1
    placed = jnp.pad(score_grads.astype(jnp.float32), ((0, 0), (0, 0), (query_rows, 0)))
    flat = jnp.pad(
        placed.reshape(head_count, query_rows * (band_len - 1)), ((0, 0), (0, query_rows))
    )
    diagonal_sums = jnp.sum(flat.reshape(head_count, query_rows, band_len), axis=1)
    return jnp.dot(
        diagonal_sums, band_pick(offset_gap, query_rows, key_rows, table_span), precision=highest
    )


def self_scores(queries, query_start, keys_part, key_start, doc_ends, table):
    query_rows = queries.shape[0]
    key_rows = keys_part.shape[0]
    query_pos = query_start + jnp.arange(query_rows, dtype=jnp.int32)
    key_pos = key_start + jnp.arange(key_rows, dtype=jnp.int32)
    offset_gap = query_start - key_start
    raw_scores = (
        jnp.einsum(
            "qhd,khd->hqk",
            split_heads(queries),
            split_heads(keys_part),
            preferred_element_type=jnp.float32,
        )
        * 0.125
    )
    allowed = (key_pos[None, :] <= query_pos[:, None]) & (
        doc_index(key_pos, doc_ends)[None, :] == doc_index(query_pos, doc_ends)[:, None]
    )
    scores = jnp.where(
        allowed[None],
        raw_scores + relative_bias(table, offset_gap, query_rows, key_rows),
        masked_out,
    )
    return (scores, allowed[None], offset_gap)


def over_blocks(step, running, pieces):
    rows_total = pieces[0].shape[0]
    block_rows = math.gcd(rows_total, 512)
    block_count = rows_total // block_rows
    stacked = tuple(
        (member.reshape(block_count, block_rows, *member.shape[1:]) for member in pieces)
    )

    def scan_step(inner_running, block_input):
        block_id, members = block_input
        return (step(inner_running, members, block_id * block_rows), None)

    result, ignored = lax.scan(
        scan_step, running, (jnp.arange(block_count, dtype=jnp.int32), stacked)
    )
    return result


def streamed(
    inputs,
    encoder,
    lengths,
    buckets,
    routes,
    norm_gains,
    self_qkv,
    self_out,
    cross_q,
    cross_kv,
    cross_out,
    rel_bias,
    router,
    expert_in,
    expert_out,
    cotangent,
):
    hidden = inputs[0].astype(jnp.float32)
    rows_dev = hidden.shape[0]
    model_width = hidden.shape[1]
    seq_count = lax.axis_size("seq")
    seq_index = lax.axis_index("seq")
    own_start = seq_index * rows_dev
    doc_ends = jnp.cumsum(lengths[0])
    bucket_pick = (
        buckets[:, None] == jnp.arange(rel_bias.shape[0], dtype=jnp.int32)[None, :]
    ).astype(jnp.float32)
    table = jnp.dot(bucket_pick, rel_bias, precision=highest).T
    normed_one, norm_one_back = jax.vjp(rms_norm, hidden, norm_gains[0])
    normed_one = normed_one.astype(jnp.bfloat16)
    qkv_all = jnp.dot(normed_one, self_qkv, preferred_element_type=jnp.float32).astype(jnp.bfloat16)
    queries = qkv_all[:, :model_width]
    keys_own = qkv_all[:, model_width : 2 * model_width]
    values_own = qkv_all[:, 2 * model_width :]

    def forward_step(running, pieces, key_start):
        top_old, denominator, summed = running
        keys_part, values_part = pieces
        scores, allowed, offset_gap = self_scores(
            queries, own_start, keys_part, key_start, doc_ends, table
        )
        top_new = jnp.maximum(top_old, jnp.max(scores, axis=-1))
        weights_raw = jnp.where(allowed, jnp.exp(scores - top_new[..., None]), 0.0)
        rescale = jnp.exp(top_old - top_new)
        denominator = denominator * rescale + jnp.sum(weights_raw, axis=-1)
        summed = summed * rescale[..., None] + jnp.einsum(
            "hqk,khd->hqd",
            weights_raw.astype(jnp.bfloat16),
            split_heads(values_part),
            preferred_element_type=jnp.float32,
        )
        return (top_new, denominator, summed)

    start_state = (
        jnp.full((H, rows_dev), masked_out, jnp.float32),
        jnp.zeros((H, rows_dev), jnp.float32),
        jnp.zeros((H, rows_dev, HD), jnp.float32),
    )
    top_score, denominator, summed = over_blocks(
        forward_step,
        start_state,
        (
            lax.all_gather(keys_own, "seq", axis=0, tiled=True),
            lax.all_gather(values_own, "seq", axis=0, tiled=True),
        ),
    )
    log_total = top_score + jnp.log(denominator)
    attended_full = (
        (summed / denominator[..., None]).transpose(1, 0, 2).reshape(rows_dev, model_width)
    )
    attended = attended_full.astype(jnp.bfloat16)
    after_self = hidden + jnp.dot(attended, self_out, preferred_element_type=jnp.float32)
    enc_kv = jnp.dot(encoder, cross_kv, preferred_element_type=jnp.float32).astype(jnp.bfloat16)
    cross_keys = split_heads(enc_kv[:, :model_width])
    cross_values = split_heads(enc_kv[:, model_width:])
    normed_two, norm_two_back = jax.vjp(rms_norm, after_self, norm_gains[1])
    normed_two = normed_two.astype(jnp.bfloat16)
    cross_queries = jnp.dot(normed_two, cross_q, preferred_element_type=jnp.float32).astype(
        jnp.bfloat16
    )
    cross_scores = (
        jnp.einsum(
            "qhd,khd->hqk",
            split_heads(cross_queries),
            cross_keys,
            preferred_element_type=jnp.float32,
        )
        * 0.125
    )
    cross_raw = jnp.exp(cross_scores - jnp.max(cross_scores, axis=-1, keepdims=True))
    cross_prob = cross_raw / jnp.sum(cross_raw, axis=-1, keepdims=True)
    cross_prob_low = cross_prob.astype(jnp.bfloat16)
    cross_att = (
        jnp.einsum("hqk,khd->qhd", cross_prob_low, cross_values, preferred_element_type=jnp.float32)
        .reshape(rows_dev, model_width)
        .astype(jnp.bfloat16)
    )
    after_cross = after_self + jnp.dot(cross_att, cross_out, preferred_element_type=jnp.float32)
    normed_three, norm_three_back = jax.vjp(rms_norm, after_cross, norm_gains[2])
    routed_in = normed_three.astype(jnp.bfloat16)
    gates = jax.nn.softmax(jnp.dot(routed_in, router, preferred_element_type=jnp.float32), axis=-1)
    expert_total = router.shape[1]
    local_experts = expert_in.shape[0]
    capacity = 5 * rows_dev // (4 * expert_total)
    route_ids = routes[0, :, 0]
    chosen = route_ids[:, None] == jnp.arange(expert_total, dtype=jnp.int32)[None, :]
    slots = jnp.sum(jnp.where(chosen, jnp.cumsum(chosen.astype(jnp.int32), axis=0), 0), axis=1) - 1
    kept = slots < capacity
    picked_gate = jnp.sum(jnp.where(chosen, gates, 0.0), axis=1)
    gate_used = picked_gate * kept.astype(jnp.float32)
    target = jnp.where(kept, route_ids * capacity + slots, -1)
    dispatch = (
        jnp.arange(expert_total * capacity, dtype=jnp.int32)[:, None] == target[None, :]
    ).astype(jnp.bfloat16)
    outgoing = (
        jnp.dot(dispatch, routed_in, preferred_element_type=jnp.float32)
        .astype(jnp.bfloat16)
        .reshape(expert_total, capacity, model_width)
    )
    arrived = lax.all_to_all(outgoing, "exp", split_axis=0, concat_axis=0, tiled=True).reshape(
        -1, local_experts, capacity, model_width
    )
    inner_pre = jnp.einsum("secd,edf->secf", arrived, expert_in, preferred_element_type=jnp.float32)
    active = jax.nn.gelu(inner_pre, approximate=True).astype(jnp.bfloat16)
    produced = jnp.einsum(
        "secf,efd->secd", active, expert_out, preferred_element_type=jnp.float32
    ).astype(jnp.bfloat16)
    returned = lax.all_to_all(
        produced.reshape(-1, capacity, model_width), "exp", split_axis=0, concat_axis=0, tiled=True
    )
    expert_rows = jnp.dot(
        dispatch.T, returned.reshape(-1, model_width), preferred_element_type=jnp.float32
    )
    layer_out = after_cross + gate_used[:, None] * expert_rows
    upstream = cotangent[0].astype(jnp.float32)
    made_grad = (upstream * gate_used[:, None]).astype(jnp.bfloat16)
    sent_grad = (
        jnp.dot(dispatch, made_grad, preferred_element_type=jnp.float32)
        .astype(jnp.bfloat16)
        .reshape(expert_total, capacity, model_width)
    )
    grad_arrived = lax.all_to_all(
        sent_grad, "exp", split_axis=0, concat_axis=0, tiled=True
    ).reshape(-1, local_experts, capacity, model_width)
    inner_again = jnp.einsum(
        "secd,edf->secf", arrived, expert_in, preferred_element_type=jnp.float32
    )
    active_again, gelu_back = jax.vjp(
        lambda value: jax.nn.gelu(value, approximate=True), inner_again
    )
    grad_out_w = jnp.einsum(
        "secf,secd->efd",
        active_again.astype(jnp.bfloat16),
        grad_arrived,
        preferred_element_type=jnp.float32,
    )
    grad_active = jnp.einsum(
        "secd,efd->secf", grad_arrived, expert_out, preferred_element_type=jnp.float32
    )
    grad_inner = gelu_back(grad_active)[0].astype(jnp.bfloat16)
    grad_in_w = jnp.einsum(
        "secd,secf->edf", arrived, grad_inner, preferred_element_type=jnp.float32
    )
    grad_sent_x = jnp.einsum(
        "secf,edf->secd", grad_inner, expert_in, preferred_element_type=jnp.float32
    ).astype(jnp.bfloat16)
    grad_back = lax.all_to_all(
        grad_sent_x.reshape(-1, capacity, model_width),
        "exp",
        split_axis=0,
        concat_axis=0,
        tiled=True,
    )
    grad_routed = jnp.dot(
        dispatch.T, grad_back.reshape(-1, model_width), preferred_element_type=jnp.float32
    )
    expert_sums = (
        lax.psum_scatter(grad_in_w, "seq", scatter_dimension=1, tiled=True),
        lax.psum_scatter(grad_out_w, "seq", scatter_dimension=1, tiled=True),
    )
    gate_grad = jnp.sum(upstream * expert_rows, axis=1) * kept.astype(jnp.float32)
    logit_grad = gates * (
        jnp.where(chosen, gate_grad[:, None], 0.0) - (picked_gate * gate_grad)[:, None]
    )
    router_grad = jnp.dot(routed_in.astype(jnp.float32).T, logit_grad, precision=highest)
    grad_normed_three = (
        jnp.dot(logit_grad, router.astype(jnp.float32).T, precision=highest) + grad_routed
    )
    grad_after_cross, gain_three = norm_three_back(grad_normed_three)
    grad_after_cross = grad_after_cross + upstream
    cross_branch = grad_after_cross.astype(jnp.bfloat16)
    cross_out_grad = jnp.dot(cross_att.T, cross_branch, preferred_element_type=jnp.float32)
    grad_cross_att = split_heads(
        jnp.dot(cross_branch, cross_out.T, preferred_element_type=jnp.float32).astype(jnp.bfloat16)
    )
    cross_prob_grad = jnp.einsum(
        "qhd,khd->hqk", grad_cross_att, cross_values, preferred_element_type=jnp.float32
    )
    cross_delta = jnp.sum(cross_prob * cross_prob_grad, axis=-1, keepdims=True)
    cross_score_grad = (cross_prob * (cross_prob_grad - cross_delta)).astype(jnp.bfloat16)
    grad_cross_queries = (
        (
            jnp.einsum(
                "hqk,khd->qhd", cross_score_grad, cross_keys, preferred_element_type=jnp.float32
            )
            * 0.125
        )
        .reshape(rows_dev, model_width)
        .astype(jnp.bfloat16)
    )
    grad_enc_keys = (
        jnp.einsum(
            "hqk,qhd->khd",
            cross_score_grad,
            split_heads(cross_queries),
            preferred_element_type=jnp.float32,
        )
        * 0.125
    )
    grad_enc_values = jnp.einsum(
        "hqk,qhd->khd", cross_prob_low, grad_cross_att, preferred_element_type=jnp.float32
    )
    enc_terms = jnp.concatenate(
        [grad_enc_keys.reshape(-1, model_width), grad_enc_values.reshape(-1, model_width)], axis=1
    )
    enc_grad_rows = lax.psum_scatter(
        enc_terms, ("seq", "exp"), scatter_dimension=0, tiled=True
    ).astype(jnp.bfloat16)
    enc_count = enc_grad_rows.shape[0]
    flat_index = seq_index * lax.axis_size("exp") + lax.axis_index("exp")
    own_enc = lax.dynamic_slice_in_dim(encoder, flat_index * enc_count, enc_count, 0)
    grad_encoder = jnp.dot(enc_grad_rows, cross_kv.T, preferred_element_type=jnp.float32)
    pair_grad = jnp.dot(own_enc.T, enc_grad_rows, preferred_element_type=jnp.float32)
    query_w_grad = jnp.dot(normed_two.T, grad_cross_queries, preferred_element_type=jnp.float32)
    grad_normed_two = jnp.dot(grad_cross_queries, cross_q.T, preferred_element_type=jnp.float32)
    grad_after_self, gain_two = norm_two_back(grad_normed_two)
    grad_after_self = grad_after_self + grad_after_cross
    self_branch = grad_after_self.astype(jnp.bfloat16)
    self_out_grad = jnp.dot(attended.T, self_branch, preferred_element_type=jnp.float32)
    grad_attended = jnp.dot(self_branch, self_out.T, preferred_element_type=jnp.float32).astype(
        jnp.bfloat16
    )
    row_delta = jnp.sum(
        split_heads(grad_attended).astype(jnp.float32) * split_heads(attended_full), axis=-1
    ).T
    stats_all = (
        lax.all_gather(log_total.T, "seq", axis=0, tiled=True),
        lax.all_gather(row_delta.T, "seq", axis=0, tiled=True),
    )

    def query_step(running, pieces, query_start):
        kv_grad, query_grads, table_grad = running
        queries_part, grads_part = pieces
        piece_rows = queries_part.shape[0]
        lse_part = lax.dynamic_slice_in_dim(stats_all[0], query_start, piece_rows, 0).T
        delta_part = lax.dynamic_slice_in_dim(stats_all[1], query_start, piece_rows, 0).T
        scores, allowed, offset_gap = self_scores(
            queries_part, query_start, keys_own, own_start, doc_ends, table
        )
        probability = jnp.where(allowed, jnp.exp(scores - lse_part[..., None]), 0.0)
        prob_grad = jnp.einsum(
            "qhd,khd->hqk",
            split_heads(grads_part),
            split_heads(values_own),
            preferred_element_type=jnp.float32,
        )
        score_grad = (probability * (prob_grad - delta_part[..., None])).astype(jnp.bfloat16)
        key_grad = (
            jnp.einsum(
                "hqk,qhd->khd",
                score_grad,
                split_heads(queries_part),
                preferred_element_type=jnp.float32,
            )
            * 0.125
        )
        value_grad = jnp.einsum(
            "hqk,qhd->khd",
            probability.astype(jnp.bfloat16),
            split_heads(grads_part),
            preferred_element_type=jnp.float32,
        )
        kv_grad = kv_grad + jnp.concatenate(
            [key_grad.reshape(-1, model_width), value_grad.reshape(-1, model_width)], axis=1
        )
        table_grad = table_grad + table_terms(score_grad, offset_gap, table.shape[1])
        query_part_grad = jnp.einsum(
            "hqk,khd->qhd", score_grad, split_heads(keys_own), preferred_element_type=jnp.float32
        ).reshape(piece_rows, model_width)
        current = lax.dynamic_slice_in_dim(query_grads, query_start, piece_rows, 0)
        query_grads = lax.dynamic_update_slice_in_dim(
            query_grads, current + query_part_grad, query_start, 0
        )
        return (kv_grad, query_grads, table_grad)

    back_start = (
        jnp.zeros((rows_dev, 2 * model_width), jnp.float32),
        jnp.zeros((seq_count * rows_dev, model_width), jnp.float32),
        jnp.zeros(table.shape, jnp.float32),
    )
    kv_grad, query_buffer, table_grad = over_blocks(
        query_step,
        back_start,
        (
            lax.all_gather(queries, "seq", axis=0, tiled=True),
            lax.all_gather(grad_attended, "seq", axis=0, tiled=True),
        ),
    )
    query_grad = lax.psum_scatter(query_buffer, "seq", scatter_dimension=0, tiled=True)
    qkv_grad = jnp.concatenate(
        [(query_grad * 0.125).astype(jnp.bfloat16), kv_grad.astype(jnp.bfloat16)], axis=1
    )
    qkv_w_grad = jnp.dot(normed_one.T, qkv_grad, preferred_element_type=jnp.float32)
    grad_normed_one = jnp.dot(qkv_grad, self_qkv.T, preferred_element_type=jnp.float32)
    grad_hidden, gain_one = norm_one_back(grad_normed_one)
    grad_input = grad_hidden + grad_after_self
    rel_grad = jnp.dot(bucket_pick.T, table_grad.T, precision=highest)
    summed_grads = lax.psum(
        (
            jnp.stack([gain_one, gain_two, gain_three]),
            qkv_w_grad,
            self_out_grad,
            query_w_grad,
            pair_grad,
            cross_out_grad,
            rel_grad,
            router_grad,
        ),
        ("seq", "exp"),
    )
    return (
        layer_out.astype(jnp.bfloat16)[None],
        grad_input[None],
        grad_encoder,
        summed_grads[0],
        summed_grads[1],
        summed_grads[2],
        summed_grads[3],
        summed_grads[4],
        summed_grads[5],
        summed_grads[6],
        summed_grads[7],
        expert_sums[0],
        expert_sums[1],
    )


F32 = jnp.float32
BF16 = jnp.bfloat16
MESH = pl.DeviceIdType.MESH
ANY = pl.BlockSpec(memory_space=pl.ANY)
VMEM = pl.BlockSpec(memory_space=pltpu.VMEM)
SMEM = pl.BlockSpec(memory_space=pltpu.SMEM)
LANES = 128


def nn(a, b):
    return lax.dot_general(a, b, (((1,), (0,)), ((), ())), preferred_element_type=F32)


def nt(a, b):
    return lax.dot_general(a, b, (((1,), (1,)), ((), ())), preferred_element_type=F32)


def tn(a, b):
    return lax.dot_general(a, b, (((0,), (0,)), ((), ())), preferred_element_type=F32)


def rms_scale(a):
    return lax.rsqrt(jnp.mean(a * a, axis=-1, keepdims=True) + epsilon)


def pair_lanes(p):
    return pl.ds(pl.multiple_of(p * LANES, LANES), LANES)


def block_of(index, size):
    return pl.ds(pl.multiple_of(index * size, size), size)


def head_stack(pair):
    lane = lax.broadcasted_iota(jnp.int32, pair.shape, 1)
    zero = jnp.zeros_like(pair)
    return jnp.concatenate([jnp.where(lane < HD, pair, zero), jnp.where(lane < HD, zero, pair)], axis=0)


def head_unstack(both, rows):
    feature = lax.broadcasted_iota(jnp.int32, (both.shape[0], rows), 0)
    return jnp.where(feature < HD, both[:, :rows], both[:, rows:]).T


def pack_slots(value, experts):
    slots = value.shape[0] // experts
    blocks = value.shape[1] // LANES
    return jnp.stack([
        jnp.concatenate(
            [value[e * slots : (e + 1) * slots, b * LANES : (b + 1) * LANES] for b in range(blocks)], axis=0
        )
        for e in range(experts)
    ])


def unpack_slots(packed, slots):
    experts, blocks = packed.shape[0], packed.shape[1] // slots
    wide = packed.astype(F32)
    return jnp.concatenate(
        [
            jnp.concatenate([wide[e, b * slots : (b + 1) * slots] for e in range(experts)], axis=0)
            for b in range(blocks)
        ],
        axis=1,
    )


class Place:
    def __init__(self):
        self.me = lax.axis_index("seq")
        self.core = lax.rem(self.me, 2)
        self.chip = lax.div(self.me, 2)
        self.partner = self.me + 1 - 2 * self.core
        self.x_chip = self.chip + 1 - 2 * lax.rem(self.chip, 2)
        self.y_chip = lax.rem(self.chip + 2, 4)
        self.far_chip = 3 - self.chip
        self.x, self.y, self.far = (c * 2 + self.core for c in (self.x_chip, self.y_chip, self.far_chip))


def enter(devices):
    barrier = pltpu.get_barrier_semaphore()
    for device in devices:
        pl.semaphore_signal(barrier, inc=1, device_id=device, device_id_type=MESH)
    pl.semaphore_wait(barrier, len(devices))


def remote(src, dst, send_sem, recv_sem, device):
    return pltpu.make_async_remote_copy(
        src_ref=src, dst_ref=dst, send_sem=send_sem, recv_sem=recv_sem, device_id=device, device_id_type=MESH
    )


class Gather:
    def __init__(self, place, every, rows, sends, recvs):
        self.place, self.every, self.sends, self.recvs = place, every, sends, recvs
        half = rows // 2 if rows < 32 else -(-rows // 32) * 16
        self.halves = pl.ds(0, half), pl.ds(half, rows - half)

    def copy(self, slot):
        place, every = self.place, self.every
        block, device = (
            lambda: (every.at[place.me], place.partner),
            lambda: (every.at[place.me], place.x),
            lambda: (every.at[place.me], place.y),
            lambda: (every.at[place.x, self.halves[0]], place.y),
            lambda: (every.at[place.y, self.halves[1]], place.x),
            lambda: (every.at[place.x], place.partner),
            lambda: (every.at[place.y], place.partner),
            lambda: (every.at[place.far], place.partner),
        )[slot]()
        return remote(block, block, self.sends.at[slot], self.recvs.at[slot], {"seq": device})

    def send(self, *slots):
        for slot in slots:
            self.copy(slot).start()

    def wait(self, *slots):
        for slot in slots:
            self.copy(slot).wait_recv()

    def start(self):
        self.send(1, 2, 0)

    def relay(self):
        self.wait(1)
        self.send(3)
        self.wait(2)
        self.send(4, 5, 6)

    def relay_far(self):
        self.wait(3, 4)
        self.send(7)

    def finish(self):
        self.wait(0, 5, 6, 7)

    def drain(self):
        for slot in range(8):
            self.copy(slot).wait_send()


class Scatter:
    def __init__(self, place, out, pair, turn, side, half, sems):
        self.place, self.out, self.pair, self.turn, self.side, self.half = place, out, pair, turn, side, half
        self.pair_sems, self.turn_sems, self.side_sems = sems

    def pair_copy(self):
        send, recv = self.pair_sems
        return remote(self.out.at[1 - self.place.core], self.pair, send, recv, {"seq": self.place.partner})

    def turn_copies(self):
        place = self.place
        send, recv = self.turn_sems
        far = self.out.at[place.core, place.far_chip]
        return (
            remote(far.at[pl.ds(0, self.half)], self.turn.at[0], send.at[0], recv.at[0], {"seq": place.x}),
            remote(far.at[pl.ds(self.half, self.half)], self.turn.at[1], send.at[1], recv.at[1], {"seq": place.y}),
        )

    def side_copies(self):
        place = self.place
        send, recv = self.side_sems
        return (
            remote(self.out.at[place.core, place.x_chip], self.side.at[0], send.at[0], recv.at[0], {"seq": place.x}),
            remote(self.out.at[place.core, place.y_chip], self.side.at[1], send.at[1], recv.at[1], {"seq": place.y}),
        )

    def start(self):
        self.pair_copy().start()

    def turn_on(self):
        core = self.place.core
        self.pair_copy().wait_recv()
        self.out[core] = (self.out[core].astype(F32) + self.pair[...].astype(F32)).astype(BF16)
        for copy in self.turn_copies():
            copy.start()

    def side_on(self):
        place = self.place
        first, second = pl.ds(0, self.half), pl.ds(self.half, self.half)
        from_x, from_y = self.turn_copies()
        from_x.wait_recv()
        at = (place.core, place.y_chip, first)
        self.out[at] = (self.out[at].astype(F32) + self.turn[0].astype(F32)).astype(BF16)
        from_y.wait_recv()
        at = (place.core, place.x_chip, second)
        self.out[at] = (self.out[at].astype(F32) + self.turn[1].astype(F32)).astype(BF16)
        for copy in self.side_copies():
            copy.start()

    def total(self):
        for copy in self.side_copies():
            copy.wait_recv()
        own = self.out[self.place.core, self.place.chip].astype(F32)
        return own + self.side[0].astype(F32) + self.side[1].astype(F32)

    def drain(self):
        self.pair_copy().wait_send()
        for copy in self.turn_copies() + self.side_copies():
            copy.wait_send()


def expert_peers(exp_index, experts):
    return [lax.rem(exp_index + d, experts) for d in range(1, experts)]


def gelu_parts(hid):
    root, cubic = 0.7978845608028654, 0.044715
    square = hid * hid
    bent = jnp.tanh(root * hid * (1.0 + cubic * square))
    half = 0.5 * (1.0 + bent)
    return hid * half, half + 0.5 * hid * (1.0 - bent * bent) * (root + 3.0 * root * cubic * square)


def rms_back(a, gain, grad):
    scale = rms_scale(a)
    weighted = grad * gain
    da = scale * weighted - a * (scale * scale * scale * jnp.mean(a * weighted, axis=-1, keepdims=True))
    return da, jnp.sum(grad * (a * scale), axis=0, keepdims=True)


def in_two(value):
    high = value.astype(BF16)
    return high, (value - high.astype(F32)).astype(BF16)


GATE_ROWS = 16


def in_three(value):
    high = value.astype(BF16)
    rest = value - high.astype(F32)
    middle = rest.astype(BF16)
    low = (rest - middle.astype(F32)).astype(BF16)
    lane = lax.broadcasted_iota(jnp.int32, (value.shape[0], GATE_ROWS), 1)
    zero = jnp.zeros((value.shape[0], GATE_ROWS), BF16)
    return jnp.where(lane == 0, high, jnp.where(lane == 1, middle, jnp.where(lane == 2, low, zero)))


def slot_gates(parts):
    return jnp.sum(parts, axis=0, keepdims=True).T


class Chunk:
    def __init__(self, place, quarters, mine, peers, src, slots, own, every, sems, gather_sems, local_sem):
        self.place, self.quarters, self.mine, self.peers = place, quarters, mine, peers
        self.src, self.slots, self.own, self.every = src, slots, own, every
        self.scatter_sems, self.gather_sems, self.local_sem = sems[:2], sems[2:], local_sem
        self.over_seq = Gather(place, every, src.shape[0], *gather_sems)

    def scatter_copies(self):
        send, recv = self.scatter_sems
        return [
            remote(self.src.at[self.quarters[1 + d]], self.slots.at[d], send.at[d], recv.at[d], {"exp": peer})
            for d, peer in enumerate(self.peers)
        ]

    def gather_copies(self):
        send, recv = self.gather_sems
        target = self.every.at[(self.place.me,) + self.quarters[0]]
        return [remote(self.own, target, send.at[d], recv.at[d], {"exp": peer}) for d, peer in enumerate(self.peers)]

    def local_copy(self):
        return pltpu.make_async_copy(self.own, self.every.at[(self.place.me,) + self.quarters[0]], self.local_sem)

    def over_exp(self, value):
        self.src[...] = value.astype(BF16)
        for copy in self.scatter_copies():
            copy.start()

    def back_over_exp(self):
        total = self.src[self.quarters[0]].astype(F32)
        for d, copy in enumerate(self.scatter_copies()):
            copy.wait_recv()
            total = total + self.slots[d].astype(F32)
        self.own[...] = total.astype(BF16)
        self.local_copy().start()
        for copy in self.gather_copies():
            copy.start()

    def spread(self):
        self.local_copy().wait()
        for copy in self.gather_copies():
            copy.wait_recv()
        self.over_seq.start()

    def drain(self):
        for copy in self.scatter_copies() + self.gather_copies():
            copy.wait_send()
        self.over_seq.drain()


def layer_kernel(
    seq_count, capacity,
    x_ref, encoder_hbm, lengths_ref, buckets_ref, routes_ref, gains_ref, qkv_hbm, so_hbm, cq_hbm, ckv_hbm, co_hbm, rel_ref,
    router_ref, g_ref, in_hbm, out_hbm,
    out_ref, dx_ref, weights_hbm, dekv_hbm, small_out_ref, gin_ref, gout_ref, genc_ref,
    left, kv_all, prob, cross_prob, ekv, w_qkv, w_so, w_cq, w_ckv, w_co, table_ref, x_all, g_all, x_in, g_in, made_back, dx_back,
    q_ref, qc_ref, x3_ref, r1_ref, r2_ref, gates_ref, chosen_ref, slots_ref,
    dr_ref, doc_ref, dqc_ref, dqkv_ref, diag_ref, total_ref,
    e_pair, e_turn, e_side, e_mine, e_exp, dekv, t_pair, t_turn, t_side,
    c_slots, c_own, right, gin_in, small_a, small_b, small_c, small_pair, small_chip, small_exp,
    load_sem, local_sem, n_send, n_recv, o_send, o_recv, m_send, m_recv, c_send, c_recv, x_send, x_recv, d_send, d_recv,
    zx_send, zx_recv, zd_send, zd_recv, zm_send, zm_recv, zg_send, zg_recv,
    ep_send, ep_recv, et_send, et_recv, es_send, es_recv, ez_send, ez_recv, eg_send, eg_recv, ea_send, ea_recv,
    tp_send, tp_recv, tt_send, tt_recv, ts_send, ts_recv, cs_send, cs_recv, cg_send, cg_recv, ca_send, ca_recv,
    r_send, r_recv, g_send, g_recv, s1_send, s1_recv, s2_send, s2_recv, s3_send, s3_recv,
):
    rows, width = x_ref.shape
    span = seq_count * rows
    pairs = width // LANES
    enc_rows = encoder_hbm.shape[0]
    hidden = in_hbm.shape[1]
    own_hidden = hidden // seq_count
    place = Place()
    me = place.me
    mine = lax.axis_index("exp")
    experts = router_ref.shape[0]
    slot_rows = experts * capacity
    peers = expert_peers(mine, experts)
    everyone = [lax.rem(me + d, seq_count) for d in range(1, seq_count)]
    part = width // seq_count
    half_rows, half_lanes = part // 2, width // (experts // 2)
    quarters = [
        (block_of(lax.div(e, experts // 2), half_rows), block_of(lax.rem(e, experts // 2), half_lanes)) for e in [mine] + peers
    ]
    at_hidden = block_of(me, own_hidden)
    own_lanes = block_of(me, rows)
    near = pl.ds(pl.multiple_of(me * rows, rows), 2 * rows)
    gather, o_gather, n2_gather, oc_gather = (
        Gather(place, left.at[i], rows, *sems)
        for i, sems in ((3, (n_send, n_recv)), (0, (o_send, o_recv)), (1, (m_send, m_recv)), (2, (c_send, c_recv)))
    )
    x_gather = Gather(place, x_all, x_all.shape[1], x_send, x_recv)
    g_gather = Gather(place, g_all, slot_rows, d_send, d_recv)

    def load(i, src, dst):
        return pltpu.make_async_copy(src, dst, load_sem.at[i])

    def exp_moves(src, dst, send, recv):
        return [remote(src.at[peer], dst.at[mine], send.at[d], recv.at[d], {"exp": peer}) for d, peer in enumerate(peers)]

    def over_exp(src, dst, send, recv):
        for copy in exp_moves(src, dst, send, recv):
            copy.start()
        dst[mine] = src[mine]

    def arrive(src, dst, send, recv):
        for copy in exp_moves(src, dst, send, recv):
            copy.wait_recv()

    load_qkv, load_ckv = load(0, qkv_hbm, w_qkv), load(1, ckv_hbm, w_ckv)
    load_so, load_cq, load_co = load(3, so_hbm, w_so), load(4, cq_hbm, w_cq), load(5, co_hbm, w_co)
    load_qkv.start()
    load_ckv.start()

    def own_slots(e):
        of_all = lax.broadcasted_iota(jnp.int32, (slot_rows, LANES), 0) - e * capacity
        lane = lax.broadcasted_iota(jnp.int32, (slot_rows, LANES), 1)
        return ((of_all == lane) & (lane < capacity)).astype(BF16)

    def self_attention(scores, mask, enc, gs_ref):
        load_enc = load(2, encoder_hbm, enc)
        load_enc.start()
        x = x_ref[...].astype(F32)
        left[3, me] = (x * rms_scale(x) * gains_ref[0:1, :]).astype(BF16)
        enter([{"seq": device} for device in everyone] + [{"exp": peer} for peer in peers])
        gather.start()

        def project(chip):
            both = left[3, pl.ds(chip * 2, 2)].reshape(2 * rows, width)
            kv_all[block_of(chip, 2 * rows), :] = nn(both, w_qkv[:, width:]).astype(BF16)

        chosen = (routes_ref[...] == lax.broadcasted_iota(jnp.int32, (LANES, rows), 0)).astype(F32).T[:, :experts]
        chosen_ref[...] = chosen
        earlier = (
            lax.broadcasted_iota(jnp.int32, (rows, rows), 1) < lax.broadcasted_iota(jnp.int32, (rows, rows), 0)
        ).astype(BF16)
        slot = jnp.sum(nn(earlier, chosen.astype(BF16)) * chosen, axis=1, keepdims=True).astype(jnp.int32)
        kept = slot < capacity
        expert = lax.broadcasted_iota(jnp.int32, (rows, experts), 1).astype(F32)
        route = jnp.sum(chosen * expert, axis=1, keepdims=True).astype(jnp.int32)
        target = jnp.where(kept, route * capacity + slot, -1)
        slots = (lax.broadcasted_iota(jnp.int32, (rows, slot_rows), 1) == target).astype(BF16)
        slots_ref[...] = slots
        gs_ref[...] = pack_slots(tn(slots, g_ref[...]), experts).astype(BF16)
        g_trip = (gs_ref, g_in, zd_send, zd_recv)
        over_exp(*g_trip)

        load_qkv.wait()
        q_ref[...] = nn(left[3, me], w_qkv[:, :width]).astype(BF16) * jnp.asarray(0.125, BF16)
        gather.wait(0)
        project(place.chip)
        load_so.start()
        load_cq.start()
        load_co.start()
        load_ckv.wait()
        load_enc.wait()
        ekv[...] = nn(enc[...], w_ckv[...]).astype(BF16)
        gather.relay()
        pick = (buckets_ref[...] == lax.broadcasted_iota(jnp.int32, (rel_ref.shape[1], LANES), 0)).astype(F32)
        table = jnp.dot(rel_ref[...], pick, precision=highest, preferred_element_type=F32)
        table = table - table[:, LANES - 1 :]
        table_ref[...] = jnp.concatenate([jnp.zeros_like(table), table], axis=1)
        query_pos = me * rows + lax.broadcasted_iota(jnp.int32, (1, rows), 1)
        start = jnp.zeros((1, rows), jnp.int32)
        end = jnp.int32(0)
        for i in range(lengths_ref.shape[1]):
            end = end + lengths_ref[0, i]
            start = jnp.where(end <= query_pos, end, start)
        key_pos = lax.broadcasted_iota(jnp.int32, (span, rows), 0)
        seen = jnp.where((key_pos >= start) & (key_pos <= query_pos), 0.0, masked_out)
        mask[...] = jnp.concatenate([seen, seen], axis=1)
        gather.wait(5, 6)
        project(place.x_chip)
        project(place.y_chip)
        gather.relay_far()
        arrive(*g_trip)
        g_all[me] = unpack_slots(g_in[...], capacity).astype(BF16)
        g_gather.start()
        gather.wait(7)
        project(place.far_chip)

        @pl.loop(0, pairs)
        def _(p):
            lanes = pair_lanes(p)
            q_both = head_stack(q_ref[:, lanes])
            scores[pl.ds(rows, span), :] = nt(kv_all[:, lanes], q_both) + mask[...]
            biases = []
            for h in range(2):
                band = jnp.broadcast_to(table_ref[pl.ds(2 * p + h, 1), :], (2 * rows, 2 * LANES))
                biases.append(pltpu.roll(band, 0, 1, stride=1, stride_axis=0)[:, :rows])
            scores[near, :] = scores[near, :] + jnp.concatenate(biases, axis=1)
            s = scores[pl.ds(rows, span), :]
            weights = jnp.exp(s - jnp.max(s, axis=0, keepdims=True))
            weights = (weights * (1.0 / jnp.sum(weights, axis=0, keepdims=True))).astype(BF16)
            prob[p] = weights
            both = tn(kv_all[:, pair_lanes(pairs + p)], weights)
            left[0, me, :, lanes] = head_unstack(both, rows).astype(BF16)

        for copy in exp_moves(*g_trip):
            copy.wait_send()

    def rest_forward(xs_ref, made_out, dx_out, slope, w_in, w_out):
        load_in, load_out = load(6, in_hbm, w_in), load(7, out_hbm, w_out)
        load_in.start()
        load_out.start()
        o_gather.start()
        g_gather.relay()
        load_so.wait()
        load_cq.wait()
        load_co.wait()
        r1 = x_ref[...].astype(F32) + nn(left[0, me], w_so[...])
        r1_ref[...] = r1
        n2 = (r1 * rms_scale(r1) * gains_ref[1:2, :]).astype(BF16)
        left[1, me] = n2
        n2_gather.start()
        qc_ref[...] = nn(n2, w_cq[...]).astype(BF16) * jnp.asarray(0.125, BF16)

        @pl.loop(0, pairs)
        def _(p):
            lanes = pair_lanes(p)
            s = nt(ekv[:, lanes], head_stack(qc_ref[:, lanes]))
            weights = jnp.exp(s - jnp.max(s, axis=0, keepdims=True))
            weights = (weights * (1.0 / jnp.sum(weights, axis=0, keepdims=True))).astype(BF16)
            cross_prob[p] = weights
            both = tn(ekv[:, pair_lanes(pairs + p)], weights)
            left[2, me, :, lanes] = head_unstack(both, rows).astype(BF16)

        oc_gather.start()
        r2 = r1_ref[...] + nn(left[2, me], w_co[...])
        r2_ref[...] = r2
        x3 = (r2 * rms_scale(r2) * gains_ref[2:3, :]).astype(BF16)
        x3_ref[...] = x3
        logits = nt(x3, router_ref[...])
        top = jnp.exp(logits - jnp.max(logits, axis=-1, keepdims=True))
        gates = top / jnp.sum(top, axis=-1, keepdims=True)
        gates_ref[...] = gates
        chosen, slots = chosen_ref[...], slots_ref[...]
        kept = jnp.sum(slots.astype(F32), axis=1, keepdims=True)
        gate_used = jnp.sum(gates * chosen, axis=1, keepdims=True) * kept
        packed_rows = x_in.shape[1] - GATE_ROWS
        xs_ref[:, :packed_rows, :] = pack_slots(tn(slots, x3), experts).astype(BF16)
        by_slot = tn(in_three(gate_used), slots).astype(BF16)
        for e in range(experts):
            xs_ref[e, packed_rows:, :] = nn(by_slot, own_slots(e)).astype(BF16)
        x_trip = (xs_ref, x_in, zx_send, zx_recv)
        over_exp(*x_trip)

        o_gather.relay()
        load_in.wait()
        load_out.wait()
        arrive(*x_trip)
        x_all[me, :slot_rows, :] = unpack_slots(x_in[:, :packed_rows, :], capacity).astype(BF16)
        gate_parts = jnp.zeros((GATE_ROWS, slot_rows), F32)
        for e in range(experts):
            gate_parts = gate_parts + nt(x_in[e, packed_rows:, :], own_slots(e))
        x_all[me, slot_rows:, :] = jnp.concatenate(
            [gate_parts, jnp.zeros((GATE_ROWS, width - slot_rows), F32)], axis=1
        ).astype(BF16)
        x_gather.start()
        n2_gather.relay()
        xs = x_all[me, :slot_rows, :]
        made = jnp.zeros(xs.shape, F32)
        for n in range(hidden // width):
            at = slice(n * width, (n + 1) * width)
            value, derivative = gelu_parts(nn(xs, w_in[:, at]))
            slope[:, at] = derivative
            made = made + nn(value.astype(BF16), w_out[at, :])
        made_out[...] = pack_slots(made, experts).astype(BF16)
        made_trip = (made_out, made_back, zm_send, zm_recv)
        over_exp(*made_trip)
        dm = (g_all[me].astype(F32) * slot_gates(gate_parts)).astype(BF16)
        dx = jnp.zeros(dm.shape, F32)
        for n in range(hidden // width):
            at = slice(n * width, (n + 1) * width)
            dh = (nt(dm, w_out[at, :]) * slope[:, at]).astype(BF16)
            dx = dx + nt(dh, w_in[:, at])
        dx_out[...] = pack_slots(dx, experts).astype(BF16)
        dx_trip = (dx_out, dx_back, zg_send, zg_recv)
        over_exp(*dx_trip)
        g_gather.relay_far()
        oc_gather.relay()
        o_gather.relay_far()
        n2_gather.relay_far()
        arrive(*made_trip)
        arrive(*dx_trip)
        for trip in (x_trip, made_trip, dx_trip):
            for copy in exp_moves(*trip):
                copy.wait_send()

    bf = lambda *n: pltpu.VMEM(n, BF16)
    f32 = lambda *n: pltpu.VMEM(n, F32)
    packed = bf(*g_in.shape)
    pl.run_scoped(self_attention, f32(span + rows, 2 * rows), f32(span, 2 * rows), bf(enc_rows, width), packed)
    pl.run_scoped(
        rest_forward, bf(*x_in.shape), packed, packed, f32(slot_rows, hidden), bf(width, hidden), bf(hidden, width)
    )

    enc_part = enc_rows // seq_count
    dekv_gather = Gather(place, dekv_hbm, experts, ea_send, ea_recv)
    started = []

    def send(src, dst, send_sem, recv_sem, device):
        copy = remote(src, dst, send_sem, recv_sem, device)
        copy.start()
        started.append(copy)
        return copy

    def backward(e_out, t_out, c_src, turned_ref, ds_ref, gin_out, w_ein, w_eout):
        load_ein, load_eout = load(8, in_hbm.at[:, at_hidden], w_ein), load(9, out_hbm.at[at_hidden, :], w_eout)
        load_ein.start()
        load_eout.start()
        enc_scatter = Scatter(
            place, e_out, e_pair, e_turn, e_side, e_turn.shape[1],
            ((ep_send.at[0], ep_recv.at[0]), (et_send, et_recv), (es_send, es_recv)),
        )
        chunks = [
            Chunk(
                place, quarters, mine, peers, c_src.at[i], c_slots.at[i], c_own.at[i], weights_hbm.at[i],
                (cs_send.at[i], cs_recv.at[i], cg_send.at[i], cg_recv.at[i]), (ca_send.at[i], ca_recv.at[i]), local_sem.at[i],
            )
            for i in range(6)
        ]

        def enc_over_exp():
            return [
                remote(e_mine.at[peer], e_exp.at[d], ez_send.at[d], ez_recv.at[d], {"exp": peer}) for d, peer in enumerate(peers)
            ]

        def dekv_over_exp():
            return [
                remote(dekv, dekv_hbm.at[me, mine], eg_send.at[d], eg_recv.at[d], {"exp": peer}) for d, peer in enumerate(peers)
            ]

        def dekv_local():
            return pltpu.make_async_copy(dekv, dekv_hbm.at[me, mine], local_sem.at[6])

        def right_copies(i):
            return [
                remote(turned_ref.at[i, block_of(peer, part), :], right.at[i, :, own_lanes], r_send.at[i, d], r_recv.at[i, d],
                       {"seq": peer})
                for d, peer in enumerate(everyone)
            ]

        def exchange(i, factor):
            turned_ref[i] = factor.T
            for copy in right_copies(i):
                copy.start()
            right[i, :, own_lanes] = turned_ref[i, block_of(me, part), :]

        def multiply(i):
            for copy in right_copies(i):
                copy.wait_recv()
            chunks[i].over_exp(nn(right[i], left[min(i, 3)].reshape(span, width)))

        def gins():
            return [
                remote(gin_out.at[peer], gin_in.at[:, at_hidden], g_send.at[d], g_recv.at[d], {"seq": peer})
                for d, peer in enumerate(everyone)
            ]

        slots = slots_ref[...]
        made = nn(slots, unpack_slots(made_back[...], capacity).astype(BF16))
        kept = jnp.sum(slots.astype(F32), axis=1, keepdims=True)
        gates = gates_ref[...]
        chosen = chosen_ref[...]
        picked = jnp.sum(gates * chosen, axis=1, keepdims=True)
        g = g_ref[...].astype(F32)
        out_ref[...] = (r2_ref[...] + (picked * kept) * made).astype(BF16)
        gate_grad = jnp.sum(g * made, axis=1, keepdims=True) * kept
        dl = gates * (chosen * gate_grad - picked * gate_grad)
        dl_high, dl_low = in_two(dl)
        x3 = x3_ref[...]
        small_a[...] = jnp.zeros_like(small_a)
        small_a[4 : 4 + experts, :width] = tn(dl_high, x3) + tn(dl_low, x3)
        dx3 = (
            nn(slots, unpack_slots(dx_back[...], capacity).astype(BF16))
            + nn(dl_high, router_ref[...]) + nn(dl_low, router_ref[...])
        )
        da, dw = rms_back(r2_ref[...], gains_ref[2:3, :], dx3)
        small_a[2:3, :width] = dw
        dr_ref[...] = g + da
        do2 = dr_ref[...].astype(BF16)
        doc_ref[...] = nt(do2, w_co[...]).astype(BF16)
        exchange(2, do2)
        x_gather.relay()
        oc_gather.relay_far()

        @pl.loop(0, pairs)
        def _(p):
            lanes, value_lanes = pair_lanes(p), pair_lanes(pairs + p)
            doc_both = head_stack(doc_ref[:, lanes])
            weights = cross_prob[p]
            wide = weights.astype(F32)
            dp = nt(ekv[:, value_lanes], doc_both)
            dc = (wide * (dp - jnp.sum(wide * dp, axis=0, keepdims=True))).astype(BF16)
            dk = nn(dc, head_stack(qc_ref[:, lanes])).astype(BF16).reshape(4, 2, enc_part, LANES)
            dv = nn(weights, doc_both).astype(BF16).reshape(4, 2, enc_part, LANES)
            for k in range(2):
                e_out[k, :, :, lanes] = dk[:, k]
                e_out[k, :, :, value_lanes] = dv[:, k]
            dqc_ref[:, lanes] = (head_unstack(tn(ekv[:, lanes], dc), rows) * 0.125).astype(BF16)

        enc_scatter.start()
        x_gather.relay_far()
        dqc = dqc_ref[...]
        exchange(1, dqc)
        da, dw = rms_back(r1_ref[...], gains_ref[1:2, :], nt(dqc, w_cq[...]))
        small_a[1:2, :width] = dw
        enc_scatter.turn_on()
        dr_ref[...] = dr_ref[...] + da
        do1 = dr_ref[...].astype(BF16)
        doc_ref[...] = nt(do1, w_so[...]).astype(BF16)
        exchange(0, do1)
        oc_gather.finish()
        multiply(2)
        n2_gather.finish()
        o_gather.finish()

        ds_ref[pl.ds(0, rows), :] = jnp.zeros((rows, 2 * rows), BF16)
        flip = (
            lax.broadcasted_iota(jnp.int32, (2 * rows, 2 * rows), 0)
            + lax.broadcasted_iota(jnp.int32, (2 * rows, 2 * rows), 1)
            == 2 * rows - 1
        ).astype(BF16)

        def terms(p):
            return Scatter(
                place, t_out.at[p], t_pair.at[p], t_turn.at[p], t_side.at[p], rows // 2,
                ((tp_send.at[p], tp_recv.at[p]), (tt_send.at[p], tt_recv.at[p]), (ts_send.at[p], ts_recv.at[p])),
            )

        def pair_back(p):
            lanes, value_lanes = pair_lanes(p), pair_lanes(pairs + p)
            do_both = head_stack(doc_ref[:, lanes])
            weights = prob[p]
            wide = weights.astype(F32)
            dp = nt(kv_all[:, value_lanes], do_both)
            ds_wide = wide * (dp - jnp.sum(wide * dp, axis=0, keepdims=True))
            ds = ds_wide.astype(BF16)
            ds_ref[pl.ds(rows, span), :] = ds
            total_ref[pl.ds(p, 1), :] = jnp.sum(ds.astype(F32), axis=0, keepdims=True)
            dk = nn(ds, head_stack(q_ref[:, lanes])).astype(BF16).reshape(4, 2, rows, LANES)
            dv = nn(weights, do_both).astype(BF16).reshape(4, 2, rows, LANES)
            for k in range(2):
                t_out[p, k, :, :, :LANES] = dk[:, k]
                t_out[p, k, :, :, LANES:] = dv[:, k]
            terms(p).start()
            dqkv_ref[:, lanes] = (head_unstack(tn(kv_all[:, lanes], ds), rows) * 0.125).astype(BF16)
            turned = nn(flip, ds_ref[near, :])
            for h in range(2):
                one = turned[:, h * rows : (h + 1) * rows]
                one = jnp.concatenate([one, jnp.zeros_like(one)], axis=1)
                one = pltpu.roll(one, 1, 1, stride=1, stride_axis=0)
                diag_ref[pl.ds(2 * p + h, 1), :] = jnp.sum(one, axis=0, keepdims=True)

        def own_terms(p):
            total = terms(p).total()
            dqkv_ref[:, pair_lanes(pairs + p)] = total[:, :LANES].astype(BF16)
            dqkv_ref[:, pair_lanes(2 * pairs + p)] = total[:, LANES:].astype(BF16)

        @pl.loop(0, pairs)
        def _(t):
            pair_back(t)
            @pl.when(t >= 1)
            def _():
                terms(jnp.maximum(t - 1, 0)).turn_on()

            @pl.when(t >= 3)
            def _():
                terms(jnp.maximum(t - 3, 0)).side_on()

            @pl.when(t >= 5)
            def _():
                own_terms(jnp.maximum(t - 5, 0))

            @pl.when(t == 1)
            def _():
                enc_scatter.side_on()

            @pl.when(t == 2)
            def _():
                multiply(1)
                chunks[2].back_over_exp()

            @pl.when(t == 3)
            def _():
                multiply(0)

            @pl.when(t == 4)
            def _():
                e_mine[...] = enc_scatter.total().astype(BF16).reshape(e_mine.shape)
                for copy in enc_over_exp():
                    copy.start()
                chunks[1].back_over_exp()


        terms(5).turn_on()
        terms(3).side_on()
        own_terms(1)
        exchange(3, dqkv_ref[:, :width])
        load_ein.wait()
        load_eout.wait()
        x_gather.finish()
        g_gather.finish()
        xs = x_all[:, :slot_rows, :].reshape(-1, width)
        parts = x_all[:, slot_rows:, : 2 * LANES].astype(F32).reshape(seq_count * GATE_ROWS, 2 * LANES).T
        dm = jnp.concatenate(
            [
                (g_all[s].astype(F32) * sum(parts[:slot_rows, s * GATE_ROWS + n : s * GATE_ROWS + n + 1] for n in range(3)))
                for s in range(seq_count)
            ],
            axis=0,
        ).astype(BF16)
        value, slope = gelu_parts(nn(xs, w_ein[...]))
        gout_ref[...] = tn(value.astype(BF16), dm)
        chunks[0].back_over_exp()
        chunks[2].spread()
        terms(4).side_on()
        terms(5).side_on()
        own_terms(2)
        total = e_mine[mine].astype(F32)
        for d, copy in enumerate(enc_over_exp()):
            copy.wait_recv()
            total = total + e_exp[d].astype(F32)
        dekv[...] = total.astype(BF16)
        dekv_local().start()
        for copy in dekv_over_exp():
            copy.start()
        dh = (nt(dm, w_eout[...]) * slope).astype(BF16)
        gin_out[...] = tn(xs, dh).astype(BF16).reshape(gin_out.shape)
        own_terms(3)
        multiply(3)
        chunks[1].spread()
        own_terms(4)
        own_terms(5)

        dqkv = dqkv_ref[...]
        exchange(4, dqkv[:, width : 2 * width])
        exchange(5, dqkv[:, 2 * width :])
        x = x_ref[...].astype(F32)
        da, dw = rms_back(x, gains_ref[0:1, :], nt(dqkv, w_qkv[...]))
        small_a[0:1, :width] = dw
        dx_ref[...] = dr_ref[...] + da
        heads = 2 * pairs
        table = diag_ref[:, 2 * rows - LANES :]
        totals = total_ref[...]
        first = jnp.sum(totals[:, :rows], axis=1, keepdims=True)
        second = jnp.sum(totals[:, rows:], axis=1, keepdims=True)
        head = lax.broadcasted_iota(jnp.int32, (heads, pairs), 0)
        pair = lax.broadcasted_iota(jnp.int32, (heads, pairs), 1)
        spread = lambda odd, v: jnp.dot(
            (head == 2 * pair + odd).astype(F32), v, precision=highest, preferred_element_type=F32
        )
        whole = spread(0, jnp.broadcast_to(first, (pairs, LANES))) + spread(1, jnp.broadcast_to(second, (pairs, LANES)))
        rest = whole - jnp.sum(table, axis=1, keepdims=True)
        lane = lax.broadcasted_iota(jnp.int32, table.shape, 1)
        table = table + jnp.where(lane == LANES - 1, rest, 0.0)
        bucket = lax.broadcasted_iota(jnp.int32, (LANES, LANES), 0)
        pick = (buckets_ref[...] == bucket).astype(F32)
        by_bucket = lax.dot_general(table, pick, (((1,), (1,)), ((), ())), precision=highest, preferred_element_type=F32)
        small_a[0:8, width : width + LANES] = by_bucket[0:8]
        small_a[0 : heads - 8, width + LANES :] = by_bucket[8:heads]
        s_pair = send(small_a, small_pair, s1_send.at[0], s1_recv.at[0], {"seq": place.partner})

        chunks[3].back_over_exp()
        multiply(4)
        multiply(5)
        for copy in gins():
            copy.start()
        gin_in[:, at_hidden] = gin_out[me]
        chunks[0].spread()
        dekv_local().wait()
        for copy in dekv_over_exp():
            copy.wait_recv()
        dekv_gather.start()
        chunks[2].over_seq.relay()
        chunks[3].spread()
        s_pair.wait_recv()
        small_b[...] = small_a[...] + small_pair[...]
        s_chip = [
            send(small_b, small_chip.at[d], s2_send.at[d], s2_recv.at[d], {"seq": device})
            for d, device in enumerate((place.x, place.y, place.far))
        ]
        chunks[4].back_over_exp()
        chunks[5].back_over_exp()
        chunks[1].over_seq.relay()
        chunks[2].over_seq.relay_far()
        genc_ref[...] = nt(dekv[...], w_ckv[...])
        chunks[4].spread()
        chunks[5].spread()
        chunks[0].over_seq.relay()
        dekv_gather.relay()
        chunks[1].over_seq.relay_far()
        total = small_b[...]
        for d, copy in enumerate(s_chip):
            copy.wait_recv()
            total = total + small_chip[d]
        small_c[...] = total
        s_exp = [
            send(small_c, small_exp.at[d], s3_send.at[d], s3_recv.at[d], {"exp": peer}) for d, peer in enumerate(peers)
        ]
        chunks[3].over_seq.relay()
        chunks[0].over_seq.relay_far()
        dekv_gather.relay_far()
        for copy in gins():
            copy.wait_recv()
        gin_ref[...] = gin_in[...]
        chunks[4].over_seq.relay()
        chunks[5].over_seq.relay()
        total = small_c[...]
        for d, copy in enumerate(s_exp):
            copy.wait_recv()
            total = total + small_exp[d]
        small_out_ref[...] = total
        for i in (3, 4, 5):
            chunks[i].over_seq.relay_far()
        for chunk in chunks:
            chunk.over_seq.finish()
        dekv_gather.finish()

        for copy in started + enc_over_exp() + dekv_over_exp() + gins():
            copy.wait_send()
        for i in range(6):
            for copy in right_copies(i):
                copy.wait_send()
        for each in (gather, o_gather, n2_gather, oc_gather, x_gather, g_gather, dekv_gather, enc_scatter):
            each.drain()
        for chunk in chunks:
            chunk.drain()

        @pl.loop(0, pairs)
        def _(p):
            terms(p).drain()


    pl.run_scoped(
        backward, bf(2, 4, enc_part, 2 * width), bf(pairs, 2, 4, rows, 2 * LANES), bf(6, part, width), bf(6, width, rows),
        bf(span + rows, 2 * rows), bf(seq_count, part, own_hidden), bf(width, own_hidden), bf(own_hidden, width),
    )


def layer_call(seq_count, capacity, x, encoder, lengths, buckets, routes, gains, qkv, so, cq, ckv, co, rel, router, g, w_in,
               w_out):
    rows, width = x.shape
    span = seq_count * rows
    pairs = width // LANES
    heads = 2 * pairs
    enc_rows = encoder.shape[0]
    experts = router.shape[0]
    slot_rows = experts * capacity
    part = width // seq_count
    enc_part = enc_rows // seq_count
    own_enc = enc_part // experts
    hidden = w_in.shape[1]
    z = experts - 1
    quarter = (part // 2, width // (experts // 2))
    small = (8, width + 2 * LANES)
    packed = (experts, capacity * pairs, LANES)
    shape = jax.ShapeDtypeStruct
    dma = lambda *n: pltpu.SemaphoreType.DMA(n)
    bf = lambda *n: pltpu.VMEM(n, BF16)
    f32 = lambda *n: pltpu.VMEM(n, F32)
    wide = bf(rows, width)
    return pl.pallas_call(
        functools.partial(layer_kernel, seq_count, capacity),
        out_shape=(
            shape((rows, width), BF16), shape((rows, width), F32), shape((6, seq_count, part, width), BF16),
            shape((seq_count, experts, own_enc, 2 * width), BF16), shape(small, F32), shape((part, hidden), BF16),
            shape((hidden // seq_count, width), F32), shape((own_enc, width), F32),
        ),
        in_specs=[VMEM, ANY, SMEM, VMEM, VMEM, VMEM, ANY, ANY, ANY, ANY, ANY, VMEM, VMEM, VMEM, ANY, ANY],
        out_specs=(VMEM, VMEM, ANY, ANY, VMEM, VMEM, VMEM, VMEM),
        scratch_shapes=[
            bf(4, seq_count, rows, width), bf(span, 2 * width), bf(pairs, span, 2 * rows), bf(pairs, enc_rows, 2 * rows),
            bf(enc_rows, 2 * width), bf(*qkv.shape), bf(*so.shape), bf(*cq.shape), bf(*ckv.shape), bf(*co.shape),
            f32(heads, 2 * LANES), bf(seq_count, slot_rows + GATE_ROWS, width), bf(seq_count, slot_rows, width),
            bf(experts, capacity * pairs + GATE_ROWS, LANES), bf(*packed), bf(*packed), bf(*packed),
            wide, wide, wide, f32(rows, width), f32(rows, width), f32(rows, experts), f32(rows, experts), bf(rows, slot_rows),
            f32(rows, width), wide, wide, bf(rows, 3 * width), f32(heads, 2 * rows), f32(pairs, 2 * rows),
            bf(4, enc_part, 2 * width), bf(2, enc_part // 2, 2 * width), bf(2, enc_part, 2 * width),
            bf(experts, own_enc, 2 * width), bf(z, own_enc, 2 * width), bf(own_enc, 2 * width),
            bf(pairs, 4, rows, 2 * LANES), bf(pairs, 2, rows // 2, 2 * LANES), bf(pairs, 2, rows, 2 * LANES),
            bf(6, z, *quarter), bf(6, *quarter), bf(6, part, span), bf(part, hidden),
            f32(*small), f32(*small), f32(*small), f32(*small), f32(3, *small), f32(z, *small),
            dma(10), dma(7)] + [dma(8)] * 12 + [dma(z)] * 8 + [
            dma(1), dma(1), dma(2), dma(2), dma(2), dma(2), dma(z), dma(z), dma(z), dma(z), dma(8), dma(8),
            dma(pairs), dma(pairs), dma(pairs, 2), dma(pairs, 2), dma(pairs, 2), dma(pairs, 2),
            dma(6, z), dma(6, z), dma(6, z), dma(6, z), dma(6, 8), dma(6, 8),
            dma(6, seq_count - 1), dma(6, seq_count - 1), dma(seq_count - 1), dma(seq_count - 1),
            dma(1), dma(1), dma(3), dma(3), dma(z), dma(z),
        ],
        compiler_params=pltpu.CompilerParams(collective_id=0, has_side_effects=True, vmem_limit_bytes=63 << 20),
        name="layer",
    )(x, encoder, lengths, buckets, routes, gains, qkv, so, cq, ckv, co, rel, router, g, w_in, w_out)


def finish_kernel(
    experts, weights_hbm, dekv_hbm, enc_hbm, small_ref, layer_hbm, dx_hbm, genc_hbm, gin_ref, gout_hbm,
    layer_out, dx_out, genc_out, gains_out, qkv_hbm, so_hbm, cq_hbm, ckv_hbm, co_hbm, rel_out, router_out, gin_out, gout_out,
    weights, dekv, enc, squares, qkv, ckv, layer, dx, genc, gin, gout, load_sem, sem,
):
    seq_count, part, width = weights.shape[1:]
    loads = [pltpu.make_async_copy(weights_hbm.at[i], weights.at[i], load_sem.at[i]) for i in range(6)] + [
        pltpu.make_async_copy(dekv_hbm, dekv, load_sem.at[6]), pltpu.make_async_copy(enc_hbm, enc, load_sem.at[7])
    ]
    through = ((gout_hbm, gout, gout_out), (dx_hbm, dx, dx_out), (layer_hbm, layer, layer_out), (genc_hbm, genc, genc_out))
    loads += [pltpu.make_async_copy(src, held, load_sem.at[8 + i]) for i, (src, held, _) in enumerate(through)]
    for load in loads:
        load.start()
    copies = []

    def store(src, dst):
        copy = pltpu.make_async_copy(src, dst, sem.at[len(copies)])
        copy.start()
        copies.append(copy)

    gains_out[...] = small_ref[0:3, :width]
    router_out[...] = small_ref[4 : 4 + experts, :width]
    heads, buckets = rel_out.shape
    rel_out[0:8, :] = small_ref[0:8, width : width + buckets]
    rel_out[8:heads, :] = small_ref[0 : heads - 8, width + LANES : width + LANES + buckets]
    gin[...] = gin_ref[...].astype(F32)
    store(gin, gin_out)

    def turn(i, target, at):
        loads[i].wait()
        for block in range(width // LANES):
            rows = slice(block * LANES, (block + 1) * LANES)
            target[:, at + block * LANES : at + (block + 1) * LANES] = (
                weights[i].reshape(seq_count * part, width)[rows, :].astype(F32).T
            )

    for i, out in enumerate((so_hbm, cq_hbm, co_hbm)):
        turn(i, squares.at[i], 0)
        store(squares.at[i], out)
    for i, (_, held, out) in enumerate(through):
        loads[8 + i].wait()
        store(held, out)
    for i in range(3):
        at = slice(i * width, (i + 1) * width)
        turn(3 + i, qkv, i * width)
        store(qkv.at[:, at], qkv_hbm.at[:, at])
    loads[6].wait()
    loads[7].wait()
    for n in range(2):
        at = slice(n * width, (n + 1) * width)
        ckv[:, at] = tn(enc[...], dekv[...].reshape(enc.shape[0], 2 * width)[:, at])
        store(ckv.at[:, at], ckv_hbm.at[:, at])
    for copy in copies:
        copy.wait()


def finish_call(heads, buckets, experts, weights, dekv, enc, small, layer, dx, genc, gin, gout):
    seq_count, part, width = weights.shape[1:]
    shape = jax.ShapeDtypeStruct
    f32 = lambda *n: shape(n, F32)
    return pl.pallas_call(
        functools.partial(finish_kernel, experts),
        out_shape=(
            shape(layer.shape, BF16), f32(*dx.shape), f32(*genc.shape), f32(3, width), f32(width, 3 * width), f32(width, width),
            f32(width, width), f32(width, 2 * width), f32(width, width), f32(heads, buckets), f32(experts, width),
            f32(*gin.shape), f32(*gout.shape),
        ),
        in_specs=[ANY, ANY, ANY, VMEM, ANY, ANY, ANY, VMEM, ANY],
        out_specs=(ANY, ANY, ANY, VMEM, ANY, ANY, ANY, ANY, ANY, VMEM, VMEM, ANY, ANY),
        scratch_shapes=[
            pltpu.VMEM(weights.shape, BF16), pltpu.VMEM(dekv.shape, BF16), pltpu.VMEM(enc.shape, BF16),
            pltpu.VMEM((3, width, width), F32), pltpu.VMEM((width, 3 * width), F32), pltpu.VMEM((width, 2 * width), F32),
            pltpu.VMEM(layer.shape, BF16), pltpu.VMEM(dx.shape, F32), pltpu.VMEM(genc.shape, F32), pltpu.VMEM(gin.shape, F32),
            pltpu.VMEM(gout.shape, F32), pltpu.SemaphoreType.DMA((13,)), pltpu.SemaphoreType.DMA((13,)),
        ],
        compiler_params=pltpu.CompilerParams(vmem_limit_bytes=60 << 20),
        name="finish",
    )(weights, dekv, enc, small, layer, dx, genc, gin, gout)


def fused(inputs, encoder, lengths, buckets, routes, norm_gains, self_qkv, self_out, cross_q, cross_kv, cross_out,
          rel_bias, router, expert_in, expert_out, cotangent):
    seq_count = lax.axis_size("seq")
    rows = inputs.shape[1]
    experts = router.shape[1]
    capacity = 5 * rows // (4 * experts)
    (layer_out, grad_input, weights, dekv, small, gin, gout, grad_encoder) = layer_call(
        seq_count, capacity, inputs[0], encoder, lengths, buckets[None, :], routes.reshape(1, rows), norm_gains, self_qkv,
        self_out, cross_q, cross_kv, cross_out, rel_bias.T, router.T, cotangent[0], expert_in[0], expert_out[0])
    (layer_out, grad_input, grad_encoder, gains, g_qkv, g_so, g_cq, g_ckv, g_co, g_rel, g_router, gin, gout) = finish_call(
        rel_bias.shape[1], rel_bias.shape[0], experts, weights, dekv, encoder, small, layer_out, grad_input, grad_encoder, gin,
        gout)
    return (layer_out[None], grad_input[None], grad_encoder, gains, g_qkv, g_so, g_cq, g_ckv, g_co, g_rel.T, g_router.T,
            gin[None], gout[None])


def on_device(*operands):
    if lax.axis_size("seq") == 8 and lax.axis_size("exp") == 4 and operands[0].shape[1] == 128:
        return fused(*operands)
    return streamed(*operands)


def solution(mesh):
    in_specs = (
        P("exp", "seq", None),
        P(),
        P("exp", None),
        P(),
        P("exp", "seq", None),
        P(),
        P(),
        P(),
        P(),
        P(),
        P(),
        P(),
        P(),
        P("exp", None, None),
        P("exp", None, None),
        P("exp", "seq", None),
    )
    out_specs = (
        P("exp", "seq", None),
        P("exp", "seq", None),
        P(("seq", "exp"), None),
        P(),
        P(),
        P(),
        P(),
        P(),
        P(),
        P(),
        P(),
        P("exp", "seq", None),
        P("exp", "seq", None),
    )
    return jax.shard_map(
        on_device, mesh=mesh, in_specs=in_specs, out_specs=out_specs, check_vma=False
    )
```

```python
import functools
import math

import jax
import jax.numpy as jnp
from jax import lax
from jax.experimental import pallas as pl
from jax.experimental.pallas import tpu as pltpu
from jax.sharding import PartitionSpec as P

H = 12
HD = 64


epsilon = 1e-06
masked_out = -1e30
highest = lax.Precision.HIGHEST


def rms_norm(value, gain):
    return value * lax.rsqrt(jnp.mean(value * value, axis=-1, keepdims=True) + epsilon) * gain


def split_heads(value):
    return value.reshape(value.shape[0], H, HD)


def doc_index(positions, doc_ends):
    return jnp.sum((positions[:, None] >= doc_ends[None, :]).astype(jnp.int32), axis=1)


def band_pick(offset_gap, query_rows, key_rows, table_span):
    band_len = query_rows + key_rows + 1
    column = jnp.arange(band_len, dtype=jnp.int32)
    distance = jnp.clip(offset_gap + query_rows - column, 0, table_span - 1)
    return (distance[:, None] == jnp.arange(table_span, dtype=jnp.int32)[None, :]).astype(
        jnp.float32
    )


def relative_bias(table, offset_gap, query_rows, key_rows):
    head_count = table.shape[0]
    band_len = query_rows + key_rows + 1
    band = jnp.dot(
        table, band_pick(offset_gap, query_rows, key_rows, table.shape[1]).T, precision=highest
    )
    tiled = jnp.broadcast_to(band[:, None, :], (head_count, query_rows, band_len)).reshape(
        head_count, query_rows * band_len
    )
    skewed = tiled[:, : query_rows * (band_len - 1)].reshape(head_count, query_rows, band_len - 1)
    return skewed[:, :, query_rows : query_rows + key_rows]


def table_terms(score_grads, offset_gap, table_span):
    head_count, query_rows, key_rows = score_grads.shape
    band_len = query_rows + key_rows + 1
    placed = jnp.pad(score_grads.astype(jnp.float32), ((0, 0), (0, 0), (query_rows, 0)))
    flat = jnp.pad(
        placed.reshape(head_count, query_rows * (band_len - 1)), ((0, 0), (0, query_rows))
    )
    diagonal_sums = jnp.sum(flat.reshape(head_count, query_rows, band_len), axis=1)
    return jnp.dot(
        diagonal_sums, band_pick(offset_gap, query_rows, key_rows, table_span), precision=highest
    )


def self_scores(queries, query_start, keys_part, key_start, doc_ends, table):
    query_rows = queries.shape[0]
    key_rows = keys_part.shape[0]
    query_pos = query_start + jnp.arange(query_rows, dtype=jnp.int32)
    key_pos = key_start + jnp.arange(key_rows, dtype=jnp.int32)
    offset_gap = query_start - key_start
    raw_scores = (
        jnp.einsum(
            "qhd,khd->hqk",
            split_heads(queries),
            split_heads(keys_part),
            preferred_element_type=jnp.float32,
        )
        * 0.125
    )
    allowed = (key_pos[None, :] <= query_pos[:, None]) & (
        doc_index(key_pos, doc_ends)[None, :] == doc_index(query_pos, doc_ends)[:, None]
    )
    scores = jnp.where(
        allowed[None],
        raw_scores + relative_bias(table, offset_gap, query_rows, key_rows),
        masked_out,
    )
    return (scores, allowed[None], offset_gap)


def over_blocks(step, running, pieces):
    rows_total = pieces[0].shape[0]
    block_rows = math.gcd(rows_total, 512)
    block_count = rows_total // block_rows
    stacked = tuple(
        (member.reshape(block_count, block_rows, *member.shape[1:]) for member in pieces)
    )

    def scan_step(inner_running, block_input):
        block_id, members = block_input
        return (step(inner_running, members, block_id * block_rows), None)

    result, ignored = lax.scan(
        scan_step, running, (jnp.arange(block_count, dtype=jnp.int32), stacked)
    )
    return result


def streamed(
    inputs,
    encoder,
    lengths,
    buckets,
    routes,
    norm_gains,
    self_qkv,
    self_out,
    cross_q,
    cross_kv,
    cross_out,
    rel_bias,
    router,
    expert_in,
    expert_out,
    cotangent,
):
    hidden = inputs[0].astype(jnp.float32)
    rows_dev = hidden.shape[0]
    model_width = hidden.shape[1]
    seq_count = lax.axis_size("seq")
    seq_index = lax.axis_index("seq")
    own_start = seq_index * rows_dev
    doc_ends = jnp.cumsum(lengths[0])
    bucket_pick = (
        buckets[:, None] == jnp.arange(rel_bias.shape[0], dtype=jnp.int32)[None, :]
    ).astype(jnp.float32)
    table = jnp.dot(bucket_pick, rel_bias, precision=highest).T
    normed_one, norm_one_back = jax.vjp(rms_norm, hidden, norm_gains[0])
    normed_one = normed_one.astype(jnp.bfloat16)
    qkv_all = jnp.dot(normed_one, self_qkv, preferred_element_type=jnp.float32).astype(jnp.bfloat16)
    queries = qkv_all[:, :model_width]
    keys_own = qkv_all[:, model_width : 2 * model_width]
    values_own = qkv_all[:, 2 * model_width :]

    def forward_step(running, pieces, key_start):
        top_old, denominator, summed = running
        keys_part, values_part = pieces
        scores, allowed, offset_gap = self_scores(
            queries, own_start, keys_part, key_start, doc_ends, table
        )
        top_new = jnp.maximum(top_old, jnp.max(scores, axis=-1))
        weights_raw = jnp.where(allowed, jnp.exp(scores - top_new[..., None]), 0.0)
        rescale = jnp.exp(top_old - top_new)
        denominator = denominator * rescale + jnp.sum(weights_raw, axis=-1)
        summed = summed * rescale[..., None] + jnp.einsum(
            "hqk,khd->hqd",
            weights_raw.astype(jnp.bfloat16),
            split_heads(values_part),
            preferred_element_type=jnp.float32,
        )
        return (top_new, denominator, summed)

    start_state = (
        jnp.full((H, rows_dev), masked_out, jnp.float32),
        jnp.zeros((H, rows_dev), jnp.float32),
        jnp.zeros((H, rows_dev, HD), jnp.float32),
    )
    top_score, denominator, summed = over_blocks(
        forward_step,
        start_state,
        (
            lax.all_gather(keys_own, "seq", axis=0, tiled=True),
            lax.all_gather(values_own, "seq", axis=0, tiled=True),
        ),
    )
    log_total = top_score + jnp.log(denominator)
    attended_full = (
        (summed / denominator[..., None]).transpose(1, 0, 2).reshape(rows_dev, model_width)
    )
    attended = attended_full.astype(jnp.bfloat16)
    after_self = hidden + jnp.dot(attended, self_out, preferred_element_type=jnp.float32)
    enc_kv = jnp.dot(encoder, cross_kv, preferred_element_type=jnp.float32).astype(jnp.bfloat16)
    cross_keys = split_heads(enc_kv[:, :model_width])
    cross_values = split_heads(enc_kv[:, model_width:])
    normed_two, norm_two_back = jax.vjp(rms_norm, after_self, norm_gains[1])
    normed_two = normed_two.astype(jnp.bfloat16)
    cross_queries = jnp.dot(normed_two, cross_q, preferred_element_type=jnp.float32).astype(
        jnp.bfloat16
    )
    cross_scores = (
        jnp.einsum(
            "qhd,khd->hqk",
            split_heads(cross_queries),
            cross_keys,
            preferred_element_type=jnp.float32,
        )
        * 0.125
    )
    cross_raw = jnp.exp(cross_scores - jnp.max(cross_scores, axis=-1, keepdims=True))
    cross_prob = cross_raw / jnp.sum(cross_raw, axis=-1, keepdims=True)
    cross_prob_low = cross_prob.astype(jnp.bfloat16)
    cross_att = (
        jnp.einsum("hqk,khd->qhd", cross_prob_low, cross_values, preferred_element_type=jnp.float32)
        .reshape(rows_dev, model_width)
        .astype(jnp.bfloat16)
    )
    after_cross = after_self + jnp.dot(cross_att, cross_out, preferred_element_type=jnp.float32)
    normed_three, norm_three_back = jax.vjp(rms_norm, after_cross, norm_gains[2])
    routed_in = normed_three.astype(jnp.bfloat16)
    gates = jax.nn.softmax(jnp.dot(routed_in, router, preferred_element_type=jnp.float32), axis=-1)
    expert_total = router.shape[1]
    local_experts = expert_in.shape[0]
    capacity = 5 * rows_dev // (4 * expert_total)
    route_ids = routes[0, :, 0]
    chosen = route_ids[:, None] == jnp.arange(expert_total, dtype=jnp.int32)[None, :]
    slots = jnp.sum(jnp.where(chosen, jnp.cumsum(chosen.astype(jnp.int32), axis=0), 0), axis=1) - 1
    kept = slots < capacity
    picked_gate = jnp.sum(jnp.where(chosen, gates, 0.0), axis=1)
    gate_used = picked_gate * kept.astype(jnp.float32)
    target = jnp.where(kept, route_ids * capacity + slots, -1)
    dispatch = (
        jnp.arange(expert_total * capacity, dtype=jnp.int32)[:, None] == target[None, :]
    ).astype(jnp.bfloat16)
    outgoing = (
        jnp.dot(dispatch, routed_in, preferred_element_type=jnp.float32)
        .astype(jnp.bfloat16)
        .reshape(expert_total, capacity, model_width)
    )
    arrived = lax.all_to_all(outgoing, "exp", split_axis=0, concat_axis=0, tiled=True).reshape(
        -1, local_experts, capacity, model_width
    )
    inner_pre = jnp.einsum("secd,edf->secf", arrived, expert_in, preferred_element_type=jnp.float32)
    active = jax.nn.gelu(inner_pre, approximate=True).astype(jnp.bfloat16)
    produced = jnp.einsum(
        "secf,efd->secd", active, expert_out, preferred_element_type=jnp.float32
    ).astype(jnp.bfloat16)
    returned = lax.all_to_all(
        produced.reshape(-1, capacity, model_width), "exp", split_axis=0, concat_axis=0, tiled=True
    )
    expert_rows = jnp.dot(
        dispatch.T, returned.reshape(-1, model_width), preferred_element_type=jnp.float32
    )
    layer_out = after_cross + gate_used[:, None] * expert_rows
    upstream = cotangent[0].astype(jnp.float32)
    made_grad = (upstream * gate_used[:, None]).astype(jnp.bfloat16)
    sent_grad = (
        jnp.dot(dispatch, made_grad, preferred_element_type=jnp.float32)
        .astype(jnp.bfloat16)
        .reshape(expert_total, capacity, model_width)
    )
    grad_arrived = lax.all_to_all(
        sent_grad, "exp", split_axis=0, concat_axis=0, tiled=True
    ).reshape(-1, local_experts, capacity, model_width)
    inner_again = jnp.einsum(
        "secd,edf->secf", arrived, expert_in, preferred_element_type=jnp.float32
    )
    active_again, gelu_back = jax.vjp(
        lambda value: jax.nn.gelu(value, approximate=True), inner_again
    )
    grad_out_w = jnp.einsum(
        "secf,secd->efd",
        active_again.astype(jnp.bfloat16),
        grad_arrived,
        preferred_element_type=jnp.float32,
    )
    grad_active = jnp.einsum(
        "secd,efd->secf", grad_arrived, expert_out, preferred_element_type=jnp.float32
    )
    grad_inner = gelu_back(grad_active)[0].astype(jnp.bfloat16)
    grad_in_w = jnp.einsum(
        "secd,secf->edf", arrived, grad_inner, preferred_element_type=jnp.float32
    )
    grad_sent_x = jnp.einsum(
        "secf,edf->secd", grad_inner, expert_in, preferred_element_type=jnp.float32
    ).astype(jnp.bfloat16)
    grad_back = lax.all_to_all(
        grad_sent_x.reshape(-1, capacity, model_width),
        "exp",
        split_axis=0,
        concat_axis=0,
        tiled=True,
    )
    grad_routed = jnp.dot(
        dispatch.T, grad_back.reshape(-1, model_width), preferred_element_type=jnp.float32
    )
    expert_sums = (
        lax.psum_scatter(grad_in_w, "seq", scatter_dimension=1, tiled=True),
        lax.psum_scatter(grad_out_w, "seq", scatter_dimension=1, tiled=True),
    )
    gate_grad = jnp.sum(upstream * expert_rows, axis=1) * kept.astype(jnp.float32)
    logit_grad = gates * (
        jnp.where(chosen, gate_grad[:, None], 0.0) - (picked_gate * gate_grad)[:, None]
    )
    router_grad = jnp.dot(routed_in.astype(jnp.float32).T, logit_grad, precision=highest)
    grad_normed_three = (
        jnp.dot(logit_grad, router.astype(jnp.float32).T, precision=highest) + grad_routed
    )
    grad_after_cross, gain_three = norm_three_back(grad_normed_three)
    grad_after_cross = grad_after_cross + upstream
    cross_branch = grad_after_cross.astype(jnp.bfloat16)
    cross_out_grad = jnp.dot(cross_att.T, cross_branch, preferred_element_type=jnp.float32)
    grad_cross_att = split_heads(
        jnp.dot(cross_branch, cross_out.T, preferred_element_type=jnp.float32).astype(jnp.bfloat16)
    )
    cross_prob_grad = jnp.einsum(
        "qhd,khd->hqk", grad_cross_att, cross_values, preferred_element_type=jnp.float32
    )
    cross_delta = jnp.sum(cross_prob * cross_prob_grad, axis=-1, keepdims=True)
    cross_score_grad = (cross_prob * (cross_prob_grad - cross_delta)).astype(jnp.bfloat16)
    grad_cross_queries = (
        (
            jnp.einsum(
                "hqk,khd->qhd", cross_score_grad, cross_keys, preferred_element_type=jnp.float32
            )
            * 0.125
        )
        .reshape(rows_dev, model_width)
        .astype(jnp.bfloat16)
    )
    grad_enc_keys = (
        jnp.einsum(
            "hqk,qhd->khd",
            cross_score_grad,
            split_heads(cross_queries),
            preferred_element_type=jnp.float32,
        )
        * 0.125
    )
    grad_enc_values = jnp.einsum(
        "hqk,qhd->khd", cross_prob_low, grad_cross_att, preferred_element_type=jnp.float32
    )
    enc_terms = jnp.concatenate(
        [grad_enc_keys.reshape(-1, model_width), grad_enc_values.reshape(-1, model_width)], axis=1
    )
    enc_grad_rows = lax.psum_scatter(
        enc_terms, ("seq", "exp"), scatter_dimension=0, tiled=True
    ).astype(jnp.bfloat16)
    enc_count = enc_grad_rows.shape[0]
    flat_index = seq_index * lax.axis_size("exp") + lax.axis_index("exp")
    own_enc = lax.dynamic_slice_in_dim(encoder, flat_index * enc_count, enc_count, 0)
    grad_encoder = jnp.dot(enc_grad_rows, cross_kv.T, preferred_element_type=jnp.float32)
    pair_grad = jnp.dot(own_enc.T, enc_grad_rows, preferred_element_type=jnp.float32)
    query_w_grad = jnp.dot(normed_two.T, grad_cross_queries, preferred_element_type=jnp.float32)
    grad_normed_two = jnp.dot(grad_cross_queries, cross_q.T, preferred_element_type=jnp.float32)
    grad_after_self, gain_two = norm_two_back(grad_normed_two)
    grad_after_self = grad_after_self + grad_after_cross
    self_branch = grad_after_self.astype(jnp.bfloat16)
    self_out_grad = jnp.dot(attended.T, self_branch, preferred_element_type=jnp.float32)
    grad_attended = jnp.dot(self_branch, self_out.T, preferred_element_type=jnp.float32).astype(
        jnp.bfloat16
    )
    row_delta = jnp.sum(
        split_heads(grad_attended).astype(jnp.float32) * split_heads(attended_full), axis=-1
    ).T
    stats_all = (
        lax.all_gather(log_total.T, "seq", axis=0, tiled=True),
        lax.all_gather(row_delta.T, "seq", axis=0, tiled=True),
    )

    def query_step(running, pieces, query_start):
        kv_grad, query_grads, table_grad = running
        queries_part, grads_part = pieces
        piece_rows = queries_part.shape[0]
        lse_part = lax.dynamic_slice_in_dim(stats_all[0], query_start, piece_rows, 0).T
        delta_part = lax.dynamic_slice_in_dim(stats_all[1], query_start, piece_rows, 0).T
        scores, allowed, offset_gap = self_scores(
            queries_part, query_start, keys_own, own_start, doc_ends, table
        )
        probability = jnp.where(allowed, jnp.exp(scores - lse_part[..., None]), 0.0)
        prob_grad = jnp.einsum(
            "qhd,khd->hqk",
            split_heads(grads_part),
            split_heads(values_own),
            preferred_element_type=jnp.float32,
        )
        score_grad = (probability * (prob_grad - delta_part[..., None])).astype(jnp.bfloat16)
        key_grad = (
            jnp.einsum(
                "hqk,qhd->khd",
                score_grad,
                split_heads(queries_part),
                preferred_element_type=jnp.float32,
            )
            * 0.125
        )
        value_grad = jnp.einsum(
            "hqk,qhd->khd",
            probability.astype(jnp.bfloat16),
            split_heads(grads_part),
            preferred_element_type=jnp.float32,
        )
        kv_grad = kv_grad + jnp.concatenate(
            [key_grad.reshape(-1, model_width), value_grad.reshape(-1, model_width)], axis=1
        )
        table_grad = table_grad + table_terms(score_grad, offset_gap, table.shape[1])
        query_part_grad = jnp.einsum(
            "hqk,khd->qhd", score_grad, split_heads(keys_own), preferred_element_type=jnp.float32
        ).reshape(piece_rows, model_width)
        current = lax.dynamic_slice_in_dim(query_grads, query_start, piece_rows, 0)
        query_grads = lax.dynamic_update_slice_in_dim(
            query_grads, current + query_part_grad, query_start, 0
        )
        return (kv_grad, query_grads, table_grad)

    back_start = (
        jnp.zeros((rows_dev, 2 * model_width), jnp.float32),
        jnp.zeros((seq_count * rows_dev, model_width), jnp.float32),
        jnp.zeros(table.shape, jnp.float32),
    )
    kv_grad, query_buffer, table_grad = over_blocks(
        query_step,
        back_start,
        (
            lax.all_gather(queries, "seq", axis=0, tiled=True),
            lax.all_gather(grad_attended, "seq", axis=0, tiled=True),
        ),
    )
    query_grad = lax.psum_scatter(query_buffer, "seq", scatter_dimension=0, tiled=True)
    qkv_grad = jnp.concatenate(
        [(query_grad * 0.125).astype(jnp.bfloat16), kv_grad.astype(jnp.bfloat16)], axis=1
    )
    qkv_w_grad = jnp.dot(normed_one.T, qkv_grad, preferred_element_type=jnp.float32)
    grad_normed_one = jnp.dot(qkv_grad, self_qkv.T, preferred_element_type=jnp.float32)
    grad_hidden, gain_one = norm_one_back(grad_normed_one)
    grad_input = grad_hidden + grad_after_self
    rel_grad = jnp.dot(bucket_pick.T, table_grad.T, precision=highest)
    summed_grads = lax.psum(
        (
            jnp.stack([gain_one, gain_two, gain_three]),
            qkv_w_grad,
            self_out_grad,
            query_w_grad,
            pair_grad,
            cross_out_grad,
            rel_grad,
            router_grad,
        ),
        ("seq", "exp"),
    )
    return (
        layer_out.astype(jnp.bfloat16)[None],
        grad_input[None],
        grad_encoder,
        summed_grads[0],
        summed_grads[1],
        summed_grads[2],
        summed_grads[3],
        summed_grads[4],
        summed_grads[5],
        summed_grads[6],
        summed_grads[7],
        expert_sums[0],
        expert_sums[1],
    )


F32 = jnp.float32
BF16 = jnp.bfloat16
MESH = pl.DeviceIdType.MESH
ANY = pl.BlockSpec(memory_space=pl.ANY)
VMEM = pl.BlockSpec(memory_space=pltpu.VMEM)
SMEM = pl.BlockSpec(memory_space=pltpu.SMEM)
LANES = 128


def nn(a, b):
    return lax.dot_general(a, b, (((1,), (0,)), ((), ())), preferred_element_type=F32)


def nt(a, b):
    return lax.dot_general(a, b, (((1,), (1,)), ((), ())), preferred_element_type=F32)


def tn(a, b):
    return lax.dot_general(a, b, (((0,), (0,)), ((), ())), preferred_element_type=F32)


def rms_scale(a):
    return lax.rsqrt(jnp.mean(a * a, axis=-1, keepdims=True) + epsilon)


def pair_lanes(p):
    return pl.ds(pl.multiple_of(p * LANES, LANES), LANES)


def block_of(index, size):
    return pl.ds(pl.multiple_of(index * size, size), size)


def head_stack(pair):
    lane = lax.broadcasted_iota(jnp.int32, pair.shape, 1)
    zero = jnp.zeros_like(pair)
    return jnp.concatenate([jnp.where(lane < HD, pair, zero), jnp.where(lane < HD, zero, pair)], axis=0)


def head_unstack(both, rows):
    feature = lax.broadcasted_iota(jnp.int32, (both.shape[0], rows), 0)
    return jnp.where(feature < HD, both[:, :rows], both[:, rows:]).T


def pack_slots(value, experts):
    slots = value.shape[0] // experts
    blocks = value.shape[1] // LANES
    return jnp.stack([
        jnp.concatenate(
            [value[e * slots : (e + 1) * slots, b * LANES : (b + 1) * LANES] for b in range(blocks)], axis=0
        )
        for e in range(experts)
    ])


def unpack_slots(packed, slots):
    experts, blocks = packed.shape[0], packed.shape[1] // slots
    wide = packed.astype(F32)
    return jnp.concatenate(
        [
            jnp.concatenate([wide[e, b * slots : (b + 1) * slots] for e in range(experts)], axis=0)
            for b in range(blocks)
        ],
        axis=1,
    )


class Place:
    def __init__(self):
        self.me = lax.axis_index("seq")
        self.core = lax.rem(self.me, 2)
        self.chip = lax.div(self.me, 2)
        self.partner = self.me + 1 - 2 * self.core
        self.x_chip = self.chip + 1 - 2 * lax.rem(self.chip, 2)
        self.y_chip = lax.rem(self.chip + 2, 4)
        self.far_chip = 3 - self.chip
        self.x, self.y, self.far = (c * 2 + self.core for c in (self.x_chip, self.y_chip, self.far_chip))


def enter(devices):
    barrier = pltpu.get_barrier_semaphore()
    for device in devices:
        pl.semaphore_signal(barrier, inc=1, device_id=device, device_id_type=MESH)
    pl.semaphore_wait(barrier, len(devices))


def remote(src, dst, send_sem, recv_sem, device):
    return pltpu.make_async_remote_copy(
        src_ref=src, dst_ref=dst, send_sem=send_sem, recv_sem=recv_sem, device_id=device, device_id_type=MESH
    )


def wait_bytes(sized, sem):
    pltpu.make_async_copy(sized, sized, sem).wait()


class Gather:
    def __init__(self, place, every, rows, send_sem, recv_sems, staged=False):
        self.place, self.every, self.send_sem, self.recv_sems, self.staged = place, every, send_sem, recv_sems, staged
        half = rows // 2 if rows < 32 else -(-rows // 32) * 16
        self.halves = pl.ds(0, half), pl.ds(half, rows - half)

    def copy(self, slot):
        place, every = self.place, self.every
        block, device, sem = (
            lambda: (every.at[place.me], place.partner, 3),
            lambda: (every.at[place.me], place.x, 0),
            lambda: (every.at[place.me], place.y, 1),
            lambda: (every.at[place.x, self.halves[0]], place.y, 2),
            lambda: (every.at[place.y, self.halves[1]], place.x, 2),
            lambda: (every.at[place.x], place.partner, 4 if self.staged else 3),
            lambda: (every.at[place.y], place.partner, 4 if self.staged else 3),
            lambda: (every.at[place.far], place.partner, 5 if self.staged else 3),
        )[slot]()
        return remote(block, block, self.send_sem, self.recv_sems.at[sem], {"seq": device})

    def send(self, *slots):
        for slot in slots:
            self.copy(slot).start()

    def arrived(self, blocks, sem):
        wait_bytes(self.every.at[pl.ds(0, blocks)], self.recv_sems.at[sem])

    def start(self):
        self.send(1, 2, 0)

    def relay(self):
        self.arrived(1, 0)
        self.send(3)
        self.arrived(1, 1)
        self.send(4, 5, 6)

    def relay_far(self):
        self.arrived(1, 2)
        self.send(7)

    def finish(self):
        self.arrived(4, 3)

    def drain(self):
        wait_bytes(self.every.at[pl.ds(0, 7)], self.send_sem)


class Scatter:
    def __init__(self, place, out, pair, turn, side, half, sems):
        self.place, self.out, self.pair, self.turn, self.side, self.half, self.sems = place, out, pair, turn, side, half, sems

    def pair_copy(self):
        return remote(self.out.at[1 - self.place.core], self.pair, self.sems.at[0], self.sems.at[2], {"seq": self.place.partner})

    def send_round(self, src, dst, recv, device):
        remote(src, dst, self.sems.at[1], self.sems.at[recv], {"seq": device}).start()

    def start(self):
        self.pair_copy().start()

    def turn_on(self):
        place = self.place
        self.pair_copy().wait_recv()
        self.out[place.core] = (self.out[place.core].astype(F32) + self.pair[...].astype(F32)).astype(BF16)
        far = self.out.at[place.core, place.far_chip]
        self.send_round(far.at[pl.ds(0, self.half)], self.turn.at[0], 3, place.x)
        self.send_round(far.at[pl.ds(self.half, self.half)], self.turn.at[1], 3, place.y)

    def side_on(self):
        place = self.place
        first, second = pl.ds(0, self.half), pl.ds(self.half, self.half)
        wait_bytes(self.turn, self.sems.at[3])
        at = (place.core, place.y_chip, first)
        self.out[at] = (self.out[at].astype(F32) + self.turn[0].astype(F32)).astype(BF16)
        at = (place.core, place.x_chip, second)
        self.out[at] = (self.out[at].astype(F32) + self.turn[1].astype(F32)).astype(BF16)
        self.send_round(self.out.at[place.core, place.x_chip], self.side.at[0], 4, place.x)
        self.send_round(self.out.at[place.core, place.y_chip], self.side.at[1], 4, place.y)

    def total(self):
        wait_bytes(self.side, self.sems.at[4])
        own = self.out[self.place.core, self.place.chip].astype(F32)
        return own + self.side[0].astype(F32) + self.side[1].astype(F32)

    def drain(self):
        self.pair_copy().wait_send()
        wait_bytes(self.out.at[0, pl.ds(0, 3)], self.sems.at[1])


def expert_peers(exp_index, experts):
    return [lax.rem(exp_index + d, experts) for d in range(1, experts)]


def gelu_parts(hid):
    root, cubic = 0.7978845608028654, 0.044715
    square = hid * hid
    bent = jnp.tanh(root * hid * (1.0 + cubic * square))
    half = 0.5 * (1.0 + bent)
    return hid * half, half + 0.5 * hid * (1.0 - bent * bent) * (root + 3.0 * root * cubic * square)


def rms_back(a, gain, grad):
    scale = rms_scale(a)
    weighted = grad * gain
    da = scale * weighted - a * (scale * scale * scale * jnp.mean(a * weighted, axis=-1, keepdims=True))
    return da, jnp.sum(grad * (a * scale), axis=0, keepdims=True)


def in_two(value):
    high = value.astype(BF16)
    return high, (value - high.astype(F32)).astype(BF16)


GATE_ROWS = 16


def in_three(value):
    high = value.astype(BF16)
    rest = value - high.astype(F32)
    middle = rest.astype(BF16)
    low = (rest - middle.astype(F32)).astype(BF16)
    lane = lax.broadcasted_iota(jnp.int32, (value.shape[0], GATE_ROWS), 1)
    zero = jnp.zeros((value.shape[0], GATE_ROWS), BF16)
    return jnp.where(lane == 0, high, jnp.where(lane == 1, middle, jnp.where(lane == 2, low, zero)))


def slot_gates(parts):
    return jnp.sum(parts, axis=0, keepdims=True).T


class Chunk:
    def __init__(self, place, quarters, peers, src, slots, own, every, sems, gather_sems, local_sem):
        self.place, self.quarters, self.peers = place, quarters, peers
        self.src, self.slots, self.own, self.every, self.sems, self.local_sem = src, slots, own, every, sems, local_sem
        self.over_seq = Gather(place, every, src.shape[0], *gather_sems)

    def local_copy(self):
        return pltpu.make_async_copy(self.own, self.every.at[(self.place.me,) + self.quarters[0]], self.local_sem)

    def over_exp(self, value):
        self.src[...] = value.astype(BF16)
        for d, peer in enumerate(self.peers):
            remote(
                self.src.at[self.quarters[1 + d]], self.slots.at[d], self.sems.at[0], self.sems.at[1], {"exp": peer}
            ).start()

    def back_over_exp(self):
        total = self.src[self.quarters[0]].astype(F32)
        wait_bytes(self.slots, self.sems.at[1])
        for d in range(len(self.peers)):
            total = total + self.slots[d].astype(F32)
        self.own[...] = total.astype(BF16)
        self.local_copy().start()
        target = self.every.at[(self.place.me,) + self.quarters[0]]
        for peer in self.peers:
            remote(self.own, target, self.sems.at[2], self.sems.at[3], {"exp": peer}).start()

    def spread(self):
        self.local_copy().wait()
        wait_bytes(self.slots, self.sems.at[3])
        self.over_seq.start()

    def drain(self):
        wait_bytes(self.slots, self.sems.at[0])
        wait_bytes(self.slots, self.sems.at[2])
        self.over_seq.drain()


def layer_kernel(
    seq_count, capacity,
    x_ref, encoder_hbm, lengths_ref, buckets_ref, routes_ref, gains_ref, qkv_hbm, so_hbm, cq_hbm, ckv_hbm, co_hbm, rel_ref,
    router_ref, g_ref, in_hbm, out_hbm,
    out_hbm_ref, dx_hbm, weights_hbm, dekv_hbm, small_hbm, gin_hbm, gout_hbm, genc_hbm,
    left, kv_all, prob, cross_prob, ekv, w_qkv, w_so, w_cq, w_ckv, w_co, table_ref, x_all, g_all, x_in, g_in, made_back, dx_back,
    q_ref, qc_ref, x3_ref, r1_ref, r2_ref, gates_ref, chosen_ref, slots_ref,
    dr_ref, doc_ref, dqc_ref, dqkv_ref, diag_ref, total_ref,
    e_pair, e_turn, e_side, e_mine, e_exp, dekv, t_pair, t_turn, t_side,
    out_ref, dx_ref, gout_ref, genc_ref, small_out_ref, c_slots, c_own, right, gin_in, small_a, small_b, small_c, small_pair, small_chip, small_exp,
    load_sem, local_sem, store_sem, n_recv, gather_send, gather_recv, trip_sem, enc_sem, enc_exp_sem, term_sem, chunk_sem,
    chunk_send, chunk_recv, right_sem, unit_send, unit_recv, small_sem,
):
    rows, width = x_ref.shape
    span = seq_count * rows
    pairs = width // LANES
    enc_rows = encoder_hbm.shape[0]
    hidden = in_hbm.shape[1]
    own_hidden = hidden // seq_count
    place = Place()
    me = place.me
    mine = lax.axis_index("exp")
    experts = router_ref.shape[0]
    slot_rows = experts * capacity
    peers = expert_peers(mine, experts)
    everyone = [lax.rem(me + d, seq_count) for d in range(1, seq_count)]
    part = width // seq_count
    half_rows, half_lanes = part // 2, width // (experts // 2)
    quarters = [
        (block_of(lax.div(e, experts // 2), half_rows), block_of(lax.rem(e, experts // 2), half_lanes)) for e in [mine] + peers
    ]
    own_lanes = block_of(me, rows)
    near = pl.ds(pl.multiple_of(me * rows, rows), 2 * rows)
    gather = Gather(place, left.at[3], rows, gather_send.at[0], n_recv, staged=True)
    o_gather, n2_gather, oc_gather = (
        Gather(place, left.at[i], rows, gather_send.at[1 + i], gather_recv.at[i]) for i in range(3)
    )
    x_gather = Gather(place, x_all, x_all.shape[1], gather_send.at[4], gather_recv.at[3])
    g_gather = Gather(place, g_all, slot_rows, gather_send.at[5], gather_recv.at[4])

    def load(i, src, dst):
        return pltpu.make_async_copy(src, dst, load_sem.at[i])

    stores = []

    def store(src, dst):
        copy = pltpu.make_async_copy(src, dst, store_sem.at[len(stores)])
        copy.start()
        stores.append(copy)

    def over_exp(src, dst, sems):
        for peer in peers:
            remote(src.at[peer], dst.at[mine], sems.at[0], sems.at[1], {"exp": peer}).start()
        dst[mine] = src[mine]

    def arrive(src, dst, sems):
        wait_bytes(src.at[pl.ds(0, experts - 1)], sems.at[1])

    def sent(src, dst, sems):
        wait_bytes(src.at[pl.ds(0, experts - 1)], sems.at[0])

    load_qkv, load_ckv = load(0, qkv_hbm, w_qkv), load(1, ckv_hbm, w_ckv)
    load_so, load_cq, load_co = load(3, so_hbm, w_so), load(4, cq_hbm, w_cq), load(5, co_hbm, w_co)
    load_qkv.start()
    load_ckv.start()

    def own_slots(e):
        of_all = lax.broadcasted_iota(jnp.int32, (slot_rows, LANES), 0) - e * capacity
        lane = lax.broadcasted_iota(jnp.int32, (slot_rows, LANES), 1)
        return ((of_all == lane) & (lane < capacity)).astype(BF16)

    def self_attention(scores, mask, enc, gs_ref):
        load_enc = load(2, encoder_hbm, enc)
        load_enc.start()
        x = x_ref[...].astype(F32)
        left[3, me] = (x * rms_scale(x) * gains_ref[0:1, :]).astype(BF16)
        enter([{"seq": device} for device in everyone] + [{"exp": peer} for peer in peers])
        gather.start()

        def project(chip):
            both = left[3, pl.ds(chip * 2, 2)].reshape(2 * rows, width)
            kv_all[block_of(chip, 2 * rows), :] = nn(both, w_qkv[:, width:]).astype(BF16)

        chosen = (routes_ref[...] == lax.broadcasted_iota(jnp.int32, (LANES, rows), 0)).astype(F32).T[:, :experts]
        chosen_ref[...] = chosen
        earlier = (
            lax.broadcasted_iota(jnp.int32, (rows, rows), 1) < lax.broadcasted_iota(jnp.int32, (rows, rows), 0)
        ).astype(BF16)
        slot = jnp.sum(nn(earlier, chosen.astype(BF16)) * chosen, axis=1, keepdims=True).astype(jnp.int32)
        kept = slot < capacity
        expert = lax.broadcasted_iota(jnp.int32, (rows, experts), 1).astype(F32)
        route = jnp.sum(chosen * expert, axis=1, keepdims=True).astype(jnp.int32)
        target = jnp.where(kept, route * capacity + slot, -1)
        slots = (lax.broadcasted_iota(jnp.int32, (rows, slot_rows), 1) == target).astype(BF16)
        slots_ref[...] = slots
        gs_ref[...] = pack_slots(tn(slots, g_ref[...]), experts).astype(BF16)
        g_trip = (gs_ref, g_in, trip_sem.at[0])
        over_exp(*g_trip)

        load_qkv.wait()
        q_ref[...] = nn(left[3, me], w_qkv[:, :width]).astype(BF16) * jnp.asarray(0.125, BF16)
        gather.arrived(1, 3)
        project(place.chip)
        load_so.start()
        load_cq.start()
        load_co.start()
        load_ckv.wait()
        load_enc.wait()
        ekv[...] = nn(enc[...], w_ckv[...]).astype(BF16)
        gather.relay()
        pick = (buckets_ref[...] == lax.broadcasted_iota(jnp.int32, (rel_ref.shape[1], LANES), 0)).astype(F32)
        table = jnp.dot(rel_ref[...], pick, precision=highest, preferred_element_type=F32)
        table = table - table[:, LANES - 1 :]
        table_ref[...] = jnp.concatenate([jnp.zeros_like(table), table], axis=1)
        query_pos = me * rows + lax.broadcasted_iota(jnp.int32, (1, rows), 1)
        start = jnp.zeros((1, rows), jnp.int32)
        end = jnp.int32(0)
        for i in range(lengths_ref.shape[1]):
            end = end + lengths_ref[0, i]
            start = jnp.where(end <= query_pos, end, start)
        key_pos = lax.broadcasted_iota(jnp.int32, (span, rows), 0)
        seen = jnp.where((key_pos >= start) & (key_pos <= query_pos), 0.0, masked_out)
        mask[...] = jnp.concatenate([seen, seen], axis=1)
        gather.arrived(2, 4)
        project(place.x_chip)
        project(place.y_chip)
        gather.relay_far()
        arrive(*g_trip)
        g_all[me] = unpack_slots(g_in[...], capacity).astype(BF16)
        g_gather.start()
        gather.arrived(1, 5)
        project(place.far_chip)

        @pl.loop(0, pairs)
        def _(p):
            lanes = pair_lanes(p)
            q_both = head_stack(q_ref[:, lanes])
            scores[pl.ds(rows, span), :] = nt(kv_all[:, lanes], q_both) + mask[...]
            biases = []
            for h in range(2):
                band = jnp.broadcast_to(table_ref[pl.ds(2 * p + h, 1), :], (2 * rows, 2 * LANES))
                biases.append(pltpu.roll(band, 0, 1, stride=1, stride_axis=0)[:, :rows])
            scores[near, :] = scores[near, :] + jnp.concatenate(biases, axis=1)
            s = scores[pl.ds(rows, span), :]
            weights = jnp.exp(s - jnp.max(s, axis=0, keepdims=True))
            weights = (weights * (1.0 / jnp.sum(weights, axis=0, keepdims=True))).astype(BF16)
            prob[p] = weights
            both = tn(kv_all[:, pair_lanes(pairs + p)], weights)
            left[0, me, :, lanes] = head_unstack(both, rows).astype(BF16)

        sent(*g_trip)

    def rest_forward(xs_ref, made_out, dx_out, slope, w_in, w_out):
        load_in, load_out = load(6, in_hbm, w_in), load(7, out_hbm, w_out)
        load_in.start()
        load_out.start()
        o_gather.start()
        g_gather.relay()
        load_so.wait()
        load_cq.wait()
        load_co.wait()
        r1 = x_ref[...].astype(F32) + nn(left[0, me], w_so[...])
        r1_ref[...] = r1
        n2 = (r1 * rms_scale(r1) * gains_ref[1:2, :]).astype(BF16)
        left[1, me] = n2
        n2_gather.start()
        qc_ref[...] = nn(n2, w_cq[...]).astype(BF16) * jnp.asarray(0.125, BF16)

        @pl.loop(0, pairs)
        def _(p):
            lanes = pair_lanes(p)
            s = nt(ekv[:, lanes], head_stack(qc_ref[:, lanes]))
            weights = jnp.exp(s - jnp.max(s, axis=0, keepdims=True))
            weights = (weights * (1.0 / jnp.sum(weights, axis=0, keepdims=True))).astype(BF16)
            cross_prob[p] = weights
            both = tn(ekv[:, pair_lanes(pairs + p)], weights)
            left[2, me, :, lanes] = head_unstack(both, rows).astype(BF16)

        oc_gather.start()
        r2 = r1_ref[...] + nn(left[2, me], w_co[...])
        r2_ref[...] = r2
        x3 = (r2 * rms_scale(r2) * gains_ref[2:3, :]).astype(BF16)
        x3_ref[...] = x3
        logits = nt(x3, router_ref[...])
        top = jnp.exp(logits - jnp.max(logits, axis=-1, keepdims=True))
        gates = top / jnp.sum(top, axis=-1, keepdims=True)
        gates_ref[...] = gates
        chosen, slots = chosen_ref[...], slots_ref[...]
        kept = jnp.sum(slots.astype(F32), axis=1, keepdims=True)
        gate_used = jnp.sum(gates * chosen, axis=1, keepdims=True) * kept
        packed_rows = x_in.shape[1] - GATE_ROWS
        xs_ref[:, :packed_rows, :] = pack_slots(tn(slots, x3), experts).astype(BF16)
        by_slot = tn(in_three(gate_used), slots).astype(BF16)
        for e in range(experts):
            xs_ref[e, packed_rows:, :] = nn(by_slot, own_slots(e)).astype(BF16)
        x_trip = (xs_ref, x_in, trip_sem.at[1])
        over_exp(*x_trip)

        o_gather.relay()
        load_in.wait()
        load_out.wait()
        arrive(*x_trip)
        x_all[me, :slot_rows, :] = unpack_slots(x_in[:, :packed_rows, :], capacity).astype(BF16)
        gate_parts = jnp.zeros((GATE_ROWS, slot_rows), F32)
        for e in range(experts):
            gate_parts = gate_parts + nt(x_in[e, packed_rows:, :], own_slots(e))
        x_all[me, slot_rows:, :] = jnp.concatenate(
            [gate_parts, jnp.zeros((GATE_ROWS, width - slot_rows), F32)], axis=1
        ).astype(BF16)
        x_gather.start()
        xs = x_all[me, :slot_rows, :]
        made = jnp.zeros(xs.shape, F32)
        for n in range(hidden // width):
            at = slice(n * width, (n + 1) * width)
            value, derivative = gelu_parts(nn(xs, w_in[:, at]))
            slope[:, at] = derivative
            made = made + nn(value.astype(BF16), w_out[at, :])
        made_out[...] = pack_slots(made, experts).astype(BF16)
        made_trip = (made_out, made_back, trip_sem.at[2])
        over_exp(*made_trip)
        n2_gather.relay()
        dm = (g_all[me].astype(F32) * slot_gates(gate_parts)).astype(BF16)
        dx = jnp.zeros(dm.shape, F32)
        for n in range(hidden // width):
            at = slice(n * width, (n + 1) * width)
            dh = (nt(dm, w_out[at, :]) * slope[:, at]).astype(BF16)
            dx = dx + nt(dh, w_in[:, at])
        dx_out[...] = pack_slots(dx, experts).astype(BF16)
        dx_trip = (dx_out, dx_back, trip_sem.at[3])
        over_exp(*dx_trip)
        g_gather.relay_far()
        o_gather.relay_far()
        arrive(*made_trip)
        arrive(*dx_trip)
        for trip in (x_trip, made_trip, dx_trip):
            sent(*trip)

    bf = lambda *n: pltpu.VMEM(n, BF16)
    f32 = lambda *n: pltpu.VMEM(n, F32)
    packed = bf(*g_in.shape)
    pl.run_scoped(self_attention, f32(span + rows, 2 * rows), f32(span, 2 * rows), bf(enc_rows, width), packed)
    pl.run_scoped(
        rest_forward, bf(*x_in.shape), packed, packed, f32(slot_rows, hidden), bf(width, hidden), bf(hidden, width)
    )

    enc_part = enc_rows // seq_count
    dekv_gather = Gather(place, dekv_hbm, experts, gather_send.at[6], gather_recv.at[5])
    def backward(e_out, t_out, c_src, turned_ref, ds_ref, gin_out, gin_window, w_ein, w_eout):
        def unit_block(j):
            return block_of(lax.rem(place.chip + j, 4) * 2 + place.core, own_hidden)

        def expert_loads(j):
            return (
                load(8 + 2 * (j % 2), in_hbm.at[:, unit_block(j)], w_ein.at[j % 2]),
                load(9 + 2 * (j % 2), out_hbm.at[unit_block(j), :], w_eout.at[j % 2]),
            )

        def gin_copy(j):
            return remote(
                gin_out.at[j], gin_in.at[:, unit_block(j)], unit_send.at[0], unit_recv.at[0], {"seq": place.partner}
            )

        def expert_units(j):
            for copy in expert_loads(j):
                copy.wait()
            xs = x_all[:, :slot_rows, :].reshape(-1, width)
            dm = g_all[...].reshape(-1, width)
            value, slope = gelu_parts(nn(xs, w_ein[j % 2]))
            if j == 0:
                gout_ref[...] = tn(value.astype(BF16), dm)
                store(gout_ref, gout_hbm)
            dh = (nt(dm, w_eout[j % 2]) * slope).astype(BF16)
            if j < 2:
                for copy in expert_loads(j + 2):
                    copy.start()
            lanes = pl.ds(pl.multiple_of((place.chip + lax.div(place.chip, 2)) * LANES, LANES), 2 * LANES)
            gin_window[...] = tn(x_all[:, :slot_rows, lanes].reshape(-1, 2 * LANES), dh)
            first = lax.rem(place.chip, 2) * (LANES // 2)
            rows_of = lambda core: pl.ds(pl.multiple_of(first + core * part, 32), part)
            gin_in[:, unit_block(j)] = gin_window[rows_of(place.core), :].astype(BF16)
            gin_out[j] = gin_window[rows_of(1 - place.core), :].astype(BF16)
            gin_copy(j).start()

        for copy in expert_loads(0) + expert_loads(1):
            copy.start()
        enc_scatter = Scatter(place, e_out, e_pair, e_turn, e_side, e_turn.shape[1], enc_sem)
        chunks = [
            Chunk(
                place, quarters, peers, c_src.at[i], c_slots.at[i], c_own.at[i], weights_hbm.at[i], chunk_sem.at[i],
                (chunk_send.at[i], chunk_recv.at[i]), local_sem.at[i],
            )
            for i in range(6)
        ]

        def enc_over_exp():
            for d, peer in enumerate(peers):
                remote(e_mine.at[peer], e_exp.at[d], enc_exp_sem.at[0], enc_exp_sem.at[1], {"exp": peer}).start()

        def dekv_over_exp():
            for peer in peers:
                remote(dekv, dekv_hbm.at[me, mine], enc_exp_sem.at[2], enc_exp_sem.at[3], {"exp": peer}).start()

        def dekv_local():
            return pltpu.make_async_copy(dekv, dekv_hbm.at[me, mine], local_sem.at[6])

        def exchange(i, factor):
            turned_ref[i] = factor.T
            for peer in everyone:
                remote(
                    turned_ref.at[i, block_of(peer, part), :], right.at[i, :, own_lanes], right_sem.at[i, 0], right_sem.at[i, 1],
                    {"seq": peer},
                ).start()
            right[i, :, own_lanes] = turned_ref[i, block_of(me, part), :]

        def multiply(i):
            wait_bytes(turned_ref.at[i, pl.ds(0, (seq_count - 1) * part), :], right_sem.at[i, 1])
            chunks[i].over_exp(nn(right[i], left[min(i, 3)].reshape(span, width)))

        slots = slots_ref[...]
        made = nn(slots, unpack_slots(made_back[...], capacity).astype(BF16))
        kept = jnp.sum(slots.astype(F32), axis=1, keepdims=True)
        gates = gates_ref[...]
        chosen = chosen_ref[...]
        picked = jnp.sum(gates * chosen, axis=1, keepdims=True)
        g = g_ref[...].astype(F32)
        out_ref[...] = (r2_ref[...] + (picked * kept) * made).astype(BF16)
        store(out_ref, out_hbm_ref)
        gate_grad = jnp.sum(g * made, axis=1, keepdims=True) * kept
        dl = gates * (chosen * gate_grad - picked * gate_grad)
        dl_high, dl_low = in_two(dl)
        x3 = x3_ref[...]
        small_a[...] = jnp.zeros_like(small_a)
        small_a[4 : 4 + experts, :width] = tn(dl_high, x3) + tn(dl_low, x3)
        dx3 = (
            nn(slots, unpack_slots(dx_back[...], capacity).astype(BF16))
            + nn(dl_high, router_ref[...]) + nn(dl_low, router_ref[...])
        )
        da, dw = rms_back(r2_ref[...], gains_ref[2:3, :], dx3)
        small_a[2:3, :width] = dw
        dr_ref[...] = g + da
        do2 = dr_ref[...].astype(BF16)
        doc_ref[...] = nt(do2, w_co[...]).astype(BF16)
        exchange(2, do2)
        oc_gather.relay()
        n2_gather.relay_far()
        x_gather.relay()

        @pl.loop(0, pairs)
        def _(p):
            lanes, value_lanes = pair_lanes(p), pair_lanes(pairs + p)
            doc_both = head_stack(doc_ref[:, lanes])
            weights = cross_prob[p]
            wide = weights.astype(F32)
            dp = nt(ekv[:, value_lanes], doc_both)
            dc = (wide * (dp - jnp.sum(wide * dp, axis=0, keepdims=True))).astype(BF16)
            dk = nn(dc, head_stack(qc_ref[:, lanes])).astype(BF16).reshape(4, 2, enc_part, LANES)
            dv = nn(weights, doc_both).astype(BF16).reshape(4, 2, enc_part, LANES)
            for k in range(2):
                e_out[k, :, :, lanes] = dk[:, k]
                e_out[k, :, :, value_lanes] = dv[:, k]
            dqc_ref[:, lanes] = (head_unstack(tn(ekv[:, lanes], dc), rows) * 0.125).astype(BF16)

        enc_scatter.start()
        oc_gather.relay_far()
        dqc = dqc_ref[...]
        exchange(1, dqc)
        da, dw = rms_back(r1_ref[...], gains_ref[1:2, :], nt(dqc, w_cq[...]))
        small_a[1:2, :width] = dw
        enc_scatter.turn_on()
        dr_ref[...] = dr_ref[...] + da
        do1 = dr_ref[...].astype(BF16)
        doc_ref[...] = nt(do1, w_so[...]).astype(BF16)
        exchange(0, do1)
        x_gather.relay_far()
        oc_gather.finish()
        multiply(2)
        n2_gather.finish()
        o_gather.finish()

        ds_ref[pl.ds(0, rows), :] = jnp.zeros((rows, 2 * rows), BF16)
        flip = (
            lax.broadcasted_iota(jnp.int32, (2 * rows, 2 * rows), 0)
            + lax.broadcasted_iota(jnp.int32, (2 * rows, 2 * rows), 1)
            == 2 * rows - 1
        ).astype(BF16)

        def terms(p):
            return Scatter(place, t_out.at[p], t_pair.at[p], t_turn.at[p], t_side.at[p], rows // 2, term_sem.at[p])

        def pair_back(p):
            lanes, value_lanes = pair_lanes(p), pair_lanes(pairs + p)
            do_both = head_stack(doc_ref[:, lanes])
            weights = prob[p]
            wide = weights.astype(F32)
            dp = nt(kv_all[:, value_lanes], do_both)
            ds_wide = wide * (dp - jnp.sum(wide * dp, axis=0, keepdims=True))
            ds = ds_wide.astype(BF16)
            ds_ref[pl.ds(rows, span), :] = ds
            total_ref[pl.ds(p, 1), :] = jnp.sum(ds.astype(F32), axis=0, keepdims=True)
            dk = nn(ds, head_stack(q_ref[:, lanes])).astype(BF16).reshape(4, 2, rows, LANES)
            dv = nn(weights, do_both).astype(BF16).reshape(4, 2, rows, LANES)
            for k in range(2):
                t_out[p, k, :, :, :LANES] = dk[:, k]
                t_out[p, k, :, :, LANES:] = dv[:, k]
            terms(p).start()
            dqkv_ref[:, lanes] = (head_unstack(tn(kv_all[:, lanes], ds), rows) * 0.125).astype(BF16)
            turned = nn(flip, ds_ref[near, :])
            for h in range(2):
                one = turned[:, h * rows : (h + 1) * rows]
                one = jnp.concatenate([one, jnp.zeros_like(one)], axis=1)
                one = pltpu.roll(one, 1, 1, stride=1, stride_axis=0)
                diag_ref[pl.ds(2 * p + h, 1), :] = jnp.sum(one, axis=0, keepdims=True)

        def own_terms(p):
            total = terms(p).total()
            dqkv_ref[:, pair_lanes(pairs + p)] = total[:, :LANES].astype(BF16)
            dqkv_ref[:, pair_lanes(2 * pairs + p)] = total[:, LANES:].astype(BF16)

        @pl.loop(0, pairs)
        def _(t):
            pair_back(t)
            @pl.when(t >= 1)
            def _():
                terms(jnp.maximum(t - 1, 0)).turn_on()

            @pl.when(t >= 3)
            def _():
                terms(jnp.maximum(t - 3, 0)).side_on()

            @pl.when(t >= 5)
            def _():
                own_terms(jnp.maximum(t - 5, 0))

            @pl.when(t == 1)
            def _():
                enc_scatter.side_on()

            @pl.when(t == 2)
            def _():
                multiply(1)
                chunks[2].back_over_exp()

            @pl.when(t == 3)
            def _():
                multiply(0)

            @pl.when(t == 4)
            def _():
                e_mine[...] = enc_scatter.total().astype(BF16).reshape(e_mine.shape)
                enc_over_exp()
                chunks[1].back_over_exp()


        last = pairs - 1
        terms(last).turn_on()
        terms(last - 2).side_on()
        exchange(3, dqkv_ref[:, :width])
        own_terms(last - 4)
        terms(last - 1).side_on()
        own_terms(last - 3)
        terms(last).side_on()
        own_terms(last - 2)
        chunks[0].back_over_exp()
        own_terms(last - 1)
        wait_bytes(e_exp, enc_exp_sem.at[1])
        total = e_mine[mine].astype(F32)
        for d in range(experts - 1):
            total = total + e_exp[d].astype(F32)
        dekv[...] = total.astype(BF16)
        dekv_local().start()
        dekv_over_exp()
        multiply(3)
        own_terms(last)

        dqkv = dqkv_ref[...]
        exchange(4, dqkv[:, width : 2 * width])
        exchange(5, dqkv[:, 2 * width :])
        chunks[2].spread()

        x = x_ref[...].astype(F32)
        da, dw = rms_back(x, gains_ref[0:1, :], nt(dqkv, w_qkv[...]))
        small_a[0:1, :width] = dw
        dx_ref[...] = dr_ref[...] + da
        store(dx_ref, dx_hbm)
        heads = 2 * pairs
        table = diag_ref[:, 2 * rows - LANES :]
        totals = total_ref[...]
        first = jnp.sum(totals[:, :rows], axis=1, keepdims=True)
        second = jnp.sum(totals[:, rows:], axis=1, keepdims=True)
        head = lax.broadcasted_iota(jnp.int32, (heads, pairs), 0)
        pair = lax.broadcasted_iota(jnp.int32, (heads, pairs), 1)
        spread = lambda odd, v: jnp.dot(
            (head == 2 * pair + odd).astype(F32), v, precision=highest, preferred_element_type=F32
        )
        whole = spread(0, jnp.broadcast_to(first, (pairs, LANES))) + spread(1, jnp.broadcast_to(second, (pairs, LANES)))
        rest = whole - jnp.sum(table, axis=1, keepdims=True)
        lane = lax.broadcasted_iota(jnp.int32, table.shape, 1)
        table = table + jnp.where(lane == LANES - 1, rest, 0.0)
        bucket = lax.broadcasted_iota(jnp.int32, (LANES, LANES), 0)
        pick = (buckets_ref[...] == bucket).astype(F32)
        by_bucket = lax.dot_general(table, pick, (((1,), (1,)), ((), ())), precision=highest, preferred_element_type=F32)
        small_a[0:8, width : width + LANES] = by_bucket[0:8]
        small_a[0 : heads - 8, width + LANES :] = by_bucket[8:heads]
        s_pair = remote(small_a, small_pair, small_sem.at[0], small_sem.at[1], {"seq": place.partner})
        s_pair.start()

        x_gather.finish()
        g_gather.finish()
        g_gather.drain()
        parts = x_all[:, slot_rows:, : 2 * LANES].astype(F32).reshape(seq_count * GATE_ROWS, 2 * LANES).T
        for n in range(seq_count):
            gate = sum(parts[:slot_rows, n * GATE_ROWS + i : n * GATE_ROWS + i + 1] for i in range(3))
            g_all[n] = (g_all[n].astype(F32) * gate).astype(BF16)
        expert_units(0)
        chunks[3].back_over_exp()
        multiply(4)
        multiply(5)
        chunks[1].spread()
        chunks[0].spread()
        dekv_local().wait()
        wait_bytes(e_exp, enc_exp_sem.at[3])
        dekv_gather.start()
        chunks[2].over_seq.relay()
        s_pair.wait_recv()
        small_b[...] = small_a[...] + small_pair[...]
        for d, device in enumerate((place.x, place.y, place.far)):
            remote(small_b, small_chip.at[d], small_sem.at[2], small_sem.at[3], {"seq": device}).start()
        expert_units(1)
        chunks[3].spread()
        chunks[4].back_over_exp()
        expert_units(2)
        chunks[5].back_over_exp()
        chunks[1].over_seq.relay()
        chunks[2].over_seq.relay_far()
        chunks[0].over_seq.relay()
        dekv_gather.relay()
        chunks[4].spread()
        genc_ref[...] = nt(dekv[...], w_ckv[...])
        store(genc_ref, genc_hbm)
        wait_bytes(small_chip, small_sem.at[3])
        small_c[...] = small_b[...] + small_chip[0] + small_chip[1] + small_chip[2]
        for d, peer in enumerate(peers):
            remote(small_c, small_exp.at[d], small_sem.at[4], small_sem.at[5], {"exp": peer}).start()
        chunks[5].spread()
        expert_units(3)
        chunks[1].over_seq.relay_far()
        chunks[3].over_seq.relay()
        chunks[0].over_seq.relay_far()
        dekv_gather.relay_far()
        chunks[4].over_seq.relay()
        chunks[5].over_seq.relay()
        wait_bytes(gin_out, unit_recv.at[0])
        store(gin_in, gin_hbm)
        wait_bytes(small_exp, small_sem.at[5])
        total = small_c[...]
        for d in range(experts - 1):
            total = total + small_exp[d]
        small_out_ref[...] = total
        store(small_out_ref, small_hbm)
        for i in (3, 4, 5):
            chunks[i].over_seq.relay_far()
        for chunk in chunks:
            chunk.over_seq.finish()
        dekv_gather.finish()

        for copy in stores:
            copy.wait()
        wait_bytes(e_exp, enc_exp_sem.at[0])
        wait_bytes(e_exp, enc_exp_sem.at[2])
        wait_bytes(gin_out, unit_send.at[0])
        s_pair.wait_send()
        wait_bytes(small_chip, small_sem.at[2])
        wait_bytes(small_exp, small_sem.at[4])
        for i in range(6):
            wait_bytes(turned_ref.at[i, pl.ds(0, (seq_count - 1) * part), :], right_sem.at[i, 0])
        for each in (gather, o_gather, n2_gather, oc_gather, x_gather, dekv_gather, enc_scatter):
            each.drain()
        for chunk in chunks:
            chunk.drain()

        @pl.loop(0, pairs)
        def _(p):
            terms(p).drain()


    pl.run_scoped(
        backward, bf(2, 4, enc_part, 2 * width), bf(pairs, 2, 4, rows, 2 * LANES), bf(6, part, width), bf(6, width, rows),
        bf(span + rows, 2 * rows), bf(4, part, own_hidden), f32(2 * LANES, own_hidden), bf(2, width, own_hidden), bf(2, own_hidden, width),
    )


def layer_call(seq_count, capacity, x, encoder, lengths, buckets, routes, gains, qkv, so, cq, ckv, co, rel, router, g, w_in,
               w_out):
    rows, width = x.shape
    span = seq_count * rows
    pairs = width // LANES
    heads = 2 * pairs
    enc_rows = encoder.shape[0]
    experts = router.shape[0]
    slot_rows = experts * capacity
    part = width // seq_count
    enc_part = enc_rows // seq_count
    own_enc = enc_part // experts
    hidden = w_in.shape[1]
    z = experts - 1
    quarter = (part // 2, width // (experts // 2))
    small = (8, width + 2 * LANES)
    packed = (experts, capacity * pairs, LANES)
    shape = jax.ShapeDtypeStruct
    dma = lambda *n: pltpu.SemaphoreType.DMA(n)
    bf = lambda *n: pltpu.VMEM(n, BF16)
    f32 = lambda *n: pltpu.VMEM(n, F32)
    wide = bf(rows, width)
    return pl.pallas_call(
        functools.partial(layer_kernel, seq_count, capacity),
        out_shape=(
            shape((rows, width), BF16), shape((rows, width), F32), shape((6, seq_count, part, width), BF16),
            shape((seq_count, experts, own_enc, 2 * width), BF16), shape(small, F32), shape((part, hidden), BF16),
            shape((hidden // seq_count, width), F32), shape((own_enc, width), F32),
        ),
        in_specs=[VMEM, ANY, SMEM, VMEM, VMEM, VMEM, ANY, ANY, ANY, ANY, ANY, VMEM, VMEM, VMEM, ANY, ANY],
        out_specs=(ANY,) * 8,
        scratch_shapes=[
            bf(4, seq_count, rows, width), bf(span, 2 * width), bf(pairs, span, 2 * rows), bf(pairs, enc_rows, 2 * rows),
            bf(enc_rows, 2 * width), bf(*qkv.shape), bf(*so.shape), bf(*cq.shape), bf(*ckv.shape), bf(*co.shape),
            f32(heads, 2 * LANES), bf(seq_count, slot_rows + GATE_ROWS, width), bf(seq_count, slot_rows, width),
            bf(experts, capacity * pairs + GATE_ROWS, LANES), bf(*packed), bf(*packed), bf(*packed),
            wide, wide, wide, f32(rows, width), f32(rows, width), f32(rows, experts), f32(rows, experts), bf(rows, slot_rows),
            f32(rows, width), wide, wide, bf(rows, 3 * width), f32(heads, 2 * rows), f32(pairs, 2 * rows),
            bf(4, enc_part, 2 * width), bf(2, enc_part // 2, 2 * width), bf(2, enc_part, 2 * width),
            bf(experts, own_enc, 2 * width), bf(z, own_enc, 2 * width), bf(own_enc, 2 * width),
            bf(pairs, 4, rows, 2 * LANES), bf(pairs, 2, rows // 2, 2 * LANES), bf(pairs, 2, rows, 2 * LANES),
            wide, f32(rows, width), f32(hidden // seq_count, width), f32(own_enc, width), f32(*small),
            bf(6, z, *quarter), bf(6, *quarter), bf(6, part, span), bf(part, hidden),
            f32(*small), f32(*small), f32(*small), f32(*small), f32(3, *small), f32(z, *small),
            dma(12), dma(7), dma(6), dma(6), dma(7), dma(6, 4), dma(4, 2), dma(5), dma(4), dma(pairs, 5), dma(6, 4),
            dma(6), dma(6, 4), dma(6, 2), dma(1), dma(1), dma(6),
        ],
        compiler_params=pltpu.CompilerParams(collective_id=0, has_side_effects=True, vmem_limit_bytes=63 << 20),
        name="layer",
    )(x, encoder, lengths, buckets, routes, gains, qkv, so, cq, ckv, co, rel, router, g, w_in, w_out)


def finish_kernel(
    experts, weights_hbm, dekv_hbm, enc_hbm, small_ref, layer_hbm, dx_hbm, genc_hbm, gin_ref, gout_hbm,
    layer_out, dx_out, genc_out, gains_out, qkv_hbm, so_hbm, cq_hbm, ckv_hbm, co_hbm, rel_out, router_out, gin_out, gout_out,
    weights, dekv, enc, squares, qkv, ckv, layer, dx, genc, gin, gout, load_sem, sem,
):
    seq_count, part, width = weights.shape[1:]
    loads = [pltpu.make_async_copy(weights_hbm.at[i], weights.at[i], load_sem.at[i]) for i in range(6)] + [
        pltpu.make_async_copy(dekv_hbm, dekv, load_sem.at[6]), pltpu.make_async_copy(enc_hbm, enc, load_sem.at[7])
    ]
    through = ((gout_hbm, gout, gout_out), (dx_hbm, dx, dx_out), (layer_hbm, layer, layer_out), (genc_hbm, genc, genc_out))
    loads += [pltpu.make_async_copy(src, held, load_sem.at[8 + i]) for i, (src, held, _) in enumerate(through)]
    for load in loads:
        load.start()
    copies = []

    def store(src, dst):
        copy = pltpu.make_async_copy(src, dst, sem.at[len(copies)])
        copy.start()
        copies.append(copy)

    gains_out[...] = small_ref[0:3, :width]
    router_out[...] = small_ref[4 : 4 + experts, :width]
    heads, buckets = rel_out.shape
    rel_out[0:8, :] = small_ref[0:8, width : width + buckets]
    rel_out[8:heads, :] = small_ref[0 : heads - 8, width + LANES : width + LANES + buckets]
    gin[...] = gin_ref[...].astype(F32)
    store(gin, gin_out)

    def turn(i, target, at):
        loads[i].wait()
        for block in range(width // LANES):
            rows = slice(block * LANES, (block + 1) * LANES)
            target[:, at + block * LANES : at + (block + 1) * LANES] = (
                weights[i].reshape(seq_count * part, width)[rows, :].astype(F32).T
            )

    for i, out in enumerate((so_hbm, cq_hbm, co_hbm)):
        turn(i, squares.at[i], 0)
        store(squares.at[i], out)
    for i, (_, held, out) in enumerate(through):
        loads[8 + i].wait()
        store(held, out)
    for i in range(3):
        at = slice(i * width, (i + 1) * width)
        turn(3 + i, qkv, i * width)
        store(qkv.at[:, at], qkv_hbm.at[:, at])
    loads[6].wait()
    loads[7].wait()
    for n in range(2):
        at = slice(n * width, (n + 1) * width)
        ckv[:, at] = tn(enc[...], dekv[...].reshape(enc.shape[0], 2 * width)[:, at])
        store(ckv.at[:, at], ckv_hbm.at[:, at])
    for copy in copies:
        copy.wait()


def finish_call(heads, buckets, experts, weights, dekv, enc, small, layer, dx, genc, gin, gout):
    seq_count, part, width = weights.shape[1:]
    shape = jax.ShapeDtypeStruct
    f32 = lambda *n: shape(n, F32)
    return pl.pallas_call(
        functools.partial(finish_kernel, experts),
        out_shape=(
            shape(layer.shape, BF16), f32(*dx.shape), f32(*genc.shape), f32(3, width), f32(width, 3 * width), f32(width, width),
            f32(width, width), f32(width, 2 * width), f32(width, width), f32(heads, buckets), f32(experts, width),
            f32(*gin.shape), f32(*gout.shape),
        ),
        in_specs=[ANY, ANY, ANY, VMEM, ANY, ANY, ANY, VMEM, ANY],
        out_specs=(ANY, ANY, ANY, VMEM, ANY, ANY, ANY, ANY, ANY, VMEM, VMEM, ANY, ANY),
        scratch_shapes=[
            pltpu.VMEM(weights.shape, BF16), pltpu.VMEM(dekv.shape, BF16), pltpu.VMEM(enc.shape, BF16),
            pltpu.VMEM((3, width, width), F32), pltpu.VMEM((width, 3 * width), F32), pltpu.VMEM((width, 2 * width), F32),
            pltpu.VMEM(layer.shape, BF16), pltpu.VMEM(dx.shape, F32), pltpu.VMEM(genc.shape, F32), pltpu.VMEM(gin.shape, F32),
            pltpu.VMEM(gout.shape, F32), pltpu.SemaphoreType.DMA((13,)), pltpu.SemaphoreType.DMA((13,)),
        ],
        compiler_params=pltpu.CompilerParams(vmem_limit_bytes=60 << 20),
        name="finish",
    )(weights, dekv, enc, small, layer, dx, genc, gin, gout)


def fused(inputs, encoder, lengths, buckets, routes, norm_gains, self_qkv, self_out, cross_q, cross_kv, cross_out,
          rel_bias, router, expert_in, expert_out, cotangent):
    seq_count = lax.axis_size("seq")
    rows = inputs.shape[1]
    experts = router.shape[1]
    capacity = 5 * rows // (4 * experts)
    (layer_out, grad_input, weights, dekv, small, gin, gout, grad_encoder) = layer_call(
        seq_count, capacity, inputs[0], encoder, lengths, buckets[None, :], routes.reshape(1, rows), norm_gains, self_qkv,
        self_out, cross_q, cross_kv, cross_out, rel_bias.T, router.T, cotangent[0], expert_in[0], expert_out[0])
    (layer_out, grad_input, grad_encoder, gains, g_qkv, g_so, g_cq, g_ckv, g_co, g_rel, g_router, gin, gout) = finish_call(
        rel_bias.shape[1], rel_bias.shape[0], experts, weights, dekv, encoder, small, layer_out, grad_input, grad_encoder, gin,
        gout)
    return (layer_out[None], grad_input[None], grad_encoder, gains, g_qkv, g_so, g_cq, g_ckv, g_co, g_rel.T, g_router.T,
            gin[None], gout[None])


def on_device(*operands):
    if lax.axis_size("seq") == 8 and lax.axis_size("exp") == 4 and operands[0].shape[1] == 128:
        return fused(*operands)
    return streamed(*operands)


def solution(mesh):
    in_specs = (
        P("exp", "seq", None),
        P(),
        P("exp", None),
        P(),
        P("exp", "seq", None),
        P(),
        P(),
        P(),
        P(),
        P(),
        P(),
        P(),
        P(),
        P("exp", None, None),
        P("exp", None, None),
        P("exp", "seq", None),
    )
    out_specs = (
        P("exp", "seq", None),
        P("exp", "seq", None),
        P(("seq", "exp"), None),
        P(),
        P(),
        P(),
        P(),
        P(),
        P(),
        P(),
        P(),
        P("exp", "seq", None),
        P("exp", "seq", None),
    )
    return jax.shard_map(
        on_device, mesh=mesh, in_specs=in_specs, out_specs=out_specs, check_vma=False
    )
```

```python
import functools
import math

import jax
import jax.numpy as jnp
from jax import lax
from jax.experimental import pallas as pl
from jax.experimental.pallas import tpu as pltpu
from jax.sharding import PartitionSpec as P

H = 12
HD = 64


epsilon = 1e-06
masked_out = -1e30
highest = lax.Precision.HIGHEST


def rms_norm(value, gain):
    return value * lax.rsqrt(jnp.mean(value * value, axis=-1, keepdims=True) + epsilon) * gain


def split_heads(value):
    return value.reshape(value.shape[0], H, HD)


def doc_index(positions, doc_ends):
    return jnp.sum((positions[:, None] >= doc_ends[None, :]).astype(jnp.int32), axis=1)


def band_pick(offset_gap, query_rows, key_rows, table_span):
    band_len = query_rows + key_rows + 1
    column = jnp.arange(band_len, dtype=jnp.int32)
    distance = jnp.clip(offset_gap + query_rows - column, 0, table_span - 1)
    return (distance[:, None] == jnp.arange(table_span, dtype=jnp.int32)[None, :]).astype(
        jnp.float32
    )


def relative_bias(table, offset_gap, query_rows, key_rows):
    head_count = table.shape[0]
    band_len = query_rows + key_rows + 1
    band = jnp.dot(
        table, band_pick(offset_gap, query_rows, key_rows, table.shape[1]).T, precision=highest
    )
    tiled = jnp.broadcast_to(band[:, None, :], (head_count, query_rows, band_len)).reshape(
        head_count, query_rows * band_len
    )
    skewed = tiled[:, : query_rows * (band_len - 1)].reshape(head_count, query_rows, band_len - 1)
    return skewed[:, :, query_rows : query_rows + key_rows]


def table_terms(score_grads, offset_gap, table_span):
    head_count, query_rows, key_rows = score_grads.shape
    band_len = query_rows + key_rows + 1
    placed = jnp.pad(score_grads.astype(jnp.float32), ((0, 0), (0, 0), (query_rows, 0)))
    flat = jnp.pad(
        placed.reshape(head_count, query_rows * (band_len - 1)), ((0, 0), (0, query_rows))
    )
    diagonal_sums = jnp.sum(flat.reshape(head_count, query_rows, band_len), axis=1)
    return jnp.dot(
        diagonal_sums, band_pick(offset_gap, query_rows, key_rows, table_span), precision=highest
    )


def self_scores(queries, query_start, keys_part, key_start, doc_ends, table):
    query_rows = queries.shape[0]
    key_rows = keys_part.shape[0]
    query_pos = query_start + jnp.arange(query_rows, dtype=jnp.int32)
    key_pos = key_start + jnp.arange(key_rows, dtype=jnp.int32)
    offset_gap = query_start - key_start
    raw_scores = (
        jnp.einsum(
            "qhd,khd->hqk",
            split_heads(queries),
            split_heads(keys_part),
            preferred_element_type=jnp.float32,
        )
        * 0.125
    )
    allowed = (key_pos[None, :] <= query_pos[:, None]) & (
        doc_index(key_pos, doc_ends)[None, :] == doc_index(query_pos, doc_ends)[:, None]
    )
    scores = jnp.where(
        allowed[None],
        raw_scores + relative_bias(table, offset_gap, query_rows, key_rows),
        masked_out,
    )
    return (scores, allowed[None], offset_gap)


def over_blocks(step, running, pieces):
    rows_total = pieces[0].shape[0]
    block_rows = math.gcd(rows_total, 512)
    block_count = rows_total // block_rows
    stacked = tuple(
        (member.reshape(block_count, block_rows, *member.shape[1:]) for member in pieces)
    )

    def scan_step(inner_running, block_input):
        block_id, members = block_input
        return (step(inner_running, members, block_id * block_rows), None)

    result, ignored = lax.scan(
        scan_step, running, (jnp.arange(block_count, dtype=jnp.int32), stacked)
    )
    return result


def streamed(
    inputs,
    encoder,
    lengths,
    buckets,
    routes,
    norm_gains,
    self_qkv,
    self_out,
    cross_q,
    cross_kv,
    cross_out,
    rel_bias,
    router,
    expert_in,
    expert_out,
    cotangent,
):
    hidden = inputs[0].astype(jnp.float32)
    rows_dev = hidden.shape[0]
    model_width = hidden.shape[1]
    seq_count = lax.axis_size("seq")
    seq_index = lax.axis_index("seq")
    own_start = seq_index * rows_dev
    doc_ends = jnp.cumsum(lengths[0])
    bucket_pick = (
        buckets[:, None] == jnp.arange(rel_bias.shape[0], dtype=jnp.int32)[None, :]
    ).astype(jnp.float32)
    table = jnp.dot(bucket_pick, rel_bias, precision=highest).T
    normed_one, norm_one_back = jax.vjp(rms_norm, hidden, norm_gains[0])
    normed_one = normed_one.astype(jnp.bfloat16)
    qkv_all = jnp.dot(normed_one, self_qkv, preferred_element_type=jnp.float32).astype(jnp.bfloat16)
    queries = qkv_all[:, :model_width]
    keys_own = qkv_all[:, model_width : 2 * model_width]
    values_own = qkv_all[:, 2 * model_width :]

    def forward_step(running, pieces, key_start):
        top_old, denominator, summed = running
        keys_part, values_part = pieces
        scores, allowed, offset_gap = self_scores(
            queries, own_start, keys_part, key_start, doc_ends, table
        )
        top_new = jnp.maximum(top_old, jnp.max(scores, axis=-1))
        weights_raw = jnp.where(allowed, jnp.exp(scores - top_new[..., None]), 0.0)
        rescale = jnp.exp(top_old - top_new)
        denominator = denominator * rescale + jnp.sum(weights_raw, axis=-1)
        summed = summed * rescale[..., None] + jnp.einsum(
            "hqk,khd->hqd",
            weights_raw.astype(jnp.bfloat16),
            split_heads(values_part),
            preferred_element_type=jnp.float32,
        )
        return (top_new, denominator, summed)

    start_state = (
        jnp.full((H, rows_dev), masked_out, jnp.float32),
        jnp.zeros((H, rows_dev), jnp.float32),
        jnp.zeros((H, rows_dev, HD), jnp.float32),
    )
    top_score, denominator, summed = over_blocks(
        forward_step,
        start_state,
        (
            lax.all_gather(keys_own, "seq", axis=0, tiled=True),
            lax.all_gather(values_own, "seq", axis=0, tiled=True),
        ),
    )
    log_total = top_score + jnp.log(denominator)
    attended_full = (
        (summed / denominator[..., None]).transpose(1, 0, 2).reshape(rows_dev, model_width)
    )
    attended = attended_full.astype(jnp.bfloat16)
    after_self = hidden + jnp.dot(attended, self_out, preferred_element_type=jnp.float32)
    enc_kv = jnp.dot(encoder, cross_kv, preferred_element_type=jnp.float32).astype(jnp.bfloat16)
    cross_keys = split_heads(enc_kv[:, :model_width])
    cross_values = split_heads(enc_kv[:, model_width:])
    normed_two, norm_two_back = jax.vjp(rms_norm, after_self, norm_gains[1])
    normed_two = normed_two.astype(jnp.bfloat16)
    cross_queries = jnp.dot(normed_two, cross_q, preferred_element_type=jnp.float32).astype(
        jnp.bfloat16
    )
    cross_scores = (
        jnp.einsum(
            "qhd,khd->hqk",
            split_heads(cross_queries),
            cross_keys,
            preferred_element_type=jnp.float32,
        )
        * 0.125
    )
    cross_raw = jnp.exp(cross_scores - jnp.max(cross_scores, axis=-1, keepdims=True))
    cross_prob = cross_raw / jnp.sum(cross_raw, axis=-1, keepdims=True)
    cross_prob_low = cross_prob.astype(jnp.bfloat16)
    cross_att = (
        jnp.einsum("hqk,khd->qhd", cross_prob_low, cross_values, preferred_element_type=jnp.float32)
        .reshape(rows_dev, model_width)
        .astype(jnp.bfloat16)
    )
    after_cross = after_self + jnp.dot(cross_att, cross_out, preferred_element_type=jnp.float32)
    normed_three, norm_three_back = jax.vjp(rms_norm, after_cross, norm_gains[2])
    routed_in = normed_three.astype(jnp.bfloat16)
    gates = jax.nn.softmax(jnp.dot(routed_in, router, preferred_element_type=jnp.float32), axis=-1)
    expert_total = router.shape[1]
    local_experts = expert_in.shape[0]
    capacity = 5 * rows_dev // (4 * expert_total)
    route_ids = routes[0, :, 0]
    chosen = route_ids[:, None] == jnp.arange(expert_total, dtype=jnp.int32)[None, :]
    slots = jnp.sum(jnp.where(chosen, jnp.cumsum(chosen.astype(jnp.int32), axis=0), 0), axis=1) - 1
    kept = slots < capacity
    picked_gate = jnp.sum(jnp.where(chosen, gates, 0.0), axis=1)
    gate_used = picked_gate * kept.astype(jnp.float32)
    target = jnp.where(kept, route_ids * capacity + slots, -1)
    dispatch = (
        jnp.arange(expert_total * capacity, dtype=jnp.int32)[:, None] == target[None, :]
    ).astype(jnp.bfloat16)
    outgoing = (
        jnp.dot(dispatch, routed_in, preferred_element_type=jnp.float32)
        .astype(jnp.bfloat16)
        .reshape(expert_total, capacity, model_width)
    )
    arrived = lax.all_to_all(outgoing, "exp", split_axis=0, concat_axis=0, tiled=True).reshape(
        -1, local_experts, capacity, model_width
    )
    inner_pre = jnp.einsum("secd,edf->secf", arrived, expert_in, preferred_element_type=jnp.float32)
    active = jax.nn.gelu(inner_pre, approximate=True).astype(jnp.bfloat16)
    produced = jnp.einsum(
        "secf,efd->secd", active, expert_out, preferred_element_type=jnp.float32
    ).astype(jnp.bfloat16)
    returned = lax.all_to_all(
        produced.reshape(-1, capacity, model_width), "exp", split_axis=0, concat_axis=0, tiled=True
    )
    expert_rows = jnp.dot(
        dispatch.T, returned.reshape(-1, model_width), preferred_element_type=jnp.float32
    )
    layer_out = after_cross + gate_used[:, None] * expert_rows
    upstream = cotangent[0].astype(jnp.float32)
    made_grad = (upstream * gate_used[:, None]).astype(jnp.bfloat16)
    sent_grad = (
        jnp.dot(dispatch, made_grad, preferred_element_type=jnp.float32)
        .astype(jnp.bfloat16)
        .reshape(expert_total, capacity, model_width)
    )
    grad_arrived = lax.all_to_all(
        sent_grad, "exp", split_axis=0, concat_axis=0, tiled=True
    ).reshape(-1, local_experts, capacity, model_width)
    inner_again = jnp.einsum(
        "secd,edf->secf", arrived, expert_in, preferred_element_type=jnp.float32
    )
    active_again, gelu_back = jax.vjp(
        lambda value: jax.nn.gelu(value, approximate=True), inner_again
    )
    grad_out_w = jnp.einsum(
        "secf,secd->efd",
        active_again.astype(jnp.bfloat16),
        grad_arrived,
        preferred_element_type=jnp.float32,
    )
    grad_active = jnp.einsum(
        "secd,efd->secf", grad_arrived, expert_out, preferred_element_type=jnp.float32
    )
    grad_inner = gelu_back(grad_active)[0].astype(jnp.bfloat16)
    grad_in_w = jnp.einsum(
        "secd,secf->edf", arrived, grad_inner, preferred_element_type=jnp.float32
    )
    grad_sent_x = jnp.einsum(
        "secf,edf->secd", grad_inner, expert_in, preferred_element_type=jnp.float32
    ).astype(jnp.bfloat16)
    grad_back = lax.all_to_all(
        grad_sent_x.reshape(-1, capacity, model_width),
        "exp",
        split_axis=0,
        concat_axis=0,
        tiled=True,
    )
    grad_routed = jnp.dot(
        dispatch.T, grad_back.reshape(-1, model_width), preferred_element_type=jnp.float32
    )
    expert_sums = (
        lax.psum_scatter(grad_in_w, "seq", scatter_dimension=1, tiled=True),
        lax.psum_scatter(grad_out_w, "seq", scatter_dimension=1, tiled=True),
    )
    gate_grad = jnp.sum(upstream * expert_rows, axis=1) * kept.astype(jnp.float32)
    logit_grad = gates * (
        jnp.where(chosen, gate_grad[:, None], 0.0) - (picked_gate * gate_grad)[:, None]
    )
    router_grad = jnp.dot(routed_in.astype(jnp.float32).T, logit_grad, precision=highest)
    grad_normed_three = (
        jnp.dot(logit_grad, router.astype(jnp.float32).T, precision=highest) + grad_routed
    )
    grad_after_cross, gain_three = norm_three_back(grad_normed_three)
    grad_after_cross = grad_after_cross + upstream
    cross_branch = grad_after_cross.astype(jnp.bfloat16)
    cross_out_grad = jnp.dot(cross_att.T, cross_branch, preferred_element_type=jnp.float32)
    grad_cross_att = split_heads(
        jnp.dot(cross_branch, cross_out.T, preferred_element_type=jnp.float32).astype(jnp.bfloat16)
    )
    cross_prob_grad = jnp.einsum(
        "qhd,khd->hqk", grad_cross_att, cross_values, preferred_element_type=jnp.float32
    )
    cross_delta = jnp.sum(cross_prob * cross_prob_grad, axis=-1, keepdims=True)
    cross_score_grad = (cross_prob * (cross_prob_grad - cross_delta)).astype(jnp.bfloat16)
    grad_cross_queries = (
        (
            jnp.einsum(
                "hqk,khd->qhd", cross_score_grad, cross_keys, preferred_element_type=jnp.float32
            )
            * 0.125
        )
        .reshape(rows_dev, model_width)
        .astype(jnp.bfloat16)
    )
    grad_enc_keys = (
        jnp.einsum(
            "hqk,qhd->khd",
            cross_score_grad,
            split_heads(cross_queries),
            preferred_element_type=jnp.float32,
        )
        * 0.125
    )
    grad_enc_values = jnp.einsum(
        "hqk,qhd->khd", cross_prob_low, grad_cross_att, preferred_element_type=jnp.float32
    )
    enc_terms = jnp.concatenate(
        [grad_enc_keys.reshape(-1, model_width), grad_enc_values.reshape(-1, model_width)], axis=1
    )
    enc_grad_rows = lax.psum_scatter(
        enc_terms, ("seq", "exp"), scatter_dimension=0, tiled=True
    ).astype(jnp.bfloat16)
    enc_count = enc_grad_rows.shape[0]
    flat_index = seq_index * lax.axis_size("exp") + lax.axis_index("exp")
    own_enc = lax.dynamic_slice_in_dim(encoder, flat_index * enc_count, enc_count, 0)
    grad_encoder = jnp.dot(enc_grad_rows, cross_kv.T, preferred_element_type=jnp.float32)
    pair_grad = jnp.dot(own_enc.T, enc_grad_rows, preferred_element_type=jnp.float32)
    query_w_grad = jnp.dot(normed_two.T, grad_cross_queries, preferred_element_type=jnp.float32)
    grad_normed_two = jnp.dot(grad_cross_queries, cross_q.T, preferred_element_type=jnp.float32)
    grad_after_self, gain_two = norm_two_back(grad_normed_two)
    grad_after_self = grad_after_self + grad_after_cross
    self_branch = grad_after_self.astype(jnp.bfloat16)
    self_out_grad = jnp.dot(attended.T, self_branch, preferred_element_type=jnp.float32)
    grad_attended = jnp.dot(self_branch, self_out.T, preferred_element_type=jnp.float32).astype(
        jnp.bfloat16
    )
    row_delta = jnp.sum(
        split_heads(grad_attended).astype(jnp.float32) * split_heads(attended_full), axis=-1
    ).T
    stats_all = (
        lax.all_gather(log_total.T, "seq", axis=0, tiled=True),
        lax.all_gather(row_delta.T, "seq", axis=0, tiled=True),
    )

    def query_step(running, pieces, query_start):
        kv_grad, query_grads, table_grad = running
        queries_part, grads_part = pieces
        piece_rows = queries_part.shape[0]
        lse_part = lax.dynamic_slice_in_dim(stats_all[0], query_start, piece_rows, 0).T
        delta_part = lax.dynamic_slice_in_dim(stats_all[1], query_start, piece_rows, 0).T
        scores, allowed, offset_gap = self_scores(
            queries_part, query_start, keys_own, own_start, doc_ends, table
        )
        probability = jnp.where(allowed, jnp.exp(scores - lse_part[..., None]), 0.0)
        prob_grad = jnp.einsum(
            "qhd,khd->hqk",
            split_heads(grads_part),
            split_heads(values_own),
            preferred_element_type=jnp.float32,
        )
        score_grad = (probability * (prob_grad - delta_part[..., None])).astype(jnp.bfloat16)
        key_grad = (
            jnp.einsum(
                "hqk,qhd->khd",
                score_grad,
                split_heads(queries_part),
                preferred_element_type=jnp.float32,
            )
            * 0.125
        )
        value_grad = jnp.einsum(
            "hqk,qhd->khd",
            probability.astype(jnp.bfloat16),
            split_heads(grads_part),
            preferred_element_type=jnp.float32,
        )
        kv_grad = kv_grad + jnp.concatenate(
            [key_grad.reshape(-1, model_width), value_grad.reshape(-1, model_width)], axis=1
        )
        table_grad = table_grad + table_terms(score_grad, offset_gap, table.shape[1])
        query_part_grad = jnp.einsum(
            "hqk,khd->qhd", score_grad, split_heads(keys_own), preferred_element_type=jnp.float32
        ).reshape(piece_rows, model_width)
        current = lax.dynamic_slice_in_dim(query_grads, query_start, piece_rows, 0)
        query_grads = lax.dynamic_update_slice_in_dim(
            query_grads, current + query_part_grad, query_start, 0
        )
        return (kv_grad, query_grads, table_grad)

    back_start = (
        jnp.zeros((rows_dev, 2 * model_width), jnp.float32),
        jnp.zeros((seq_count * rows_dev, model_width), jnp.float32),
        jnp.zeros(table.shape, jnp.float32),
    )
    kv_grad, query_buffer, table_grad = over_blocks(
        query_step,
        back_start,
        (
            lax.all_gather(queries, "seq", axis=0, tiled=True),
            lax.all_gather(grad_attended, "seq", axis=0, tiled=True),
        ),
    )
    query_grad = lax.psum_scatter(query_buffer, "seq", scatter_dimension=0, tiled=True)
    qkv_grad = jnp.concatenate(
        [(query_grad * 0.125).astype(jnp.bfloat16), kv_grad.astype(jnp.bfloat16)], axis=1
    )
    qkv_w_grad = jnp.dot(normed_one.T, qkv_grad, preferred_element_type=jnp.float32)
    grad_normed_one = jnp.dot(qkv_grad, self_qkv.T, preferred_element_type=jnp.float32)
    grad_hidden, gain_one = norm_one_back(grad_normed_one)
    grad_input = grad_hidden + grad_after_self
    rel_grad = jnp.dot(bucket_pick.T, table_grad.T, precision=highest)
    summed_grads = lax.psum(
        (
            jnp.stack([gain_one, gain_two, gain_three]),
            qkv_w_grad,
            self_out_grad,
            query_w_grad,
            pair_grad,
            cross_out_grad,
            rel_grad,
            router_grad,
        ),
        ("seq", "exp"),
    )
    return (
        layer_out.astype(jnp.bfloat16)[None],
        grad_input[None],
        grad_encoder,
        summed_grads[0],
        summed_grads[1],
        summed_grads[2],
        summed_grads[3],
        summed_grads[4],
        summed_grads[5],
        summed_grads[6],
        summed_grads[7],
        expert_sums[0],
        expert_sums[1],
    )


F32 = jnp.float32
BF16 = jnp.bfloat16
MESH = pl.DeviceIdType.MESH
ANY = pl.BlockSpec(memory_space=pl.ANY)
VMEM = pl.BlockSpec(memory_space=pltpu.VMEM)
SMEM = pl.BlockSpec(memory_space=pltpu.SMEM)
LANES = 128


def nn(a, b):
    return lax.dot_general(a, b, (((1,), (0,)), ((), ())), preferred_element_type=F32)


def nt(a, b):
    return lax.dot_general(a, b, (((1,), (1,)), ((), ())), preferred_element_type=F32)


def tn(a, b):
    return lax.dot_general(a, b, (((0,), (0,)), ((), ())), preferred_element_type=F32)


def rms_scale(a):
    return lax.rsqrt(jnp.mean(a * a, axis=-1, keepdims=True) + epsilon)


def pair_lanes(p):
    return pl.ds(pl.multiple_of(p * LANES, LANES), LANES)


def block_of(index, size):
    return pl.ds(pl.multiple_of(index * size, size), size)


def head_stack(pair):
    lane = lax.broadcasted_iota(jnp.int32, pair.shape, 1)
    zero = jnp.zeros_like(pair)
    return jnp.concatenate([jnp.where(lane < HD, pair, zero), jnp.where(lane < HD, zero, pair)], axis=0)


def head_unstack(both, rows):
    feature = lax.broadcasted_iota(jnp.int32, (both.shape[0], rows), 0)
    return jnp.where(feature < HD, both[:, :rows], both[:, rows:]).T


def pack_slots(value, experts):
    slots = value.shape[0] // experts
    blocks = value.shape[1] // LANES
    return jnp.stack([
        jnp.concatenate(
            [value[e * slots : (e + 1) * slots, b * LANES : (b + 1) * LANES] for b in range(blocks)], axis=0
        )
        for e in range(experts)
    ])


def unpack_slots(packed, slots):
    experts, blocks = packed.shape[0], packed.shape[1] // slots
    wide = packed.astype(F32)
    return jnp.concatenate(
        [
            jnp.concatenate([wide[e, b * slots : (b + 1) * slots] for e in range(experts)], axis=0)
            for b in range(blocks)
        ],
        axis=1,
    )


class Place:
    def __init__(self):
        self.me = lax.axis_index("seq")
        self.core = lax.rem(self.me, 2)
        self.chip = lax.div(self.me, 2)
        self.partner = self.me + 1 - 2 * self.core
        self.x_chip = self.chip + 1 - 2 * lax.rem(self.chip, 2)
        self.y_chip = lax.rem(self.chip + 2, 4)
        self.far_chip = 3 - self.chip
        self.x, self.y, self.far = (c * 2 + self.core for c in (self.x_chip, self.y_chip, self.far_chip))


def enter(devices):
    barrier = pltpu.get_barrier_semaphore()
    for device in devices:
        pl.semaphore_signal(barrier, inc=1, device_id=device, device_id_type=MESH)
    pl.semaphore_wait(barrier, len(devices))


def remote(src, dst, send_sem, recv_sem, device):
    return pltpu.make_async_remote_copy(
        src_ref=src, dst_ref=dst, send_sem=send_sem, recv_sem=recv_sem, device_id=device, device_id_type=MESH
    )


def wait_bytes(sized, sem):
    pltpu.make_async_copy(sized, sized, sem).wait()


class Gather:
    def __init__(self, place, every, rows, send_sem, recv_sems, staged=False):
        self.place, self.every, self.send_sem, self.recv_sems, self.staged = place, every, send_sem, recv_sems, staged
        half = rows // 2 if rows < 32 else -(-rows // 32) * 16
        self.halves = pl.ds(0, half), pl.ds(half, rows - half)

    def copy(self, slot):
        place, every = self.place, self.every
        block, device, sem = (
            lambda: (every.at[place.me], place.partner, 3),
            lambda: (every.at[place.me], place.x, 0),
            lambda: (every.at[place.me], place.y, 1),
            lambda: (every.at[place.x, self.halves[0]], place.y, 2),
            lambda: (every.at[place.y, self.halves[1]], place.x, 2),
            lambda: (every.at[place.x], place.partner, 4 if self.staged else 3),
            lambda: (every.at[place.y], place.partner, 4 if self.staged else 3),
            lambda: (every.at[place.far], place.partner, 5 if self.staged else 3),
        )[slot]()
        return remote(block, block, self.send_sem, self.recv_sems.at[sem], {"seq": device})

    def send(self, *slots):
        for slot in slots:
            self.copy(slot).start()

    def arrived(self, blocks, sem):
        wait_bytes(self.every.at[pl.ds(0, blocks)], self.recv_sems.at[sem])

    def start(self):
        self.send(1, 2, 0)

    def relay(self):
        self.arrived(1, 0)
        self.send(3)
        self.arrived(1, 1)
        self.send(4, 5, 6)

    def relay_far(self):
        self.arrived(1, 2)
        self.send(7)

    def finish(self):
        self.arrived(4, 3)

    def drain(self):
        wait_bytes(self.every.at[pl.ds(0, 7)], self.send_sem)


class Scatter:
    def __init__(self, place, out, pair, turn, side, half, sems):
        self.place, self.out, self.pair, self.turn, self.side, self.half, self.sems = place, out, pair, turn, side, half, sems

    def pair_copy(self):
        return remote(self.out.at[1 - self.place.core], self.pair, self.sems.at[0], self.sems.at[2], {"seq": self.place.partner})

    def send_round(self, src, dst, recv, device):
        remote(src, dst, self.sems.at[1], self.sems.at[recv], {"seq": device}).start()

    def start(self):
        self.pair_copy().start()

    def turn_on(self):
        place = self.place
        self.pair_copy().wait_recv()
        self.out[place.core] = (self.out[place.core].astype(F32) + self.pair[...].astype(F32)).astype(BF16)
        far = self.out.at[place.core, place.far_chip]
        self.send_round(far.at[pl.ds(0, self.half)], self.turn.at[0], 3, place.x)
        self.send_round(far.at[pl.ds(self.half, self.half)], self.turn.at[1], 3, place.y)

    def side_on(self):
        place = self.place
        first, second = pl.ds(0, self.half), pl.ds(self.half, self.half)
        wait_bytes(self.turn, self.sems.at[3])
        at = (place.core, place.y_chip, first)
        self.out[at] = (self.out[at].astype(F32) + self.turn[0].astype(F32)).astype(BF16)
        at = (place.core, place.x_chip, second)
        self.out[at] = (self.out[at].astype(F32) + self.turn[1].astype(F32)).astype(BF16)
        self.send_round(self.out.at[place.core, place.x_chip], self.side.at[0], 4, place.x)
        self.send_round(self.out.at[place.core, place.y_chip], self.side.at[1], 4, place.y)

    def total(self):
        wait_bytes(self.side, self.sems.at[4])
        own = self.out[self.place.core, self.place.chip].astype(F32)
        return own + self.side[0].astype(F32) + self.side[1].astype(F32)

    def drain(self):
        self.pair_copy().wait_send()
        wait_bytes(self.out.at[0, pl.ds(0, 3)], self.sems.at[1])


def expert_peers(exp_index, experts):
    return [lax.rem(exp_index + d, experts) for d in range(1, experts)]


def gelu_parts(hid):
    root, cubic = 0.7978845608028654, 0.044715
    square = hid * hid
    bent = jnp.tanh(root * hid * (1.0 + cubic * square))
    half = 0.5 * (1.0 + bent)
    return hid * half, half + 0.5 * hid * (1.0 - bent * bent) * (root + 3.0 * root * cubic * square)


def rms_back(a, gain, grad):
    scale = rms_scale(a)
    weighted = grad * gain
    da = scale * weighted - a * (scale * scale * scale * jnp.mean(a * weighted, axis=-1, keepdims=True))
    return da, jnp.sum(grad * (a * scale), axis=0, keepdims=True)


def in_two(value):
    high = value.astype(BF16)
    return high, (value - high.astype(F32)).astype(BF16)


GATE_ROWS = 16


def in_three(value):
    high = value.astype(BF16)
    rest = value - high.astype(F32)
    middle = rest.astype(BF16)
    low = (rest - middle.astype(F32)).astype(BF16)
    lane = lax.broadcasted_iota(jnp.int32, (value.shape[0], GATE_ROWS), 1)
    zero = jnp.zeros((value.shape[0], GATE_ROWS), BF16)
    return jnp.where(lane == 0, high, jnp.where(lane == 1, middle, jnp.where(lane == 2, low, zero)))


def slot_gates(parts):
    return jnp.sum(parts, axis=0, keepdims=True).T


class Chunk:
    def __init__(self, place, quarters, peers, src, slots, own, every, sems, gather_sems, local_sem):
        self.place, self.quarters, self.peers = place, quarters, peers
        self.src, self.slots, self.own, self.every, self.sems, self.local_sem = src, slots, own, every, sems, local_sem
        self.over_seq = Gather(place, every, src.shape[0], *gather_sems)

    def local_copy(self):
        return pltpu.make_async_copy(self.own, self.every.at[(self.place.me,) + self.quarters[0]], self.local_sem)

    def over_exp(self, value):
        self.src[...] = value.astype(BF16)
        for d, peer in enumerate(self.peers):
            remote(
                self.src.at[self.quarters[1 + d]], self.slots.at[d], self.sems.at[0], self.sems.at[1], {"exp": peer}
            ).start()

    def back_over_exp(self):
        total = self.src[self.quarters[0]].astype(F32)
        wait_bytes(self.slots, self.sems.at[1])
        for d in range(len(self.peers)):
            total = total + self.slots[d].astype(F32)
        self.own[...] = total.astype(BF16)
        self.local_copy().start()
        target = self.every.at[(self.place.me,) + self.quarters[0]]
        for peer in self.peers:
            remote(self.own, target, self.sems.at[2], self.sems.at[3], {"exp": peer}).start()

    def spread(self):
        self.local_copy().wait()
        wait_bytes(self.slots, self.sems.at[3])
        self.over_seq.start()

    def drain(self):
        wait_bytes(self.slots, self.sems.at[0])
        wait_bytes(self.slots, self.sems.at[2])
        self.over_seq.drain()


def layer_kernel(
    seq_count, capacity,
    x_ref, encoder_hbm, lengths_ref, buckets_ref, routes_ref, gains_ref, qkv_hbm, so_hbm, cq_hbm, ckv_hbm, co_hbm, rel_ref,
    router_ref, g_ref, in_hbm, out_hbm,
    out_hbm_ref, dx_hbm, weights_hbm, dekv_hbm, small_hbm, gin_hbm, gout_hbm, genc_hbm,
    left, kv_all, prob, cross_prob, ekv, w_qkv, w_so, w_cq, w_ckv, w_co, table_ref, x_all, g_all, x_in, g_in, made_back, dx_back,
    q_ref, qc_ref, x3_ref, r1_ref, r2_ref, gates_ref, chosen_ref, slots_ref,
    dr_ref, doc_ref, dqc_ref, dqkv_ref, diag_ref, total_ref,
    e_pair, e_turn, e_side, e_mine, e_exp, dekv, t_pair, t_turn, t_side,
    out_ref, dx_ref, gout_ref, genc_ref, small_out_ref, c_slots, c_own, right, gin_in, small_a, small_b, small_c, small_pair, small_chip, small_exp,
    load_sem, local_sem, store_sem, n_recv, gather_send, gather_recv, trip_sem, enc_sem, enc_exp_sem, term_sem, chunk_sem,
    chunk_send, chunk_recv, right_sem, unit_send, unit_recv, small_sem,
):
    rows, width = x_ref.shape
    span = seq_count * rows
    pairs = width // LANES
    enc_rows = encoder_hbm.shape[0]
    hidden = in_hbm.shape[1]
    own_hidden = hidden // seq_count
    place = Place()
    me = place.me
    mine = lax.axis_index("exp")
    experts = router_ref.shape[0]
    slot_rows = experts * capacity
    peers = expert_peers(mine, experts)
    everyone = [lax.rem(me + d, seq_count) for d in range(1, seq_count)]
    part = width // seq_count
    half_rows, half_lanes = part // 2, width // (experts // 2)
    quarters = [
        (block_of(lax.div(e, experts // 2), half_rows), block_of(lax.rem(e, experts // 2), half_lanes)) for e in [mine] + peers
    ]
    own_lanes = block_of(me, rows)
    near = pl.ds(pl.multiple_of(me * rows, rows), 2 * rows)
    gather = Gather(place, left.at[3], rows, gather_send.at[0], n_recv, staged=True)
    o_gather, n2_gather, oc_gather = (
        Gather(place, left.at[i], rows, gather_send.at[1 + i], gather_recv.at[i]) for i in range(3)
    )
    x_gather = Gather(place, x_all, x_all.shape[1], gather_send.at[4], gather_recv.at[3])
    g_gather = Gather(place, g_all, slot_rows, gather_send.at[5], gather_recv.at[4])

    def load(i, src, dst):
        return pltpu.make_async_copy(src, dst, load_sem.at[i])

    stores = []

    def store(src, dst):
        copy = pltpu.make_async_copy(src, dst, store_sem.at[len(stores)])
        copy.start()
        stores.append(copy)

    def over_exp(src, dst, sems):
        for peer in peers:
            remote(src.at[peer], dst.at[mine], sems.at[0], sems.at[1], {"exp": peer}).start()
        dst[mine] = src[mine]

    def arrive(src, dst, sems):
        wait_bytes(src.at[pl.ds(0, experts - 1)], sems.at[1])

    def sent(src, dst, sems):
        wait_bytes(src.at[pl.ds(0, experts - 1)], sems.at[0])

    load_qkv, load_ckv = load(0, qkv_hbm, w_qkv), load(1, ckv_hbm, w_ckv)
    load_so, load_cq, load_co = load(3, so_hbm, w_so), load(4, cq_hbm, w_cq), load(5, co_hbm, w_co)
    load_qkv.start()
    load_ckv.start()

    def own_slots(e):
        of_all = lax.broadcasted_iota(jnp.int32, (slot_rows, LANES), 0) - e * capacity
        lane = lax.broadcasted_iota(jnp.int32, (slot_rows, LANES), 1)
        return ((of_all == lane) & (lane < capacity)).astype(BF16)

    def self_attention(scores, mask, enc, gs_ref):
        load_enc = load(2, encoder_hbm, enc)
        load_enc.start()
        x = x_ref[...].astype(F32)
        left[3, me] = (x * rms_scale(x) * gains_ref[0:1, :]).astype(BF16)
        enter([{"seq": device} for device in everyone] + [{"exp": peer} for peer in peers])
        gather.start()

        def project(chip):
            both = left[3, pl.ds(chip * 2, 2)].reshape(2 * rows, width)
            kv_all[block_of(chip, 2 * rows), :] = nn(both, w_qkv[:, width:]).astype(BF16)

        chosen = (routes_ref[...] == lax.broadcasted_iota(jnp.int32, (LANES, rows), 0)).astype(F32).T[:, :experts]
        chosen_ref[...] = chosen
        earlier = (
            lax.broadcasted_iota(jnp.int32, (rows, rows), 1) < lax.broadcasted_iota(jnp.int32, (rows, rows), 0)
        ).astype(BF16)
        slot = jnp.sum(nn(earlier, chosen.astype(BF16)) * chosen, axis=1, keepdims=True).astype(jnp.int32)
        kept = slot < capacity
        expert = lax.broadcasted_iota(jnp.int32, (rows, experts), 1).astype(F32)
        route = jnp.sum(chosen * expert, axis=1, keepdims=True).astype(jnp.int32)
        target = jnp.where(kept, route * capacity + slot, -1)
        slots = (lax.broadcasted_iota(jnp.int32, (rows, slot_rows), 1) == target).astype(BF16)
        slots_ref[...] = slots
        gs_ref[...] = pack_slots(tn(slots, g_ref[...]), experts).astype(BF16)
        g_trip = (gs_ref, g_in, trip_sem.at[0])
        over_exp(*g_trip)

        load_qkv.wait()
        q_ref[...] = nn(left[3, me], w_qkv[:, :width]).astype(BF16) * jnp.asarray(0.125, BF16)
        gather.arrived(1, 3)
        project(place.chip)
        load_so.start()
        load_cq.start()
        load_co.start()
        load_ckv.wait()
        load_enc.wait()
        ekv[...] = nn(enc[...], w_ckv[...]).astype(BF16)
        gather.relay()
        pick = (buckets_ref[...] == lax.broadcasted_iota(jnp.int32, (rel_ref.shape[1], LANES), 0)).astype(F32)
        table = jnp.dot(rel_ref[...], pick, precision=highest, preferred_element_type=F32)
        table = table - table[:, LANES - 1 :]
        table_ref[...] = jnp.concatenate([jnp.zeros_like(table), table], axis=1)
        query_pos = me * rows + lax.broadcasted_iota(jnp.int32, (1, rows), 1)
        start = jnp.zeros((1, rows), jnp.int32)
        end = jnp.int32(0)
        for i in range(lengths_ref.shape[1]):
            end = end + lengths_ref[0, i]
            start = jnp.where(end <= query_pos, end, start)
        key_pos = lax.broadcasted_iota(jnp.int32, (span, rows), 0)
        seen = jnp.where((key_pos >= start) & (key_pos <= query_pos), 0.0, masked_out)
        mask[...] = jnp.concatenate([seen, seen], axis=1)
        gather.arrived(2, 4)
        project(place.x_chip)
        project(place.y_chip)
        gather.relay_far()
        arrive(*g_trip)
        g_all[me] = unpack_slots(g_in[...], capacity).astype(BF16)
        g_gather.start()
        gather.arrived(1, 5)
        project(place.far_chip)

        def attend(p, scores):
            lanes = pair_lanes(p)
            q_both = head_stack(q_ref[:, lanes])
            scores[pl.ds(rows, span), :] = nt(kv_all[:, lanes], q_both) + mask[...]
            biases = []
            for h in range(2):
                band = jnp.broadcast_to(table_ref[pl.ds(2 * p + h, 1), :], (2 * rows, 2 * LANES))
                biases.append(pltpu.roll(band, 0, 1, stride=1, stride_axis=0)[:, :rows])
            scores[near, :] = scores[near, :] + jnp.concatenate(biases, axis=1)
            s = scores[pl.ds(rows, span), :]
            weights = jnp.exp(s - jnp.max(s, axis=0, keepdims=True))
            weights = (weights * (1.0 / jnp.sum(weights, axis=0, keepdims=True))).astype(BF16)
            prob[p] = weights
            both = tn(kv_all[:, pair_lanes(pairs + p)], weights)
            left[0, me, :, lanes] = head_unstack(both, rows).astype(BF16)

        @pl.loop(0, pairs, step=2)
        def _(first):
            for side in range(2):
                attend(first + side, scores.at[side])

        sent(*g_trip)

    def rest_forward(xs_ref, made_out, dx_out, slope, w_in, w_out):
        load_in, load_out = load(6, in_hbm, w_in), load(7, out_hbm, w_out)
        load_in.start()
        load_out.start()
        o_gather.start()
        g_gather.relay()
        load_so.wait()
        load_cq.wait()
        load_co.wait()
        r1 = x_ref[...].astype(F32) + nn(left[0, me], w_so[...])
        r1_ref[...] = r1
        n2 = (r1 * rms_scale(r1) * gains_ref[1:2, :]).astype(BF16)
        left[1, me] = n2
        n2_gather.start()
        qc_ref[...] = nn(n2, w_cq[...]).astype(BF16) * jnp.asarray(0.125, BF16)

        @pl.loop(0, pairs, unroll=2)
        def _(p):
            lanes = pair_lanes(p)
            s = nt(ekv[:, lanes], head_stack(qc_ref[:, lanes]))
            weights = jnp.exp(s - jnp.max(s, axis=0, keepdims=True))
            weights = (weights * (1.0 / jnp.sum(weights, axis=0, keepdims=True))).astype(BF16)
            cross_prob[p] = weights
            both = tn(ekv[:, pair_lanes(pairs + p)], weights)
            left[2, me, :, lanes] = head_unstack(both, rows).astype(BF16)

        oc_gather.start()
        r2 = r1_ref[...] + nn(left[2, me], w_co[...])
        r2_ref[...] = r2
        x3 = (r2 * rms_scale(r2) * gains_ref[2:3, :]).astype(BF16)
        x3_ref[...] = x3
        logits = nt(x3, router_ref[...])
        top = jnp.exp(logits - jnp.max(logits, axis=-1, keepdims=True))
        gates = top / jnp.sum(top, axis=-1, keepdims=True)
        gates_ref[...] = gates
        chosen, slots = chosen_ref[...], slots_ref[...]
        kept = jnp.sum(slots.astype(F32), axis=1, keepdims=True)
        gate_used = jnp.sum(gates * chosen, axis=1, keepdims=True) * kept
        packed_rows = x_in.shape[1] - GATE_ROWS
        xs_ref[:, :packed_rows, :] = pack_slots(tn(slots, x3), experts).astype(BF16)
        by_slot = tn(in_three(gate_used), slots).astype(BF16)
        for e in range(experts):
            xs_ref[e, packed_rows:, :] = nn(by_slot, own_slots(e)).astype(BF16)
        x_trip = (xs_ref, x_in, trip_sem.at[1])
        over_exp(*x_trip)

        o_gather.relay()
        load_in.wait()
        load_out.wait()
        arrive(*x_trip)
        x_all[me, :slot_rows, :] = unpack_slots(x_in[:, :packed_rows, :], capacity).astype(BF16)
        gate_parts = jnp.zeros((GATE_ROWS, slot_rows), F32)
        for e in range(experts):
            gate_parts = gate_parts + nt(x_in[e, packed_rows:, :], own_slots(e))
        x_all[me, slot_rows:, :] = jnp.concatenate(
            [gate_parts, jnp.zeros((GATE_ROWS, width - slot_rows), F32)], axis=1
        ).astype(BF16)
        x_gather.start()
        xs = x_all[me, :slot_rows, :]
        made = jnp.zeros(xs.shape, F32)
        for n in range(hidden // width):
            at = slice(n * width, (n + 1) * width)
            value, derivative = gelu_parts(nn(xs, w_in[:, at]))
            slope[:, at] = derivative
            made = made + nn(value.astype(BF16), w_out[at, :])
        made_out[...] = pack_slots(made, experts).astype(BF16)
        made_trip = (made_out, made_back, trip_sem.at[2])
        over_exp(*made_trip)
        n2_gather.relay()
        dm = (g_all[me].astype(F32) * slot_gates(gate_parts)).astype(BF16)
        dx = jnp.zeros(dm.shape, F32)
        for n in range(hidden // width):
            at = slice(n * width, (n + 1) * width)
            dh = (nt(dm, w_out[at, :]) * slope[:, at]).astype(BF16)
            dx = dx + nt(dh, w_in[:, at])
        dx_out[...] = pack_slots(dx, experts).astype(BF16)
        dx_trip = (dx_out, dx_back, trip_sem.at[3])
        over_exp(*dx_trip)
        g_gather.relay_far()
        o_gather.relay_far()
        arrive(*made_trip)
        arrive(*dx_trip)
        for trip in (x_trip, made_trip, dx_trip):
            sent(*trip)

    bf = lambda *n: pltpu.VMEM(n, BF16)
    f32 = lambda *n: pltpu.VMEM(n, F32)
    packed = bf(*g_in.shape)
    pl.run_scoped(self_attention, f32(2, span + rows, 2 * rows), f32(span, 2 * rows), bf(enc_rows, width), packed)
    pl.run_scoped(
        rest_forward, bf(*x_in.shape), packed, packed, f32(slot_rows, hidden), bf(width, hidden), bf(hidden, width)
    )

    enc_part = enc_rows // seq_count
    dekv_gather = Gather(place, dekv_hbm, experts, gather_send.at[6], gather_recv.at[5])
    def backward(e_out, t_out, c_src, turned_ref, ds_ref, gin_out, gin_window, w_ein, w_eout):
        def unit_block(j):
            return block_of(lax.rem(place.chip + j, 4) * 2 + place.core, own_hidden)

        def expert_loads(j):
            return (
                load(8 + 2 * (j % 2), in_hbm.at[:, unit_block(j)], w_ein.at[j % 2]),
                load(9 + 2 * (j % 2), out_hbm.at[unit_block(j), :], w_eout.at[j % 2]),
            )

        def gin_copy(j):
            return remote(
                gin_out.at[j], gin_in.at[:, unit_block(j)], unit_send.at[0], unit_recv.at[0], {"seq": place.partner}
            )

        def expert_units(j):
            for copy in expert_loads(j):
                copy.wait()
            xs = x_all[:, :slot_rows, :].reshape(-1, width)
            dm = g_all[...].reshape(-1, width)
            value, slope = gelu_parts(nn(xs, w_ein[j % 2]))
            if j == 0:
                gout_ref[...] = tn(value.astype(BF16), dm)
                store(gout_ref, gout_hbm)
            dh = (nt(dm, w_eout[j % 2]) * slope).astype(BF16)
            if j < 2:
                for copy in expert_loads(j + 2):
                    copy.start()
            lanes = pl.ds(pl.multiple_of((place.chip + lax.div(place.chip, 2)) * LANES, LANES), 2 * LANES)
            gin_window[...] = tn(x_all[:, :slot_rows, lanes].reshape(-1, 2 * LANES), dh)
            first = lax.rem(place.chip, 2) * (LANES // 2)
            rows_of = lambda core: pl.ds(pl.multiple_of(first + core * part, 32), part)
            gin_in[:, unit_block(j)] = gin_window[rows_of(place.core), :].astype(BF16)
            gin_out[j] = gin_window[rows_of(1 - place.core), :].astype(BF16)
            gin_copy(j).start()

        for copy in expert_loads(0) + expert_loads(1):
            copy.start()
        enc_scatter = Scatter(place, e_out, e_pair, e_turn, e_side, e_turn.shape[1], enc_sem)
        chunks = [
            Chunk(
                place, quarters, peers, c_src.at[i], c_slots.at[i], c_own.at[i], weights_hbm.at[i], chunk_sem.at[i],
                (chunk_send.at[i], chunk_recv.at[i]), local_sem.at[i],
            )
            for i in range(6)
        ]

        def enc_over_exp():
            for d, peer in enumerate(peers):
                remote(e_mine.at[peer], e_exp.at[d], enc_exp_sem.at[0], enc_exp_sem.at[1], {"exp": peer}).start()

        def dekv_over_exp():
            for peer in peers:
                remote(dekv, dekv_hbm.at[me, mine], enc_exp_sem.at[2], enc_exp_sem.at[3], {"exp": peer}).start()

        def dekv_local():
            return pltpu.make_async_copy(dekv, dekv_hbm.at[me, mine], local_sem.at[6])

        def exchange(i, factor):
            turned_ref[i] = factor.T
            for peer in everyone:
                remote(
                    turned_ref.at[i, block_of(peer, part), :], right.at[i, :, own_lanes], right_sem.at[i, 0], right_sem.at[i, 1],
                    {"seq": peer},
                ).start()
            right[i, :, own_lanes] = turned_ref[i, block_of(me, part), :]

        def multiply(i):
            wait_bytes(turned_ref.at[i, pl.ds(0, (seq_count - 1) * part), :], right_sem.at[i, 1])
            chunks[i].over_exp(nn(right[i], left[min(i, 3)].reshape(span, width)))

        slots = slots_ref[...]
        made = nn(slots, unpack_slots(made_back[...], capacity).astype(BF16))
        kept = jnp.sum(slots.astype(F32), axis=1, keepdims=True)
        gates = gates_ref[...]
        chosen = chosen_ref[...]
        picked = jnp.sum(gates * chosen, axis=1, keepdims=True)
        g = g_ref[...].astype(F32)
        out_ref[...] = (r2_ref[...] + (picked * kept) * made).astype(BF16)
        store(out_ref, out_hbm_ref)
        gate_grad = jnp.sum(g * made, axis=1, keepdims=True) * kept
        dl = gates * (chosen * gate_grad - picked * gate_grad)
        dl_high, dl_low = in_two(dl)
        x3 = x3_ref[...]
        small_a[...] = jnp.zeros_like(small_a)
        small_a[4 : 4 + experts, :width] = tn(dl_high, x3) + tn(dl_low, x3)
        dx3 = (
            nn(slots, unpack_slots(dx_back[...], capacity).astype(BF16))
            + nn(dl_high, router_ref[...]) + nn(dl_low, router_ref[...])
        )
        da, dw = rms_back(r2_ref[...], gains_ref[2:3, :], dx3)
        small_a[2:3, :width] = dw
        dr_ref[...] = g + da
        do2 = dr_ref[...].astype(BF16)
        doc_ref[...] = nt(do2, w_co[...]).astype(BF16)
        exchange(2, do2)
        oc_gather.relay()
        n2_gather.relay_far()
        x_gather.relay()

        @pl.loop(0, pairs, unroll=2)
        def _(p):
            lanes, value_lanes = pair_lanes(p), pair_lanes(pairs + p)
            doc_both = head_stack(doc_ref[:, lanes])
            weights = cross_prob[p]
            wide = weights.astype(F32)
            dp = nt(ekv[:, value_lanes], doc_both)
            dc = (wide * (dp - jnp.sum(wide * dp, axis=0, keepdims=True))).astype(BF16)
            dk = nn(dc, head_stack(qc_ref[:, lanes])).astype(BF16).reshape(4, 2, enc_part, LANES)
            dv = nn(weights, doc_both).astype(BF16).reshape(4, 2, enc_part, LANES)
            for k in range(2):
                e_out[k, :, :, lanes] = dk[:, k]
                e_out[k, :, :, value_lanes] = dv[:, k]
            dqc_ref[:, lanes] = (head_unstack(tn(ekv[:, lanes], dc), rows) * 0.125).astype(BF16)

        enc_scatter.start()
        dqc = dqc_ref[...]
        exchange(1, dqc)
        da, dw = rms_back(r1_ref[...], gains_ref[1:2, :], nt(dqc, w_cq[...]))
        small_a[1:2, :width] = dw
        enc_scatter.turn_on()
        dr_ref[...] = dr_ref[...] + da
        do1 = dr_ref[...].astype(BF16)
        doc_ref[...] = nt(do1, w_so[...]).astype(BF16)
        exchange(0, do1)
        oc_gather.relay_far()
        n2_gather.finish()
        o_gather.finish()

        ds_ref[pl.ds(0, rows), :] = jnp.zeros((rows, 2 * rows), BF16)
        flip = (
            lax.broadcasted_iota(jnp.int32, (2 * rows, 2 * rows), 0)
            + lax.broadcasted_iota(jnp.int32, (2 * rows, 2 * rows), 1)
            == 2 * rows - 1
        ).astype(BF16)

        def terms(p):
            return Scatter(place, t_out.at[p], t_pair.at[p], t_turn.at[p], t_side.at[p], rows // 2, term_sem.at[p])

        def pair_back(p):
            lanes, value_lanes = pair_lanes(p), pair_lanes(pairs + p)
            do_both = head_stack(doc_ref[:, lanes])
            weights = prob[p]
            wide = weights.astype(F32)
            dp = nt(kv_all[:, value_lanes], do_both)
            ds_wide = wide * (dp - jnp.sum(wide * dp, axis=0, keepdims=True))
            ds = ds_wide.astype(BF16)
            ds_ref[pl.ds(rows, span), :] = ds
            total_ref[pl.ds(p, 1), :] = jnp.sum(ds.astype(F32), axis=0, keepdims=True)
            dk = nn(ds, head_stack(q_ref[:, lanes])).astype(BF16).reshape(4, 2, rows, LANES)
            dv = nn(weights, do_both).astype(BF16).reshape(4, 2, rows, LANES)
            for k in range(2):
                t_out[p, k, :, :, :LANES] = dk[:, k]
                t_out[p, k, :, :, LANES:] = dv[:, k]
            terms(p).start()
            dqkv_ref[:, lanes] = (head_unstack(tn(kv_all[:, lanes], ds), rows) * 0.125).astype(BF16)
            turned = nn(flip, ds_ref[near, :])
            for h in range(2):
                one = turned[:, h * rows : (h + 1) * rows]
                one = jnp.concatenate([one, jnp.zeros_like(one)], axis=1)
                one = pltpu.roll(one, 1, 1, stride=1, stride_axis=0)
                diag_ref[pl.ds(2 * p + h, 1), :] = jnp.sum(one, axis=0, keepdims=True)

        def own_terms(p):
            total = terms(p).total()
            dqkv_ref[:, pair_lanes(pairs + p)] = total[:, :LANES].astype(BF16)
            dqkv_ref[:, pair_lanes(2 * pairs + p)] = total[:, LANES:].astype(BF16)

        @pl.loop(0, pairs)
        def _(t):
            pair_back(t)
            @pl.when(t >= 1)
            def _():
                terms(jnp.maximum(t - 1, 0)).turn_on()

            @pl.when(t >= 3)
            def _():
                terms(jnp.maximum(t - 3, 0)).side_on()

            @pl.when(t >= 5)
            def _():
                own_terms(jnp.maximum(t - 5, 0))

            @pl.when(t == 0)
            def _():
                oc_gather.finish()
                multiply(2)

            @pl.when(t == 1)
            def _():
                x_gather.relay_far()
                enc_scatter.side_on()

            @pl.when(t == 2)
            def _():
                multiply(1)

            @pl.when(t == 5)
            def _():
                chunks[2].back_over_exp()

            @pl.when(t == 3)
            def _():
                multiply(0)

            @pl.when(t == 4)
            def _():
                e_mine[...] = enc_scatter.total().astype(BF16).reshape(e_mine.shape)
                enc_over_exp()


        last = pairs - 1
        terms(last).turn_on()
        terms(last - 2).side_on()
        exchange(3, dqkv_ref[:, :width])
        own_terms(last - 4)
        terms(last - 1).side_on()
        own_terms(last - 3)
        terms(last).side_on()
        own_terms(last - 2)
        chunks[1].back_over_exp()
        chunks[0].back_over_exp()
        own_terms(last - 1)
        wait_bytes(e_exp, enc_exp_sem.at[1])
        total = e_mine[mine].astype(F32)
        for d in range(experts - 1):
            total = total + e_exp[d].astype(F32)
        dekv[...] = total.astype(BF16)
        dekv_local().start()
        multiply(3)
        dekv_over_exp()
        own_terms(last)

        dqkv = dqkv_ref[...]
        exchange(4, dqkv[:, width : 2 * width])
        exchange(5, dqkv[:, 2 * width :])

        x = x_ref[...].astype(F32)
        da, dw = rms_back(x, gains_ref[0:1, :], nt(dqkv, w_qkv[...]))
        small_a[0:1, :width] = dw
        dx_ref[...] = dr_ref[...] + da
        store(dx_ref, dx_hbm)
        heads = 2 * pairs
        table = diag_ref[:, 2 * rows - LANES :]
        totals = total_ref[...]
        first = jnp.sum(totals[:, :rows], axis=1, keepdims=True)
        second = jnp.sum(totals[:, rows:], axis=1, keepdims=True)
        head = lax.broadcasted_iota(jnp.int32, (heads, pairs), 0)
        pair = lax.broadcasted_iota(jnp.int32, (heads, pairs), 1)
        spread = lambda odd, v: jnp.dot(
            (head == 2 * pair + odd).astype(F32), v, precision=highest, preferred_element_type=F32
        )
        whole = spread(0, jnp.broadcast_to(first, (pairs, LANES))) + spread(1, jnp.broadcast_to(second, (pairs, LANES)))
        rest = whole - jnp.sum(table, axis=1, keepdims=True)
        lane = lax.broadcasted_iota(jnp.int32, table.shape, 1)
        table = table + jnp.where(lane == LANES - 1, rest, 0.0)
        bucket = lax.broadcasted_iota(jnp.int32, (LANES, LANES), 0)
        pick = (buckets_ref[...] == bucket).astype(F32)
        by_bucket = lax.dot_general(table, pick, (((1,), (1,)), ((), ())), precision=highest, preferred_element_type=F32)
        small_a[0:8, width : width + LANES] = by_bucket[0:8]
        small_a[0 : heads - 8, width + LANES :] = by_bucket[8:heads]
        s_pair = remote(small_a, small_pair, small_sem.at[0], small_sem.at[1], {"seq": place.partner})
        s_pair.start()

        x_gather.finish()
        g_gather.finish()
        g_gather.drain()
        parts = x_all[:, slot_rows:, : 2 * LANES].astype(F32).reshape(seq_count * GATE_ROWS, 2 * LANES).T
        for n in range(seq_count):
            gate = sum(parts[:slot_rows, n * GATE_ROWS + i : n * GATE_ROWS + i + 1] for i in range(3))
            g_all[n] = (g_all[n].astype(F32) * gate).astype(BF16)
        expert_units(0)
        chunks[3].back_over_exp()
        multiply(4)
        multiply(5)
        chunks[2].spread()
        chunks[1].spread()
        chunks[0].spread()
        dekv_local().wait()
        wait_bytes(e_exp, enc_exp_sem.at[3])
        dekv_gather.start()
        s_pair.wait_recv()
        small_b[...] = small_a[...] + small_pair[...]
        for d, device in enumerate((place.x, place.y, place.far)):
            remote(small_b, small_chip.at[d], small_sem.at[2], small_sem.at[3], {"seq": device}).start()
        expert_units(1)
        chunks[3].spread()
        chunks[4].back_over_exp()
        expert_units(2)
        chunks[5].back_over_exp()
        genc_ref[...] = nt(dekv[...], w_ckv[...])
        store(genc_ref, genc_hbm)
        wait_bytes(small_chip, small_sem.at[3])
        small_c[...] = small_b[...] + small_chip[0] + small_chip[1] + small_chip[2]
        for d, peer in enumerate(peers):
            remote(small_c, small_exp.at[d], small_sem.at[4], small_sem.at[5], {"exp": peer}).start()
        chunks[4].spread()
        chunks[2].over_seq.relay()
        chunks[1].over_seq.relay()
        chunks[5].spread()
        chunks[0].over_seq.relay()
        dekv_gather.relay()
        chunks[3].over_seq.relay()
        expert_units(3)
        wait_bytes(e_exp, enc_exp_sem.at[0])
        wait_bytes(e_exp, enc_exp_sem.at[2])
        s_pair.wait_send()
        wait_bytes(small_chip, small_sem.at[2])
        for i in range(6):
            wait_bytes(turned_ref.at[i, pl.ds(0, (seq_count - 1) * part), :], right_sem.at[i, 0])
        for each in (gather, o_gather, n2_gather, oc_gather, x_gather, enc_scatter):
            each.drain()

        @pl.loop(0, pairs)
        def _(p):
            terms(p).drain()

        chunks[4].over_seq.relay()
        wait_bytes(gin_out, unit_recv.at[0])
        store(gin_in, gin_hbm)
        wait_bytes(small_exp, small_sem.at[5])
        total = small_c[...]
        for d in range(experts - 1):
            total = total + small_exp[d]
        small_out_ref[...] = total
        store(small_out_ref, small_hbm)
        chunks[5].over_seq.relay()
        for i in (2, 1, 0):
            chunks[i].over_seq.relay_far()
        dekv_gather.relay_far()
        for i in (3, 4, 5):
            chunks[i].over_seq.relay_far()
        for chunk in chunks:
            chunk.over_seq.finish()
        dekv_gather.finish()

        wait_bytes(gin_out, unit_send.at[0])
        wait_bytes(small_exp, small_sem.at[4])
        dekv_gather.drain()
        for chunk in chunks:
            chunk.drain()
        for copy in stores:
            copy.wait()

    pl.run_scoped(
        backward, bf(2, 4, enc_part, 2 * width), bf(pairs, 2, 4, rows, 2 * LANES), bf(6, part, width), bf(6, width, rows),
        bf(span + rows, 2 * rows), bf(4, part, own_hidden), f32(2 * LANES, own_hidden), bf(2, width, own_hidden), bf(2, own_hidden, width),
    )


def layer_call(seq_count, capacity, x, encoder, lengths, buckets, routes, gains, qkv, so, cq, ckv, co, rel, router, g, w_in,
               w_out):
    rows, width = x.shape
    span = seq_count * rows
    pairs = width // LANES
    heads = 2 * pairs
    enc_rows = encoder.shape[0]
    experts = router.shape[0]
    slot_rows = experts * capacity
    part = width // seq_count
    enc_part = enc_rows // seq_count
    own_enc = enc_part // experts
    hidden = w_in.shape[1]
    z = experts - 1
    quarter = (part // 2, width // (experts // 2))
    small = (8, width + 2 * LANES)
    packed = (experts, capacity * pairs, LANES)
    shape = jax.ShapeDtypeStruct
    dma = lambda *n: pltpu.SemaphoreType.DMA(n)
    bf = lambda *n: pltpu.VMEM(n, BF16)
    f32 = lambda *n: pltpu.VMEM(n, F32)
    wide = bf(rows, width)
    return pl.pallas_call(
        functools.partial(layer_kernel, seq_count, capacity),
        out_shape=(
            shape((rows, width), BF16), shape((rows, width), F32), shape((6, seq_count, part, width), BF16),
            shape((seq_count, experts, own_enc, 2 * width), BF16), shape(small, F32), shape((part, hidden), BF16),
            shape((hidden // seq_count, width), F32), shape((own_enc, width), F32),
        ),
        in_specs=[VMEM, ANY, SMEM, VMEM, VMEM, VMEM, ANY, ANY, ANY, ANY, ANY, VMEM, VMEM, VMEM, ANY, ANY],
        out_specs=(ANY,) * 8,
        scratch_shapes=[
            bf(4, seq_count, rows, width), bf(span, 2 * width), bf(pairs, span, 2 * rows), bf(pairs, enc_rows, 2 * rows),
            bf(enc_rows, 2 * width), bf(*qkv.shape), bf(*so.shape), bf(*cq.shape), bf(*ckv.shape), bf(*co.shape),
            f32(heads, 2 * LANES), bf(seq_count, slot_rows + GATE_ROWS, width), bf(seq_count, slot_rows, width),
            bf(experts, capacity * pairs + GATE_ROWS, LANES), bf(*packed), bf(*packed), bf(*packed),
            wide, wide, wide, f32(rows, width), f32(rows, width), f32(rows, experts), f32(rows, experts), bf(rows, slot_rows),
            f32(rows, width), wide, wide, bf(rows, 3 * width), f32(heads, 2 * rows), f32(pairs, 2 * rows),
            bf(4, enc_part, 2 * width), bf(2, enc_part // 2, 2 * width), bf(2, enc_part, 2 * width),
            bf(experts, own_enc, 2 * width), bf(z, own_enc, 2 * width), bf(own_enc, 2 * width),
            bf(pairs, 4, rows, 2 * LANES), bf(pairs, 2, rows // 2, 2 * LANES), bf(pairs, 2, rows, 2 * LANES),
            wide, f32(rows, width), f32(hidden // seq_count, width), f32(own_enc, width), f32(*small),
            bf(6, z, *quarter), bf(6, *quarter), bf(6, part, span), bf(part, hidden),
            f32(*small), f32(*small), f32(*small), f32(*small), f32(3, *small), f32(z, *small),
            dma(12), dma(7), dma(6), dma(6), dma(7), dma(6, 4), dma(4, 2), dma(5), dma(4), dma(pairs, 5), dma(6, 4),
            dma(6), dma(6, 4), dma(6, 2), dma(1), dma(1), dma(6),
        ],
        compiler_params=pltpu.CompilerParams(collective_id=0, has_side_effects=True, vmem_limit_bytes=63 << 20),
        name="layer",
    )(x, encoder, lengths, buckets, routes, gains, qkv, so, cq, ckv, co, rel, router, g, w_in, w_out)


def finish_kernel(
    experts, weights_hbm, dekv_hbm, enc_hbm, small_ref, layer_hbm, dx_hbm, genc_hbm, gin_ref, gout_hbm,
    layer_out, dx_out, genc_out, gains_out, qkv_hbm, so_hbm, cq_hbm, ckv_hbm, co_hbm, rel_out, router_out, gin_out, gout_out,
    weights, dekv, enc, squares, qkv, ckv, layer, dx, genc, gin, gout, load_sem, sem,
):
    seq_count, part, width = weights.shape[1:]
    loads = [pltpu.make_async_copy(weights_hbm.at[i], weights.at[i], load_sem.at[i]) for i in range(6)] + [
        pltpu.make_async_copy(dekv_hbm, dekv, load_sem.at[6]), pltpu.make_async_copy(enc_hbm, enc, load_sem.at[7])
    ]
    through = ((gout_hbm, gout, gout_out), (dx_hbm, dx, dx_out), (layer_hbm, layer, layer_out), (genc_hbm, genc, genc_out))
    loads += [pltpu.make_async_copy(src, held, load_sem.at[8 + i]) for i, (src, held, _) in enumerate(through)]
    for load in loads[8:] + loads[6:8] + loads[:6]:
        load.start()
    copies = []

    def store(src, dst):
        copy = pltpu.make_async_copy(src, dst, sem.at[len(copies)])
        copy.start()
        copies.append(copy)

    gains_out[...] = small_ref[0:3, :width]
    router_out[...] = small_ref[4 : 4 + experts, :width]
    heads, buckets = rel_out.shape
    rel_out[0:8, :] = small_ref[0:8, width : width + buckets]
    rel_out[8:heads, :] = small_ref[0 : heads - 8, width + LANES : width + LANES + buckets]
    gin[...] = gin_ref[...].astype(F32)
    store(gin, gin_out)

    for i, (_, held, out) in enumerate(through):
        loads[8 + i].wait()
        store(held, out)
    loads[6].wait()
    loads[7].wait()
    for n in range(2):
        at = slice(n * width, (n + 1) * width)
        ckv[:, at] = tn(enc[...], dekv[...].reshape(enc.shape[0], 2 * width)[:, at])
        store(ckv.at[:, at], ckv_hbm.at[:, at])
    def turn(i, target, at):
        loads[i].wait()
        for block in range(width // LANES):
            rows = slice(block * LANES, (block + 1) * LANES)
            target[:, at + block * LANES : at + (block + 1) * LANES] = (
                weights[i].reshape(seq_count * part, width)[rows, :].T.astype(F32)
            )

    for i, out in enumerate((so_hbm, cq_hbm, co_hbm)):
        turn(i, squares.at[i], 0)
        store(squares.at[i], out)
    for i in range(3):
        at = slice(i * width, (i + 1) * width)
        turn(3 + i, qkv, i * width)
        store(qkv.at[:, at], qkv_hbm.at[:, at])
    for copy in copies:
        copy.wait()


def finish_call(heads, buckets, experts, weights, dekv, enc, small, layer, dx, genc, gin, gout):
    seq_count, part, width = weights.shape[1:]
    shape = jax.ShapeDtypeStruct
    f32 = lambda *n: shape(n, F32)
    return pl.pallas_call(
        functools.partial(finish_kernel, experts),
        out_shape=(
            shape(layer.shape, BF16), f32(*dx.shape), f32(*genc.shape), f32(3, width), f32(width, 3 * width), f32(width, width),
            f32(width, width), f32(width, 2 * width), f32(width, width), f32(heads, buckets), f32(experts, width),
            f32(*gin.shape), f32(*gout.shape),
        ),
        in_specs=[ANY, ANY, ANY, VMEM, ANY, ANY, ANY, VMEM, ANY],
        out_specs=(ANY, ANY, ANY, VMEM, ANY, ANY, ANY, ANY, ANY, VMEM, VMEM, ANY, ANY),
        scratch_shapes=[
            pltpu.VMEM(weights.shape, BF16), pltpu.VMEM(dekv.shape, BF16), pltpu.VMEM(enc.shape, BF16),
            pltpu.VMEM((3, width, width), F32), pltpu.VMEM((width, 3 * width), F32), pltpu.VMEM((width, 2 * width), F32),
            pltpu.VMEM(layer.shape, BF16), pltpu.VMEM(dx.shape, F32), pltpu.VMEM(genc.shape, F32), pltpu.VMEM(gin.shape, F32),
            pltpu.VMEM(gout.shape, F32), pltpu.SemaphoreType.DMA((13,)), pltpu.SemaphoreType.DMA((13,)),
        ],
        compiler_params=pltpu.CompilerParams(vmem_limit_bytes=60 << 20),
        name="finish",
    )(weights, dekv, enc, small, layer, dx, genc, gin, gout)


def fused(inputs, encoder, lengths, buckets, routes, norm_gains, self_qkv, self_out, cross_q, cross_kv, cross_out,
          rel_bias, router, expert_in, expert_out, cotangent):
    seq_count = lax.axis_size("seq")
    rows = inputs.shape[1]
    experts = router.shape[1]
    capacity = 5 * rows // (4 * experts)
    (layer_out, grad_input, weights, dekv, small, gin, gout, grad_encoder) = layer_call(
        seq_count, capacity, inputs[0], encoder, lengths, buckets[None, :], routes.reshape(1, rows), norm_gains, self_qkv,
        self_out, cross_q, cross_kv, cross_out, rel_bias.T, router.T, cotangent[0], expert_in[0], expert_out[0])
    (layer_out, grad_input, grad_encoder, gains, g_qkv, g_so, g_cq, g_ckv, g_co, g_rel, g_router, gin, gout) = finish_call(
        rel_bias.shape[1], rel_bias.shape[0], experts, weights, dekv, encoder, small, layer_out, grad_input, grad_encoder, gin,
        gout)
    return (layer_out[None], grad_input[None], grad_encoder, gains, g_qkv, g_so, g_cq, g_ckv, g_co, g_rel.T, g_router.T,
            gin[None], gout[None])


def on_device(*operands):
    if lax.axis_size("seq") == 8 and lax.axis_size("exp") == 4 and operands[0].shape[1] == 128:
        return fused(*operands)
    return streamed(*operands)


def solution(mesh):
    in_specs = (
        P("exp", "seq", None),
        P(),
        P("exp", None),
        P(),
        P("exp", "seq", None),
        P(),
        P(),
        P(),
        P(),
        P(),
        P(),
        P(),
        P(),
        P("exp", None, None),
        P("exp", None, None),
        P("exp", "seq", None),
    )
    out_specs = (
        P("exp", "seq", None),
        P("exp", "seq", None),
        P(("seq", "exp"), None),
        P(),
        P(),
        P(),
        P(),
        P(),
        P(),
        P(),
        P(),
        P("exp", "seq", None),
        P("exp", "seq", None),
    )
    return jax.shard_map(
        on_device, mesh=mesh, in_specs=in_specs, out_specs=out_specs, check_vma=False
    )
```

```python
import functools
import math

import jax
import jax.numpy as jnp
from jax import lax
from jax.experimental import pallas as pl
from jax.experimental.pallas import tpu as pltpu
from jax.sharding import PartitionSpec as P

H = 12
HD = 64


epsilon = 1e-06
masked_out = -1e30
highest = lax.Precision.HIGHEST


def rms_norm(value, gain):
    return value * lax.rsqrt(jnp.mean(value * value, axis=-1, keepdims=True) + epsilon) * gain


def split_heads(value):
    return value.reshape(value.shape[0], H, HD)


def doc_index(positions, doc_ends):
    return jnp.sum((positions[:, None] >= doc_ends[None, :]).astype(jnp.int32), axis=1)


def band_pick(offset_gap, query_rows, key_rows, table_span):
    band_len = query_rows + key_rows + 1
    column = jnp.arange(band_len, dtype=jnp.int32)
    distance = jnp.clip(offset_gap + query_rows - column, 0, table_span - 1)
    return (distance[:, None] == jnp.arange(table_span, dtype=jnp.int32)[None, :]).astype(
        jnp.float32
    )


def relative_bias(table, offset_gap, query_rows, key_rows):
    head_count = table.shape[0]
    band_len = query_rows + key_rows + 1
    band = jnp.dot(
        table, band_pick(offset_gap, query_rows, key_rows, table.shape[1]).T, precision=highest
    )
    tiled = jnp.broadcast_to(band[:, None, :], (head_count, query_rows, band_len)).reshape(
        head_count, query_rows * band_len
    )
    skewed = tiled[:, : query_rows * (band_len - 1)].reshape(head_count, query_rows, band_len - 1)
    return skewed[:, :, query_rows : query_rows + key_rows]


def table_terms(score_grads, offset_gap, table_span):
    head_count, query_rows, key_rows = score_grads.shape
    band_len = query_rows + key_rows + 1
    placed = jnp.pad(score_grads.astype(jnp.float32), ((0, 0), (0, 0), (query_rows, 0)))
    flat = jnp.pad(
        placed.reshape(head_count, query_rows * (band_len - 1)), ((0, 0), (0, query_rows))
    )
    diagonal_sums = jnp.sum(flat.reshape(head_count, query_rows, band_len), axis=1)
    return jnp.dot(
        diagonal_sums, band_pick(offset_gap, query_rows, key_rows, table_span), precision=highest
    )


def self_scores(queries, query_start, keys_part, key_start, doc_ends, table):
    query_rows = queries.shape[0]
    key_rows = keys_part.shape[0]
    query_pos = query_start + jnp.arange(query_rows, dtype=jnp.int32)
    key_pos = key_start + jnp.arange(key_rows, dtype=jnp.int32)
    offset_gap = query_start - key_start
    raw_scores = (
        jnp.einsum(
            "qhd,khd->hqk",
            split_heads(queries),
            split_heads(keys_part),
            preferred_element_type=jnp.float32,
        )
        * 0.125
    )
    allowed = (key_pos[None, :] <= query_pos[:, None]) & (
        doc_index(key_pos, doc_ends)[None, :] == doc_index(query_pos, doc_ends)[:, None]
    )
    scores = jnp.where(
        allowed[None],
        raw_scores + relative_bias(table, offset_gap, query_rows, key_rows),
        masked_out,
    )
    return (scores, allowed[None], offset_gap)


def over_blocks(step, running, pieces):
    rows_total = pieces[0].shape[0]
    block_rows = math.gcd(rows_total, 512)
    block_count = rows_total // block_rows
    stacked = tuple(
        (member.reshape(block_count, block_rows, *member.shape[1:]) for member in pieces)
    )

    def scan_step(inner_running, block_input):
        block_id, members = block_input
        return (step(inner_running, members, block_id * block_rows), None)

    result, ignored = lax.scan(
        scan_step, running, (jnp.arange(block_count, dtype=jnp.int32), stacked)
    )
    return result


def streamed(
    inputs,
    encoder,
    lengths,
    buckets,
    routes,
    norm_gains,
    self_qkv,
    self_out,
    cross_q,
    cross_kv,
    cross_out,
    rel_bias,
    router,
    expert_in,
    expert_out,
    cotangent,
):
    hidden = inputs[0].astype(jnp.float32)
    rows_dev = hidden.shape[0]
    model_width = hidden.shape[1]
    seq_count = lax.axis_size("seq")
    seq_index = lax.axis_index("seq")
    own_start = seq_index * rows_dev
    doc_ends = jnp.cumsum(lengths[0])
    bucket_pick = (
        buckets[:, None] == jnp.arange(rel_bias.shape[0], dtype=jnp.int32)[None, :]
    ).astype(jnp.float32)
    table = jnp.dot(bucket_pick, rel_bias, precision=highest).T
    normed_one, norm_one_back = jax.vjp(rms_norm, hidden, norm_gains[0])
    normed_one = normed_one.astype(jnp.bfloat16)
    qkv_all = jnp.dot(normed_one, self_qkv, preferred_element_type=jnp.float32).astype(jnp.bfloat16)
    queries = qkv_all[:, :model_width]
    keys_own = qkv_all[:, model_width : 2 * model_width]
    values_own = qkv_all[:, 2 * model_width :]

    def forward_step(running, pieces, key_start):
        top_old, denominator, summed = running
        keys_part, values_part = pieces
        scores, allowed, offset_gap = self_scores(
            queries, own_start, keys_part, key_start, doc_ends, table
        )
        top_new = jnp.maximum(top_old, jnp.max(scores, axis=-1))
        weights_raw = jnp.where(allowed, jnp.exp(scores - top_new[..., None]), 0.0)
        rescale = jnp.exp(top_old - top_new)
        denominator = denominator * rescale + jnp.sum(weights_raw, axis=-1)
        summed = summed * rescale[..., None] + jnp.einsum(
            "hqk,khd->hqd",
            weights_raw.astype(jnp.bfloat16),
            split_heads(values_part),
            preferred_element_type=jnp.float32,
        )
        return (top_new, denominator, summed)

    start_state = (
        jnp.full((H, rows_dev), masked_out, jnp.float32),
        jnp.zeros((H, rows_dev), jnp.float32),
        jnp.zeros((H, rows_dev, HD), jnp.float32),
    )
    top_score, denominator, summed = over_blocks(
        forward_step,
        start_state,
        (
            lax.all_gather(keys_own, "seq", axis=0, tiled=True),
            lax.all_gather(values_own, "seq", axis=0, tiled=True),
        ),
    )
    log_total = top_score + jnp.log(denominator)
    attended_full = (
        (summed / denominator[..., None]).transpose(1, 0, 2).reshape(rows_dev, model_width)
    )
    attended = attended_full.astype(jnp.bfloat16)
    after_self = hidden + jnp.dot(attended, self_out, preferred_element_type=jnp.float32)
    enc_kv = jnp.dot(encoder, cross_kv, preferred_element_type=jnp.float32).astype(jnp.bfloat16)
    cross_keys = split_heads(enc_kv[:, :model_width])
    cross_values = split_heads(enc_kv[:, model_width:])
    normed_two, norm_two_back = jax.vjp(rms_norm, after_self, norm_gains[1])
    normed_two = normed_two.astype(jnp.bfloat16)
    cross_queries = jnp.dot(normed_two, cross_q, preferred_element_type=jnp.float32).astype(
        jnp.bfloat16
    )
    cross_scores = (
        jnp.einsum(
            "qhd,khd->hqk",
            split_heads(cross_queries),
            cross_keys,
            preferred_element_type=jnp.float32,
        )
        * 0.125
    )
    cross_raw = jnp.exp(cross_scores - jnp.max(cross_scores, axis=-1, keepdims=True))
    cross_prob = cross_raw / jnp.sum(cross_raw, axis=-1, keepdims=True)
    cross_prob_low = cross_prob.astype(jnp.bfloat16)
    cross_att = (
        jnp.einsum("hqk,khd->qhd", cross_prob_low, cross_values, preferred_element_type=jnp.float32)
        .reshape(rows_dev, model_width)
        .astype(jnp.bfloat16)
    )
    after_cross = after_self + jnp.dot(cross_att, cross_out, preferred_element_type=jnp.float32)
    normed_three, norm_three_back = jax.vjp(rms_norm, after_cross, norm_gains[2])
    routed_in = normed_three.astype(jnp.bfloat16)
    gates = jax.nn.softmax(jnp.dot(routed_in, router, preferred_element_type=jnp.float32), axis=-1)
    expert_total = router.shape[1]
    local_experts = expert_in.shape[0]
    capacity = 5 * rows_dev // (4 * expert_total)
    route_ids = routes[0, :, 0]
    chosen = route_ids[:, None] == jnp.arange(expert_total, dtype=jnp.int32)[None, :]
    slots = jnp.sum(jnp.where(chosen, jnp.cumsum(chosen.astype(jnp.int32), axis=0), 0), axis=1) - 1
    kept = slots < capacity
    picked_gate = jnp.sum(jnp.where(chosen, gates, 0.0), axis=1)
    gate_used = picked_gate * kept.astype(jnp.float32)
    target = jnp.where(kept, route_ids * capacity + slots, -1)
    dispatch = (
        jnp.arange(expert_total * capacity, dtype=jnp.int32)[:, None] == target[None, :]
    ).astype(jnp.bfloat16)
    outgoing = (
        jnp.dot(dispatch, routed_in, preferred_element_type=jnp.float32)
        .astype(jnp.bfloat16)
        .reshape(expert_total, capacity, model_width)
    )
    arrived = lax.all_to_all(outgoing, "exp", split_axis=0, concat_axis=0, tiled=True).reshape(
        -1, local_experts, capacity, model_width
    )
    inner_pre = jnp.einsum("secd,edf->secf", arrived, expert_in, preferred_element_type=jnp.float32)
    active = jax.nn.gelu(inner_pre, approximate=True).astype(jnp.bfloat16)
    produced = jnp.einsum(
        "secf,efd->secd", active, expert_out, preferred_element_type=jnp.float32
    ).astype(jnp.bfloat16)
    returned = lax.all_to_all(
        produced.reshape(-1, capacity, model_width), "exp", split_axis=0, concat_axis=0, tiled=True
    )
    expert_rows = jnp.dot(
        dispatch.T, returned.reshape(-1, model_width), preferred_element_type=jnp.float32
    )
    layer_out = after_cross + gate_used[:, None] * expert_rows
    upstream = cotangent[0].astype(jnp.float32)
    made_grad = (upstream * gate_used[:, None]).astype(jnp.bfloat16)
    sent_grad = (
        jnp.dot(dispatch, made_grad, preferred_element_type=jnp.float32)
        .astype(jnp.bfloat16)
        .reshape(expert_total, capacity, model_width)
    )
    grad_arrived = lax.all_to_all(
        sent_grad, "exp", split_axis=0, concat_axis=0, tiled=True
    ).reshape(-1, local_experts, capacity, model_width)
    inner_again = jnp.einsum(
        "secd,edf->secf", arrived, expert_in, preferred_element_type=jnp.float32
    )
    active_again, gelu_back = jax.vjp(
        lambda value: jax.nn.gelu(value, approximate=True), inner_again
    )
    grad_out_w = jnp.einsum(
        "secf,secd->efd",
        active_again.astype(jnp.bfloat16),
        grad_arrived,
        preferred_element_type=jnp.float32,
    )
    grad_active = jnp.einsum(
        "secd,efd->secf", grad_arrived, expert_out, preferred_element_type=jnp.float32
    )
    grad_inner = gelu_back(grad_active)[0].astype(jnp.bfloat16)
    grad_in_w = jnp.einsum(
        "secd,secf->edf", arrived, grad_inner, preferred_element_type=jnp.float32
    )
    grad_sent_x = jnp.einsum(
        "secf,edf->secd", grad_inner, expert_in, preferred_element_type=jnp.float32
    ).astype(jnp.bfloat16)
    grad_back = lax.all_to_all(
        grad_sent_x.reshape(-1, capacity, model_width),
        "exp",
        split_axis=0,
        concat_axis=0,
        tiled=True,
    )
    grad_routed = jnp.dot(
        dispatch.T, grad_back.reshape(-1, model_width), preferred_element_type=jnp.float32
    )
    expert_sums = (
        lax.psum_scatter(grad_in_w, "seq", scatter_dimension=1, tiled=True),
        lax.psum_scatter(grad_out_w, "seq", scatter_dimension=1, tiled=True),
    )
    gate_grad = jnp.sum(upstream * expert_rows, axis=1) * kept.astype(jnp.float32)
    logit_grad = gates * (
        jnp.where(chosen, gate_grad[:, None], 0.0) - (picked_gate * gate_grad)[:, None]
    )
    router_grad = jnp.dot(routed_in.astype(jnp.float32).T, logit_grad, precision=highest)
    grad_normed_three = (
        jnp.dot(logit_grad, router.astype(jnp.float32).T, precision=highest) + grad_routed
    )
    grad_after_cross, gain_three = norm_three_back(grad_normed_three)
    grad_after_cross = grad_after_cross + upstream
    cross_branch = grad_after_cross.astype(jnp.bfloat16)
    cross_out_grad = jnp.dot(cross_att.T, cross_branch, preferred_element_type=jnp.float32)
    grad_cross_att = split_heads(
        jnp.dot(cross_branch, cross_out.T, preferred_element_type=jnp.float32).astype(jnp.bfloat16)
    )
    cross_prob_grad = jnp.einsum(
        "qhd,khd->hqk", grad_cross_att, cross_values, preferred_element_type=jnp.float32
    )
    cross_delta = jnp.sum(cross_prob * cross_prob_grad, axis=-1, keepdims=True)
    cross_score_grad = (cross_prob * (cross_prob_grad - cross_delta)).astype(jnp.bfloat16)
    grad_cross_queries = (
        (
            jnp.einsum(
                "hqk,khd->qhd", cross_score_grad, cross_keys, preferred_element_type=jnp.float32
            )
            * 0.125
        )
        .reshape(rows_dev, model_width)
        .astype(jnp.bfloat16)
    )
    grad_enc_keys = (
        jnp.einsum(
            "hqk,qhd->khd",
            cross_score_grad,
            split_heads(cross_queries),
            preferred_element_type=jnp.float32,
        )
        * 0.125
    )
    grad_enc_values = jnp.einsum(
        "hqk,qhd->khd", cross_prob_low, grad_cross_att, preferred_element_type=jnp.float32
    )
    enc_terms = jnp.concatenate(
        [grad_enc_keys.reshape(-1, model_width), grad_enc_values.reshape(-1, model_width)], axis=1
    )
    enc_grad_rows = lax.psum_scatter(
        enc_terms, ("seq", "exp"), scatter_dimension=0, tiled=True
    ).astype(jnp.bfloat16)
    enc_count = enc_grad_rows.shape[0]
    flat_index = seq_index * lax.axis_size("exp") + lax.axis_index("exp")
    own_enc = lax.dynamic_slice_in_dim(encoder, flat_index * enc_count, enc_count, 0)
    grad_encoder = jnp.dot(enc_grad_rows, cross_kv.T, preferred_element_type=jnp.float32)
    pair_grad = jnp.dot(own_enc.T, enc_grad_rows, preferred_element_type=jnp.float32)
    query_w_grad = jnp.dot(normed_two.T, grad_cross_queries, preferred_element_type=jnp.float32)
    grad_normed_two = jnp.dot(grad_cross_queries, cross_q.T, preferred_element_type=jnp.float32)
    grad_after_self, gain_two = norm_two_back(grad_normed_two)
    grad_after_self = grad_after_self + grad_after_cross
    self_branch = grad_after_self.astype(jnp.bfloat16)
    self_out_grad = jnp.dot(attended.T, self_branch, preferred_element_type=jnp.float32)
    grad_attended = jnp.dot(self_branch, self_out.T, preferred_element_type=jnp.float32).astype(
        jnp.bfloat16
    )
    row_delta = jnp.sum(
        split_heads(grad_attended).astype(jnp.float32) * split_heads(attended_full), axis=-1
    ).T
    stats_all = (
        lax.all_gather(log_total.T, "seq", axis=0, tiled=True),
        lax.all_gather(row_delta.T, "seq", axis=0, tiled=True),
    )

    def query_step(running, pieces, query_start):
        kv_grad, query_grads, table_grad = running
        queries_part, grads_part = pieces
        piece_rows = queries_part.shape[0]
        lse_part = lax.dynamic_slice_in_dim(stats_all[0], query_start, piece_rows, 0).T
        delta_part = lax.dynamic_slice_in_dim(stats_all[1], query_start, piece_rows, 0).T
        scores, allowed, offset_gap = self_scores(
            queries_part, query_start, keys_own, own_start, doc_ends, table
        )
        probability = jnp.where(allowed, jnp.exp(scores - lse_part[..., None]), 0.0)
        prob_grad = jnp.einsum(
            "qhd,khd->hqk",
            split_heads(grads_part),
            split_heads(values_own),
            preferred_element_type=jnp.float32,
        )
        score_grad = (probability * (prob_grad - delta_part[..., None])).astype(jnp.bfloat16)
        key_grad = (
            jnp.einsum(
                "hqk,qhd->khd",
                score_grad,
                split_heads(queries_part),
                preferred_element_type=jnp.float32,
            )
            * 0.125
        )
        value_grad = jnp.einsum(
            "hqk,qhd->khd",
            probability.astype(jnp.bfloat16),
            split_heads(grads_part),
            preferred_element_type=jnp.float32,
        )
        kv_grad = kv_grad + jnp.concatenate(
            [key_grad.reshape(-1, model_width), value_grad.reshape(-1, model_width)], axis=1
        )
        table_grad = table_grad + table_terms(score_grad, offset_gap, table.shape[1])
        query_part_grad = jnp.einsum(
            "hqk,khd->qhd", score_grad, split_heads(keys_own), preferred_element_type=jnp.float32
        ).reshape(piece_rows, model_width)
        current = lax.dynamic_slice_in_dim(query_grads, query_start, piece_rows, 0)
        query_grads = lax.dynamic_update_slice_in_dim(
            query_grads, current + query_part_grad, query_start, 0
        )
        return (kv_grad, query_grads, table_grad)

    back_start = (
        jnp.zeros((rows_dev, 2 * model_width), jnp.float32),
        jnp.zeros((seq_count * rows_dev, model_width), jnp.float32),
        jnp.zeros(table.shape, jnp.float32),
    )
    kv_grad, query_buffer, table_grad = over_blocks(
        query_step,
        back_start,
        (
            lax.all_gather(queries, "seq", axis=0, tiled=True),
            lax.all_gather(grad_attended, "seq", axis=0, tiled=True),
        ),
    )
    query_grad = lax.psum_scatter(query_buffer, "seq", scatter_dimension=0, tiled=True)
    qkv_grad = jnp.concatenate(
        [(query_grad * 0.125).astype(jnp.bfloat16), kv_grad.astype(jnp.bfloat16)], axis=1
    )
    qkv_w_grad = jnp.dot(normed_one.T, qkv_grad, preferred_element_type=jnp.float32)
    grad_normed_one = jnp.dot(qkv_grad, self_qkv.T, preferred_element_type=jnp.float32)
    grad_hidden, gain_one = norm_one_back(grad_normed_one)
    grad_input = grad_hidden + grad_after_self
    rel_grad = jnp.dot(bucket_pick.T, table_grad.T, precision=highest)
    summed_grads = lax.psum(
        (
            jnp.stack([gain_one, gain_two, gain_three]),
            qkv_w_grad,
            self_out_grad,
            query_w_grad,
            pair_grad,
            cross_out_grad,
            rel_grad,
            router_grad,
        ),
        ("seq", "exp"),
    )
    return (
        layer_out.astype(jnp.bfloat16)[None],
        grad_input[None],
        grad_encoder,
        summed_grads[0],
        summed_grads[1],
        summed_grads[2],
        summed_grads[3],
        summed_grads[4],
        summed_grads[5],
        summed_grads[6],
        summed_grads[7],
        expert_sums[0],
        expert_sums[1],
    )


F32 = jnp.float32
BF16 = jnp.bfloat16
MESH = pl.DeviceIdType.MESH
ANY = pl.BlockSpec(memory_space=pl.ANY)
VMEM = pl.BlockSpec(memory_space=pltpu.VMEM)
SMEM = pl.BlockSpec(memory_space=pltpu.SMEM)
LANES = 128


def nn(a, b):
    return lax.dot_general(a, b, (((1,), (0,)), ((), ())), preferred_element_type=F32)


def nt(a, b):
    return lax.dot_general(a, b, (((1,), (1,)), ((), ())), preferred_element_type=F32)


def tn(a, b):
    return lax.dot_general(a, b, (((0,), (0,)), ((), ())), preferred_element_type=F32)


def rms_scale(a):
    return lax.rsqrt(jnp.mean(a * a, axis=-1, keepdims=True) + epsilon)


def pair_lanes(p):
    return pl.ds(pl.multiple_of(p * LANES, LANES), LANES)


def block_of(index, size):
    return pl.ds(pl.multiple_of(index * size, size), size)


def head_stack(pair):
    lane = lax.broadcasted_iota(jnp.int32, pair.shape, 1)
    zero = jnp.zeros_like(pair)
    return jnp.concatenate([jnp.where(lane < HD, pair, zero), jnp.where(lane < HD, zero, pair)], axis=0)


def head_unstack(both, rows):
    feature = lax.broadcasted_iota(jnp.int32, (both.shape[0], rows), 0)
    return jnp.where(feature < HD, both[:, :rows], both[:, rows:]).T


def pack_slots(value, experts):
    slots = value.shape[0] // experts
    blocks = value.shape[1] // LANES
    return jnp.stack([
        jnp.concatenate(
            [value[e * slots : (e + 1) * slots, b * LANES : (b + 1) * LANES] for b in range(blocks)], axis=0
        )
        for e in range(experts)
    ])


def unpack_slots(packed, slots):
    experts, blocks = packed.shape[0], packed.shape[1] // slots
    wide = packed.astype(F32)
    return jnp.concatenate(
        [
            jnp.concatenate([wide[e, b * slots : (b + 1) * slots] for e in range(experts)], axis=0)
            for b in range(blocks)
        ],
        axis=1,
    )


class Place:
    def __init__(self):
        self.me = lax.axis_index("seq")
        self.core = lax.rem(self.me, 2)
        self.chip = lax.div(self.me, 2)
        self.partner = self.me + 1 - 2 * self.core
        self.x_chip = self.chip + 1 - 2 * lax.rem(self.chip, 2)
        self.y_chip = lax.rem(self.chip + 2, 4)
        self.far_chip = 3 - self.chip
        self.x, self.y, self.far = (c * 2 + self.core for c in (self.x_chip, self.y_chip, self.far_chip))


def enter(devices):
    barrier = pltpu.get_barrier_semaphore()
    for device in devices:
        pl.semaphore_signal(barrier, inc=1, device_id=device, device_id_type=MESH)
    pl.semaphore_wait(barrier, len(devices))


def remote(src, dst, send_sem, recv_sem, device):
    return pltpu.make_async_remote_copy(
        src_ref=src, dst_ref=dst, send_sem=send_sem, recv_sem=recv_sem, device_id=device, device_id_type=MESH
    )


def wait_bytes(sized, sem):
    pltpu.make_async_copy(sized, sized, sem).wait()


class Gather:
    def __init__(self, place, every, rows, send_sem, recv_sems, staged=False):
        self.place, self.every, self.send_sem, self.recv_sems, self.staged = place, every, send_sem, recv_sems, staged
        half = rows // 2 if rows < 32 else -(-rows // 32) * 16
        self.halves = pl.ds(0, half), pl.ds(half, rows - half)

    def copy(self, slot):
        place, every = self.place, self.every
        block, device, sem = (
            lambda: (every.at[place.me], place.partner, 3),
            lambda: (every.at[place.me], place.x, 0),
            lambda: (every.at[place.me], place.y, 1),
            lambda: (every.at[place.x, self.halves[0]], place.y, 2),
            lambda: (every.at[place.y, self.halves[1]], place.x, 2),
            lambda: (every.at[place.x], place.partner, 4 if self.staged else 3),
            lambda: (every.at[place.y], place.partner, 4 if self.staged else 3),
            lambda: (every.at[place.far], place.partner, 5 if self.staged else 3),
        )[slot]()
        return remote(block, block, self.send_sem, self.recv_sems.at[sem], {"seq": device})

    def send(self, *slots):
        for slot in slots:
            self.copy(slot).start()

    def arrived(self, blocks, sem):
        wait_bytes(self.every.at[pl.ds(0, blocks)], self.recv_sems.at[sem])

    def start(self):
        self.send(1, 2, 0)

    def relay(self):
        self.arrived(1, 0)
        self.send(3)
        self.arrived(1, 1)
        self.send(4, 5, 6)

    def relay_far(self):
        self.arrived(1, 2)
        self.send(7)

    def finish(self):
        self.arrived(4, 3)

    def drain(self):
        wait_bytes(self.every.at[pl.ds(0, 7)], self.send_sem)


class Scatter:
    def __init__(self, place, out, pair, turn, side, half, sems):
        self.place, self.out, self.pair, self.turn, self.side, self.half, self.sems = place, out, pair, turn, side, half, sems

    def pair_copy(self):
        return remote(self.out.at[1 - self.place.core], self.pair, self.sems.at[0], self.sems.at[2], {"seq": self.place.partner})

    def send_round(self, src, dst, recv, device):
        remote(src, dst, self.sems.at[1], self.sems.at[recv], {"seq": device}).start()

    def start(self):
        self.pair_copy().start()

    def turn_on(self):
        place = self.place
        self.pair_copy().wait_recv()
        self.out[place.core] = (self.out[place.core].astype(F32) + self.pair[...].astype(F32)).astype(BF16)
        far = self.out.at[place.core, place.far_chip]
        self.send_round(far.at[pl.ds(0, self.half)], self.turn.at[0], 3, place.x)
        self.send_round(far.at[pl.ds(self.half, self.half)], self.turn.at[1], 3, place.y)

    def side_on(self):
        place = self.place
        first, second = pl.ds(0, self.half), pl.ds(self.half, self.half)
        wait_bytes(self.turn, self.sems.at[3])
        at = (place.core, place.y_chip, first)
        self.out[at] = (self.out[at].astype(F32) + self.turn[0].astype(F32)).astype(BF16)
        at = (place.core, place.x_chip, second)
        self.out[at] = (self.out[at].astype(F32) + self.turn[1].astype(F32)).astype(BF16)
        self.send_round(self.out.at[place.core, place.x_chip], self.side.at[0], 4, place.x)
        self.send_round(self.out.at[place.core, place.y_chip], self.side.at[1], 4, place.y)

    def total(self):
        wait_bytes(self.side, self.sems.at[4])
        own = self.out[self.place.core, self.place.chip].astype(F32)
        return own + self.side[0].astype(F32) + self.side[1].astype(F32)

    def drain(self):
        self.pair_copy().wait_send()
        wait_bytes(self.out.at[0, pl.ds(0, 3)], self.sems.at[1])


def expert_peers(exp_index, experts):
    return [lax.rem(exp_index + d, experts) for d in range(1, experts)]


def gelu_parts(hid):
    root, cubic = 0.7978845608028654, 0.044715
    square = hid * hid
    bent = jnp.tanh(root * hid * (1.0 + cubic * square))
    half = 0.5 * (1.0 + bent)
    return hid * half, half + 0.5 * hid * (1.0 - bent * bent) * (root + 3.0 * root * cubic * square)


def rms_back(a, gain, grad):
    scale = rms_scale(a)
    weighted = grad * gain
    da = scale * weighted - a * (scale * scale * scale * jnp.mean(a * weighted, axis=-1, keepdims=True))
    return da, jnp.sum(grad * (a * scale), axis=0, keepdims=True)


def in_two(value):
    high = value.astype(BF16)
    return high, (value - high.astype(F32)).astype(BF16)


GATE_ROWS = 16


def in_three(value):
    high = value.astype(BF16)
    rest = value - high.astype(F32)
    middle = rest.astype(BF16)
    low = (rest - middle.astype(F32)).astype(BF16)
    lane = lax.broadcasted_iota(jnp.int32, (value.shape[0], GATE_ROWS), 1)
    zero = jnp.zeros((value.shape[0], GATE_ROWS), BF16)
    return jnp.where(lane == 0, high, jnp.where(lane == 1, middle, jnp.where(lane == 2, low, zero)))


def slot_gates(parts):
    return jnp.sum(parts, axis=0, keepdims=True).T


class Chunk:
    def __init__(self, place, quarters, peers, src, slots, own, every, sems, gather_sems, local_sem):
        self.place, self.quarters, self.peers = place, quarters, peers
        self.src, self.slots, self.own, self.every, self.sems, self.local_sem = src, slots, own, every, sems, local_sem
        self.over_seq = Gather(place, every, src.shape[0], *gather_sems)

    def local_copy(self):
        return pltpu.make_async_copy(self.own, self.every.at[(self.place.me,) + self.quarters[0]], self.local_sem)

    def over_exp(self, value):
        self.src[...] = value.astype(BF16)
        for d, peer in enumerate(self.peers):
            remote(
                self.src.at[self.quarters[1 + d]], self.slots.at[d], self.sems.at[0], self.sems.at[1], {"exp": peer}
            ).start()

    def back_over_exp(self):
        total = self.src[self.quarters[0]].astype(F32)
        wait_bytes(self.slots, self.sems.at[1])
        for d in range(len(self.peers)):
            total = total + self.slots[d].astype(F32)
        self.own[...] = total.astype(BF16)
        self.local_copy().start()
        target = self.every.at[(self.place.me,) + self.quarters[0]]
        for peer in self.peers:
            remote(self.own, target, self.sems.at[2], self.sems.at[3], {"exp": peer}).start()

    def spread(self):
        self.local_copy().wait()
        wait_bytes(self.slots, self.sems.at[3])
        self.over_seq.start()

    def relay(self):
        self.over_seq.relay()

    def relay_far(self):
        self.over_seq.relay_far()

    def drain(self):
        wait_bytes(self.slots, self.sems.at[0])
        wait_bytes(self.slots, self.sems.at[2])
        self.over_seq.drain()


class WideChunk(Chunk):
    def quarter(self, device, first=0, rows=None):
        at, lanes = self.quarters[0]
        rows = at.size if rows is None else rows
        return self.every.at[device, pl.ds(pl.multiple_of(at.start + first, 16), rows), lanes]

    def same_core(self):
        return [c * 2 + self.place.core for c in range(4)]

    def send_quarter(self, block, sem, device):
        remote(block, block, self.sems.at[4], self.over_seq.recv_sems.at[sem], {"seq": device}).start()

    def back_over_exp(self):
        total = self.src[self.quarters[0]].astype(F32)
        wait_bytes(self.slots, self.sems.at[1])
        for d in range(len(self.peers)):
            total = total + self.slots[d].astype(F32)
        self.own[...] = total.astype(BF16)
        self.local_copy().start()

    def spread(self):
        place = self.place
        self.local_copy().wait()
        for sem, device in enumerate((place.x, place.y)):
            self.send_quarter(self.quarter(place.me), sem, device)

    def relay(self):
        place = self.place
        rows = self.quarters[0][0].size
        half = -(-rows // 32) * 16
        wait_bytes(self.own, self.over_seq.recv_sems.at[0])
        self.send_quarter(self.quarter(place.x, 0, half), 2, place.y)
        wait_bytes(self.own, self.over_seq.recv_sems.at[1])
        self.send_quarter(self.quarter(place.y, half, rows - half), 2, place.x)

    def cross(self):
        wait_bytes(self.own, self.over_seq.recv_sems.at[2])
        for peer in self.peers:
            for device in self.same_core():
                block = self.quarter(device)
                remote(block, block, self.sems.at[2], self.sems.at[3], {"exp": peer}).start()

    def relay_far(self):
        wait_bytes(self.every.at[pl.ds(0, len(self.peers))], self.sems.at[3])
        for device in self.same_core():
            block = self.every.at[device]
            remote(block, block, self.over_seq.send_sem, self.over_seq.recv_sems.at[3], {"seq": self.place.partner}).start()

    def drain(self):
        wait_bytes(self.slots, self.sems.at[0])
        wait_bytes(self.every.at[pl.ds(0, len(self.peers))], self.sems.at[2])
        wait_bytes(self.slots, self.sems.at[4])
        wait_bytes(self.every.at[pl.ds(0, 4)], self.over_seq.send_sem)


def layer_kernel(
    seq_count, capacity,
    x_ref, encoder_hbm, lengths_ref, buckets_ref, routes_ref, gains_ref, qkv_hbm, so_hbm, cq_hbm, ckv_hbm, co_hbm, rel_ref,
    router_ref, g_ref, in_hbm, out_hbm,
    out_hbm_ref, dx_hbm, weights_hbm, dekv_hbm, small_hbm, gin_hbm, gout_hbm, genc_hbm,
    left, kv_all, prob, cross_prob, ekv, w_qkv, w_so, w_cq, w_ckv, w_co, table_ref, x_all, g_all, x_in, g_in, made_back, dx_back,
    q_ref, qc_ref, x3_ref, r1_ref, r2_ref, gates_ref, chosen_ref, slots_ref,
    dr_ref, doc_ref, dqc_ref, dqkv_ref, diag_ref, total_ref,
    e_pair, e_turn, e_side, e_mine, e_exp, dekv, t_pair, t_turn, t_side,
    out_ref, dx_ref, gout_ref, genc_ref, small_out_ref, c_slots, c_own, right, gin_in, small_a, small_b, small_c, small_pair, small_chip, small_exp,
    load_sem, local_sem, store_sem, n_recv, gather_send, gather_recv, trip_sem, enc_sem, enc_exp_sem, term_sem, chunk_sem,
    chunk_send, chunk_recv, right_sem, unit_send, unit_recv, small_sem,
):
    rows, width = x_ref.shape
    span = seq_count * rows
    pairs = width // LANES
    enc_rows = encoder_hbm.shape[0]
    hidden = in_hbm.shape[1]
    own_hidden = hidden // seq_count
    place = Place()
    me = place.me
    mine = lax.axis_index("exp")
    experts = router_ref.shape[0]
    slot_rows = experts * capacity
    peers = expert_peers(mine, experts)
    everyone = [lax.rem(me + d, seq_count) for d in range(1, seq_count)]
    part = width // seq_count
    half_rows, half_lanes = part // 2, width // (experts // 2)
    quarters = [
        (block_of(lax.div(e, experts // 2), half_rows), block_of(lax.rem(e, experts // 2), half_lanes)) for e in [mine] + peers
    ]
    own_lanes = block_of(me, rows)
    near = pl.ds(pl.multiple_of(me * rows, rows), 2 * rows)
    gather = Gather(place, left.at[3], rows, gather_send.at[0], n_recv, staged=True)
    o_gather, n2_gather, oc_gather = (
        Gather(place, left.at[i], rows, gather_send.at[1 + i], gather_recv.at[i]) for i in range(3)
    )
    x_gather = Gather(place, x_all, x_all.shape[1], gather_send.at[4], gather_recv.at[3])
    g_gather = Gather(place, g_all, slot_rows, gather_send.at[5], gather_recv.at[4])

    def load(i, src, dst):
        return pltpu.make_async_copy(src, dst, load_sem.at[i])

    stores = []

    def store(src, dst):
        copy = pltpu.make_async_copy(src, dst, store_sem.at[len(stores)])
        copy.start()
        stores.append(copy)

    def over_exp(src, dst, sems):
        for peer in peers:
            remote(src.at[peer], dst.at[mine], sems.at[0], sems.at[1], {"exp": peer}).start()
        dst[mine] = src[mine]

    def arrive(src, dst, sems):
        wait_bytes(src.at[pl.ds(0, experts - 1)], sems.at[1])

    def sent(src, dst, sems):
        wait_bytes(src.at[pl.ds(0, experts - 1)], sems.at[0])

    load_qkv, load_ckv = load(0, qkv_hbm, w_qkv), load(1, ckv_hbm, w_ckv)
    load_so, load_cq, load_co = load(3, so_hbm, w_so), load(4, cq_hbm, w_cq), load(5, co_hbm, w_co)
    load_qkv.start()
    load_ckv.start()

    def own_slots(e):
        of_all = lax.broadcasted_iota(jnp.int32, (slot_rows, LANES), 0) - e * capacity
        lane = lax.broadcasted_iota(jnp.int32, (slot_rows, LANES), 1)
        return ((of_all == lane) & (lane < capacity)).astype(BF16)

    def self_attention(scores, mask, enc, gs_ref):
        load_enc = load(2, encoder_hbm, enc)
        load_enc.start()
        x = x_ref[...].astype(F32)
        left[3, me] = (x * rms_scale(x) * gains_ref[0:1, :]).astype(BF16)
        enter([{"seq": device} for device in everyone] + [{"exp": peer} for peer in peers])
        gather.start()

        def project(chip):
            both = left[3, pl.ds(chip * 2, 2)].reshape(2 * rows, width)
            kv_all[block_of(chip, 2 * rows), :] = nn(both, w_qkv[:, width:]).astype(BF16)

        chosen = (routes_ref[...] == lax.broadcasted_iota(jnp.int32, (LANES, rows), 0)).astype(F32).T[:, :experts]
        chosen_ref[...] = chosen
        earlier = (
            lax.broadcasted_iota(jnp.int32, (rows, rows), 1) < lax.broadcasted_iota(jnp.int32, (rows, rows), 0)
        ).astype(BF16)
        slot = jnp.sum(nn(earlier, chosen.astype(BF16)) * chosen, axis=1, keepdims=True).astype(jnp.int32)
        kept = slot < capacity
        expert = lax.broadcasted_iota(jnp.int32, (rows, experts), 1).astype(F32)
        route = jnp.sum(chosen * expert, axis=1, keepdims=True).astype(jnp.int32)
        target = jnp.where(kept, route * capacity + slot, -1)
        slots = (lax.broadcasted_iota(jnp.int32, (rows, slot_rows), 1) == target).astype(BF16)
        slots_ref[...] = slots
        gs_ref[...] = pack_slots(tn(slots, g_ref[...]), experts).astype(BF16)
        g_trip = (gs_ref, g_in, trip_sem.at[0])
        over_exp(*g_trip)

        load_qkv.wait()
        q_ref[...] = nn(left[3, me], w_qkv[:, :width]).astype(BF16) * jnp.asarray(0.125, BF16)
        gather.arrived(1, 3)
        project(place.chip)
        load_so.start()
        load_cq.start()
        load_co.start()
        load_ckv.wait()
        load_enc.wait()
        ekv[...] = nn(enc[...], w_ckv[...]).astype(BF16)
        gather.relay()
        pick = (buckets_ref[...] == lax.broadcasted_iota(jnp.int32, (rel_ref.shape[1], LANES), 0)).astype(F32)
        table = jnp.dot(rel_ref[...], pick, precision=highest, preferred_element_type=F32)
        table = table - table[:, LANES - 1 :]
        table_ref[...] = jnp.concatenate([jnp.zeros_like(table), table], axis=1)
        query_pos = me * rows + lax.broadcasted_iota(jnp.int32, (1, rows), 1)
        start = jnp.zeros((1, rows), jnp.int32)
        end = jnp.int32(0)
        for i in range(lengths_ref.shape[1]):
            end = end + lengths_ref[0, i]
            start = jnp.where(end <= query_pos, end, start)
        key_pos = lax.broadcasted_iota(jnp.int32, (span, rows), 0)
        seen = jnp.where((key_pos >= start) & (key_pos <= query_pos), 0.0, masked_out)
        mask[...] = jnp.concatenate([seen, seen], axis=1)
        gather.arrived(2, 4)
        project(place.x_chip)
        project(place.y_chip)
        gather.relay_far()
        arrive(*g_trip)
        g_all[me] = unpack_slots(g_in[...], capacity).astype(BF16)
        g_gather.start()
        gather.arrived(1, 5)
        project(place.far_chip)

        def attend(p, scores):
            lanes = pair_lanes(p)
            q_both = head_stack(q_ref[:, lanes])
            scores[pl.ds(rows, span), :] = nt(kv_all[:, lanes], q_both) + mask[...]
            biases = []
            for h in range(2):
                band = jnp.broadcast_to(table_ref[pl.ds(2 * p + h, 1), :], (2 * rows, 2 * LANES))
                biases.append(pltpu.roll(band, 0, 1, stride=1, stride_axis=0)[:, :rows])
            scores[near, :] = scores[near, :] + jnp.concatenate(biases, axis=1)
            s = scores[pl.ds(rows, span), :]
            weights = jnp.exp(s - jnp.max(s, axis=0, keepdims=True))
            weights = (weights * (1.0 / jnp.sum(weights, axis=0, keepdims=True))).astype(BF16)
            prob[p] = weights
            both = tn(kv_all[:, pair_lanes(pairs + p)], weights)
            left[0, me, :, lanes] = head_unstack(both, rows).astype(BF16)

        @pl.loop(0, pairs, step=2)
        def _(first):
            for side in range(2):
                attend(first + side, scores.at[side])

        sent(*g_trip)

    def rest_forward(xs_ref, made_out, dx_out, slope, w_in, w_out):
        load_in, load_out = load(6, in_hbm, w_in), load(7, out_hbm, w_out)
        load_in.start()
        load_out.start()
        o_gather.start()
        g_gather.relay()
        load_so.wait()
        load_cq.wait()
        load_co.wait()
        r1 = x_ref[...].astype(F32) + nn(left[0, me], w_so[...])
        r1_ref[...] = r1
        n2 = (r1 * rms_scale(r1) * gains_ref[1:2, :]).astype(BF16)
        left[1, me] = n2
        n2_gather.start()
        qc_ref[...] = nn(n2, w_cq[...]).astype(BF16) * jnp.asarray(0.125, BF16)

        @pl.loop(0, pairs, unroll=2)
        def _(p):
            lanes = pair_lanes(p)
            s = nt(ekv[:, lanes], head_stack(qc_ref[:, lanes]))
            weights = jnp.exp(s - jnp.max(s, axis=0, keepdims=True))
            weights = (weights * (1.0 / jnp.sum(weights, axis=0, keepdims=True))).astype(BF16)
            cross_prob[p] = weights
            both = tn(ekv[:, pair_lanes(pairs + p)], weights)
            left[2, me, :, lanes] = head_unstack(both, rows).astype(BF16)

        oc_gather.start()
        r2 = r1_ref[...] + nn(left[2, me], w_co[...])
        r2_ref[...] = r2
        x3 = (r2 * rms_scale(r2) * gains_ref[2:3, :]).astype(BF16)
        x3_ref[...] = x3
        logits = nt(x3, router_ref[...])
        top = jnp.exp(logits - jnp.max(logits, axis=-1, keepdims=True))
        gates = top / jnp.sum(top, axis=-1, keepdims=True)
        gates_ref[...] = gates
        chosen, slots = chosen_ref[...], slots_ref[...]
        kept = jnp.sum(slots.astype(F32), axis=1, keepdims=True)
        gate_used = jnp.sum(gates * chosen, axis=1, keepdims=True) * kept
        packed_rows = x_in.shape[1] - GATE_ROWS
        xs_ref[:, :packed_rows, :] = pack_slots(tn(slots, x3), experts).astype(BF16)
        by_slot = tn(in_three(gate_used), slots).astype(BF16)
        for e in range(experts):
            xs_ref[e, packed_rows:, :] = nn(by_slot, own_slots(e)).astype(BF16)
        x_trip = (xs_ref, x_in, trip_sem.at[1])
        over_exp(*x_trip)

        o_gather.relay()
        load_in.wait()
        load_out.wait()
        arrive(*x_trip)
        x_all[me, :slot_rows, :] = unpack_slots(x_in[:, :packed_rows, :], capacity).astype(BF16)
        gate_parts = jnp.zeros((GATE_ROWS, slot_rows), F32)
        for e in range(experts):
            gate_parts = gate_parts + nt(x_in[e, packed_rows:, :], own_slots(e))
        x_all[me, slot_rows:, :] = jnp.concatenate(
            [gate_parts, jnp.zeros((GATE_ROWS, width - slot_rows), F32)], axis=1
        ).astype(BF16)
        x_gather.start()
        xs = x_all[me, :slot_rows, :]
        made = jnp.zeros(xs.shape, F32)
        for n in range(hidden // width):
            at = slice(n * width, (n + 1) * width)
            value, derivative = gelu_parts(nn(xs, w_in[:, at]))
            slope[:, at] = derivative
            made = made + nn(value.astype(BF16), w_out[at, :])
        made_out[...] = pack_slots(made, experts).astype(BF16)
        made_trip = (made_out, made_back, trip_sem.at[2])
        over_exp(*made_trip)
        n2_gather.relay()
        dm = (g_all[me].astype(F32) * slot_gates(gate_parts)).astype(BF16)
        dx = jnp.zeros(dm.shape, F32)
        for n in range(hidden // width):
            at = slice(n * width, (n + 1) * width)
            dh = (nt(dm, w_out[at, :]) * slope[:, at]).astype(BF16)
            dx = dx + nt(dh, w_in[:, at])
        dx_out[...] = pack_slots(dx, experts).astype(BF16)
        dx_trip = (dx_out, dx_back, trip_sem.at[3])
        over_exp(*dx_trip)
        g_gather.relay_far()
        o_gather.relay_far()
        arrive(*made_trip)
        arrive(*dx_trip)
        for trip in (x_trip, made_trip, dx_trip):
            sent(*trip)

    bf = lambda *n: pltpu.VMEM(n, BF16)
    f32 = lambda *n: pltpu.VMEM(n, F32)
    packed = bf(*g_in.shape)
    pl.run_scoped(self_attention, f32(2, span + rows, 2 * rows), f32(span, 2 * rows), bf(enc_rows, width), packed)
    pl.run_scoped(
        rest_forward, bf(*x_in.shape), packed, packed, f32(slot_rows, hidden), bf(width, hidden), bf(hidden, width)
    )

    enc_part = enc_rows // seq_count
    dekv_gather = Gather(place, dekv_hbm, experts, gather_send.at[6], gather_recv.at[5])
    def backward(e_out, t_out, c_src, turned_ref, ds_ref, gin_out, gin_window, w_ein, w_eout):
        def unit_block(j):
            return block_of(lax.rem(place.chip + j, 4) * 2 + place.core, own_hidden)

        def expert_loads(j):
            return (
                load(8 + 2 * (j % 2), in_hbm.at[:, unit_block(j)], w_ein.at[j % 2]),
                load(9 + 2 * (j % 2), out_hbm.at[unit_block(j), :], w_eout.at[j % 2]),
            )

        def gin_copy(j):
            return remote(
                gin_out.at[j], gin_in.at[:, unit_block(j)], unit_send.at[0], unit_recv.at[0], {"seq": place.partner}
            )

        def expert_units(j):
            for copy in expert_loads(j):
                copy.wait()
            xs = x_all[:, :slot_rows, :].reshape(-1, width)
            dm = g_all[...].reshape(-1, width)
            value, slope = gelu_parts(nn(xs, w_ein[j % 2]))
            if j == 0:
                gout_ref[...] = tn(value.astype(BF16), dm)
                store(gout_ref, gout_hbm)
            dh = (nt(dm, w_eout[j % 2]) * slope).astype(BF16)
            if j < 2:
                for copy in expert_loads(j + 2):
                    copy.start()
            lanes = pl.ds(pl.multiple_of((place.chip + lax.div(place.chip, 2)) * LANES, LANES), 2 * LANES)
            gin_window[...] = tn(x_all[:, :slot_rows, lanes].reshape(-1, 2 * LANES), dh)
            first = lax.rem(place.chip, 2) * (LANES // 2)
            rows_of = lambda core: pl.ds(pl.multiple_of(first + core * part, 32), part)
            gin_in[:, unit_block(j)] = gin_window[rows_of(place.core), :].astype(BF16)
            gin_out[j] = gin_window[rows_of(1 - place.core), :].astype(BF16)
            gin_copy(j).start()

        for copy in expert_loads(0) + expert_loads(1):
            copy.start()
        enc_scatter = Scatter(place, e_out, e_pair, e_turn, e_side, e_turn.shape[1], enc_sem)
        wide = (2,)
        chunks = [
            (WideChunk if i in wide else Chunk)(
                place, quarters, peers, c_src.at[i], c_slots.at[i], c_own.at[i], weights_hbm.at[i], chunk_sem.at[i],
                (chunk_send.at[i], chunk_recv.at[i]), local_sem.at[i],
            )
            for i in range(6)
        ]

        def enc_over_exp():
            for d, peer in enumerate(peers):
                remote(e_mine.at[peer], e_exp.at[d], enc_exp_sem.at[0], enc_exp_sem.at[1], {"exp": peer}).start()

        def dekv_over_exp():
            for peer in peers:
                remote(dekv, dekv_hbm.at[me, mine], enc_exp_sem.at[2], enc_exp_sem.at[3], {"exp": peer}).start()

        def dekv_local():
            return pltpu.make_async_copy(dekv, dekv_hbm.at[me, mine], local_sem.at[6])

        def exchange(i, factor):
            turned_ref[i] = factor.T
            for peer in everyone:
                remote(
                    turned_ref.at[i, block_of(peer, part), :], right.at[i, :, own_lanes], right_sem.at[i, 0], right_sem.at[i, 1],
                    {"seq": peer},
                ).start()
            right[i, :, own_lanes] = turned_ref[i, block_of(me, part), :]

        def multiply(i):
            wait_bytes(turned_ref.at[i, pl.ds(0, (seq_count - 1) * part), :], right_sem.at[i, 1])
            chunks[i].over_exp(nn(right[i], left[min(i, 3)].reshape(span, width)))

        slots = slots_ref[...]
        made = nn(slots, unpack_slots(made_back[...], capacity).astype(BF16))
        kept = jnp.sum(slots.astype(F32), axis=1, keepdims=True)
        gates = gates_ref[...]
        chosen = chosen_ref[...]
        picked = jnp.sum(gates * chosen, axis=1, keepdims=True)
        g = g_ref[...].astype(F32)
        out_ref[...] = (r2_ref[...] + (picked * kept) * made).astype(BF16)
        store(out_ref, out_hbm_ref)
        gate_grad = jnp.sum(g * made, axis=1, keepdims=True) * kept
        dl = gates * (chosen * gate_grad - picked * gate_grad)
        dl_high, dl_low = in_two(dl)
        x3 = x3_ref[...]
        small_a[...] = jnp.zeros_like(small_a)
        small_a[4 : 4 + experts, :width] = tn(dl_high, x3) + tn(dl_low, x3)
        dx3 = (
            nn(slots, unpack_slots(dx_back[...], capacity).astype(BF16))
            + nn(dl_high, router_ref[...]) + nn(dl_low, router_ref[...])
        )
        da, dw = rms_back(r2_ref[...], gains_ref[2:3, :], dx3)
        small_a[2:3, :width] = dw
        dr_ref[...] = g + da
        do2 = dr_ref[...].astype(BF16)
        doc_ref[...] = nt(do2, w_co[...]).astype(BF16)
        exchange(2, do2)
        oc_gather.relay()
        n2_gather.relay_far()
        x_gather.relay()

        @pl.loop(0, pairs, unroll=2)
        def _(p):
            lanes, value_lanes = pair_lanes(p), pair_lanes(pairs + p)
            doc_both = head_stack(doc_ref[:, lanes])
            weights = cross_prob[p]
            wide = weights.astype(F32)
            dp = nt(ekv[:, value_lanes], doc_both)
            dc = (wide * (dp - jnp.sum(wide * dp, axis=0, keepdims=True))).astype(BF16)
            dk = nn(dc, head_stack(qc_ref[:, lanes])).astype(BF16).reshape(4, 2, enc_part, LANES)
            dv = nn(weights, doc_both).astype(BF16).reshape(4, 2, enc_part, LANES)
            for k in range(2):
                e_out[k, :, :, lanes] = dk[:, k]
                e_out[k, :, :, value_lanes] = dv[:, k]
            dqc_ref[:, lanes] = (head_unstack(tn(ekv[:, lanes], dc), rows) * 0.125).astype(BF16)

        enc_scatter.start()
        dqc = dqc_ref[...]
        exchange(1, dqc)
        da, dw = rms_back(r1_ref[...], gains_ref[1:2, :], nt(dqc, w_cq[...]))
        small_a[1:2, :width] = dw
        enc_scatter.turn_on()
        dr_ref[...] = dr_ref[...] + da
        do1 = dr_ref[...].astype(BF16)
        doc_ref[...] = nt(do1, w_so[...]).astype(BF16)
        exchange(0, do1)
        oc_gather.relay_far()
        n2_gather.finish()
        o_gather.finish()

        ds_ref[pl.ds(0, rows), :] = jnp.zeros((rows, 2 * rows), BF16)
        flip = (
            lax.broadcasted_iota(jnp.int32, (2 * rows, 2 * rows), 0)
            + lax.broadcasted_iota(jnp.int32, (2 * rows, 2 * rows), 1)
            == 2 * rows - 1
        ).astype(BF16)

        def terms(p):
            return Scatter(place, t_out.at[p], t_pair.at[p], t_turn.at[p], t_side.at[p], rows // 2, term_sem.at[p])

        def pair_back(p):
            lanes, value_lanes = pair_lanes(p), pair_lanes(pairs + p)
            do_both = head_stack(doc_ref[:, lanes])
            weights = prob[p]
            wide = weights.astype(F32)
            dp = nt(kv_all[:, value_lanes], do_both)
            ds_wide = wide * (dp - jnp.sum(wide * dp, axis=0, keepdims=True))
            ds = ds_wide.astype(BF16)
            ds_ref[pl.ds(rows, span), :] = ds
            total_ref[pl.ds(p, 1), :] = jnp.sum(ds.astype(F32), axis=0, keepdims=True)
            dk = nn(ds, head_stack(q_ref[:, lanes])).astype(BF16).reshape(4, 2, rows, LANES)
            dv = nn(weights, do_both).astype(BF16).reshape(4, 2, rows, LANES)
            for k in range(2):
                t_out[p, k, :, :, :LANES] = dk[:, k]
                t_out[p, k, :, :, LANES:] = dv[:, k]
            terms(p).start()
            dqkv_ref[:, lanes] = (head_unstack(tn(kv_all[:, lanes], ds), rows) * 0.125).astype(BF16)
            turned = nn(flip, ds_ref[near, :])
            for h in range(2):
                one = turned[:, h * rows : (h + 1) * rows]
                one = jnp.concatenate([one, jnp.zeros_like(one)], axis=1)
                one = pltpu.roll(one, 1, 1, stride=1, stride_axis=0)
                diag_ref[pl.ds(2 * p + h, 1), :] = jnp.sum(one, axis=0, keepdims=True)

        def own_terms(p):
            total = terms(p).total()
            dqkv_ref[:, pair_lanes(pairs + p)] = total[:, :LANES].astype(BF16)
            dqkv_ref[:, pair_lanes(2 * pairs + p)] = total[:, LANES:].astype(BF16)

        @pl.loop(0, pairs)
        def _(t):
            pair_back(t)
            @pl.when(t >= 1)
            def _():
                terms(jnp.maximum(t - 1, 0)).turn_on()

            @pl.when(t >= 3)
            def _():
                terms(jnp.maximum(t - 3, 0)).side_on()

            @pl.when(t >= 5)
            def _():
                own_terms(jnp.maximum(t - 5, 0))

            @pl.when(t == 0)
            def _():
                oc_gather.finish()
                multiply(2)

            @pl.when(t == 1)
            def _():
                x_gather.relay_far()
                enc_scatter.side_on()

            @pl.when(t == 2)
            def _():
                multiply(1)

            @pl.when(t == 3)
            def _():
                multiply(0)
                chunks[2].back_over_exp()

            @pl.when(t == 4)
            def _():
                e_mine[...] = enc_scatter.total().astype(BF16).reshape(e_mine.shape)
                enc_over_exp()
                chunks[1].back_over_exp()


        last = pairs - 1
        terms(last).turn_on()
        terms(last - 2).side_on()
        exchange(3, dqkv_ref[:, :width])
        own_terms(last - 4)
        terms(last - 1).side_on()
        own_terms(last - 3)
        terms(last).side_on()
        own_terms(last - 2)
        multiply(3)
        chunks[0].back_over_exp()
        own_terms(last - 1)
        wait_bytes(e_exp, enc_exp_sem.at[1])
        total = e_mine[mine].astype(F32)
        for d in range(experts - 1):
            total = total + e_exp[d].astype(F32)
        dekv[...] = total.astype(BF16)
        dekv_local().start()
        dekv_over_exp()
        own_terms(last)

        dqkv = dqkv_ref[...]
        exchange(4, dqkv[:, width : 2 * width])
        exchange(5, dqkv[:, 2 * width :])
        chunks[2].spread()
        chunks[1].spread()

        x = x_ref[...].astype(F32)
        da, dw = rms_back(x, gains_ref[0:1, :], nt(dqkv, w_qkv[...]))
        small_a[0:1, :width] = dw
        dx_ref[...] = dr_ref[...] + da
        store(dx_ref, dx_hbm)
        heads = 2 * pairs
        table = diag_ref[:, 2 * rows - LANES :]
        totals = total_ref[...]
        first = jnp.sum(totals[:, :rows], axis=1, keepdims=True)
        second = jnp.sum(totals[:, rows:], axis=1, keepdims=True)
        head = lax.broadcasted_iota(jnp.int32, (heads, pairs), 0)
        pair = lax.broadcasted_iota(jnp.int32, (heads, pairs), 1)
        spread = lambda odd, v: jnp.dot(
            (head == 2 * pair + odd).astype(F32), v, precision=highest, preferred_element_type=F32
        )
        whole = spread(0, jnp.broadcast_to(first, (pairs, LANES))) + spread(1, jnp.broadcast_to(second, (pairs, LANES)))
        rest = whole - jnp.sum(table, axis=1, keepdims=True)
        lane = lax.broadcasted_iota(jnp.int32, table.shape, 1)
        table = table + jnp.where(lane == LANES - 1, rest, 0.0)
        bucket = lax.broadcasted_iota(jnp.int32, (LANES, LANES), 0)
        pick = (buckets_ref[...] == bucket).astype(F32)
        by_bucket = lax.dot_general(table, pick, (((1,), (1,)), ((), ())), precision=highest, preferred_element_type=F32)
        small_a[0:8, width : width + LANES] = by_bucket[0:8]
        small_a[0 : heads - 8, width + LANES :] = by_bucket[8:heads]
        s_pair = remote(small_a, small_pair, small_sem.at[0], small_sem.at[1], {"seq": place.partner})
        s_pair.start()

        x_gather.finish()
        g_gather.finish()
        g_gather.drain()
        parts = x_all[:, slot_rows:, : 2 * LANES].astype(F32).reshape(seq_count * GATE_ROWS, 2 * LANES).T
        for n in range(seq_count):
            gate = sum(parts[:slot_rows, n * GATE_ROWS + i : n * GATE_ROWS + i + 1] for i in range(3))
            g_all[n] = (g_all[n].astype(F32) * gate).astype(BF16)
        expert_units(0)
        multiply(4)
        multiply(5)
        chunks[3].back_over_exp()
        s_pair.wait_recv()
        small_b[...] = small_a[...] + small_pair[...]
        for d, device in enumerate((place.x, place.y, place.far)):
            remote(small_b, small_chip.at[d], small_sem.at[2], small_sem.at[3], {"seq": device}).start()
        expert_units(1)
        chunks[2].relay()
        chunks[0].spread()
        dekv_local().wait()
        wait_bytes(e_exp, enc_exp_sem.at[3])
        dekv_gather.start()
        chunks[4].back_over_exp()
        chunks[1].relay()
        chunks[5].back_over_exp()
        chunks[0].relay()
        genc_ref[...] = nt(dekv[...], w_ckv[...])
        store(genc_ref, genc_hbm)
        wait_bytes(small_chip, small_sem.at[3])
        small_c[...] = small_b[...] + small_chip[0] + small_chip[1] + small_chip[2]
        for d, peer in enumerate(peers):
            remote(small_c, small_exp.at[d], small_sem.at[4], small_sem.at[5], {"exp": peer}).start()
        chunks[2].cross()
        expert_units(2)
        dekv_gather.relay()
        chunks[3].spread()
        chunks[4].spread()
        chunks[5].spread()
        chunks[3].relay()
        expert_units(3)
        wait_bytes(e_exp, enc_exp_sem.at[0])
        wait_bytes(e_exp, enc_exp_sem.at[2])
        s_pair.wait_send()
        wait_bytes(small_chip, small_sem.at[2])
        for i in range(6):
            wait_bytes(turned_ref.at[i, pl.ds(0, (seq_count - 1) * part), :], right_sem.at[i, 0])
        for each in (gather, o_gather, n2_gather, oc_gather, x_gather, enc_scatter):
            each.drain()

        @pl.loop(0, pairs)
        def _(p):
            terms(p).drain()

        chunks[4].relay()
        chunks[5].relay()
        wait_bytes(gin_out, unit_recv.at[0])
        store(gin_in, gin_hbm)
        wait_bytes(small_exp, small_sem.at[5])
        total = small_c[...]
        for d in range(experts - 1):
            total = total + small_exp[d]
        small_out_ref[...] = total
        store(small_out_ref, small_hbm)
        for i in (1, 0):
            chunks[i].relay_far()
        dekv_gather.relay_far()
        for i in (3, 2, 4, 5):
            chunks[i].relay_far()
        for chunk in chunks:
            chunk.over_seq.finish()
        dekv_gather.finish()

        wait_bytes(gin_out, unit_send.at[0])
        wait_bytes(small_exp, small_sem.at[4])
        dekv_gather.drain()
        for chunk in chunks:
            chunk.drain()
        for copy in stores:
            copy.wait()

    pl.run_scoped(
        backward, bf(2, 4, enc_part, 2 * width), bf(pairs, 2, 4, rows, 2 * LANES), bf(6, part, width), bf(6, width, rows),
        bf(span + rows, 2 * rows), bf(4, part, own_hidden), f32(2 * LANES, own_hidden), bf(2, width, own_hidden), bf(2, own_hidden, width),
    )


def layer_call(seq_count, capacity, x, encoder, lengths, buckets, routes, gains, qkv, so, cq, ckv, co, rel, router, g, w_in,
               w_out):
    rows, width = x.shape
    span = seq_count * rows
    pairs = width // LANES
    heads = 2 * pairs
    enc_rows = encoder.shape[0]
    experts = router.shape[0]
    slot_rows = experts * capacity
    part = width // seq_count
    enc_part = enc_rows // seq_count
    own_enc = enc_part // experts
    hidden = w_in.shape[1]
    z = experts - 1
    quarter = (part // 2, width // (experts // 2))
    small = (8, width + 2 * LANES)
    packed = (experts, capacity * pairs, LANES)
    shape = jax.ShapeDtypeStruct
    dma = lambda *n: pltpu.SemaphoreType.DMA(n)
    bf = lambda *n: pltpu.VMEM(n, BF16)
    f32 = lambda *n: pltpu.VMEM(n, F32)
    wide = bf(rows, width)
    return pl.pallas_call(
        functools.partial(layer_kernel, seq_count, capacity),
        out_shape=(
            shape((rows, width), BF16), shape((rows, width), F32), shape((6, seq_count, part, width), BF16),
            shape((seq_count, experts, own_enc, 2 * width), BF16), shape(small, F32), shape((part, hidden), BF16),
            shape((hidden // seq_count, width), F32), shape((own_enc, width), F32),
        ),
        in_specs=[VMEM, ANY, SMEM, VMEM, VMEM, VMEM, ANY, ANY, ANY, ANY, ANY, VMEM, VMEM, VMEM, ANY, ANY],
        out_specs=(ANY,) * 8,
        scratch_shapes=[
            bf(4, seq_count, rows, width), bf(span, 2 * width), bf(pairs, span, 2 * rows), bf(pairs, enc_rows, 2 * rows),
            bf(enc_rows, 2 * width), bf(*qkv.shape), bf(*so.shape), bf(*cq.shape), bf(*ckv.shape), bf(*co.shape),
            f32(heads, 2 * LANES), bf(seq_count, slot_rows + GATE_ROWS, width), bf(seq_count, slot_rows, width),
            bf(experts, capacity * pairs + GATE_ROWS, LANES), bf(*packed), bf(*packed), bf(*packed),
            wide, wide, wide, f32(rows, width), f32(rows, width), f32(rows, experts), f32(rows, experts), bf(rows, slot_rows),
            f32(rows, width), wide, wide, bf(rows, 3 * width), f32(heads, 2 * rows), f32(pairs, 2 * rows),
            bf(4, enc_part, 2 * width), bf(2, enc_part // 2, 2 * width), bf(2, enc_part, 2 * width),
            bf(experts, own_enc, 2 * width), bf(z, own_enc, 2 * width), bf(own_enc, 2 * width),
            bf(pairs, 4, rows, 2 * LANES), bf(pairs, 2, rows // 2, 2 * LANES), bf(pairs, 2, rows, 2 * LANES),
            wide, f32(rows, width), f32(hidden // seq_count, width), f32(own_enc, width), f32(*small),
            bf(6, z, *quarter), bf(6, *quarter), bf(6, part, span), bf(part, hidden),
            f32(*small), f32(*small), f32(*small), f32(*small), f32(3, *small), f32(z, *small),
            dma(12), dma(7), dma(6), dma(6), dma(7), dma(6, 4), dma(4, 2), dma(5), dma(4), dma(pairs, 5), dma(6, 5),
            dma(6), dma(6, 4), dma(6, 2), dma(1), dma(1), dma(6),
        ],
        compiler_params=pltpu.CompilerParams(collective_id=0, has_side_effects=True, vmem_limit_bytes=63 << 20),
        name="layer",
    )(x, encoder, lengths, buckets, routes, gains, qkv, so, cq, ckv, co, rel, router, g, w_in, w_out)


def finish_kernel(
    experts, weights_hbm, dekv_hbm, enc_hbm, small_ref, layer_hbm, dx_hbm, genc_hbm, gin_ref, gout_hbm,
    layer_out, dx_out, genc_out, gains_out, qkv_hbm, so_hbm, cq_hbm, ckv_hbm, co_hbm, rel_out, router_out, gin_out, gout_out,
    weights, dekv, enc, squares, qkv, ckv, layer, dx, genc, gin, gout, load_sem, sem,
):
    seq_count, part, width = weights.shape[1:]
    loads = [pltpu.make_async_copy(weights_hbm.at[i], weights.at[i], load_sem.at[i]) for i in range(6)] + [
        pltpu.make_async_copy(dekv_hbm, dekv, load_sem.at[6]), pltpu.make_async_copy(enc_hbm, enc, load_sem.at[7])
    ]
    through = ((gout_hbm, gout, gout_out), (dx_hbm, dx, dx_out), (layer_hbm, layer, layer_out), (genc_hbm, genc, genc_out))
    loads += [pltpu.make_async_copy(src, held, load_sem.at[8 + i]) for i, (src, held, _) in enumerate(through)]
    for load in loads[8:] + loads[6:8] + loads[:6]:
        load.start()
    copies = []

    def store(src, dst):
        copy = pltpu.make_async_copy(src, dst, sem.at[len(copies)])
        copy.start()
        copies.append(copy)

    gains_out[...] = small_ref[0:3, :width]
    router_out[...] = small_ref[4 : 4 + experts, :width]
    heads, buckets = rel_out.shape
    rel_out[0:8, :] = small_ref[0:8, width : width + buckets]
    rel_out[8:heads, :] = small_ref[0 : heads - 8, width + LANES : width + LANES + buckets]
    gin[...] = gin_ref[...].astype(F32)
    store(gin, gin_out)

    for i, (_, held, out) in enumerate(through):
        loads[8 + i].wait()
        store(held, out)
    loads[6].wait()
    loads[7].wait()
    for n in range(2):
        at = slice(n * width, (n + 1) * width)
        ckv[:, at] = tn(enc[...], dekv[...].reshape(enc.shape[0], 2 * width)[:, at])
        store(ckv.at[:, at], ckv_hbm.at[:, at])
    def turn(i, target, at):
        loads[i].wait()
        for block in range(width // LANES):
            rows = slice(block * LANES, (block + 1) * LANES)
            target[:, at + block * LANES : at + (block + 1) * LANES] = (
                weights[i].reshape(seq_count * part, width)[rows, :].T.astype(F32)
            )

    for i, out in enumerate((so_hbm, cq_hbm, co_hbm)):
        turn(i, squares.at[i], 0)
        store(squares.at[i], out)
    for i in range(3):
        at = slice(i * width, (i + 1) * width)
        turn(3 + i, qkv, i * width)
        store(qkv.at[:, at], qkv_hbm.at[:, at])
    for copy in copies:
        copy.wait()


def finish_call(heads, buckets, experts, weights, dekv, enc, small, layer, dx, genc, gin, gout):
    seq_count, part, width = weights.shape[1:]
    shape = jax.ShapeDtypeStruct
    f32 = lambda *n: shape(n, F32)
    return pl.pallas_call(
        functools.partial(finish_kernel, experts),
        out_shape=(
            shape(layer.shape, BF16), f32(*dx.shape), f32(*genc.shape), f32(3, width), f32(width, 3 * width), f32(width, width),
            f32(width, width), f32(width, 2 * width), f32(width, width), f32(heads, buckets), f32(experts, width),
            f32(*gin.shape), f32(*gout.shape),
        ),
        in_specs=[ANY, ANY, ANY, VMEM, ANY, ANY, ANY, VMEM, ANY],
        out_specs=(ANY, ANY, ANY, VMEM, ANY, ANY, ANY, ANY, ANY, VMEM, VMEM, ANY, ANY),
        scratch_shapes=[
            pltpu.VMEM(weights.shape, BF16), pltpu.VMEM(dekv.shape, BF16), pltpu.VMEM(enc.shape, BF16),
            pltpu.VMEM((3, width, width), F32), pltpu.VMEM((width, 3 * width), F32), pltpu.VMEM((width, 2 * width), F32),
            pltpu.VMEM(layer.shape, BF16), pltpu.VMEM(dx.shape, F32), pltpu.VMEM(genc.shape, F32), pltpu.VMEM(gin.shape, F32),
            pltpu.VMEM(gout.shape, F32), pltpu.SemaphoreType.DMA((13,)), pltpu.SemaphoreType.DMA((13,)),
        ],
        compiler_params=pltpu.CompilerParams(vmem_limit_bytes=60 << 20),
        name="finish",
    )(weights, dekv, enc, small, layer, dx, genc, gin, gout)


def fused(inputs, encoder, lengths, buckets, routes, norm_gains, self_qkv, self_out, cross_q, cross_kv, cross_out,
          rel_bias, router, expert_in, expert_out, cotangent):
    seq_count = lax.axis_size("seq")
    rows = inputs.shape[1]
    experts = router.shape[1]
    capacity = 5 * rows // (4 * experts)
    (layer_out, grad_input, weights, dekv, small, gin, gout, grad_encoder) = layer_call(
        seq_count, capacity, inputs[0], encoder, lengths, buckets[None, :], routes.reshape(1, rows), norm_gains, self_qkv,
        self_out, cross_q, cross_kv, cross_out, rel_bias.T, router.T, cotangent[0], expert_in[0], expert_out[0])
    (layer_out, grad_input, grad_encoder, gains, g_qkv, g_so, g_cq, g_ckv, g_co, g_rel, g_router, gin, gout) = finish_call(
        rel_bias.shape[1], rel_bias.shape[0], experts, weights, dekv, encoder, small, layer_out, grad_input, grad_encoder, gin,
        gout)
    return (layer_out[None], grad_input[None], grad_encoder, gains, g_qkv, g_so, g_cq, g_ckv, g_co, g_rel.T, g_router.T,
            gin[None], gout[None])


def on_device(*operands):
    if lax.axis_size("seq") == 8 and lax.axis_size("exp") == 4 and operands[0].shape[1] == 128:
        return fused(*operands)
    return streamed(*operands)


def solution(mesh):
    in_specs = (
        P("exp", "seq", None),
        P(),
        P("exp", None),
        P(),
        P("exp", "seq", None),
        P(),
        P(),
        P(),
        P(),
        P(),
        P(),
        P(),
        P(),
        P("exp", None, None),
        P("exp", None, None),
        P("exp", "seq", None),
    )
    out_specs = (
        P("exp", "seq", None),
        P("exp", "seq", None),
        P(("seq", "exp"), None),
        P(),
        P(),
        P(),
        P(),
        P(),
        P(),
        P(),
        P(),
        P("exp", "seq", None),
        P("exp", "seq", None),
    )
    return jax.shard_map(
        on_device, mesh=mesh, in_specs=in_specs, out_specs=out_specs, check_vma=False
    )
```
